128 devices in a mesh: grp: 8 (over y, core), sub: 8 (over x_hi, z), chip: 2 (over x_lo).
Axes of the slice: x: 4 (x_hi: 2, x_lo: 2; x = x_hi * 2 + x_lo), y: 4, z: 4, core: 2. Of those that a mesh axis runs over, the one named last changes fastest.
Arguments:
- right_side: float32 [64, 1048576], P(None, ('grp', 'sub', 'chip')), may hold values from -6 to 6
- diag_tiles: float32 [8192, 128, 128], P(('grp', 'sub', 'chip')), as said below
- remote_tiles: float32 [2048, 2, 128, 128], P(('grp', 'sub', 'chip')), as said below
- slot_counts: int32 [128, 16], P(('grp', 'sub', 'chip')), may hold values from 0 to 2, as said below
- slot_blocks: int32 [128, 16, 2], P(('grp', 'sub', 'chip')), may hold values from 0 to 63, as said below
- fine_map: int32 [1048576], P(('grp', 'sub', 'chip')), may hold values from 0 to 63, as said below
- coarse_map: int32 [8192], P('grp'), may hold values from 0 to 63, as said below
- level1_ops: float32 [8, 1024, 1024], P('grp'), as said below
- coarsest_inverse: float32 [512, 512], replicated, as said below
Outputs:
- solution: float32 [64, 1048576], P(None, ('grp', 'sub', 'chip'))
- residual: float32 [64, 1048576], P(None, ('grp', 'sub', 'chip'))
The draws below stay inside these ranges and needn't reach their ends.
Inputs may be any that keep to these rules, and one draw needn't show every extreme that they name: slot_counts[d, q] equals slot_counts[e, i] for the devices d = g * 16 + i and e = g * 16 + q of one group; it is zero for q = i. `slot_blocks`: the 32 slots of one device name distinct tiles. remote_tiles[d * 16 + q, c] is the transpose of remote_tiles[e * 16 + i, c] for d = g * 16 + i and e = g * 16 + q; entries are nonnegative. `fine_map`: each aggregate holds the same number of vertices. `coarse_map`: each aggregate holds the same number of level-one vertices. `diag_tiles`: symmetric; each diagonal entry exceeds the sum of the magnitudes of the other entries of its row together with the live coupling weights of its vertex. `level1_ops`: symmetric, diagonally dominant by rows. `coarsest_inverse`: symmetric, diagonally dominant by rows.
All inputs are finite; a program needn't handle non-finite values.
Results may differ from the reference program's by a relative error of at most 0.0003.
Values sent between devices are 32-bit elements; how exact they have to be, the bound alone decides.
No kernel may reach another device: no remote copies, remote signals or barrier semaphores. Data moves between devices by JAX's collectives and lax.ppermute only.
A program may use at most 128 MiB of HBM per device.

```python
import math
import jax
import jax.numpy as jnp
from jax import lax

COLS = 64
TILE = 128
BLK = 64
CAP = 2
AGG_DEV = 64
AGG2 = 64
ITERS = 2
NP = 16
V_DEV = 8192
NV = 1048576
NC1 = 1024
NC2 = 512
DEVICES = 128


def shared_remote(key):
    key = jax.random.fold_in(key, 12)
    devs = jnp.arange(DEVICES, dtype=jnp.int32)[:, None, None]
    peer = jnp.arange(NP, dtype=jnp.int32)[None, :, None]
    slot = jnp.arange(CAP, dtype=jnp.int32)[None, None, :]
    own_slot = devs % NP
    group = devs // NP
    lower = jnp.minimum(own_slot, peer)
    upper = jnp.maximum(own_slot, peer)
    pair = ((group * NP + lower) * NP + upper) * CAP + slot
    flip = jnp.broadcast_to(own_slot > peer, pair.shape)

    def single(number, turned):
        tile_values = jax.random.uniform(jax.random.fold_in(key, number), (TILE, TILE), jnp.float32, 0.0, 2.0 / TILE)
        return jnp.where(turned, tile_values.T, tile_values)
    tiles = jax.vmap(single)(pair.reshape(-1), flip.reshape(-1))
    return tiles.reshape(DEVICES * NP, CAP, TILE, TILE)


def shared_counts(key):
    key = jax.random.fold_in(key, 13)
    groups = DEVICES // NP
    raw = jax.random.randint(key, (groups, NP, NP), 0, CAP + 1)
    row = jnp.arange(NP, dtype=jnp.int32)[:, None]
    col = jnp.arange(NP, dtype=jnp.int32)[None, :]
    sym = jnp.where(row < col, raw, jnp.swapaxes(raw, 1, 2))
    sym = jnp.where(row == col, 0, sym)
    marked = (row == 0) & (col == 1) | (row == 1) & (col == 0)
    sym = jnp.where(marked, CAP, sym)
    return sym.reshape(DEVICES, NP).astype(jnp.int32)


def shared_blocks(key):
    key = jax.random.fold_in(key, 14)
    first, second = jax.random.split(key)
    keys = jax.random.split(first, DEVICES)
    perms = jax.vmap(lambda single: jax.random.permutation(single, BLK))(keys).astype(jnp.int32)
    position = jnp.arange(BLK, dtype=jnp.int32)[None, :]
    top = BLK - 1
    swapped = jnp.where(perms == top, perms[:, 0:1], jnp.where(position == 0, top, perms))
    swapped = jnp.where(swapped == 0, swapped[:, 1:2], jnp.where(position == 1, 0, swapped))
    chosen = jax.random.randint(second, (), 0, DEVICES)
    device_ids = jnp.arange(DEVICES, dtype=jnp.int32)[:, None]
    perms = jnp.where(device_ids == chosen, swapped, perms)
    return perms[:, :NP * CAP].reshape(DEVICES, NP, CAP).astype(jnp.int32)


def draw_diag_tiles(key, part):
    own_key = jax.random.fold_in(key, 11)
    first, second, third = jax.random.split(own_key, 3)
    count = DEVICES * BLK
    base = jax.random.uniform(first, (count, TILE, TILE), jnp.float32, 0.0, 2.0 / TILE)
    scales = jnp.exp(jax.random.uniform(second, (count, TILE), jnp.float32, math.log(0.7), math.log(1.4)))
    unit = jnp.eye(TILE, dtype=jnp.float32)
    weights = 0.5 * (base + jnp.swapaxes(base, 1, 2)) * (1.0 - unit) * scales[:, :, None] * scales[:, None, :]
    inner = jnp.sum(weights, axis=2)
    column_sums = jnp.sum(shared_remote(key), axis=2).reshape(DEVICES, NP * CAP, TILE)
    counts = shared_counts(key)
    live = (jnp.arange(CAP, dtype=jnp.int32)[None, None, :] < counts[:, :, None]).astype(jnp.float32).reshape(DEVICES, NP * CAP)
    blocks = shared_blocks(key).reshape(DEVICES, NP * CAP)
    onehot = (blocks[:, :, None] == jnp.arange(BLK, dtype=jnp.int32)[None, None, :]).astype(jnp.float32)
    extra = jnp.einsum('dcb,dct->dbt', onehot * live[:, :, None], column_sums, precision=lax.Precision.HIGHEST)
    factor = jax.random.uniform(third, (count, TILE), jnp.float32, 1.02, 1.06)
    degree = (inner + extra.reshape(count, TILE)) * factor
    return degree[:, :, None] * unit - weights


def draw_remote_tiles(key, part):
    return shared_remote(key)


def draw_slot_counts(key, part):
    return shared_counts(key)


def draw_slot_blocks(key, part):
    return shared_blocks(key)


def draw_fine_map(key, part):
    key = jax.random.fold_in(key, 15)
    keys = jax.random.split(key, DEVICES)
    perms = jax.vmap(lambda single: jax.random.permutation(single, V_DEV))(keys)
    return (perms % AGG_DEV).reshape(-1).astype(jnp.int32)


def draw_coarse_map(key, part):
    key = jax.random.fold_in(key, 16)
    groups = DEVICES // NP
    keys = jax.random.split(key, groups)
    perms = jax.vmap(lambda single: jax.random.permutation(single, NC1))(keys)
    return (perms % AGG2).reshape(-1).astype(jnp.int32)


def draw_level1_ops(key, part):
    key = jax.random.fold_in(key, 17)
    first, second = jax.random.split(key)
    groups = DEVICES // NP
    base = jax.random.uniform(first, (groups, NC1, NC1), jnp.float32, 0.0, 2.0 / NC1)
    unit = jnp.eye(NC1, dtype=jnp.float32)
    weights = 0.5 * (base + jnp.swapaxes(base, 1, 2)) * (1.0 - unit)
    degree = jax.random.uniform(second, (groups, NC1), jnp.float32, 2.5, 4.0)
    return degree[:, :, None] * unit - weights


def draw_coarsest_inverse(key, part):
    key = jax.random.fold_in(key, 18)
    first, second = jax.random.split(key)
    base = jax.random.uniform(first, (NC2, NC2), jnp.float32, -0.4 / NC2, 0.4 / NC2)
    unit = jnp.eye(NC2, dtype=jnp.float32)
    weights = 0.5 * (base + base.T) * (1.0 - unit)
    degree = jax.random.uniform(second, (NC2,), jnp.float32, 0.5, 1.5)
    return degree[:, None] * unit + weights


def block_levels(key, shape, cuts, low, high):
    gain, own = 1.0, jax.random.fold_in(key, 6)
    for dim, parts in cuts:
        heights = jnp.exp(jax.random.uniform(jax.random.fold_in(own, dim), (parts,), jnp.float32, low / len(cuts), high / len(cuts)))
        gain = gain * jnp.repeat(heights, shape[dim] // parts).reshape([-1 if axis == dim else 1 for axis in range(len(shape))])
    return gain


def centred(rng, shape, deviation, reach, pieces=(), kind=jnp.bfloat16):
    values = deviation * jax.random.normal(rng, shape, jnp.float32)
    if pieces:
        values = values * block_levels(rng, shape, pieces, -0.22, 0.18)
    return jnp.clip(values, -reach, reach).astype(kind)


def setup_inputs(seed: int = 0) -> dict:
    seeds = jax.random.split(jax.random.key(seed), 10)
    right_side = centred(seeds[0], (COLS, NV), 1.0, 6.0, ((1, 128),), jnp.float32)
    diag_tiles = draw_diag_tiles(jax.random.fold_in(seeds[9], 71), 0)
    remote_tiles = draw_remote_tiles(jax.random.fold_in(seeds[9], 71), 0)
    slot_counts = draw_slot_counts(jax.random.fold_in(seeds[9], 71), 0)
    slot_blocks = draw_slot_blocks(jax.random.fold_in(seeds[9], 71), 0)
    fine_map = draw_fine_map(jax.random.fold_in(seeds[9], 71), 0)
    coarse_map = draw_coarse_map(jax.random.fold_in(seeds[9], 71), 0)
    level1_ops = draw_level1_ops(jax.random.fold_in(seeds[9], 71), 0)
    coarsest_inverse = draw_coarsest_inverse(jax.random.fold_in(seeds[9], 71), 0)
    return {"right_side": right_side, "diag_tiles": diag_tiles, "remote_tiles": remote_tiles, "slot_counts": slot_counts, "slot_blocks": slot_blocks, "fine_map": fine_map, "coarse_map": coarse_map, "level1_ops": level1_ops, "coarsest_inverse": coarsest_inverse}


OMEGA = 0.6
HIGH = lax.Precision.HIGHEST


def fine_apply(vector, diag_tiles, remote_tiles, slot_counts, slot_blocks):
    devs = jnp.arange(DEVICES, dtype=jnp.int32)
    shaped = vector.reshape(COLS, DEVICES, BLK, TILE)
    result = jnp.einsum("kdbt,dbts->kdbs", shaped, diag_tiles.reshape(DEVICES, BLK, TILE, TILE), precision=HIGH)
    peer_ids = (devs // NP * NP)[:, None] + jnp.arange(NP, dtype=jnp.int32)[None, :]
    own_slot = devs % NP
    partner_blocks = slot_blocks[peer_ids, own_slot[:, None], :]
    arrived = shaped[:, peer_ids[:, :, None], partner_blocks, :]
    live = (jnp.arange(CAP, dtype=jnp.int32)[None, None, :] < slot_counts[:, :, None]).astype(jnp.float32)
    coupled = jnp.einsum("kdqcu,dqcuv->kdqcv", arrived, remote_tiles.reshape(DEVICES, NP, CAP, TILE, TILE), precision=HIGH)
    coupled = coupled * live[None, :, :, :, None]
    result = result.at[:, devs[:, None, None], slot_blocks, :].add(-coupled)
    return result.reshape(COLS, NV)


def reference(right_side, diag_tiles, remote_tiles, slot_counts, slot_blocks, fine_map, coarse_map, level1_ops, coarsest_inverse):
    groups = DEVICES // NP
    fine_diag = jnp.diagonal(diag_tiles, axis1=1, axis2=2).reshape(NV)
    coarse_index = jnp.arange(NV, dtype=jnp.int32) // V_DEV * AGG_DEV + fine_map
    coarsest_index = jnp.arange(groups * NC1, dtype=jnp.int32) // NC1 * AGG2 + coarse_map
    level_diag = jnp.diagonal(level1_ops, axis1=1, axis2=2)

    def apply_fine(vector):
        return fine_apply(vector, diag_tiles, remote_tiles, slot_counts, slot_blocks)

    def apply_level(values):
        return jnp.einsum("kgn,gnm->kgm", values, level1_ops, precision=HIGH)

    def level_one(coarse_resid):
        grouped = coarse_resid.reshape(COLS, groups, NC1)
        guess = OMEGA * grouped / level_diag
        left = (grouped - apply_level(guess)).reshape(COLS, groups * NC1)
        lowest = jax.ops.segment_sum(left.T, coarsest_index, num_segments=NC2).T
        correction = jnp.dot(lowest, coarsest_inverse, precision=HIGH)
        guess = guess + correction[:, coarsest_index].reshape(COLS, groups, NC1)
        guess = guess + OMEGA * (grouped - apply_level(guess)) / level_diag
        return guess.reshape(COLS, groups * NC1)

    def precondition(resid):
        guess = OMEGA * resid / fine_diag
        left = resid - apply_fine(guess)
        coarse_resid = jax.ops.segment_sum(left.T, coarse_index, num_segments=DEVICES * AGG_DEV).T
        guess = guess + level_one(coarse_resid)[:, coarse_index]
        return guess + OMEGA * (resid - apply_fine(guess)) / fine_diag

    solution = jnp.zeros((COLS, NV), jnp.float32)
    residual = right_side
    search = precondition(residual)
    rho = jnp.sum(residual * search, axis=1)
    for step in range(ITERS):
        image = apply_fine(search)
        alpha = rho / jnp.sum(search * image, axis=1)
        solution = solution + alpha[:, None] * search
        residual = residual - alpha[:, None] * image
        if step + 1 < ITERS:
            pre = precondition(residual)
            rho_next = jnp.sum(residual * pre, axis=1)
            search = pre + (rho_next / rho)[:, None] * search
            rho = rho_next
    return solution, residual
```

```python
import functools

import jax
import jax.numpy as jnp
from jax import lax
from jax.experimental import pallas as pl
from jax.experimental.pallas import tpu as pltpu
from jax.sharding import PartitionSpec as P

OMEGA = 0.6
F32 = jnp.float32
BF16 = jnp.bfloat16
COLS = 64
TILE = 128
BLK = 64
SLOTS = 32
PEERS = 16
GROUPS = 8
AGG = 64
NC1 = 1024
STEP = 4
NSTEP = SLOTS // STEP
SIDE = 72
ROWS = 40
VMEM_LIMIT = 56 * 1024 * 1024

GROUP_AXES = ("sub", "chip")
ALL_AXES = ("grp", "sub", "chip")


def params():
    return pltpu.CompilerParams(vmem_limit_bytes=VMEM_LIMIT)


def cost(flops, moved):
    return pl.CostEstimate(flops=flops, bytes_accessed=moved, transcendentals=0)


def split2(x):
    hi = x.astype(BF16)
    lo = (x - hi.astype(F32)).astype(BF16)
    return hi, lo


def split3(x):
    hi = x.astype(BF16)
    rest = x - hi.astype(F32)
    mid = rest.astype(BF16)
    lo = (rest - mid.astype(F32)).astype(BF16)
    return hi, mid, lo


def dot(a, b):
    return jnp.dot(a, b, preferred_element_type=F32)


def dot_nt(a, b):
    return lax.dot_general(a, b, (((1,), (1,)), ((), ())), preferred_element_type=F32)


def mm(x, whi, wlo, nt=False):
    op = dot_nt if nt else dot
    rows = x.shape[0]
    hi, lo = split2(x)
    both = op(jnp.concatenate([hi, lo], axis=0), whi)
    return both[:rows] + both[rows:] + op(hi, wlo)


def mm_exact(x, w, nt=False):
    op = dot_nt if nt else dot
    rows = x.shape[0]
    hi, mid, lo = split3(x)
    three = op(jnp.concatenate([hi, mid, lo], axis=0), w)
    return three[:rows] + three[rows : 2 * rows] + three[2 * rows :]


def exact_mm(w, x):
    hi, mid, lo = split3(x)
    return dot(w, hi) + dot(w, mid) + dot(w, lo)


def eye_mask():
    r = lax.broadcasted_iota(jnp.int32, (TILE, TILE), 0)
    c = lax.broadcasted_iota(jnp.int32, (TILE, TILE), 1)
    return r, c


def tile_diag(tile):
    r, c = eye_mask()
    return jnp.sum(jnp.where(r == c, tile, 0.0), axis=0, keepdims=True)


def off_diag(tile):
    r, c = eye_mask()
    return jnp.where(r == c, 0.0, tile)


def one_hot(row):
    r = lax.broadcasted_iota(jnp.int32, (AGG, row.shape[1]), 0)
    return jnp.where(r == row, 1.0, 0.0).astype(BF16)


def pack_rows(x):
    wide = jnp.concatenate([x[:32], x[32:]], axis=1)
    return wide


def column(row):
    return jnp.broadcast_to(row, (TILE, TILE)).T


def boundary_kernel(slots, *refs):
    tiles, cols, maps, first, second = refs[:STEP], refs[STEP : 2 * STEP], refs[2 * STEP], refs[-2], refs[-1]
    step = pl.program_id(0)
    for i in range(STEP):
        tile = tiles[i][0]
        diag = tile_diag(tile)
        first[i] = OMEGA * cols[i][...] / diag
        r = lax.broadcasted_iota(jnp.int32, (64, TILE), 0)
        c = lax.broadcasted_iota(jnp.int32, (64, TILE), 1)
        below = pltpu.roll(tile[64:], 64, 1)
        second[i, 0:64] = jnp.where((c < 64) & (r > c), below, tile[:64])
        row = maps[slots[step * STEP + i]].astype(F32)
        r8 = lax.broadcasted_iota(jnp.int32, (8, TILE), 0)
        second[i, 64:72] = jnp.where(r8 == 0, diag, jnp.where(r8 == 1, row, 0.0))


def boundary_pack(slot_list, diag_tiles, right_side, maps):
    def tile_spec(i):
        return pl.BlockSpec((1, TILE, TILE), lambda s, p: (p[s * STEP + i], 0, 0))

    def col_spec(i):
        return pl.BlockSpec((COLS, TILE), lambda s, p: (0, p[s * STEP + i]))

    grid = pltpu.PrefetchScalarGridSpec(
        num_scalar_prefetch=1,
        grid=(NSTEP,),
        in_specs=[tile_spec(i) for i in range(STEP)]
        + [col_spec(i) for i in range(STEP)]
        + [pl.BlockSpec((BLK, 1, TILE), lambda s, p: (0, 0, 0))],
        out_specs=[
            pl.BlockSpec((STEP, COLS, TILE), lambda s, p: (s, 0, 0)),
            pl.BlockSpec((STEP, SIDE, TILE), lambda s, p: (s, 0, 0)),
        ],
    )
    return pl.pallas_call(
        boundary_kernel,
        grid_spec=grid,
        out_shape=[
            jax.ShapeDtypeStruct((SLOTS, COLS, TILE), F32),
            jax.ShapeDtypeStruct((SLOTS, SIDE, TILE), F32),
        ],
        compiler_params=params(),
        name="boundary_pack",
    )(slot_list, *([diag_tiles] * STEP), *([right_side] * STEP), maps)


def local_kernel(perm, counts, *refs):
    n = 2 * STEP
    tiles, cols = refs[:n], refs[n : 2 * n]
    remote, maps = refs[2 * n : 2 * n + 2]
    b_slot, b_rest, d_slot, d_rest, hi_rest, lo_rest, rs, rr = refs[2 * n + 2 :]
    step = pl.program_id(0)

    @pl.when(step == 0)
    def _():
        rr[...] = jnp.zeros_like(rr)

    total = rr[...]
    for i in range(n):
        tile = tiles[i][0]
        diag = tile_diag(tile)
        off_hi, off_lo = split2(off_diag(tile))
        b = cols[i][...]
        x = OMEGA * b / diag
        y = b - OMEGA * b - mm(x, off_hi, off_lo)
        slot = i < STEP
        k = i % STEP
        index = perm[(0 if slot else SLOTS) + step * STEP + k]
        spread = one_hot(maps[index])
        total = total + mm_exact(y, spread, nt=True)
        if slot:
            b_slot[k] = b
            d_slot[k] = diag
            j = step * STEP + k
            live = (j % 2) < counts[j // 2]
            rem = remote[k] * jnp.where(live, 1.0, 0.0)
            hi, lo = split2(rem)
            rs[k] = dot_nt(spread, hi) + dot_nt(spread, lo)
        else:
            b_rest[k] = b
            d_rest[k] = diag
            hi_rest[k] = off_hi
            lo_rest[k] = off_lo
    rr[...] = total


def local_part(perm, counts, diag_tiles, right_side, remote, maps):
    def where(i):
        return (0 if i < STEP else SLOTS) + i % STEP

    def tile_spec(i):
        return pl.BlockSpec((1, TILE, TILE), lambda s, p, c: (p[s * STEP + where(i)], 0, 0))

    def col_spec(i):
        return pl.BlockSpec((COLS, TILE), lambda s, p, c: (0, p[s * STEP + where(i)]))

    def out(*shape):
        return pl.BlockSpec((STEP,) + shape, lambda s, p, c: (s, 0, 0))

    n = 2 * STEP
    grid = pltpu.PrefetchScalarGridSpec(
        num_scalar_prefetch=2,
        grid=(NSTEP,),
        in_specs=[tile_spec(i) for i in range(n)]
        + [col_spec(i) for i in range(n)]
        + [
            pl.BlockSpec((STEP, TILE, TILE), lambda s, p, c: (s, 0, 0)),
            pl.BlockSpec((BLK, 1, TILE), lambda s, p, c: (0, 0, 0)),
        ],
        out_specs=[
            out(COLS, TILE),
            out(COLS, TILE),
            out(1, TILE),
            out(1, TILE),
            out(TILE, TILE),
            out(TILE, TILE),
            out(AGG, TILE),
            pl.BlockSpec((COLS, AGG), lambda s, p, c: (0, 0)),
        ],
    )

    def sds(shape, dtype=F32):
        return jax.ShapeDtypeStruct((SLOTS,) + shape, dtype)

    return pl.pallas_call(
        local_kernel,
        grid_spec=grid,
        out_shape=[
            sds((COLS, TILE)),
            sds((COLS, TILE)),
            sds((1, TILE)),
            sds((1, TILE)),
            sds((TILE, TILE), BF16),
            sds((TILE, TILE), BF16),
            sds((AGG, TILE)),
            jax.ShapeDtypeStruct((COLS, AGG), F32),
        ],
        compiler_params=params(),
        cost_estimate=cost(2 * 64 * 3 * 64 * 128 * 128, 16 << 20),
        name="local_part",
    )(perm, counts, *([diag_tiles] * n), *([right_side] * n), remote, maps)


def coarse_kernel(op, cmap, g_out, d_out):
    spread = one_hot(cmap[...])
    product = exact_spread(spread, op)
    pieces = []
    for i in range(NC1 // TILE):
        pieces.append(tile_diag(op[i * TILE : (i + 1) * TILE, i * TILE : (i + 1) * TILE]))
    diag = jnp.concatenate(pieces, axis=1)
    inverse = 1.0 / diag
    d_out[...] = inverse
    g_out[...] = spread.astype(F32) - OMEGA * product * inverse


def exact_spread(spread, op):
    total = None
    for i in range(NC1 // 256):
        rows = slice(i * 256, (i + 1) * 256)
        hi, lo = split2(op[rows, :])
        part = dot(spread[:, rows], hi) + dot(spread[:, rows], lo)
        total = part if total is None else total + part
    return total


def coarse_setup(op, cmap):
    return pl.pallas_call(
        coarse_kernel,
        out_shape=[jax.ShapeDtypeStruct((AGG, NC1), F32), jax.ShapeDtypeStruct((1, NC1), F32)],
        compiler_params=params(),
        cost_estimate=cost(2 * 2 * 64 * 1024 * 1024, 5 << 20),
        name="coarse_setup",
    )(op, cmap)


def first_restrict_kernel(arrived, rs, rr, out):
    total = rr[...]
    for j in range(SLOTS):
        hi, lo = split2(rs[j])
        total = total + mm(arrived[j], hi, lo, nt=True)
    packed = pack_rows(total)
    for q in range(PEERS):
        out[q, 0:32] = packed
        out[q, 32:40] = jnp.zeros((8, TILE), F32)


def first_restrict(arrived, rs, rr):
    return pl.pallas_call(
        first_restrict_kernel,
        out_shape=jax.ShapeDtypeStruct((PEERS, ROWS, TILE), F32),
        compiler_params=params(),
        name="first_restrict",
    )(arrived, rs, rr)


def pair_kernel(perm, counts, *refs):
    tiles, side, remote, hi_out, lo_out, diag_out, map_out = (refs[:STEP],) + tuple(refs[STEP:])
    step = pl.program_id(0)
    r = lax.broadcasted_iota(jnp.int32, (64, TILE), 0)
    c = lax.broadcasted_iota(jnp.int32, (64, TILE), 1)
    for k in range(STEP):
        own = off_diag(tiles[k][0])
        packed = side[k, 0:64]
        top = jnp.where((c >= 64) | (r < c), packed, 0.0)
        bottom = pltpu.roll(jnp.where((c < 64) & (r > c), packed, 0.0), 64, 1)
        half = jnp.concatenate([top, bottom], axis=0)
        other = half + half.T
        j = step * STEP + k
        live = (j % 2) < counts[j // 2]
        rem = remote[k] * jnp.where(live, -1.0, 0.0)
        block = jnp.concatenate(
            [jnp.concatenate([own, rem.T], axis=1), jnp.concatenate([rem, other], axis=1)], axis=0
        )
        hi, lo = split2(block)
        hi_out[k] = hi
        lo_out[k] = lo
        diag_out[k] = side[k, 64:65]
        map_out[k] = side[k, 65:66].astype(jnp.int32)


def pair_setup(perm, counts, diag_tiles, side, remote):
    def tile_spec(i):
        return pl.BlockSpec((1, TILE, TILE), lambda s, p, c: (p[s * STEP + i], 0, 0))

    def spec(*shape):
        return pl.BlockSpec((STEP,) + shape, lambda s, p, c: (s, 0, 0))

    grid = pltpu.PrefetchScalarGridSpec(
        num_scalar_prefetch=2,
        grid=(NSTEP,),
        in_specs=[tile_spec(i) for i in range(STEP)] + [spec(SIDE, TILE), spec(TILE, TILE)],
        out_specs=[spec(2 * TILE, 2 * TILE), spec(2 * TILE, 2 * TILE), spec(1, TILE), spec(1, TILE)],
    )
    return pl.pallas_call(
        pair_kernel,
        grid_spec=grid,
        out_shape=[
            jax.ShapeDtypeStruct((SLOTS, 2 * TILE, 2 * TILE), BF16),
            jax.ShapeDtypeStruct((SLOTS, 2 * TILE, 2 * TILE), BF16),
            jax.ShapeDtypeStruct((SLOTS, 1, TILE), F32),
            jax.ShapeDtypeStruct((SLOTS, 1, TILE), jnp.int32),
        ],
        compiler_params=params(),
        cost_estimate=cost(2 * 64 * 3 * 64 * 128 * 128, 16 << 20),
        name="pair_setup",
    )(perm, counts, *([diag_tiles] * STEP), side, remote)


def gathered_rows(ref, count):
    lane = lax.broadcasted_iota(jnp.int32, (32, TILE), 1) < 64
    tops, bottoms = [], []
    for q in range(0, count, 2):
        a, b = ref[q, 0:32], ref[q + 1, 0:32]
        tops.append(jnp.where(lane, a, pltpu.roll(b, 64, 1)))
        bottoms.append(jnp.where(lane, pltpu.roll(a, 64, 1), b))
    return jnp.concatenate([jnp.concatenate(tops, axis=1), jnp.concatenate(bottoms, axis=1)], axis=0)


def lowest_kernel(arrived, g, x_out, out):
    x = gathered_rows(arrived, PEERS)
    x_out[...] = x
    hi, lo = split2(g[...])
    packed = pack_rows(mm(x, hi, lo, nt=True))
    extra = arrived[0, 32:40]
    for q in range(1, PEERS):
        extra = extra + arrived[q, 32:40]
    for q in range(GROUPS):
        out[q, 0:32] = packed
        out[q, 32:40] = extra


def lowest_part(arrived, g):
    return pl.pallas_call(
        lowest_kernel,
        out_shape=[
            jax.ShapeDtypeStruct((COLS, NC1), F32),
            jax.ShapeDtypeStruct((GROUPS, ROWS, TILE), F32),
        ],
        compiler_params=params(),
        name="lowest_part",
    )(arrived, g)


def smooth_kernel(x_ref, inverse_ref, op, out):
    inverse = inverse_ref[...]
    scaled = x_ref[...] * inverse
    total = None
    for i in range(NC1 // 256):
        rows = slice(i * 256, (i + 1) * 256)
        hi, lo = split2(op[rows, :])
        part = mm(scaled[:, rows], hi, lo)
        total = part if total is None else total + part
    out[...] = 2.0 * OMEGA * scaled - OMEGA * OMEGA * total * inverse


def smooth_part(x, inverse, op):
    return pl.pallas_call(
        smooth_kernel,
        out_shape=jax.ShapeDtypeStruct((COLS, NC1), F32),
        compiler_params=params(),
        cost_estimate=cost(2 * 3 * 64 * 1024 * 1024, 5 << 20),
        name="smooth_part",
    )(x, inverse, op)


def correct_kernel(arrived, inverse_cols, g, h, e_out, dots):
    low = gathered_rows(arrived, GROUPS)
    hi, lo = split2(inverse_cols[...])
    corr = mm(low, hi, lo)
    ghi, glo = split2(g[...])
    e = h[...] + mm(corr, ghi, glo)
    for q in range(PEERS):
        e_out[q] = e[:, q * AGG : (q + 1) * AGG]
    extra = arrived[0, 32:40]
    for q in range(1, GROUPS):
        extra = extra + arrived[q, 32:40]
    dots[...] = extra


def correct_part(arrived, inverse_cols, g, h):
    return pl.pallas_call(
        correct_kernel,
        out_shape=[jax.ShapeDtypeStruct((PEERS, COLS, AGG), F32), jax.ShapeDtypeStruct((8, TILE), F32)],
        compiler_params=params(),
        name="correct_part",
    )(arrived, inverse_cols, g, h)


def apply_block(x, diag, hi, lo):
    xh, xl = split2(x)
    rows = x.shape[0]
    both = dot(jnp.concatenate([xh, xl], axis=0), hi)
    kept = xh.astype(F32) + xl.astype(F32)
    return both[:rows] + both[rows:] + dot(xh, lo) + kept[:, : diag.shape[1]] * diag


def lift(parts, row):
    rows = parts.shape[0] // 3
    three = dot(parts, one_hot(row))
    return three[:rows] + three[rows : 2 * rows] + three[2 * rows :]


def three_parts(e):
    return jnp.concatenate(split3(e), axis=0)


def forward_kernel(
    perm, member, e_own, e_peer, b_slot, b_rest, d_slot, d_rest, x_peer, d_peer, m_peer, hi_pair, lo_pair,
    hi_rest, lo_rest, maps, z_out, w_out, ws_out, out, acc_rr, acc_bz, acc_zw
):
    step = pl.program_id(0)

    @pl.when(step == 0)
    def _():
        acc_rr[...] = jnp.zeros_like(acc_rr)
        acc_bz[...] = jnp.zeros_like(acc_bz)
        acc_zw[...] = jnp.zeros_like(acc_zw)

    e_mine = three_parts(e_own[0])
    e_theirs = [three_parts(e_peer[q]) for q in range(STEP // 2)]
    rr, bz, zw = acc_rr[...], acc_bz[...], acc_zw[...]
    for k in range(STEP):
        index = perm[step * STEP + k]
        row = maps[index]
        diag = jnp.concatenate([d_slot[k], d_peer[k]], axis=1)
        rdiag = OMEGA / diag
        b_own = b_slot[k]
        xp = x_peer[k]
        b_full = jnp.concatenate([b_own, xp * (d_peer[k] * (1.0 / OMEGA))], axis=1)
        up = jnp.concatenate([lift(e_mine, row), lift(e_theirs[k // 2], m_peer[k])], axis=1)
        x = jnp.concatenate([b_own * rdiag[:, :TILE], xp], axis=1) + up
        hi, lo = hi_pair[k], lo_pair[k]
        z = x + (b_full - apply_block(x, diag, hi, lo)) * rdiag
        w = apply_block(z, diag, hi, lo)
        x1 = w * rdiag
        y = w[:, :TILE] - apply_block(x1, diag[:, :TILE], hi[:, :TILE], lo[:, :TILE])
        rr = rr + mm_exact(y, one_hot(row), nt=True)
        bz = bz + b_own * z[:, :TILE]
        zw = zw + z[:, :TILE] * w[:, :TILE]
        z_out[0, k] = z[:, :TILE]
        w_out[0, k] = w[:, :TILE]
        ws_out[k] = w[:, TILE:]
    for k in range(STEP):
        index = perm[SLOTS + step * STEP + k]
        row = maps[index]
        diag = d_rest[k]
        rdiag = OMEGA / diag
        b_own = b_rest[k]
        x = b_own * rdiag + lift(e_mine, row)
        hi, lo = hi_rest[k], lo_rest[k]
        z = x + (b_own - apply_block(x, diag, hi, lo)) * rdiag
        w = apply_block(z, diag, hi, lo)
        x1 = w * rdiag
        y = w - apply_block(x1, diag, hi, lo)
        rr = rr + mm_exact(y, one_hot(row), nt=True)
        bz = bz + b_own * z
        zw = zw + z * w
        z_out[1, k] = z
        w_out[1, k] = w
    acc_rr[...] = rr
    acc_bz[...] = bz
    acc_zw[...] = zw

    @pl.when(step == NSTEP - 1)
    def _():
        packed = pack_rows(rr)
        sums = jnp.sum(jnp.concatenate([bz, zw], axis=0).T, axis=0, keepdims=True)
        r8 = lax.broadcasted_iota(jnp.int32, (8, TILE), 0)
        extra = jnp.where(r8 == 0, sums, 0.0)
        for q in range(PEERS):
            out[q, 0:32] = packed
            out[q, 32:40] = extra


def step_spec(*shape):
    return pl.BlockSpec((STEP,) + shape, lambda s, p, m: (s, 0, 0))


def pair_spec():
    return pl.BlockSpec((2, STEP, COLS, TILE), lambda s, p, m: (0, s, 0, 0))


def e_specs():
    return [
        pl.BlockSpec((1, COLS, AGG), lambda s, p, m: (m[0], 0, 0)),
        pl.BlockSpec((STEP // 2, COLS, AGG), lambda s, p, m: (s, 0, 0)),
    ]


def forward_part(perm, member, e, b_slot, b_rest, d_slot, d_rest, x_peer, d_peer, m_peer, hi_pair, lo_pair, hi_rest, lo_rest, maps):
    grid = pltpu.PrefetchScalarGridSpec(
        num_scalar_prefetch=2,
        grid=(NSTEP,),
        in_specs=e_specs()
        + [
            step_spec(COLS, TILE),
            step_spec(COLS, TILE),
            step_spec(1, TILE),
            step_spec(1, TILE),
            step_spec(COLS, TILE),
            step_spec(1, TILE),
            step_spec(1, TILE),
            step_spec(2 * TILE, 2 * TILE),
            step_spec(2 * TILE, 2 * TILE),
            step_spec(TILE, TILE),
            step_spec(TILE, TILE),
            pl.BlockSpec((BLK, 1, TILE), lambda s, p, m: (0, 0, 0)),
        ],
        out_specs=[
            pair_spec(),
            pair_spec(),
            step_spec(COLS, TILE),
            pl.BlockSpec((PEERS, ROWS, TILE), lambda s, p, m: (0, 0, 0)),
        ],
        scratch_shapes=[pltpu.VMEM((COLS, AGG), F32), pltpu.VMEM((COLS, TILE), F32), pltpu.VMEM((COLS, TILE), F32)],
    )
    return pl.pallas_call(
        forward_kernel,
        grid_spec=grid,
        out_shape=[
            jax.ShapeDtypeStruct((2, SLOTS, COLS, TILE), F32),
            jax.ShapeDtypeStruct((2, SLOTS, COLS, TILE), F32),
            jax.ShapeDtypeStruct((SLOTS, COLS, TILE), F32),
            jax.ShapeDtypeStruct((PEERS, ROWS, TILE), F32),
        ],
        compiler_params=params(),
        name="forward_part",
    )(perm, member, e, e, b_slot, b_rest, d_slot, d_rest, x_peer, d_peer, m_peer, hi_pair, lo_pair, hi_rest, lo_rest, maps)


def second_kernel(
    perm, member, e_own, e_peer, dots, b_slot, b_rest, d_slot, d_rest, d_peer, m_peer, hi_pair, lo_pair,
    hi_rest, lo_rest, maps, z_in, w_in, w_peer, v_out, u_out, out, acc_a, acc_b, acc_c
):
    step = pl.program_id(0)

    @pl.when(step == 0)
    def _():
        acc_a[...] = jnp.zeros_like(acc_a)
        acc_b[...] = jnp.zeros_like(acc_b)
        acc_c[...] = jnp.zeros_like(acc_c)

    col = column(dots[0:1])
    alpha = col[:COLS] / col[COLS:]
    e_mine = three_parts(e_own[0])
    e_theirs = [three_parts(e_peer[q]) for q in range(STEP // 2)]
    sums = [acc_a[...], acc_b[...], acc_c[...]]

    def gather(b, z, w, v, u):
        r1 = b - alpha * w
        z1 = z - alpha * v
        az1 = w - alpha * u
        sums[0] = sums[0] + r1 * z1
        sums[1] = sums[1] + z1 * az1
        sums[2] = sums[2] + (z1 * w + z * az1)

    for k in range(STEP):
        row = maps[perm[step * STEP + k]]
        diag = jnp.concatenate([d_slot[k], d_peer[k]], axis=1)
        rdiag = OMEGA / diag
        w_own = w_in[0, k]
        w = jnp.concatenate([w_own, w_peer[k]], axis=1)
        up = jnp.concatenate([lift(e_mine, row), lift(e_theirs[k // 2], m_peer[k])], axis=1)
        x = w * rdiag + up
        hi, lo = hi_pair[k], lo_pair[k]
        v = x + (w - apply_block(x, diag, hi, lo)) * rdiag
        u = apply_block(v, diag[:, :TILE], hi[:, :TILE], lo[:, :TILE])
        v_own = v[:, :TILE]
        v_out[0, k] = v_own
        u_out[0, k] = u
        gather(b_slot[k], z_in[0, k], w_own, v_own, u)
    for k in range(STEP):
        row = maps[perm[SLOTS + step * STEP + k]]
        diag = d_rest[k]
        rdiag = OMEGA / diag
        w = w_in[1, k]
        x = w * rdiag + lift(e_mine, row)
        hi, lo = hi_rest[k], lo_rest[k]
        v = x + (w - apply_block(x, diag, hi, lo)) * rdiag
        u = apply_block(v, diag, hi, lo)
        v_out[1, k] = v
        u_out[1, k] = u
        gather(b_rest[k], z_in[1, k], w, v, u)
    acc_a[...] = sums[0]
    acc_b[...] = sums[1]
    acc_c[...] = sums[2]

    @pl.when(step == NSTEP - 1)
    def _():
        first = jnp.sum(jnp.concatenate([sums[0], sums[1]], axis=0).T, axis=0, keepdims=True)
        last = jnp.sum(jnp.concatenate([sums[2], sums[2]], axis=0).T, axis=0, keepdims=True)
        r8 = lax.broadcasted_iota(jnp.int32, (8, TILE), 0)
        extra = jnp.where(r8 == 0, first, jnp.where(r8 == 1, last, 0.0))
        for q in range(GROUPS * PEERS):
            out[q] = extra


def second_part(perm, member, e, dots, b_slot, b_rest, d_slot, d_rest, d_peer, m_peer, hi_pair, lo_pair, hi_rest, lo_rest, maps, z, w, w_peer):
    grid = pltpu.PrefetchScalarGridSpec(
        num_scalar_prefetch=2,
        grid=(NSTEP,),
        in_specs=e_specs()
        + [
            pl.BlockSpec((8, TILE), lambda s, p, m: (0, 0)),
            step_spec(COLS, TILE),
            step_spec(COLS, TILE),
            step_spec(1, TILE),
            step_spec(1, TILE),
            step_spec(1, TILE),
            step_spec(1, TILE),
            step_spec(2 * TILE, 2 * TILE),
            step_spec(2 * TILE, 2 * TILE),
            step_spec(TILE, TILE),
            step_spec(TILE, TILE),
            pl.BlockSpec((BLK, 1, TILE), lambda s, p, m: (0, 0, 0)),
            pair_spec(),
            pair_spec(),
            step_spec(COLS, TILE),
        ],
        out_specs=[
            pair_spec(),
            pair_spec(),
            pl.BlockSpec((GROUPS * PEERS, 8, TILE), lambda s, p, m: (0, 0, 0)),
        ],
        scratch_shapes=[pltpu.VMEM((COLS, TILE), F32)] * 3,
    )
    return pl.pallas_call(
        second_kernel,
        grid_spec=grid,
        out_shape=[
            jax.ShapeDtypeStruct((2, SLOTS, COLS, TILE), F32),
            jax.ShapeDtypeStruct((2, SLOTS, COLS, TILE), F32),
            jax.ShapeDtypeStruct((GROUPS * PEERS, 8, TILE), F32),
        ],
        compiler_params=params(),
        name="second_part",
    )(perm, member, e, e, dots, b_slot, b_rest, d_slot, d_rest, d_peer, m_peer, hi_pair, lo_pair, hi_rest, lo_rest, maps, z, w, w_peer)


def combine_kernel(perm, dots, arrived, b_slot, b_rest, z, w, v, u, solution, residual, coef):
    step = pl.program_id(0)

    @pl.when(step == 0)
    def _():
        total = arrived[0]
        for q in range(1, GROUPS * PEERS):
            total = total + arrived[q]
        old = column(dots[0:1])
        one = column(total[0:1])
        two = column(total[1:2])
        rho, zw = old[:COLS], old[COLS:]
        rho_next, zz = one[:COLS], one[COLS:]
        cross = two[:COLS]
        alpha = rho / zw
        beta = rho_next / rho
        alpha_next = rho_next / (zz + beta * cross + beta * beta * zw)
        coef[0] = alpha
        coef[1] = beta
        coef[2] = alpha_next

    alpha, beta, alpha_next = coef[0], coef[1], coef[2]
    for half, b_ref in ((0, b_slot), (1, b_rest)):
        for k in range(STEP):
            index = perm[half * SLOTS + step * STEP + k]
            at = pl.ds(pl.multiple_of(index * TILE, TILE), TILE)
            z0, w0 = z[half, k], w[half, k]
            z1 = z0 - alpha * v[half, k]
            az1 = w0 - alpha * u[half, k]
            solution[:, at] = alpha * z0 + alpha_next * (z1 + beta * z0)
            residual[:, at] = b_ref[k] - alpha * w0 - alpha_next * (az1 + beta * w0)


def combine(perm, dots, arrived, b_slot, b_rest, z, w, v, u):
    def pair():
        return pl.BlockSpec((2, STEP, COLS, TILE), lambda s, p: (0, s, 0, 0))

    def single():
        return pl.BlockSpec((STEP, COLS, TILE), lambda s, p: (s, 0, 0))

    def whole():
        return pl.BlockSpec((COLS, BLK * TILE), lambda s, p: (0, 0))

    grid = pltpu.PrefetchScalarGridSpec(
        num_scalar_prefetch=1,
        grid=(NSTEP,),
        in_specs=[
            pl.BlockSpec((8, TILE), lambda s, p: (0, 0)),
            pl.BlockSpec((GROUPS * PEERS, 8, TILE), lambda s, p: (0, 0, 0)),
            single(),
            single(),
            pair(),
            pair(),
            pair(),
            pair(),
        ],
        out_specs=[whole(), whole()],
        scratch_shapes=[pltpu.VMEM((3, COLS, TILE), F32)],
    )
    return pl.pallas_call(
        combine_kernel,
        grid_spec=grid,
        out_shape=[jax.ShapeDtypeStruct((COLS, BLK * TILE), F32)] * 2,
        compiler_params=params(),
        name="combine",
    )(perm, dots, arrived, b_slot, b_rest, z, w, v, u)


def exchange(x, axes):
    return lax.all_to_all(x, axes, 0, 0, tiled=True)


def on_device(
    right_side,
    diag_tiles,
    remote_tiles,
    slot_counts,
    slot_blocks,
    fine_map,
    coarse_map,
    level1_ops,
    coarsest_inverse,
):
    group = lax.axis_index("grp")
    member = lax.axis_index(GROUP_AXES).astype(jnp.int32).reshape(1)
    slot_list = slot_blocks.reshape(SLOTS)
    counts = slot_counts.reshape(PEERS)
    maps = fine_map.reshape(BLK, 1, TILE)
    remote = remote_tiles.reshape(SLOTS, TILE, TILE)
    operator = level1_ops[0]

    first, second = boundary_pack(slot_list, diag_tiles, right_side, maps)
    x_peer = exchange(first.reshape(PEERS, 2 * COLS, TILE), GROUP_AXES).reshape(SLOTS, COLS, TILE)
    side = exchange(second.reshape(PEERS, 2 * SIDE, TILE), GROUP_AXES).reshape(SLOTS, SIDE, TILE)

    tile_ids = jnp.arange(BLK, dtype=jnp.int32)
    free = jnp.logical_not(jnp.any(slot_list[:, None] == tile_ids[None, :], axis=0)).astype(jnp.int32)
    rank = jnp.sum(jnp.where(tile_ids[None, :] < tile_ids[:, None], free[None, :], 0), axis=1)
    chosen = (rank[None, :] == jnp.arange(SLOTS, dtype=jnp.int32)[:, None]) & (free[None, :] == 1)
    rest_list = jnp.sum(jnp.where(chosen, tile_ids[None, :], 0), axis=1)
    perm = jnp.concatenate([slot_list, rest_list])

    b_slot, b_rest, d_slot, d_rest, hi_rest, lo_rest, rs, rr_local = local_part(
        perm, counts, diag_tiles, right_side, remote, maps
    )
    g, inverse = coarse_setup(operator, coarse_map.reshape(1, NC1))
    inverse_cols = lax.dynamic_slice_in_dim(coarsest_inverse, group * AGG, AGG, 1)

    def level_one(arrived):
        x, outgoing = lowest_part(arrived, g)
        lows = exchange(outgoing, "grp")
        h = smooth_part(x, inverse, operator)
        return correct_part(lows, inverse_cols, g, h)

    gathered = exchange(first_restrict(x_peer, rs, rr_local), GROUP_AXES)
    hi_pair, lo_pair, d_peer, m_peer = pair_setup(perm, counts, diag_tiles, side, remote)
    e, _ = level_one(gathered)
    z, w, w_peer, outgoing = forward_part(
        perm, member, e, b_slot, b_rest, d_slot, d_rest, x_peer, d_peer, m_peer, hi_pair, lo_pair, hi_rest, lo_rest, maps
    )
    e, dots = level_one(exchange(outgoing, GROUP_AXES))
    v, u, outgoing = second_part(
        perm, member, e, dots, b_slot, b_rest, d_slot, d_rest, d_peer, m_peer, hi_pair, lo_pair, hi_rest, lo_rest, maps, z, w, w_peer
    )
    sums = exchange(outgoing, ALL_AXES)
    return tuple(combine(perm, dots, sums, b_slot, b_rest, z, w, v, u))


def solution(mesh):
    placed = (
        P(None, ("grp", "sub", "chip")),
        P(("grp", "sub", "chip"), None, None),
        P(("grp", "sub", "chip"), None, None, None),
        P(("grp", "sub", "chip"), None),
        P(("grp", "sub", "chip"), None, None),
        P(("grp", "sub", "chip")),
        P("grp"),
        P("grp", None, None),
        P(),
    )
    return jax.shard_map(
        on_device,
        mesh=mesh,
        in_specs=placed,
        out_specs=(P(None, ("grp", "sub", "chip")), P(None, ("grp", "sub", "chip"))),
        check_vma=False,
    )
```

```python
import functools

import jax
import jax.numpy as jnp
from jax import lax
from jax.experimental import pallas as pl
from jax.experimental.pallas import tpu as pltpu
from jax.sharding import PartitionSpec as P

OMEGA = 0.6
F32 = jnp.float32
BF16 = jnp.bfloat16
COLS = 64
TILE = 128
BLK = 64
SLOTS = 32
PEERS = 16
GROUPS = 8
AGG = 64
NC1 = 1024
STEP = 8
NSTEP = SLOTS // STEP
SIDE = 136
ROWS = 40
VMEM_LIMIT = 24 * 1024 * 1024

GROUP_AXES = ("sub", "chip")
ALL_AXES = ("grp", "sub", "chip")


def params():
    return pltpu.CompilerParams(vmem_limit_bytes=VMEM_LIMIT)


def cost(flops, moved):
    return pl.CostEstimate(flops=flops, bytes_accessed=moved, transcendentals=0)


def split2(x):
    hi = x.astype(BF16)
    lo = (x - hi.astype(F32)).astype(BF16)
    return hi, lo


def split3(x):
    hi = x.astype(BF16)
    rest = x - hi.astype(F32)
    mid = rest.astype(BF16)
    lo = (rest - mid.astype(F32)).astype(BF16)
    return hi, mid, lo


def dot(a, b):
    return jnp.dot(a, b, preferred_element_type=F32)


def dot_nt(a, b):
    return lax.dot_general(a, b, (((1,), (1,)), ((), ())), preferred_element_type=F32)


def mm(x, whi, wlo, nt=False):
    op = dot_nt if nt else dot
    rows = x.shape[0]
    hi, lo = split2(x)
    both = op(jnp.concatenate([hi, lo], axis=0), whi)
    return both[:rows] + both[rows:] + op(hi, wlo)


def mm_exact(x, w, nt=False):
    op = dot_nt if nt else dot
    rows = x.shape[0]
    hi, mid, lo = split3(x)
    three = op(jnp.concatenate([hi, mid, lo], axis=0), w)
    return three[:rows] + three[rows : 2 * rows] + three[2 * rows :]


def exact_mm(w, x):
    hi, mid, lo = split3(x)
    return dot(w, hi) + dot(w, mid) + dot(w, lo)


def eye_mask():
    r = lax.broadcasted_iota(jnp.int32, (TILE, TILE), 0)
    c = lax.broadcasted_iota(jnp.int32, (TILE, TILE), 1)
    return r, c


def tile_diag(tile):
    r, c = eye_mask()
    return jnp.sum(jnp.where(r == c, tile, 0.0), axis=0, keepdims=True)


def off_diag(tile):
    r, c = eye_mask()
    return jnp.where(r == c, 0.0, tile)


def one_hot(row):
    r = lax.broadcasted_iota(jnp.int32, (AGG, row.shape[1]), 0)
    return jnp.where(r == row, 1.0, 0.0).astype(BF16)


def pack_rows(x):
    wide = jnp.concatenate([x[:32], x[32:]], axis=1)
    return wide


def column(row):
    return jnp.broadcast_to(row, (TILE, TILE)).T


def boundary_kernel(slots, *refs):
    tiles, cols, maps, out = refs[:STEP], refs[STEP : 2 * STEP], refs[2 * STEP], refs[-1]
    step = pl.program_id(0)
    for i in range(STEP):
        tile = tiles[i][0]
        diag = tile_diag(tile)
        out[i, 0:64] = OMEGA * cols[i][...] / diag
        r = lax.broadcasted_iota(jnp.int32, (64, TILE), 0)
        c = lax.broadcasted_iota(jnp.int32, (64, TILE), 1)
        below = pltpu.roll(tile[64:], 64, 1)
        out[i, 64:128] = jnp.where((c < 64) & (r > c), below, tile[:64])
        row = maps[slots[step * STEP + i]].astype(F32)
        r8 = lax.broadcasted_iota(jnp.int32, (8, TILE), 0)
        out[i, 128:136] = jnp.where(r8 == 0, diag, jnp.where(r8 == 1, row, 0.0))


def boundary_pack(slot_list, diag_tiles, right_side, maps):
    def tile_spec(i):
        return pl.BlockSpec((1, TILE, TILE), lambda s, p: (p[s * STEP + i], 0, 0))

    def col_spec(i):
        return pl.BlockSpec((COLS, TILE), lambda s, p: (0, p[s * STEP + i]))

    grid = pltpu.PrefetchScalarGridSpec(
        num_scalar_prefetch=1,
        grid=(NSTEP,),
        in_specs=[tile_spec(i) for i in range(STEP)]
        + [col_spec(i) for i in range(STEP)]
        + [pl.BlockSpec((BLK, 1, TILE), lambda s, p: (0, 0, 0))],
        out_specs=pl.BlockSpec((STEP, SIDE, TILE), lambda s, p: (s, 0, 0)),
    )
    return pl.pallas_call(
        boundary_kernel,
        grid_spec=grid,
        out_shape=jax.ShapeDtypeStruct((SLOTS, SIDE, TILE), F32),
        compiler_params=params(),
        name="boundary_pack",
    )(slot_list, *([diag_tiles] * STEP), *([right_side] * STEP), maps)


def local_kernel(perm, counts, *refs):
    n = 2 * STEP
    tiles, cols = refs[:n], refs[n : 2 * n]
    remote, maps = refs[2 * n : 2 * n + 2]
    b_slot, b_rest, d_slot, d_rest, hi_rest, lo_rest, rs, rr = refs[2 * n + 2 :]
    step = pl.program_id(0)

    @pl.when(step == 0)
    def _():
        rr[...] = jnp.zeros_like(rr)

    index = [perm[(0 if i < STEP else SLOTS) + step * STEP + i % STEP] for i in range(n)]
    tile = [tiles[i][0] for i in range(n)]
    diag = [tile_diag(t) for t in tile]
    off = [split2(off_diag(t)) for t in tile]
    b = [cols[i][...] for i in range(n)]
    x = [OMEGA * bb / d for bb, d in zip(b, diag)]
    y = [bb - OMEGA * bb - mm(xx, *o) for bb, xx, o in zip(b, x, off)]
    spread = [one_hot(maps[i]) for i in index]
    total = rr[...]
    for yy, sp in zip(y, spread):
        total = total + mm_exact(yy, sp, nt=True)
    for k in range(STEP):
        b_slot[k] = b[k]
        d_slot[k] = diag[k]
        b_rest[k] = b[STEP + k]
        d_rest[k] = diag[STEP + k]
        hi_rest[k], lo_rest[k] = off[STEP + k]
    scaled = []
    for k in range(STEP):
        j = step * STEP + k
        live = (j % 2) < counts[j // 2]
        scaled.append(split2(remote[k] * jnp.where(live, 1.0, 0.0)))
    for k in range(STEP):
        rs[k] = dot_nt(spread[k], scaled[k][0]) + dot_nt(spread[k], scaled[k][1])
    rr[...] = total


def local_part(perm, counts, diag_tiles, right_side, remote, maps):
    def where(i):
        return (0 if i < STEP else SLOTS) + i % STEP

    def tile_spec(i):
        return pl.BlockSpec((1, TILE, TILE), lambda s, p, c: (p[s * STEP + where(i)], 0, 0))

    def col_spec(i):
        return pl.BlockSpec((COLS, TILE), lambda s, p, c: (0, p[s * STEP + where(i)]))

    def out(*shape):
        return pl.BlockSpec((STEP,) + shape, lambda s, p, c: (s, 0, 0))

    n = 2 * STEP
    grid = pltpu.PrefetchScalarGridSpec(
        num_scalar_prefetch=2,
        grid=(NSTEP,),
        in_specs=[tile_spec(i) for i in range(n)]
        + [col_spec(i) for i in range(n)]
        + [
            pl.BlockSpec((STEP, TILE, TILE), lambda s, p, c: (s, 0, 0)),
            pl.BlockSpec((BLK, 1, TILE), lambda s, p, c: (0, 0, 0)),
        ],
        out_specs=[
            out(COLS, TILE),
            out(COLS, TILE),
            out(1, TILE),
            out(1, TILE),
            out(TILE, TILE),
            out(TILE, TILE),
            out(AGG, TILE),
            pl.BlockSpec((COLS, AGG), lambda s, p, c: (0, 0)),
        ],
    )

    def sds(shape, dtype=F32):
        return jax.ShapeDtypeStruct((SLOTS,) + shape, dtype)

    return pl.pallas_call(
        local_kernel,
        grid_spec=grid,
        out_shape=[
            sds((COLS, TILE)),
            sds((COLS, TILE)),
            sds((1, TILE)),
            sds((1, TILE)),
            sds((TILE, TILE), BF16),
            sds((TILE, TILE), BF16),
            sds((AGG, TILE)),
            jax.ShapeDtypeStruct((COLS, AGG), F32),
        ],
        compiler_params=params(),
        cost_estimate=cost(2 * 64 * 3 * 64 * 128 * 128, 16 << 20),
        name="local_part",
    )(perm, counts, *([diag_tiles] * n), *([right_side] * n), remote, maps)


def coarse_kernel(op, cmap, g_out, d_out):
    spread = one_hot(cmap[...])
    product = exact_spread(spread, op)
    pieces = []
    for i in range(NC1 // TILE):
        pieces.append(tile_diag(op[i * TILE : (i + 1) * TILE, i * TILE : (i + 1) * TILE]))
    diag = jnp.concatenate(pieces, axis=1)
    inverse = 1.0 / diag
    d_out[...] = inverse
    g_out[...] = spread.astype(F32) - OMEGA * product * inverse


def exact_spread(spread, op):
    total = None
    for i in range(NC1 // 256):
        rows = slice(i * 256, (i + 1) * 256)
        hi, lo = split2(op[rows, :])
        part = dot(spread[:, rows], hi) + dot(spread[:, rows], lo)
        total = part if total is None else total + part
    return total


def coarse_setup(op, cmap):
    return pl.pallas_call(
        coarse_kernel,
        out_shape=[jax.ShapeDtypeStruct((AGG, NC1), F32), jax.ShapeDtypeStruct((1, NC1), F32)],
        compiler_params=params(),
        cost_estimate=cost(2 * 2 * 64 * 1024 * 1024, 5 << 20),
        name="coarse_setup",
    )(op, cmap)


def first_restrict_kernel(arrived, rs, rr, out):
    total = rr[...]
    for j in range(SLOTS):
        hi, lo = split2(rs[j])
        total = total + mm(arrived[j, 0:64], hi, lo, nt=True)
    packed = pack_rows(total)
    for q in range(PEERS):
        out[q, 0:32] = packed
        out[q, 32:40] = jnp.zeros((8, TILE), F32)


def first_restrict(arrived, rs, rr):
    return pl.pallas_call(
        first_restrict_kernel,
        out_shape=jax.ShapeDtypeStruct((PEERS, ROWS, TILE), F32),
        compiler_params=params(),
        name="first_restrict",
    )(arrived, rs, rr)


def pair_kernel(perm, counts, *refs):
    tiles, side, remote, hi_out, lo_out, diag_out, map_out = (refs[:STEP],) + tuple(refs[STEP:])
    step = pl.program_id(0)
    r = lax.broadcasted_iota(jnp.int32, (64, TILE), 0)
    c = lax.broadcasted_iota(jnp.int32, (64, TILE), 1)
    for k in range(STEP):
        own = off_diag(tiles[k][0])
        packed = side[k, 64:128]
        top = jnp.where((c >= 64) | (r < c), packed, 0.0)
        bottom = pltpu.roll(jnp.where((c < 64) & (r > c), packed, 0.0), 64, 1)
        half = jnp.concatenate([top, bottom], axis=0)
        other = half + half.T
        j = step * STEP + k
        live = (j % 2) < counts[j // 2]
        rem = remote[k] * jnp.where(live, -1.0, 0.0)
        block = jnp.concatenate(
            [jnp.concatenate([own, rem.T], axis=1), jnp.concatenate([rem, other], axis=1)], axis=0
        )
        hi, lo = split2(block)
        hi_out[k] = hi
        lo_out[k] = lo
        diag_out[k] = side[k, 128:129]
        map_out[k] = side[k, 129:130].astype(jnp.int32)


def pair_setup(perm, counts, diag_tiles, side, remote):
    def tile_spec(i):
        return pl.BlockSpec((1, TILE, TILE), lambda s, p, c: (p[s * STEP + i], 0, 0))

    def spec(*shape):
        return pl.BlockSpec((STEP,) + shape, lambda s, p, c: (s, 0, 0))

    grid = pltpu.PrefetchScalarGridSpec(
        num_scalar_prefetch=2,
        grid=(NSTEP,),
        in_specs=[tile_spec(i) for i in range(STEP)] + [spec(SIDE, TILE), spec(TILE, TILE)],
        out_specs=[spec(2 * TILE, 2 * TILE), spec(2 * TILE, 2 * TILE), spec(1, TILE), spec(1, TILE)],
    )
    return pl.pallas_call(
        pair_kernel,
        grid_spec=grid,
        out_shape=[
            jax.ShapeDtypeStruct((SLOTS, 2 * TILE, 2 * TILE), BF16),
            jax.ShapeDtypeStruct((SLOTS, 2 * TILE, 2 * TILE), BF16),
            jax.ShapeDtypeStruct((SLOTS, 1, TILE), F32),
            jax.ShapeDtypeStruct((SLOTS, 1, TILE), jnp.int32),
        ],
        compiler_params=params(),
        cost_estimate=cost(2 * 64 * 3 * 64 * 128 * 128, 16 << 20),
        name="pair_setup",
    )(perm, counts, *([diag_tiles] * STEP), side, remote)


def gathered_rows(ref, count):
    lane = lax.broadcasted_iota(jnp.int32, (32, TILE), 1) < 64
    tops, bottoms = [], []
    for q in range(0, count, 2):
        a, b = ref[q, 0:32], ref[q + 1, 0:32]
        tops.append(jnp.where(lane, a, pltpu.roll(b, 64, 1)))
        bottoms.append(jnp.where(lane, pltpu.roll(a, 64, 1), b))
    return jnp.concatenate([jnp.concatenate(tops, axis=1), jnp.concatenate(bottoms, axis=1)], axis=0)


def lowest_kernel(arrived, g, x_out, out):
    x = gathered_rows(arrived, PEERS)
    x_out[...] = x
    hi, lo = split2(g[...])
    packed = pack_rows(mm(x, hi, lo, nt=True))
    extra = arrived[0, 32:40]
    for q in range(1, PEERS):
        extra = extra + arrived[q, 32:40]
    for q in range(GROUPS):
        out[q, 0:32] = packed
        out[q, 32:40] = extra


def lowest_part(arrived, g):
    return pl.pallas_call(
        lowest_kernel,
        out_shape=[
            jax.ShapeDtypeStruct((COLS, NC1), F32),
            jax.ShapeDtypeStruct((GROUPS, ROWS, TILE), F32),
        ],
        compiler_params=params(),
        name="lowest_part",
    )(arrived, g)


def smooth_kernel(x_ref, inverse_ref, op, out):
    inverse = inverse_ref[...]
    scaled = x_ref[...] * inverse
    total = None
    for i in range(NC1 // 256):
        rows = slice(i * 256, (i + 1) * 256)
        hi, lo = split2(op[rows, :])
        part = mm(scaled[:, rows], hi, lo)
        total = part if total is None else total + part
    out[...] = 2.0 * OMEGA * scaled - OMEGA * OMEGA * total * inverse


def smooth_part(x, inverse, op):
    return pl.pallas_call(
        smooth_kernel,
        out_shape=jax.ShapeDtypeStruct((COLS, NC1), F32),
        compiler_params=params(),
        cost_estimate=cost(2 * 3 * 64 * 1024 * 1024, 5 << 20),
        name="smooth_part",
    )(x, inverse, op)


def correct_kernel(arrived, inverse_cols, g, h, e_out, dots):
    low = gathered_rows(arrived, GROUPS)
    hi, lo = split2(inverse_cols[...])
    corr = mm(low, hi, lo)
    ghi, glo = split2(g[...])
    e = h[...] + mm(corr, ghi, glo)
    for q in range(PEERS):
        e_out[q] = e[:, q * AGG : (q + 1) * AGG]
    extra = arrived[0, 32:40]
    for q in range(1, GROUPS):
        extra = extra + arrived[q, 32:40]
    dots[...] = extra


def correct_part(arrived, inverse_cols, g, h):
    return pl.pallas_call(
        correct_kernel,
        out_shape=[jax.ShapeDtypeStruct((PEERS, COLS, AGG), F32), jax.ShapeDtypeStruct((8, TILE), F32)],
        compiler_params=params(),
        name="correct_part",
    )(arrived, inverse_cols, g, h)


def apply_block(x, diag, hi, lo):
    xh, xl = split2(x)
    rows = x.shape[0]
    both = dot(jnp.concatenate([xh, xl], axis=0), hi)
    kept = xh.astype(F32) + xl.astype(F32)
    return both[:rows] + both[rows:] + dot(xh, lo) + kept[:, : diag.shape[1]] * diag


def lift(parts, row):
    rows = parts.shape[0] // 3
    three = dot(parts, one_hot(row))
    return three[:rows] + three[rows : 2 * rows] + three[2 * rows :]


def three_parts(e):
    return jnp.concatenate(split3(e), axis=0)


def forward_kernel(
    perm, member, e_own, e_peer, b_slot, b_rest, d_slot, d_rest, x_peer, d_peer, m_peer, hi_pair, lo_pair,
    hi_rest, lo_rest, maps, z_out, w_out, ws_out, out, acc_rr, acc_bz, acc_zw
):
    step = pl.program_id(0)

    @pl.when(step == 0)
    def _():
        acc_rr[...] = jnp.zeros_like(acc_rr)
        acc_bz[...] = jnp.zeros_like(acc_bz)
        acc_zw[...] = jnp.zeros_like(acc_zw)

    e_mine = three_parts(e_own[0])
    e_theirs = [three_parts(e_peer[q]) for q in range(STEP // 2)]
    rr, bz, zw = acc_rr[...], acc_bz[...], acc_zw[...]
    pairs, rest = range(STEP), range(STEP)
    rows = [maps[perm[step * STEP + k]] for k in pairs] + [maps[perm[SLOTS + step * STEP + k]] for k in rest]
    b_own = [b_slot[k] for k in pairs] + [b_rest[k] for k in rest]
    diag = [jnp.concatenate([d_slot[k], d_peer[k]], axis=1) for k in pairs] + [d_rest[k] for k in rest]
    rdiag = [OMEGA / d for d in diag]
    mats = [(hi_pair[k], lo_pair[k]) for k in pairs] + [(hi_rest[k], lo_rest[k]) for k in rest]
    full = [
        jnp.concatenate([b_own[k], x_peer[k] * (d_peer[k] * (1.0 / OMEGA))], axis=1) for k in pairs
    ] + b_own[STEP:]
    ups = [lift(e_mine, row) for row in rows]
    ups_peer = [lift(e_theirs[k // 2], m_peer[k]) for k in pairs]
    ups = [jnp.concatenate([ups[k], ups_peer[k]], axis=1) for k in pairs] + ups[STEP:]
    x = [f * rd + up for f, rd, up in zip(full, rdiag, ups)]
    image = [apply_block(xx, d, *m) for xx, d, m in zip(x, diag, mats)]
    z = [xx + (f - im) * rd for xx, f, im, rd in zip(x, full, image, rdiag)]
    w = [apply_block(zz, d, *m) for zz, d, m in zip(z, diag, mats)]
    x1 = [ww * rd for ww, rd in zip(w, rdiag)]
    left = [(m[0][:, :TILE], m[1][:, :TILE]) for m in mats]
    y = [
        ww[:, :TILE] - apply_block(xx, d[:, :TILE], *m) for ww, xx, d, m in zip(w, x1, diag, left)
    ]
    for row, yy in zip(rows, y):
        rr = rr + mm_exact(yy, one_hot(row), nt=True)
    for i in range(2 * STEP):
        zz, ww = z[i][:, :TILE], w[i][:, :TILE]
        bz = bz + b_own[i] * zz
        zw = zw + zz * ww
        z_out[i // STEP, i % STEP] = zz
        w_out[i // STEP, i % STEP] = ww
    for k in pairs:
        ws_out[k] = w[k][:, TILE:]
    acc_rr[...] = rr
    acc_bz[...] = bz
    acc_zw[...] = zw

    @pl.when(step == NSTEP - 1)
    def _():
        packed = pack_rows(rr)
        sums = jnp.sum(jnp.concatenate([bz, zw], axis=0).T, axis=0, keepdims=True)
        r8 = lax.broadcasted_iota(jnp.int32, (8, TILE), 0)
        extra = jnp.where(r8 == 0, sums, 0.0)
        for q in range(PEERS):
            out[q, 0:32] = packed
            out[q, 32:40] = extra


def step_spec(*shape):
    return pl.BlockSpec((STEP,) + shape, lambda s, p, m: (s, 0, 0))


def pair_spec():
    return pl.BlockSpec((2, STEP, COLS, TILE), lambda s, p, m: (0, s, 0, 0))


def e_specs():
    return [
        pl.BlockSpec((1, COLS, AGG), lambda s, p, m: (m[0], 0, 0)),
        pl.BlockSpec((STEP // 2, COLS, AGG), lambda s, p, m: (s, 0, 0)),
    ]


def forward_part(perm, member, e, b_slot, b_rest, d_slot, d_rest, x_peer, d_peer, m_peer, hi_pair, lo_pair, hi_rest, lo_rest, maps):
    grid = pltpu.PrefetchScalarGridSpec(
        num_scalar_prefetch=2,
        grid=(NSTEP,),
        in_specs=e_specs()
        + [
            step_spec(COLS, TILE),
            step_spec(COLS, TILE),
            step_spec(1, TILE),
            step_spec(1, TILE),
            step_spec(COLS, TILE),
            step_spec(1, TILE),
            step_spec(1, TILE),
            step_spec(2 * TILE, 2 * TILE),
            step_spec(2 * TILE, 2 * TILE),
            step_spec(TILE, TILE),
            step_spec(TILE, TILE),
            pl.BlockSpec((BLK, 1, TILE), lambda s, p, m: (0, 0, 0)),
        ],
        out_specs=[
            pair_spec(),
            pair_spec(),
            step_spec(COLS, TILE),
            pl.BlockSpec((PEERS, ROWS, TILE), lambda s, p, m: (0, 0, 0)),
        ],
        scratch_shapes=[pltpu.VMEM((COLS, AGG), F32), pltpu.VMEM((COLS, TILE), F32), pltpu.VMEM((COLS, TILE), F32)],
    )
    return pl.pallas_call(
        forward_kernel,
        grid_spec=grid,
        out_shape=[
            jax.ShapeDtypeStruct((2, SLOTS, COLS, TILE), F32),
            jax.ShapeDtypeStruct((2, SLOTS, COLS, TILE), F32),
            jax.ShapeDtypeStruct((SLOTS, COLS, TILE), F32),
            jax.ShapeDtypeStruct((PEERS, ROWS, TILE), F32),
        ],
        compiler_params=params(),
        name="forward_part",
    )(perm, member, e, e, b_slot, b_rest, d_slot, d_rest, x_peer, d_peer, m_peer, hi_pair, lo_pair, hi_rest, lo_rest, maps)


def second_kernel(
    perm, member, e_own, e_peer, dots, b_slot, b_rest, d_slot, d_rest, d_peer, m_peer, hi_pair, lo_pair,
    hi_rest, lo_rest, maps, z_in, w_in, w_peer, v_out, u_out, out, acc_a, acc_b, acc_c
):
    step = pl.program_id(0)

    @pl.when(step == 0)
    def _():
        acc_a[...] = jnp.zeros_like(acc_a)
        acc_b[...] = jnp.zeros_like(acc_b)
        acc_c[...] = jnp.zeros_like(acc_c)

    col = column(dots[0:1])
    alpha = col[:COLS] / col[COLS:]
    e_mine = three_parts(e_own[0])
    e_theirs = [three_parts(e_peer[q]) for q in range(STEP // 2)]
    sums = [acc_a[...], acc_b[...], acc_c[...]]

    def gather(b, z, w, v, u):
        r1 = b - alpha * w
        z1 = z - alpha * v
        az1 = w - alpha * u
        sums[0] = sums[0] + r1 * z1
        sums[1] = sums[1] + z1 * az1
        sums[2] = sums[2] + (z1 * w + z * az1)

    pairs, rest = range(STEP), range(STEP)
    rows = [maps[perm[step * STEP + k]] for k in pairs] + [maps[perm[SLOTS + step * STEP + k]] for k in rest]
    diag = [jnp.concatenate([d_slot[k], d_peer[k]], axis=1) for k in pairs] + [d_rest[k] for k in rest]
    rdiag = [OMEGA / d for d in diag]
    mats = [(hi_pair[k], lo_pair[k]) for k in pairs] + [(hi_rest[k], lo_rest[k]) for k in rest]
    w = [jnp.concatenate([w_in[0, k], w_peer[k]], axis=1) for k in pairs] + [w_in[1, k] for k in rest]
    ups = [lift(e_mine, row) for row in rows]
    ups_peer = [lift(e_theirs[k // 2], m_peer[k]) for k in pairs]
    ups = [jnp.concatenate([ups[k], ups_peer[k]], axis=1) for k in pairs] + ups[STEP:]
    x = [ww * rd + up for ww, rd, up in zip(w, rdiag, ups)]
    image = [apply_block(xx, d, *m) for xx, d, m in zip(x, diag, mats)]
    v = [xx + (ww - im) * rd for xx, ww, im, rd in zip(x, w, image, rdiag)]
    left = [(m[0][:, :TILE], m[1][:, :TILE]) for m in mats]
    u = [apply_block(vv, d[:, :TILE], *m) for vv, d, m in zip(v, diag, left)]
    for i in range(2 * STEP):
        vv, b_ref = v[i][:, :TILE], (b_slot if i < STEP else b_rest)
        v_out[i // STEP, i % STEP] = vv
        u_out[i // STEP, i % STEP] = u[i]
        gather(b_ref[i % STEP], z_in[i // STEP, i % STEP], w[i][:, :TILE], vv, u[i])
    acc_a[...] = sums[0]
    acc_b[...] = sums[1]
    acc_c[...] = sums[2]

    @pl.when(step == NSTEP - 1)
    def _():
        first = jnp.sum(jnp.concatenate([sums[0], sums[1]], axis=0).T, axis=0, keepdims=True)
        last = jnp.sum(jnp.concatenate([sums[2], sums[2]], axis=0).T, axis=0, keepdims=True)
        r8 = lax.broadcasted_iota(jnp.int32, (8, TILE), 0)
        extra = jnp.where(r8 == 0, first, jnp.where(r8 == 1, last, 0.0))
        for q in range(GROUPS * PEERS):
            out[q] = extra


def second_part(perm, member, e, dots, b_slot, b_rest, d_slot, d_rest, d_peer, m_peer, hi_pair, lo_pair, hi_rest, lo_rest, maps, z, w, w_peer):
    grid = pltpu.PrefetchScalarGridSpec(
        num_scalar_prefetch=2,
        grid=(NSTEP,),
        in_specs=e_specs()
        + [
            pl.BlockSpec((8, TILE), lambda s, p, m: (0, 0)),
            step_spec(COLS, TILE),
            step_spec(COLS, TILE),
            step_spec(1, TILE),
            step_spec(1, TILE),
            step_spec(1, TILE),
            step_spec(1, TILE),
            step_spec(2 * TILE, 2 * TILE),
            step_spec(2 * TILE, 2 * TILE),
            step_spec(TILE, TILE),
            step_spec(TILE, TILE),
            pl.BlockSpec((BLK, 1, TILE), lambda s, p, m: (0, 0, 0)),
            pair_spec(),
            pair_spec(),
            step_spec(COLS, TILE),
        ],
        out_specs=[
            pair_spec(),
            pair_spec(),
            pl.BlockSpec((GROUPS * PEERS, 8, TILE), lambda s, p, m: (0, 0, 0)),
        ],
        scratch_shapes=[pltpu.VMEM((COLS, TILE), F32)] * 3,
    )
    return pl.pallas_call(
        second_kernel,
        grid_spec=grid,
        out_shape=[
            jax.ShapeDtypeStruct((2, SLOTS, COLS, TILE), F32),
            jax.ShapeDtypeStruct((2, SLOTS, COLS, TILE), F32),
            jax.ShapeDtypeStruct((GROUPS * PEERS, 8, TILE), F32),
        ],
        compiler_params=params(),
        name="second_part",
    )(perm, member, e, e, dots, b_slot, b_rest, d_slot, d_rest, d_peer, m_peer, hi_pair, lo_pair, hi_rest, lo_rest, maps, z, w, w_peer)


def combine_kernel(perm, dots, arrived, b_slot, b_rest, z, w, v, u, solution, residual, coef):
    step = pl.program_id(0)

    @pl.when(step == 0)
    def _():
        total = arrived[0]
        for q in range(1, GROUPS * PEERS):
            total = total + arrived[q]
        old = column(dots[0:1])
        one = column(total[0:1])
        two = column(total[1:2])
        rho, zw = old[:COLS], old[COLS:]
        rho_next, zz = one[:COLS], one[COLS:]
        cross = two[:COLS]
        alpha = rho / zw
        beta = rho_next / rho
        alpha_next = rho_next / (zz + beta * cross + beta * beta * zw)
        coef[0] = alpha
        coef[1] = beta
        coef[2] = alpha_next

    alpha, beta, alpha_next = coef[0], coef[1], coef[2]
    for half, b_ref in ((0, b_slot), (1, b_rest)):
        for k in range(STEP):
            index = perm[half * SLOTS + step * STEP + k]
            at = pl.ds(pl.multiple_of(index * TILE, TILE), TILE)
            z0, w0 = z[half, k], w[half, k]
            z1 = z0 - alpha * v[half, k]
            az1 = w0 - alpha * u[half, k]
            solution[:, at] = alpha * z0 + alpha_next * (z1 + beta * z0)
            residual[:, at] = b_ref[k] - alpha * w0 - alpha_next * (az1 + beta * w0)


def combine(perm, dots, arrived, b_slot, b_rest, z, w, v, u):
    def pair():
        return pl.BlockSpec((2, STEP, COLS, TILE), lambda s, p: (0, s, 0, 0))

    def single():
        return pl.BlockSpec((STEP, COLS, TILE), lambda s, p: (s, 0, 0))

    def whole():
        return pl.BlockSpec((COLS, BLK * TILE), lambda s, p: (0, 0))

    grid = pltpu.PrefetchScalarGridSpec(
        num_scalar_prefetch=1,
        grid=(NSTEP,),
        in_specs=[
            pl.BlockSpec((8, TILE), lambda s, p: (0, 0)),
            pl.BlockSpec((GROUPS * PEERS, 8, TILE), lambda s, p: (0, 0, 0)),
            single(),
            single(),
            pair(),
            pair(),
            pair(),
            pair(),
        ],
        out_specs=[whole(), whole()],
        scratch_shapes=[pltpu.VMEM((3, COLS, TILE), F32)],
    )
    return pl.pallas_call(
        combine_kernel,
        grid_spec=grid,
        out_shape=[jax.ShapeDtypeStruct((COLS, BLK * TILE), F32)] * 2,
        compiler_params=params(),
        name="combine",
    )(perm, dots, arrived, b_slot, b_rest, z, w, v, u)


def exchange(x, axes):
    return lax.all_to_all(x, axes, 0, 0, tiled=True)


def on_device(
    right_side,
    diag_tiles,
    remote_tiles,
    slot_counts,
    slot_blocks,
    fine_map,
    coarse_map,
    level1_ops,
    coarsest_inverse,
):
    group = lax.axis_index("grp")
    member = lax.axis_index(GROUP_AXES).astype(jnp.int32).reshape(1)
    slot_list = slot_blocks.reshape(SLOTS)
    counts = slot_counts.reshape(PEERS)
    maps = fine_map.reshape(BLK, 1, TILE)
    remote = remote_tiles.reshape(SLOTS, TILE, TILE)
    operator = level1_ops[0]

    outgoing = boundary_pack(slot_list, diag_tiles, right_side, maps)
    side = exchange(outgoing.reshape(PEERS, 2 * SIDE, TILE), GROUP_AXES).reshape(SLOTS, SIDE, TILE)

    tile_ids = jnp.arange(BLK, dtype=jnp.int32)
    free = jnp.logical_not(jnp.any(slot_list[:, None] == tile_ids[None, :], axis=0)).astype(jnp.int32)
    rank = jnp.sum(jnp.where(tile_ids[None, :] < tile_ids[:, None], free[None, :], 0), axis=1)
    chosen = (rank[None, :] == jnp.arange(SLOTS, dtype=jnp.int32)[:, None]) & (free[None, :] == 1)
    rest_list = jnp.sum(jnp.where(chosen, tile_ids[None, :], 0), axis=1)
    perm = jnp.concatenate([slot_list, rest_list])

    b_slot, b_rest, d_slot, d_rest, hi_rest, lo_rest, rs, rr_local = local_part(
        perm, counts, diag_tiles, right_side, remote, maps
    )
    g, inverse = coarse_setup(operator, coarse_map.reshape(1, NC1))
    inverse_cols = lax.dynamic_slice_in_dim(coarsest_inverse, group * AGG, AGG, 1)

    def level_one(arrived):
        x, outgoing = lowest_part(arrived, g)
        lows = exchange(outgoing, "grp")
        h = smooth_part(x, inverse, operator)
        return correct_part(lows, inverse_cols, g, h)

    gathered = exchange(first_restrict(side, rs, rr_local), GROUP_AXES)
    hi_pair, lo_pair, d_peer, m_peer = pair_setup(perm, counts, diag_tiles, side, remote)
    e, _ = level_one(gathered)
    z, w, w_peer, outgoing = forward_part(
        perm, member, e, b_slot, b_rest, d_slot, d_rest, side, d_peer, m_peer, hi_pair, lo_pair, hi_rest, lo_rest, maps
    )
    e, dots = level_one(exchange(outgoing, GROUP_AXES))
    v, u, outgoing = second_part(
        perm, member, e, dots, b_slot, b_rest, d_slot, d_rest, d_peer, m_peer, hi_pair, lo_pair, hi_rest, lo_rest, maps, z, w, w_peer
    )
    sums = exchange(outgoing, ALL_AXES)
    return tuple(combine(perm, dots, sums, b_slot, b_rest, z, w, v, u))


def solution(mesh):
    placed = (
        P(None, ("grp", "sub", "chip")),
        P(("grp", "sub", "chip"), None, None),
        P(("grp", "sub", "chip"), None, None, None),
        P(("grp", "sub", "chip"), None),
        P(("grp", "sub", "chip"), None, None),
        P(("grp", "sub", "chip")),
        P("grp"),
        P("grp", None, None),
        P(),
    )
    return jax.shard_map(
        on_device,
        mesh=mesh,
        in_specs=placed,
        out_specs=(P(None, ("grp", "sub", "chip")), P(None, ("grp", "sub", "chip"))),
        check_vma=False,
    )
```

```python
import functools

import jax
import jax.numpy as jnp
from jax import lax
from jax.experimental import pallas as pl
from jax.experimental.pallas import tpu as pltpu
from jax.sharding import PartitionSpec as P

OMEGA = 0.6
F32 = jnp.float32
BF16 = jnp.bfloat16
COLS = 64
TILE = 128
BLK = 64
SLOTS = 32
PEERS = 16
GROUPS = 8
AGG = 64
NC1 = 1024
STEP = 8
NSTEP = SLOTS // STEP
SIDE = 136
ROWS = 40
VMEM_LIMIT = 24 * 1024 * 1024

GROUP_AXES = ("sub", "chip")
ALL_AXES = ("grp", "sub", "chip")


def params():
    return pltpu.CompilerParams(vmem_limit_bytes=VMEM_LIMIT)


def hbm(x):
    return pltpu.with_memory_space_constraint(x, pltpu.HBM)


def far(shape, dtype=F32):
    return pltpu.HBM(shape, dtype)


def cost(flops, moved):
    return pl.CostEstimate(flops=flops, bytes_accessed=moved, transcendentals=0)


def split2(x):
    hi = x.astype(BF16)
    lo = (x - hi.astype(F32)).astype(BF16)
    return hi, lo


def dot(a, b):
    return jnp.dot(a, b, preferred_element_type=F32)


def dot_nt(a, b):
    return lax.dot_general(a, b, (((1,), (1,)), ((), ())), preferred_element_type=F32)


def mm(x, whi, wlo, nt=False):
    op = dot_nt if nt else dot
    rows = x.shape[0]
    hi, lo = split2(x)
    both = op(jnp.concatenate([hi, lo], axis=0), whi)
    return both[:rows] + both[rows:] + op(hi, wlo)


def mm_exact(x, w, nt=False):
    op = dot_nt if nt else dot
    rows = x.shape[0]
    two = op(jnp.concatenate(split2(x), axis=0), w)
    return two[:rows] + two[rows:]


def beside(a, b):
    return jnp.concatenate([a, b], axis=1)


def eye_mask():
    r = lax.broadcasted_iota(jnp.int32, (TILE, TILE), 0)
    c = lax.broadcasted_iota(jnp.int32, (TILE, TILE), 1)
    return r, c


def tile_diag(tile):
    r, c = eye_mask()
    return jnp.sum(jnp.where(r == c, tile, 0.0), axis=0, keepdims=True)


def off_diag(tile):
    r, c = eye_mask()
    return jnp.where(r == c, 0.0, tile)


def one_hot(row):
    r = lax.broadcasted_iota(jnp.int32, (AGG, row.shape[1]), 0)
    return jnp.where(r == row, 1.0, 0.0).astype(BF16)


def pack_rows(x):
    wide = jnp.concatenate([x[:32], x[32:]], axis=1)
    return wide


def column(row):
    return jnp.broadcast_to(row, (TILE, TILE)).T


def boundary_kernel(slots, maps, tiles, cols, out, tile_buf, col_buf, out_buf, tile_sem, col_sem, out_sem):
    def tile_copy(j):
        return pltpu.make_async_copy(tiles.at[slots[0, j // 2, j % 2]], tile_buf.at[j], tile_sem.at[j])

    def col_copy(j):
        at = pl.ds(pl.multiple_of(slots[0, j // 2, j % 2] * TILE, TILE), TILE)
        return pltpu.make_async_copy(cols.at[:, at], col_buf.at[j], col_sem.at[j])

    def out_copy(j):
        return pltpu.make_async_copy(out_buf.at[j], out.at[j], out_sem.at[j])

    for j in range(SLOTS):
        tile_copy(j).start()
        col_copy(j).start()
    r = lax.broadcasted_iota(jnp.int32, (64, TILE), 0)
    c = lax.broadcasted_iota(jnp.int32, (64, TILE), 1)
    r8 = lax.broadcasted_iota(jnp.int32, (8, TILE), 0)
    for j in range(SLOTS):
        tile_copy(j).wait()
        col_copy(j).wait()
        tile = tile_buf[j]
        diag = tile_diag(tile)
        out_buf[j, 0:64] = col_buf[j] * (OMEGA / diag)
        below = pltpu.roll(tile[64:], 64, 1)
        out_buf[j, 64:128] = jnp.where((c < 64) & (r > c), below, tile[:64])
        row = maps[pl.ds(slots[0, j // 2, j % 2], 1)].astype(F32)
        out_buf[j, 128:136] = jnp.where(r8 == 0, diag, jnp.where(r8 == 1, row, 0.0))
        out_copy(j).start()
    for j in range(SLOTS):
        out_copy(j).wait()


def boundary_pack(slot_blocks, diag_tiles, right_side, maps):
    return pl.pallas_call(
        boundary_kernel,
        in_specs=[
            pl.BlockSpec(memory_space=pltpu.SMEM),
            pl.BlockSpec(memory_space=pltpu.VMEM),
            pl.BlockSpec(memory_space=pl.ANY),
            pl.BlockSpec(memory_space=pl.ANY),
        ],
        out_specs=pl.BlockSpec(memory_space=pl.ANY),
        out_shape=far((SLOTS, SIDE, TILE)),
        scratch_shapes=[
            pltpu.VMEM((SLOTS, TILE, TILE), F32),
            pltpu.VMEM((SLOTS, COLS, TILE), F32),
            pltpu.VMEM((SLOTS, SIDE, TILE), F32),
            pltpu.SemaphoreType.DMA((SLOTS,)),
            pltpu.SemaphoreType.DMA((SLOTS,)),
            pltpu.SemaphoreType.DMA((SLOTS,)),
        ],
        compiler_params=params(),
        name="boundary_pack",
    )(slot_blocks, maps, hbm(diag_tiles), hbm(right_side))


def local_kernel(perm, counts, *refs):
    n = 2 * STEP
    tiles, cols = refs[:n], refs[n : 2 * n]
    remote, maps = refs[2 * n : 2 * n + 2]
    b_slot, b_rest, d_slot, d_rest, hi_rest, lo_rest, rs, rr = refs[2 * n + 2 :]
    step = pl.program_id(0)

    @pl.when(step == 0)
    def _():
        rr[...] = jnp.zeros_like(rr)

    index = [perm[(0 if i < STEP else SLOTS) + step * STEP + i % STEP] for i in range(n)]
    tile = [tiles[i][0] for i in range(n)]
    diag = [tile_diag(t) for t in tile]
    off = [split2(off_diag(t)) for t in tile]
    b = [cols[i][...] for i in range(n)]
    x = [OMEGA * bb / d for bb, d in zip(b, diag)]
    y = [bb - OMEGA * bb - mm(xx, *o) for bb, xx, o in zip(b, x, off)]
    spread = [one_hot(maps[pl.ds(i, 1)]) for i in index]
    total = rr[...]
    for i in range(0, n, 2):
        total = total + mm_exact(beside(y[i], y[i + 1]), beside(spread[i], spread[i + 1]), nt=True)
    for k in range(STEP):
        b_slot[k] = b[k]
        d_slot[k] = diag[k]
        b_rest[k] = b[STEP + k]
        d_rest[k] = diag[STEP + k]
        hi_rest[k], lo_rest[k] = off[STEP + k]
    scaled = []
    for k in range(STEP):
        j = step * STEP + k
        live = (j % 2) < counts[j // 2]
        scaled.append(split2(remote[k] * jnp.where(live, 1.0, 0.0)))
    for k in range(STEP):
        rs[k] = dot_nt(spread[k], scaled[k][0]) + dot_nt(spread[k], scaled[k][1])
    rr[...] = total


def local_part(perm, counts, diag_tiles, right_side, remote, maps):
    def where(i):
        return (0 if i < STEP else SLOTS) + i % STEP

    def tile_spec(i):
        return pl.BlockSpec((1, TILE, TILE), lambda s, p, c: (p[s * STEP + where(i)], 0, 0))

    def col_spec(i):
        return pl.BlockSpec((COLS, TILE), lambda s, p, c: (0, p[s * STEP + where(i)]))

    def out(*shape):
        return pl.BlockSpec((STEP,) + shape, lambda s, p, c: (s, 0, 0))

    n = 2 * STEP
    grid = pltpu.PrefetchScalarGridSpec(
        num_scalar_prefetch=2,
        grid=(NSTEP,),
        in_specs=[tile_spec(i) for i in range(n)]
        + [col_spec(i) for i in range(n)]
        + [
            pl.BlockSpec((STEP, TILE, TILE), lambda s, p, c: (s, 0, 0)),
            pl.BlockSpec((BLK, TILE), lambda s, p, c: (0, 0)),
        ],
        out_specs=[
            out(COLS, TILE),
            out(COLS, TILE),
            out(1, TILE),
            out(1, TILE),
            out(TILE, TILE),
            out(TILE, TILE),
            out(AGG, TILE),
            pl.BlockSpec((COLS, AGG), lambda s, p, c: (0, 0)),
        ],
    )

    def sds(shape, dtype=F32):
        return far((SLOTS,) + shape, dtype)

    return pl.pallas_call(
        local_kernel,
        grid_spec=grid,
        out_shape=[
            sds((COLS, TILE)),
            sds((COLS, TILE)),
            sds((1, TILE)),
            sds((1, TILE)),
            sds((TILE, TILE), BF16),
            sds((TILE, TILE), BF16),
            sds((AGG, TILE)),
            jax.ShapeDtypeStruct((COLS, AGG), F32),
        ],
        compiler_params=params(),
        cost_estimate=cost(2 * 64 * 3 * 64 * 128 * 128, 16 << 20),
        name="local_part",
    )(perm, counts, *([hbm(diag_tiles)] * n), *([hbm(right_side)] * n), hbm(remote), maps)


def coarse_kernel(op, cmap, g_out, d_out):
    spread = one_hot(cmap[...])
    product = exact_spread(spread, op)
    pieces = []
    for i in range(NC1 // TILE):
        pieces.append(tile_diag(op[i * TILE : (i + 1) * TILE, i * TILE : (i + 1) * TILE]))
    diag = jnp.concatenate(pieces, axis=1)
    inverse = 1.0 / diag
    d_out[...] = inverse
    g_out[...] = spread.astype(F32) - OMEGA * product * inverse


def exact_spread(spread, op):
    total = None
    for i in range(NC1 // 256):
        rows = slice(i * 256, (i + 1) * 256)
        hi, lo = split2(op[rows, :])
        part = dot(spread[:, rows], hi) + dot(spread[:, rows], lo)
        total = part if total is None else total + part
    return total


def coarse_setup(op, cmap):
    return pl.pallas_call(
        coarse_kernel,
        out_shape=[jax.ShapeDtypeStruct((AGG, NC1), F32), jax.ShapeDtypeStruct((1, NC1), F32)],
        compiler_params=params(),
        cost_estimate=cost(2 * 2 * 64 * 1024 * 1024, 5 << 20),
        name="coarse_setup",
    )(op, cmap)


def first_restrict_kernel(arrived, rs, rr, out, acc):
    step = pl.program_id(0)

    @pl.when(step == 0)
    def _():
        acc[...] = rr[...]

    total = acc[...]
    for j in range(0, STEP, 2):
        hi, lo = split2(beside(rs[j], rs[j + 1]))
        total = total + mm(beside(arrived[j], arrived[j + 1]), hi, lo, nt=True)
    acc[...] = total

    @pl.when(step == NSTEP - 1)
    def _():
        packed = pack_rows(total)
        for q in range(PEERS):
            out[q, 0:32] = packed
            out[q, 32:40] = jnp.zeros((8, TILE), F32)


def first_restrict(arrived, rs, rr):
    return pl.pallas_call(
        first_restrict_kernel,
        grid=(NSTEP,),
        in_specs=[
            pl.BlockSpec((STEP, COLS, TILE), lambda s: (s, 0, 0)),
            pl.BlockSpec((STEP, AGG, TILE), lambda s: (s, 0, 0)),
            pl.BlockSpec((COLS, AGG), lambda s: (0, 0)),
        ],
        out_specs=pl.BlockSpec((PEERS, ROWS, TILE), lambda s: (0, 0, 0)),
        out_shape=jax.ShapeDtypeStruct((PEERS, ROWS, TILE), F32),
        scratch_shapes=[pltpu.VMEM((COLS, AGG), F32)],
        compiler_params=params(),
        name="first_restrict",
    )(hbm(arrived), hbm(rs), rr)


def pair_kernel(perm, counts, *refs):
    tiles, side, remote, hi_out, lo_out, diag_out, map_out = (refs[:STEP],) + tuple(refs[STEP:])
    step = pl.program_id(0)
    r = lax.broadcasted_iota(jnp.int32, (64, TILE), 0)
    c = lax.broadcasted_iota(jnp.int32, (64, TILE), 1)
    for k in range(STEP):
        own = off_diag(tiles[k][0])
        packed = side[k, 64:128]
        top = jnp.where((c >= 64) | (r < c), packed, 0.0)
        bottom = pltpu.roll(jnp.where((c < 64) & (r > c), packed, 0.0), 64, 1)
        half = jnp.concatenate([top, bottom], axis=0)
        other = half + half.T
        j = step * STEP + k
        live = (j % 2) < counts[j // 2]
        rem = remote[k] * jnp.where(live, -1.0, 0.0)
        block = jnp.concatenate(
            [jnp.concatenate([own, rem.T], axis=1), jnp.concatenate([rem, other], axis=1)], axis=0
        )
        hi, lo = split2(block)
        hi_out[k] = hi
        lo_out[k] = lo
        diag_out[k] = side[k, 128:129]
        map_out[k] = side[k, 129:130].astype(jnp.int32)


def pair_setup(perm, counts, diag_tiles, side, remote):
    def tile_spec(i):
        return pl.BlockSpec((1, TILE, TILE), lambda s, p, c: (p[s * STEP + i], 0, 0))

    def spec(*shape):
        return pl.BlockSpec((STEP,) + shape, lambda s, p, c: (s, 0, 0))

    grid = pltpu.PrefetchScalarGridSpec(
        num_scalar_prefetch=2,
        grid=(NSTEP,),
        in_specs=[tile_spec(i) for i in range(STEP)] + [spec(SIDE, TILE), spec(TILE, TILE)],
        out_specs=[spec(2 * TILE, 2 * TILE), spec(2 * TILE, 2 * TILE), spec(1, TILE), spec(1, TILE)],
    )
    return pl.pallas_call(
        pair_kernel,
        grid_spec=grid,
        out_shape=[
            far((SLOTS, 2 * TILE, 2 * TILE), BF16),
            far((SLOTS, 2 * TILE, 2 * TILE), BF16),
            far((SLOTS, 1, TILE)),
            far((SLOTS, 1, TILE), jnp.int32),
        ],
        compiler_params=params(),
        cost_estimate=cost(2 * 64 * 3 * 64 * 128 * 128, 16 << 20),
        name="pair_setup",
    )(perm, counts, *([hbm(diag_tiles)] * STEP), hbm(side), hbm(remote))


def gathered_rows(ref, count):
    lane = lax.broadcasted_iota(jnp.int32, (32, TILE), 1) < 64
    tops, bottoms = [], []
    for q in range(0, count, 2):
        a, b = ref[q, 0:32], ref[q + 1, 0:32]
        tops.append(jnp.where(lane, a, pltpu.roll(b, 64, 1)))
        bottoms.append(jnp.where(lane, pltpu.roll(a, 64, 1), b))
    return jnp.concatenate([jnp.concatenate(tops, axis=1), jnp.concatenate(bottoms, axis=1)], axis=0)


def lowest_kernel(arrived, g, x_out, out):
    x = gathered_rows(arrived, PEERS)
    x_out[...] = x
    hi, lo = split2(g[...])
    packed = pack_rows(mm(x, hi, lo, nt=True))
    extra = arrived[0, 32:40]
    for q in range(1, PEERS):
        extra = extra + arrived[q, 32:40]
    for q in range(GROUPS):
        out[q, 0:32] = packed
        out[q, 32:40] = extra


def lowest_part(arrived, g):
    return pl.pallas_call(
        lowest_kernel,
        out_shape=[
            jax.ShapeDtypeStruct((COLS, NC1), F32),
            jax.ShapeDtypeStruct((GROUPS, ROWS, TILE), F32),
        ],
        compiler_params=params(),
        name="lowest_part",
    )(arrived, g)


def smooth_kernel(x_ref, inverse_ref, op, out):
    inverse = inverse_ref[...]
    scaled = x_ref[...] * inverse
    total = None
    for i in range(NC1 // 256):
        rows = slice(i * 256, (i + 1) * 256)
        hi, lo = split2(op[rows, :])
        part = mm(scaled[:, rows], hi, lo)
        total = part if total is None else total + part
    out[...] = 2.0 * OMEGA * scaled - OMEGA * OMEGA * total * inverse


def smooth_part(x, inverse, op):
    return pl.pallas_call(
        smooth_kernel,
        out_shape=jax.ShapeDtypeStruct((COLS, NC1), F32),
        compiler_params=params(),
        cost_estimate=cost(2 * 3 * 64 * 1024 * 1024, 5 << 20),
        name="smooth_part",
    )(x, inverse, op)


def correct_kernel(arrived, inverse_cols, g, h, e_out, dots):
    low = gathered_rows(arrived, GROUPS)
    hi, lo = split2(inverse_cols[...])
    corr = mm(low, hi, lo)
    ghi, glo = split2(g[...])
    e = h[...] + mm(corr, ghi, glo)
    for q in range(PEERS):
        e_out[q] = e[:, q * AGG : (q + 1) * AGG]
    extra = arrived[0, 32:40]
    for q in range(1, GROUPS):
        extra = extra + arrived[q, 32:40]
    dots[...] = extra


def correct_part(arrived, inverse_cols, g, h):
    return pl.pallas_call(
        correct_kernel,
        out_shape=[jax.ShapeDtypeStruct((PEERS, COLS, AGG), F32), jax.ShapeDtypeStruct((8, TILE), F32)],
        compiler_params=params(),
        name="correct_part",
    )(arrived, inverse_cols, g, h)


def apply_block(x, diag, hi, lo):
    xh, xl = split2(x)
    rows = x.shape[0]
    both = dot(jnp.concatenate([xh, xl], axis=0), hi)
    kept = xh.astype(F32) + xl.astype(F32)
    return both[:rows] + both[rows:] + dot(xh, lo) + kept[:, : diag.shape[1]] * diag


def lift(parts, spread):
    rows = parts.shape[0] // 2
    two = dot(parts, spread)
    return two[:rows] + two[rows:]


def two_parts(e):
    return jnp.concatenate(split2(e), axis=0)


def pair_spread(own, peer):
    none = jnp.zeros_like(own)
    return jnp.concatenate([beside(own, none), beside(none, peer)], axis=0)


def forward_kernel(
    perm, member, e_own, e_peer, b_slot, b_rest, d_slot, d_rest, x_peer, d_peer, m_peer, hi_pair, lo_pair,
    hi_rest, lo_rest, maps, z_out, w_out, ws_out, out, acc_rr, acc_bz, acc_zw
):
    step = pl.program_id(0)

    @pl.when(step == 0)
    def _():
        acc_rr[...] = jnp.zeros_like(acc_rr)
        acc_bz[...] = jnp.zeros_like(acc_bz)
        acc_zw[...] = jnp.zeros_like(acc_zw)

    e_mine = two_parts(e_own[0])
    e_both = [two_parts(beside(e_own[0], e_peer[q])) for q in range(STEP // 2)]
    rr, bz, zw = acc_rr[...], acc_bz[...], acc_zw[...]
    pairs, rest = range(STEP), range(STEP)
    rows = [maps[pl.ds(perm[at + step * STEP + k], 1)] for at in (0, SLOTS) for k in pairs]
    b_own = [b_slot[k] for k in pairs] + [b_rest[k] for k in rest]
    diag = [jnp.concatenate([d_slot[k], d_peer[k]], axis=1) for k in pairs] + [d_rest[k] for k in rest]
    rdiag = [OMEGA / d for d in diag]
    mats = [(hi_pair[k], lo_pair[k]) for k in pairs] + [(hi_rest[k], lo_rest[k]) for k in rest]
    full = [
        jnp.concatenate([b_own[k], x_peer[k] * (d_peer[k] * (1.0 / OMEGA))], axis=1) for k in pairs
    ] + b_own[STEP:]
    spread = [one_hot(row) for row in rows]
    ups = [lift(e_both[k // 2], pair_spread(spread[k], one_hot(m_peer[k]))) for k in pairs]
    ups = ups + [lift(e_mine, sp) for sp in spread[STEP:]]
    x = [f * rd + up for f, rd, up in zip(full, rdiag, ups)]
    image = [apply_block(xx, d, *m) for xx, d, m in zip(x, diag, mats)]
    z = [xx + (f - im) * rd for xx, f, im, rd in zip(x, full, image, rdiag)]
    w = [apply_block(zz, d, *m) for zz, d, m in zip(z, diag, mats)]
    x1 = [ww * rd for ww, rd in zip(w, rdiag)]
    left = [(m[0][:, :TILE], m[1][:, :TILE]) for m in mats]
    y = [
        ww[:, :TILE] - apply_block(xx, d[:, :TILE], *m) for ww, xx, d, m in zip(w, x1, diag, left)
    ]
    for i in range(0, 2 * STEP, 2):
        rr = rr + mm_exact(beside(y[i], y[i + 1]), beside(spread[i], spread[i + 1]), nt=True)
    for i in range(2 * STEP):
        zz, ww = z[i][:, :TILE], w[i][:, :TILE]
        bz = bz + b_own[i] * zz
        zw = zw + zz * ww
        z_out[i // STEP, i % STEP] = zz
        w_out[i // STEP, i % STEP] = ww
    for k in pairs:
        ws_out[k] = w[k][:, TILE:]
    acc_rr[...] = rr
    acc_bz[...] = bz
    acc_zw[...] = zw

    @pl.when(step == NSTEP - 1)
    def _():
        packed = pack_rows(rr)
        sums = jnp.sum(jnp.concatenate([bz, zw], axis=0).T, axis=0, keepdims=True)
        r8 = lax.broadcasted_iota(jnp.int32, (8, TILE), 0)
        extra = jnp.where(r8 == 0, sums, 0.0)
        for q in range(PEERS):
            out[q, 0:32] = packed
            out[q, 32:40] = extra


def step_spec(*shape):
    return pl.BlockSpec((STEP,) + shape, lambda s, p, m: (s, 0, 0))


def pair_spec():
    return pl.BlockSpec((2, STEP, COLS, TILE), lambda s, p, m: (0, s, 0, 0))


def e_specs():
    return [
        pl.BlockSpec((1, COLS, AGG), lambda s, p, m: (m[0], 0, 0)),
        pl.BlockSpec((STEP // 2, COLS, AGG), lambda s, p, m: (s, 0, 0)),
    ]


def forward_part(perm, member, e, b_slot, b_rest, d_slot, d_rest, x_peer, d_peer, m_peer, hi_pair, lo_pair, hi_rest, lo_rest, maps):
    grid = pltpu.PrefetchScalarGridSpec(
        num_scalar_prefetch=2,
        grid=(NSTEP,),
        in_specs=e_specs()
        + [
            step_spec(COLS, TILE),
            step_spec(COLS, TILE),
            step_spec(1, TILE),
            step_spec(1, TILE),
            step_spec(COLS, TILE),
            step_spec(1, TILE),
            step_spec(1, TILE),
            step_spec(2 * TILE, 2 * TILE),
            step_spec(2 * TILE, 2 * TILE),
            step_spec(TILE, TILE),
            step_spec(TILE, TILE),
            pl.BlockSpec((BLK, TILE), lambda s, p, m: (0, 0)),
        ],
        out_specs=[
            pair_spec(),
            pair_spec(),
            step_spec(COLS, TILE),
            pl.BlockSpec((PEERS, ROWS, TILE), lambda s, p, m: (0, 0, 0)),
        ],
        scratch_shapes=[pltpu.VMEM((COLS, AGG), F32), pltpu.VMEM((COLS, TILE), F32), pltpu.VMEM((COLS, TILE), F32)],
    )
    return pl.pallas_call(
        forward_kernel,
        grid_spec=grid,
        out_shape=[
            far((2, SLOTS, COLS, TILE)),
            far((2, SLOTS, COLS, TILE)),
            far((SLOTS, COLS, TILE)),
            jax.ShapeDtypeStruct((PEERS, ROWS, TILE), F32),
        ],
        compiler_params=params(),
        name="forward_part",
    )(perm, member, e, e, *map(hbm, (b_slot, b_rest, d_slot, d_rest, x_peer, d_peer, m_peer, hi_pair, lo_pair, hi_rest, lo_rest)), maps)


def second_kernel(
    perm, member, e_own, e_peer, dots, b_slot, b_rest, d_slot, d_rest, d_peer, m_peer, hi_pair, lo_pair,
    hi_rest, lo_rest, maps, z_in, w_in, w_peer, v_out, u_out, out, acc_a, acc_b, acc_c
):
    step = pl.program_id(0)

    @pl.when(step == 0)
    def _():
        acc_a[...] = jnp.zeros_like(acc_a)
        acc_b[...] = jnp.zeros_like(acc_b)
        acc_c[...] = jnp.zeros_like(acc_c)

    col = column(dots[0:1])
    alpha = col[:COLS] / col[COLS:]
    e_mine = two_parts(e_own[0])
    e_both = [two_parts(beside(e_own[0], e_peer[q])) for q in range(STEP // 2)]
    sums = [acc_a[...], acc_b[...], acc_c[...]]

    def gather(b, z, w, v, u):
        r1 = b - alpha * w
        z1 = z - alpha * v
        az1 = w - alpha * u
        sums[0] = sums[0] + r1 * z1
        sums[1] = sums[1] + z1 * az1
        sums[2] = sums[2] + (z1 * w + z * az1)

    pairs, rest = range(STEP), range(STEP)
    rows = [maps[pl.ds(perm[at + step * STEP + k], 1)] for at in (0, SLOTS) for k in pairs]
    diag = [jnp.concatenate([d_slot[k], d_peer[k]], axis=1) for k in pairs] + [d_rest[k] for k in rest]
    rdiag = [OMEGA / d for d in diag]
    mats = [(hi_pair[k], lo_pair[k]) for k in pairs] + [(hi_rest[k], lo_rest[k]) for k in rest]
    w = [jnp.concatenate([w_in[0, k], w_peer[k]], axis=1) for k in pairs] + [w_in[1, k] for k in rest]
    spread = [one_hot(row) for row in rows]
    ups = [lift(e_both[k // 2], pair_spread(spread[k], one_hot(m_peer[k]))) for k in pairs]
    ups = ups + [lift(e_mine, sp) for sp in spread[STEP:]]
    x = [ww * rd + up for ww, rd, up in zip(w, rdiag, ups)]
    image = [apply_block(xx, d, *m) for xx, d, m in zip(x, diag, mats)]
    v = [xx + (ww - im) * rd for xx, ww, im, rd in zip(x, w, image, rdiag)]
    left = [(m[0][:, :TILE], m[1][:, :TILE]) for m in mats]
    u = [apply_block(vv, d[:, :TILE], *m) for vv, d, m in zip(v, diag, left)]
    for i in range(2 * STEP):
        vv, b_ref = v[i][:, :TILE], (b_slot if i < STEP else b_rest)
        v_out[i // STEP, i % STEP] = vv
        u_out[i // STEP, i % STEP] = u[i]
        gather(b_ref[i % STEP], z_in[i // STEP, i % STEP], w[i][:, :TILE], vv, u[i])
    acc_a[...] = sums[0]
    acc_b[...] = sums[1]
    acc_c[...] = sums[2]

    @pl.when(step == NSTEP - 1)
    def _():
        first = jnp.sum(jnp.concatenate([sums[0], sums[1]], axis=0).T, axis=0, keepdims=True)
        last = jnp.sum(jnp.concatenate([sums[2], sums[2]], axis=0).T, axis=0, keepdims=True)
        r8 = lax.broadcasted_iota(jnp.int32, (8, TILE), 0)
        extra = jnp.where(r8 == 0, first, jnp.where(r8 == 1, last, 0.0))
        for q in range(GROUPS * PEERS):
            out[q] = extra


def second_part(perm, member, e, dots, b_slot, b_rest, d_slot, d_rest, d_peer, m_peer, hi_pair, lo_pair, hi_rest, lo_rest, maps, z, w, w_peer):
    grid = pltpu.PrefetchScalarGridSpec(
        num_scalar_prefetch=2,
        grid=(NSTEP,),
        in_specs=e_specs()
        + [
            pl.BlockSpec((8, TILE), lambda s, p, m: (0, 0)),
            step_spec(COLS, TILE),
            step_spec(COLS, TILE),
            step_spec(1, TILE),
            step_spec(1, TILE),
            step_spec(1, TILE),
            step_spec(1, TILE),
            step_spec(2 * TILE, 2 * TILE),
            step_spec(2 * TILE, 2 * TILE),
            step_spec(TILE, TILE),
            step_spec(TILE, TILE),
            pl.BlockSpec((BLK, TILE), lambda s, p, m: (0, 0)),
            pair_spec(),
            pair_spec(),
            step_spec(COLS, TILE),
        ],
        out_specs=[
            pair_spec(),
            pair_spec(),
            pl.BlockSpec((GROUPS * PEERS, 8, TILE), lambda s, p, m: (0, 0, 0)),
        ],
        scratch_shapes=[pltpu.VMEM((COLS, TILE), F32)] * 3,
    )
    return pl.pallas_call(
        second_kernel,
        grid_spec=grid,
        out_shape=[
            far((2, SLOTS, COLS, TILE)),
            far((2, SLOTS, COLS, TILE)),
            jax.ShapeDtypeStruct((GROUPS * PEERS, 8, TILE), F32),
        ],
        compiler_params=params(),
        name="second_part",
    )(perm, member, e, e, dots, *map(hbm, (b_slot, b_rest, d_slot, d_rest, d_peer, m_peer, hi_pair, lo_pair, hi_rest, lo_rest)), maps, *map(hbm, (z, w, w_peer)))


def combine_kernel(perm, dots, arrived, b_slot, b_rest, z, w, v, u, solution, residual, coef):
    step = pl.program_id(0)

    @pl.when(step == 0)
    def _():
        total = arrived[0]
        for q in range(1, GROUPS * PEERS):
            total = total + arrived[q]
        old = column(dots[0:1])
        one = column(total[0:1])
        two = column(total[1:2])
        rho, zw = old[:COLS], old[COLS:]
        rho_next, zz = one[:COLS], one[COLS:]
        cross = two[:COLS]
        alpha = rho / zw
        beta = rho_next / rho
        alpha_next = rho_next / (zz + beta * cross + beta * beta * zw)
        coef[0] = alpha
        coef[1] = beta
        coef[2] = alpha_next

    alpha, beta, alpha_next = coef[0], coef[1], coef[2]
    for half, b_ref in ((0, b_slot), (1, b_rest)):
        for k in range(STEP):
            index = perm[half * SLOTS + step * STEP + k]
            at = pl.ds(pl.multiple_of(index * TILE, TILE), TILE)
            z0, w0 = z[half, k], w[half, k]
            z1 = z0 - alpha * v[half, k]
            az1 = w0 - alpha * u[half, k]
            solution[:, at] = alpha * z0 + alpha_next * (z1 + beta * z0)
            residual[:, at] = b_ref[k] - alpha * w0 - alpha_next * (az1 + beta * w0)


def combine(perm, dots, arrived, b_slot, b_rest, z, w, v, u):
    def pair():
        return pl.BlockSpec((2, STEP, COLS, TILE), lambda s, p: (0, s, 0, 0))

    def single():
        return pl.BlockSpec((STEP, COLS, TILE), lambda s, p: (s, 0, 0))

    def whole():
        return pl.BlockSpec((COLS, BLK * TILE), lambda s, p: (0, 0))

    grid = pltpu.PrefetchScalarGridSpec(
        num_scalar_prefetch=1,
        grid=(NSTEP,),
        in_specs=[
            pl.BlockSpec((8, TILE), lambda s, p: (0, 0)),
            pl.BlockSpec((GROUPS * PEERS, 8, TILE), lambda s, p: (0, 0, 0)),
            single(),
            single(),
            pair(),
            pair(),
            pair(),
            pair(),
        ],
        out_specs=[whole(), whole()],
        scratch_shapes=[pltpu.VMEM((3, COLS, TILE), F32)],
    )
    return pl.pallas_call(
        combine_kernel,
        grid_spec=grid,
        out_shape=[jax.ShapeDtypeStruct((COLS, BLK * TILE), F32)] * 2,
        compiler_params=params(),
        name="combine",
    )(perm, dots, arrived, b_slot, b_rest, z, w, v, u)


def exchange(x, axes):
    return lax.all_to_all(x, axes, 0, 0, tiled=True)


def on_device(
    right_side,
    diag_tiles,
    remote_tiles,
    slot_counts,
    slot_blocks,
    fine_map,
    coarse_map,
    level1_ops,
    coarsest_inverse,
):
    group = lax.axis_index("grp")
    member = lax.axis_index(GROUP_AXES).astype(jnp.int32).reshape(1)
    slot_list = slot_blocks.reshape(SLOTS)
    counts = slot_counts.reshape(PEERS)
    maps = fine_map.reshape(BLK, TILE)
    remote = remote_tiles.reshape(SLOTS, TILE, TILE)
    operator = level1_ops[0]

    outgoing = boundary_pack(slot_blocks, diag_tiles, right_side, maps)
    side = exchange(outgoing.reshape(PEERS, 2 * SIDE, TILE), GROUP_AXES).reshape(SLOTS, SIDE, TILE)

    tile_ids = jnp.arange(BLK, dtype=jnp.int32)
    free = jnp.logical_not(jnp.any(slot_list[:, None] == tile_ids[None, :], axis=0)).astype(jnp.int32)
    rank = jnp.sum(jnp.where(tile_ids[None, :] < tile_ids[:, None], free[None, :], 0), axis=1)
    chosen = (rank[None, :] == jnp.arange(SLOTS, dtype=jnp.int32)[:, None]) & (free[None, :] == 1)
    rest_list = jnp.sum(jnp.where(chosen, tile_ids[None, :], 0), axis=1)
    perm = jnp.concatenate([slot_list, rest_list])

    b_slot, b_rest, d_slot, d_rest, hi_rest, lo_rest, rs, rr_local = local_part(
        perm, counts, diag_tiles, right_side, remote, maps
    )
    g, inverse = coarse_setup(operator, coarse_map.reshape(1, NC1))
    inverse_cols = lax.dynamic_slice_in_dim(coarsest_inverse, group * AGG, AGG, 1)

    def level_one(arrived):
        x, outgoing = lowest_part(arrived, g)
        lows = exchange(outgoing, "grp")
        h = smooth_part(x, inverse, operator)
        return correct_part(lows, inverse_cols, g, h)

    gathered = exchange(first_restrict(side, rs, rr_local), GROUP_AXES)
    hi_pair, lo_pair, d_peer, m_peer = pair_setup(perm, counts, diag_tiles, side, remote)
    e, _ = level_one(gathered)
    z, w, w_peer, outgoing = forward_part(
        perm, member, e, b_slot, b_rest, d_slot, d_rest, side, d_peer, m_peer, hi_pair, lo_pair, hi_rest, lo_rest, maps
    )
    e, dots = level_one(exchange(outgoing, GROUP_AXES))
    v, u, outgoing = second_part(
        perm, member, e, dots, b_slot, b_rest, d_slot, d_rest, d_peer, m_peer, hi_pair, lo_pair, hi_rest, lo_rest, maps, z, w, w_peer
    )
    sums = exchange(outgoing, ALL_AXES)
    return tuple(combine(perm, dots, sums, b_slot, b_rest, z, w, v, u))


def solution(mesh):
    placed = (
        P(None, ("grp", "sub", "chip")),
        P(("grp", "sub", "chip"), None, None),
        P(("grp", "sub", "chip"), None, None, None),
        P(("grp", "sub", "chip"), None),
        P(("grp", "sub", "chip"), None, None),
        P(("grp", "sub", "chip")),
        P("grp"),
        P("grp", None, None),
        P(),
    )
    return jax.shard_map(
        on_device,
        mesh=mesh,
        in_specs=placed,
        out_specs=(P(None, ("grp", "sub", "chip")), P(None, ("grp", "sub", "chip"))),
        check_vma=False,
    )
```

```python
import functools

import jax
import jax.numpy as jnp
from jax import lax
from jax.experimental import pallas as pl
from jax.experimental.pallas import tpu as pltpu
from jax.sharding import PartitionSpec as P

OMEGA = 0.6
F32 = jnp.float32
BF16 = jnp.bfloat16
COLS = 64
TILE = 128
BLK = 64
SLOTS = 32
PEERS = 16
GROUPS = 8
AGG = 64
NC1 = 1024
STEP = 8
NSTEP = SLOTS // STEP
SIDE = 136
ROWS = 40
VMEM_LIMIT = 24 * 1024 * 1024

GROUP_AXES = ("sub", "chip")
ALL_AXES = ("grp", "sub", "chip")


def params():
    return pltpu.CompilerParams(vmem_limit_bytes=VMEM_LIMIT)


def hbm(x):
    return pltpu.with_memory_space_constraint(x, pltpu.HBM)


def far(shape, dtype=F32):
    return pltpu.HBM(shape, dtype)


def cost(flops, moved):
    return pl.CostEstimate(flops=flops, bytes_accessed=moved, transcendentals=0)


def split2(x):
    hi = x.astype(BF16)
    lo = (x - hi.astype(F32)).astype(BF16)
    return hi, lo


def dot(a, b):
    return jnp.dot(a, b, preferred_element_type=F32)


def dot_nt(a, b):
    return lax.dot_general(a, b, (((1,), (1,)), ((), ())), preferred_element_type=F32)


def mm(x, whi, wlo, nt=False):
    op = dot_nt if nt else dot
    rows = x.shape[0]
    hi, lo = split2(x)
    both = op(jnp.concatenate([hi, lo], axis=0), whi)
    return both[:rows] + both[rows:] + op(hi, wlo)


def mm_exact(x, w, nt=False):
    op = dot_nt if nt else dot
    rows = x.shape[0]
    two = op(jnp.concatenate(split2(x), axis=0), w)
    return two[:rows] + two[rows:]


def beside(a, b):
    return jnp.concatenate([a, b], axis=1)


def eye_mask():
    r = lax.broadcasted_iota(jnp.int32, (TILE, TILE), 0)
    c = lax.broadcasted_iota(jnp.int32, (TILE, TILE), 1)
    return r, c


def tile_diag(tile):
    r, c = eye_mask()
    return jnp.sum(jnp.where(r == c, tile, 0.0), axis=0, keepdims=True)


def off_diag(tile):
    r, c = eye_mask()
    return jnp.where(r == c, 0.0, tile)


def one_hot(row):
    r = lax.broadcasted_iota(jnp.int32, (AGG, row.shape[1]), 0)
    return jnp.where(r == row, 1.0, 0.0).astype(BF16)


def pack_rows(x):
    wide = jnp.concatenate([x[:32], x[32:]], axis=1)
    return wide


def column(row):
    return jnp.broadcast_to(row, (TILE, TILE)).T


def boundary_kernel(slots, maps, tiles, cols, out, tile_buf, col_buf, out_buf, tile_sem, col_sem, out_sem):
    def tile_copy(j):
        return pltpu.make_async_copy(tiles.at[slots[0, j // 2, j % 2]], tile_buf.at[j], tile_sem.at[j])

    def col_copy(j):
        at = pl.ds(pl.multiple_of(slots[0, j // 2, j % 2] * TILE, TILE), TILE)
        return pltpu.make_async_copy(cols.at[:, at], col_buf.at[j], col_sem.at[j])

    def out_copy(j):
        return pltpu.make_async_copy(out_buf.at[j], out.at[j], out_sem.at[j])

    for j in range(SLOTS):
        tile_copy(j).start()
        col_copy(j).start()
    r = lax.broadcasted_iota(jnp.int32, (64, TILE), 0)
    c = lax.broadcasted_iota(jnp.int32, (64, TILE), 1)
    r8 = lax.broadcasted_iota(jnp.int32, (8, TILE), 0)
    for j in range(SLOTS):
        tile_copy(j).wait()
        col_copy(j).wait()
        tile = tile_buf[j]
        diag = tile_diag(tile)
        out_buf[j, 0:64] = col_buf[j] * (OMEGA / diag)
        below = pltpu.roll(tile[64:], 64, 1)
        out_buf[j, 64:128] = jnp.where((c < 64) & (r > c), below, tile[:64])
        row = maps[pl.ds(slots[0, j // 2, j % 2], 1)].astype(F32)
        out_buf[j, 128:136] = jnp.where(r8 == 0, diag, jnp.where(r8 == 1, row, 0.0))
        out_copy(j).start()
    for j in range(SLOTS):
        out_copy(j).wait()


def boundary_pack(slot_blocks, diag_tiles, right_side, maps):
    return pl.pallas_call(
        boundary_kernel,
        in_specs=[
            pl.BlockSpec(memory_space=pltpu.SMEM),
            pl.BlockSpec(memory_space=pltpu.VMEM),
            pl.BlockSpec(memory_space=pl.ANY),
            pl.BlockSpec(memory_space=pl.ANY),
        ],
        out_specs=pl.BlockSpec(memory_space=pl.ANY),
        out_shape=far((SLOTS, SIDE, TILE)),
        scratch_shapes=[
            pltpu.VMEM((SLOTS, TILE, TILE), F32),
            pltpu.VMEM((SLOTS, COLS, TILE), F32),
            pltpu.VMEM((SLOTS, SIDE, TILE), F32),
            pltpu.SemaphoreType.DMA((SLOTS,)),
            pltpu.SemaphoreType.DMA((SLOTS,)),
            pltpu.SemaphoreType.DMA((SLOTS,)),
        ],
        compiler_params=params(),
        name="boundary_pack",
    )(slot_blocks, maps, hbm(diag_tiles), hbm(right_side))


def local_kernel(perm, counts, *refs):
    n = 2 * STEP
    tiles, cols = refs[:n], refs[n : 2 * n]
    remote, maps = refs[2 * n : 2 * n + 2]
    b_slot, b_rest, d_slot, d_rest, hi_rest, lo_rest, rs, rr = refs[2 * n + 2 :]
    step = pl.program_id(0)

    @pl.when(step == 0)
    def _():
        rr[...] = jnp.zeros_like(rr)

    index = [perm[(0 if i < STEP else SLOTS) + step * STEP + i % STEP] for i in range(n)]
    tile = [tiles[i][0] for i in range(n)]
    diag = [tile_diag(t) for t in tile]
    off = [split2(off_diag(t)) for t in tile]
    b = [cols[i][...] for i in range(n)]
    x = [OMEGA * bb / d for bb, d in zip(b, diag)]
    y = [bb - OMEGA * bb - mm(xx, *o) for bb, xx, o in zip(b, x, off)]
    spread = [one_hot(maps[pl.ds(i, 1)]) for i in index]
    total = rr[...]
    for i in range(0, n, 2):
        total = total + mm_exact(beside(y[i], y[i + 1]), beside(spread[i], spread[i + 1]), nt=True)
    for k in range(STEP):
        b_slot[k] = b[k]
        d_slot[k] = diag[k]
        b_rest[k] = b[STEP + k]
        d_rest[k] = diag[STEP + k]
        hi_rest[k], lo_rest[k] = off[STEP + k]
    scaled = []
    for k in range(STEP):
        j = step * STEP + k
        live = (j % 2) < counts[j // 2]
        scaled.append(split2(remote[k] * jnp.where(live, 1.0, 0.0)))
    for k in range(STEP):
        rs[k] = dot_nt(spread[k], scaled[k][0]) + dot_nt(spread[k], scaled[k][1])
    rr[...] = total


def local_part(perm, counts, diag_tiles, right_side, remote, maps):
    def where(i):
        return (0 if i < STEP else SLOTS) + i % STEP

    def tile_spec(i):
        return pl.BlockSpec((1, TILE, TILE), lambda s, p, c: (p[s * STEP + where(i)], 0, 0))

    def col_spec(i):
        return pl.BlockSpec((COLS, TILE), lambda s, p, c: (0, p[s * STEP + where(i)]))

    def out(*shape):
        return pl.BlockSpec((STEP,) + shape, lambda s, p, c: (s, 0, 0))

    n = 2 * STEP
    grid = pltpu.PrefetchScalarGridSpec(
        num_scalar_prefetch=2,
        grid=(NSTEP,),
        in_specs=[tile_spec(i) for i in range(n)]
        + [col_spec(i) for i in range(n)]
        + [
            pl.BlockSpec((STEP, TILE, TILE), lambda s, p, c: (s, 0, 0)),
            pl.BlockSpec((BLK, TILE), lambda s, p, c: (0, 0)),
        ],
        out_specs=[
            out(COLS, TILE),
            out(COLS, TILE),
            out(1, TILE),
            out(1, TILE),
            out(TILE, TILE),
            out(TILE, TILE),
            out(AGG, TILE),
            pl.BlockSpec((COLS, AGG), lambda s, p, c: (0, 0)),
        ],
    )

    def sds(shape, dtype=F32):
        return far((SLOTS,) + shape, dtype)

    return pl.pallas_call(
        local_kernel,
        grid_spec=grid,
        out_shape=[
            sds((COLS, TILE)),
            sds((COLS, TILE)),
            sds((1, TILE)),
            sds((1, TILE)),
            sds((TILE, TILE), BF16),
            sds((TILE, TILE), BF16),
            sds((AGG, TILE)),
            jax.ShapeDtypeStruct((COLS, AGG), F32),
        ],
        compiler_params=params(),
        cost_estimate=cost(2 * 64 * 3 * 64 * 128 * 128, 16 << 20),
        name="local_part",
    )(perm, counts, *([hbm(diag_tiles)] * n), *([hbm(right_side)] * n), hbm(remote), maps)


def coarse_kernel(op, cmap, g_out, d_out):
    spread = one_hot(cmap[...])
    product = exact_spread(spread, op)
    pieces = []
    for i in range(NC1 // TILE):
        pieces.append(tile_diag(op[i * TILE : (i + 1) * TILE, i * TILE : (i + 1) * TILE]))
    diag = jnp.concatenate(pieces, axis=1)
    inverse = 1.0 / diag
    d_out[...] = inverse
    g_out[...] = spread.astype(F32) - OMEGA * product * inverse


def exact_spread(spread, op):
    total = None
    for i in range(NC1 // 256):
        rows = slice(i * 256, (i + 1) * 256)
        hi, lo = split2(op[rows, :])
        part = dot(spread[:, rows], hi) + dot(spread[:, rows], lo)
        total = part if total is None else total + part
    return total


def coarse_setup(op, cmap):
    return pl.pallas_call(
        coarse_kernel,
        out_shape=[jax.ShapeDtypeStruct((AGG, NC1), F32), jax.ShapeDtypeStruct((1, NC1), F32)],
        compiler_params=params(),
        cost_estimate=cost(2 * 2 * 64 * 1024 * 1024, 5 << 20),
        name="coarse_setup",
    )(op, cmap)


def first_restrict_kernel(arrived, rs, rr, out, acc):
    step = pl.program_id(0)

    @pl.when(step == 0)
    def _():
        acc[...] = rr[...]

    total = acc[...]
    for j in range(0, STEP, 2):
        hi, lo = split2(beside(rs[j], rs[j + 1]))
        total = total + mm(beside(arrived[j], arrived[j + 1]), hi, lo, nt=True)
    acc[...] = total

    @pl.when(step == NSTEP - 1)
    def _():
        packed = pack_rows(total)
        for q in range(PEERS):
            out[q, 0:32] = packed
            out[q, 32:40] = jnp.zeros((8, TILE), F32)


def first_restrict(arrived, rs, rr):
    return pl.pallas_call(
        first_restrict_kernel,
        grid=(NSTEP,),
        in_specs=[
            pl.BlockSpec((STEP, COLS, TILE), lambda s: (s, 0, 0)),
            pl.BlockSpec((STEP, AGG, TILE), lambda s: (s, 0, 0)),
            pl.BlockSpec((COLS, AGG), lambda s: (0, 0)),
        ],
        out_specs=pl.BlockSpec((PEERS, ROWS, TILE), lambda s: (0, 0, 0)),
        out_shape=jax.ShapeDtypeStruct((PEERS, ROWS, TILE), F32),
        scratch_shapes=[pltpu.VMEM((COLS, AGG), F32)],
        compiler_params=params(),
        name="first_restrict",
    )(hbm(arrived), hbm(rs), rr)


def pair_kernel(perm, counts, *refs):
    tiles, side, remote, hi_out, lo_out, diag_out, map_out, x_out = (refs[:STEP],) + tuple(refs[STEP:])
    step = pl.program_id(0)
    r = lax.broadcasted_iota(jnp.int32, (64, TILE), 0)
    c = lax.broadcasted_iota(jnp.int32, (64, TILE), 1)
    for k in range(STEP):
        own = off_diag(tiles[k][0])
        packed = side[k, 64:128]
        top = jnp.where((c >= 64) | (r < c), packed, 0.0)
        bottom = pltpu.roll(jnp.where((c < 64) & (r > c), packed, 0.0), 64, 1)
        half = jnp.concatenate([top, bottom], axis=0)
        other = half + half.T
        j = step * STEP + k
        live = (j % 2) < counts[j // 2]
        rem = remote[k] * jnp.where(live, -1.0, 0.0)
        block = jnp.concatenate(
            [jnp.concatenate([own, rem.T], axis=1), jnp.concatenate([rem, other], axis=1)], axis=0
        )
        hi, lo = split2(block)
        hi_out[k] = hi
        lo_out[k] = lo
        x_out[k] = side[k, 0:64]
        diag_out[k] = side[k, 128:129]
        map_out[k] = side[k, 129:130].astype(jnp.int32)


def pair_setup(perm, counts, diag_tiles, side, remote):
    def tile_spec(i):
        return pl.BlockSpec((1, TILE, TILE), lambda s, p, c: (p[s * STEP + i], 0, 0))

    def spec(*shape):
        return pl.BlockSpec((STEP,) + shape, lambda s, p, c: (s, 0, 0))

    grid = pltpu.PrefetchScalarGridSpec(
        num_scalar_prefetch=2,
        grid=(NSTEP,),
        in_specs=[tile_spec(i) for i in range(STEP)] + [spec(SIDE, TILE), spec(TILE, TILE)],
        out_specs=[spec(2 * TILE, 2 * TILE), spec(2 * TILE, 2 * TILE), spec(1, TILE), spec(1, TILE), spec(COLS, TILE)],
    )
    return pl.pallas_call(
        pair_kernel,
        grid_spec=grid,
        out_shape=[
            far((SLOTS, 2 * TILE, 2 * TILE), BF16),
            far((SLOTS, 2 * TILE, 2 * TILE), BF16),
            far((SLOTS, 1, TILE)),
            far((SLOTS, 1, TILE), jnp.int32),
            far((SLOTS, COLS, TILE)),
        ],
        compiler_params=params(),
        cost_estimate=cost(2 * 64 * 3 * 64 * 128 * 128, 16 << 20),
        name="pair_setup",
    )(perm, counts, *([hbm(diag_tiles)] * STEP), hbm(side), hbm(remote))


def gathered_rows(ref, count):
    lane = lax.broadcasted_iota(jnp.int32, (32, TILE), 1) < 64
    tops, bottoms = [], []
    for q in range(0, count, 2):
        a, b = ref[q, 0:32], ref[q + 1, 0:32]
        tops.append(jnp.where(lane, a, pltpu.roll(b, 64, 1)))
        bottoms.append(jnp.where(lane, pltpu.roll(a, 64, 1), b))
    return jnp.concatenate([jnp.concatenate(tops, axis=1), jnp.concatenate(bottoms, axis=1)], axis=0)


def lowest_kernel(arrived, g, x_out, out):
    x = gathered_rows(arrived, PEERS)
    x_out[...] = x
    hi, lo = split2(g[...])
    packed = pack_rows(mm(x, hi, lo, nt=True))
    extra = arrived[0, 32:40]
    for q in range(1, PEERS):
        extra = extra + arrived[q, 32:40]
    for q in range(GROUPS):
        out[q, 0:32] = packed
        out[q, 32:40] = extra


def lowest_part(arrived, g):
    return pl.pallas_call(
        lowest_kernel,
        out_shape=[
            jax.ShapeDtypeStruct((COLS, NC1), F32),
            jax.ShapeDtypeStruct((GROUPS, ROWS, TILE), F32),
        ],
        compiler_params=params(),
        name="lowest_part",
    )(arrived, g)


def correct_kernel(arrived, inverse_cols, g, x_ref, inverse_ref, op, e_out, dots):
    inverse = inverse_ref[...]
    scaled = x_ref[...] * inverse
    total = None
    for i in range(NC1 // 256):
        rows = slice(i * 256, (i + 1) * 256)
        hi, lo = split2(op[rows, :])
        term = mm(scaled[:, rows], hi, lo)
        total = term if total is None else total + term
    low = gathered_rows(arrived, GROUPS)
    hi, lo = split2(inverse_cols[...])
    corr = mm(low, hi, lo)
    ghi, glo = split2(g[...])
    e = 2.0 * OMEGA * scaled - OMEGA * OMEGA * total * inverse + mm(corr, ghi, glo)
    for q in range(PEERS):
        e_out[q] = e[:, q * AGG : (q + 1) * AGG]
    extra = arrived[0, 32:40]
    for q in range(1, GROUPS):
        extra = extra + arrived[q, 32:40]
    dots[...] = extra


def correct_part(arrived, inverse_cols, g, x, inverse, op):
    return pl.pallas_call(
        correct_kernel,
        out_shape=[jax.ShapeDtypeStruct((PEERS, COLS, AGG), F32), jax.ShapeDtypeStruct((8, TILE), F32)],
        compiler_params=params(),
        name="correct_part",
    )(arrived, inverse_cols, g, x, inverse, op)


def apply_block(x, diag, hi, lo):
    xh, xl = split2(x)
    rows = x.shape[0]
    both = dot(jnp.concatenate([xh, xl], axis=0), hi)
    kept = xh.astype(F32) + xl.astype(F32)
    return both[:rows] + both[rows:] + dot(xh, lo) + kept[:, : diag.shape[1]] * diag


def lift(parts, spread):
    rows = parts.shape[0] // 2
    two = dot(parts, spread)
    return two[:rows] + two[rows:]


def two_parts(e):
    return jnp.concatenate(split2(e), axis=0)


def pair_spread(own, peer):
    none = jnp.zeros_like(own)
    return jnp.concatenate([beside(own, none), beside(none, peer)], axis=0)


def forward_kernel(
    perm, member, e, b_slot, b_rest, d_slot, d_rest, x_peer, d_peer, m_peer, hi_pair, lo_pair,
    hi_rest, lo_rest, maps, z_out, w_out, ws_out, out, acc_rr, acc_bz, acc_zw
):
    acc_rr[...] = jnp.zeros_like(acc_rr)
    acc_bz[...] = jnp.zeros_like(acc_bz)
    acc_zw[...] = jnp.zeros_like(acc_zw)
    e_own = e.at[pl.ds(member[0], 1)]
    views = (e, b_slot, b_rest, d_slot, d_rest, x_peer, d_peer, m_peer, hi_pair, lo_pair, hi_rest, lo_rest, ws_out)

    @pl.loop(0, NSTEP)
    def _(step):
        e_peer, *parts = [v.at[part(step, v.shape[0])] for v in views]
        both = [v.at[:, part(step, SLOTS)] for v in (z_out, w_out)]
        forward_step(step, perm, e_own, e_peer, *parts[:-1], maps, *both, parts[-1], acc_rr, acc_bz, acc_zw)

    packed = pack_rows(acc_rr[...])
    sums = jnp.sum(jnp.concatenate([acc_bz[...], acc_zw[...]], axis=0).T, axis=0, keepdims=True)
    r8 = lax.broadcasted_iota(jnp.int32, (8, TILE), 0)
    extra = jnp.where(r8 == 0, sums, 0.0)
    for q in range(PEERS):
        out[q, 0:32] = packed
        out[q, 32:40] = extra


def part(step, count):
    size = count // NSTEP
    return pl.ds(step * size, size)


def forward_step(
    step, perm, e_own, e_peer, b_slot, b_rest, d_slot, d_rest, x_peer, d_peer, m_peer, hi_pair, lo_pair,
    hi_rest, lo_rest, maps, z_out, w_out, ws_out, acc_rr, acc_bz, acc_zw
):
    e_mine = two_parts(e_own[0])
    e_both = [two_parts(beside(e_own[0], e_peer[q])) for q in range(STEP // 2)]
    rr, bz, zw = acc_rr[...], acc_bz[...], acc_zw[...]
    pairs, rest = range(STEP), range(STEP)
    rows = [maps[pl.ds(perm[at + step * STEP + k], 1)] for at in (0, SLOTS) for k in pairs]
    b_own = [b_slot[k] for k in pairs] + [b_rest[k] for k in rest]
    diag = [jnp.concatenate([d_slot[k], d_peer[k]], axis=1) for k in pairs] + [d_rest[k] for k in rest]
    rdiag = [OMEGA / d for d in diag]
    mats = [(hi_pair[k], lo_pair[k]) for k in pairs] + [(hi_rest[k], lo_rest[k]) for k in rest]
    full = [
        jnp.concatenate([b_own[k], x_peer[k] * (d_peer[k] * (1.0 / OMEGA))], axis=1) for k in pairs
    ] + b_own[STEP:]
    spread = [one_hot(row) for row in rows]
    ups = [lift(e_both[k // 2], pair_spread(spread[k], one_hot(m_peer[k]))) for k in pairs]
    ups = ups + [lift(e_mine, sp) for sp in spread[STEP:]]
    x = [f * rd + up for f, rd, up in zip(full, rdiag, ups)]
    image = [apply_block(xx, d, *m) for xx, d, m in zip(x, diag, mats)]
    z = [xx + (f - im) * rd for xx, f, im, rd in zip(x, full, image, rdiag)]
    w = [apply_block(zz, d, *m) for zz, d, m in zip(z, diag, mats)]
    x1 = [ww * rd for ww, rd in zip(w, rdiag)]
    left = [(m[0][:, :TILE], m[1][:, :TILE]) for m in mats]
    y = [
        ww[:, :TILE] - apply_block(xx, d[:, :TILE], *m) for ww, xx, d, m in zip(w, x1, diag, left)
    ]
    for i in range(0, 2 * STEP, 2):
        rr = rr + mm_exact(beside(y[i], y[i + 1]), beside(spread[i], spread[i + 1]), nt=True)
    for i in range(2 * STEP):
        zz, ww = z[i][:, :TILE], w[i][:, :TILE]
        bz = bz + b_own[i] * zz
        zw = zw + zz * ww
        z_out[i // STEP, i % STEP] = zz
        w_out[i // STEP, i % STEP] = ww
    for k in pairs:
        ws_out[k] = w[k][:, TILE:]
    acc_rr[...] = rr
    acc_bz[...] = bz
    acc_zw[...] = zw


def in_vmem(count):
    return [pl.BlockSpec(memory_space=pltpu.SMEM)] * 2 + [pl.BlockSpec(memory_space=pltpu.VMEM)] * count


def forward_part(perm, member, *arrays):
    return pl.pallas_call(
        forward_kernel,
        in_specs=in_vmem(len(arrays)),
        out_specs=[pl.BlockSpec(memory_space=pltpu.VMEM)] * 4,
        out_shape=[
            jax.ShapeDtypeStruct((2, SLOTS, COLS, TILE), F32),
            jax.ShapeDtypeStruct((2, SLOTS, COLS, TILE), F32),
            jax.ShapeDtypeStruct((SLOTS, COLS, TILE), F32),
            jax.ShapeDtypeStruct((PEERS, ROWS, TILE), F32),
        ],
        scratch_shapes=[pltpu.VMEM((COLS, AGG), F32), pltpu.VMEM((COLS, TILE), F32), pltpu.VMEM((COLS, TILE), F32)],
        compiler_params=params(),
        name="forward_part",
    )(perm, member, *arrays)


def second_kernel(
    perm, member, e, dots, b_slot, b_rest, d_slot, d_rest, d_peer, m_peer, hi_pair, lo_pair,
    hi_rest, lo_rest, maps, z_in, w_in, w_peer, v_out, u_out, out, acc_a, acc_b, acc_c, acc_alpha
):
    acc_a[...] = jnp.zeros_like(acc_a)
    acc_b[...] = jnp.zeros_like(acc_b)
    acc_c[...] = jnp.zeros_like(acc_c)
    col = column(dots[0:1])
    acc_alpha[...] = col[:COLS] / col[COLS:]
    e_own = e.at[pl.ds(member[0], 1)]
    views = (e, b_slot, b_rest, d_slot, d_rest, d_peer, m_peer, hi_pair, lo_pair, hi_rest, lo_rest, w_peer)

    @pl.loop(0, NSTEP)
    def _(step):
        e_peer, *parts = [v.at[part(step, v.shape[0])] for v in views]
        z_part, w_part, v_part, u_part = [v.at[:, part(step, SLOTS)] for v in (z_in, w_in, v_out, u_out)]
        second_step(
            step, perm, e_own, e_peer, *parts[:-1], maps, z_part, w_part, parts[-1], v_part, u_part,
            acc_a, acc_b, acc_c, acc_alpha
        )

    first = jnp.sum(jnp.concatenate([acc_a[...], acc_b[...]], axis=0).T, axis=0, keepdims=True)
    last = jnp.sum(jnp.concatenate([acc_c[...], acc_c[...]], axis=0).T, axis=0, keepdims=True)
    r8 = lax.broadcasted_iota(jnp.int32, (8, TILE), 0)
    extra = jnp.where(r8 == 0, first, jnp.where(r8 == 1, last, 0.0))
    for q in range(GROUPS * PEERS):
        out[q] = extra


def second_step(
    step, perm, e_own, e_peer, b_slot, b_rest, d_slot, d_rest, d_peer, m_peer, hi_pair, lo_pair,
    hi_rest, lo_rest, maps, z_in, w_in, w_peer, v_out, u_out, acc_a, acc_b, acc_c, acc_alpha
):
    alpha = acc_alpha[...]
    e_mine = two_parts(e_own[0])
    e_both = [two_parts(beside(e_own[0], e_peer[q])) for q in range(STEP // 2)]
    sums = [acc_a[...], acc_b[...], acc_c[...]]

    def gather(b, z, w, v, u):
        r1 = b - alpha * w
        z1 = z - alpha * v
        az1 = w - alpha * u
        sums[0] = sums[0] + r1 * z1
        sums[1] = sums[1] + z1 * az1
        sums[2] = sums[2] + (z1 * w + z * az1)

    pairs, rest = range(STEP), range(STEP)
    rows = [maps[pl.ds(perm[at + step * STEP + k], 1)] for at in (0, SLOTS) for k in pairs]
    diag = [jnp.concatenate([d_slot[k], d_peer[k]], axis=1) for k in pairs] + [d_rest[k] for k in rest]
    rdiag = [OMEGA / d for d in diag]
    mats = [(hi_pair[k], lo_pair[k]) for k in pairs] + [(hi_rest[k], lo_rest[k]) for k in rest]
    w = [jnp.concatenate([w_in[0, k], w_peer[k]], axis=1) for k in pairs] + [w_in[1, k] for k in rest]
    spread = [one_hot(row) for row in rows]
    ups = [lift(e_both[k // 2], pair_spread(spread[k], one_hot(m_peer[k]))) for k in pairs]
    ups = ups + [lift(e_mine, sp) for sp in spread[STEP:]]
    x = [ww * rd + up for ww, rd, up in zip(w, rdiag, ups)]
    image = [apply_block(xx, d, *m) for xx, d, m in zip(x, diag, mats)]
    v = [xx + (ww - im) * rd for xx, ww, im, rd in zip(x, w, image, rdiag)]
    left = [(m[0][:, :TILE], m[1][:, :TILE]) for m in mats]
    u = [apply_block(vv, d[:, :TILE], *m) for vv, d, m in zip(v, diag, left)]
    for i in range(2 * STEP):
        vv, b_ref = v[i][:, :TILE], (b_slot if i < STEP else b_rest)
        v_out[i // STEP, i % STEP] = vv
        u_out[i // STEP, i % STEP] = u[i]
        gather(b_ref[i % STEP], z_in[i // STEP, i % STEP], w[i][:, :TILE], vv, u[i])
    acc_a[...] = sums[0]
    acc_b[...] = sums[1]
    acc_c[...] = sums[2]


def second_part(perm, member, *arrays):
    return pl.pallas_call(
        second_kernel,
        in_specs=in_vmem(len(arrays)),
        out_specs=[pl.BlockSpec(memory_space=pltpu.VMEM)] * 3,
        out_shape=[
            jax.ShapeDtypeStruct((2, SLOTS, COLS, TILE), F32),
            jax.ShapeDtypeStruct((2, SLOTS, COLS, TILE), F32),
            jax.ShapeDtypeStruct((GROUPS * PEERS, 8, TILE), F32),
        ],
        scratch_shapes=[pltpu.VMEM((COLS, TILE), F32)] * 4,
        compiler_params=params(),
        name="second_part",
    )(perm, member, *arrays)


def combine_kernel(perm, dots, arrived, b_slot, b_rest, z, w, v, u, solution, residual, coef):
    step = pl.program_id(0)

    @pl.when(step == 0)
    def _():
        total = arrived[0]
        for q in range(1, GROUPS * PEERS):
            total = total + arrived[q]
        old = column(dots[0:1])
        one = column(total[0:1])
        two = column(total[1:2])
        rho, zw = old[:COLS], old[COLS:]
        rho_next, zz = one[:COLS], one[COLS:]
        cross = two[:COLS]
        alpha = rho / zw
        beta = rho_next / rho
        alpha_next = rho_next / (zz + beta * cross + beta * beta * zw)
        coef[0] = alpha
        coef[1] = beta
        coef[2] = alpha_next

    alpha, beta, alpha_next = coef[0], coef[1], coef[2]
    for half, b_ref in ((0, b_slot), (1, b_rest)):
        for k in range(STEP):
            index = perm[half * SLOTS + step * STEP + k]
            at = pl.ds(pl.multiple_of(index * TILE, TILE), TILE)
            z0, w0 = z[half, k], w[half, k]
            z1 = z0 - alpha * v[half, k]
            az1 = w0 - alpha * u[half, k]
            solution[:, at] = alpha * z0 + alpha_next * (z1 + beta * z0)
            residual[:, at] = b_ref[k] - alpha * w0 - alpha_next * (az1 + beta * w0)


def combine(perm, dots, arrived, b_slot, b_rest, z, w, v, u):
    def pair():
        return pl.BlockSpec((2, STEP, COLS, TILE), lambda s, p: (0, s, 0, 0))

    def single():
        return pl.BlockSpec((STEP, COLS, TILE), lambda s, p: (s, 0, 0))

    def whole():
        return pl.BlockSpec((COLS, BLK * TILE), lambda s, p: (0, 0))

    grid = pltpu.PrefetchScalarGridSpec(
        num_scalar_prefetch=1,
        grid=(NSTEP,),
        in_specs=[
            pl.BlockSpec((8, TILE), lambda s, p: (0, 0)),
            pl.BlockSpec((GROUPS * PEERS, 8, TILE), lambda s, p: (0, 0, 0)),
            single(),
            single(),
            pair(),
            pair(),
            pair(),
            pair(),
        ],
        out_specs=[whole(), whole()],
        scratch_shapes=[pltpu.VMEM((3, COLS, TILE), F32)],
    )
    return pl.pallas_call(
        combine_kernel,
        grid_spec=grid,
        out_shape=[jax.ShapeDtypeStruct((COLS, BLK * TILE), F32)] * 2,
        compiler_params=params(),
        name="combine",
    )(perm, dots, arrived, b_slot, b_rest, z, w, v, u)


def exchange(x, axes):
    return lax.all_to_all(x, axes, 0, 0, tiled=True)


def on_device(
    right_side,
    diag_tiles,
    remote_tiles,
    slot_counts,
    slot_blocks,
    fine_map,
    coarse_map,
    level1_ops,
    coarsest_inverse,
):
    group = lax.axis_index("grp")
    member = lax.axis_index(GROUP_AXES).astype(jnp.int32).reshape(1)
    slot_list = slot_blocks.reshape(SLOTS)
    counts = slot_counts.reshape(PEERS)
    maps = fine_map.reshape(BLK, TILE)
    remote = remote_tiles.reshape(SLOTS, TILE, TILE)
    operator = level1_ops[0]

    outgoing = boundary_pack(slot_blocks, diag_tiles, right_side, maps)
    side = exchange(outgoing.reshape(PEERS, 2 * SIDE, TILE), GROUP_AXES).reshape(SLOTS, SIDE, TILE)

    tile_ids = jnp.arange(BLK, dtype=jnp.int32)
    free = jnp.logical_not(jnp.any(slot_list[:, None] == tile_ids[None, :], axis=0)).astype(jnp.int32)
    rank = jnp.sum(jnp.where(tile_ids[None, :] < tile_ids[:, None], free[None, :], 0), axis=1)
    chosen = (rank[None, :] == jnp.arange(SLOTS, dtype=jnp.int32)[:, None]) & (free[None, :] == 1)
    rest_list = jnp.sum(jnp.where(chosen, tile_ids[None, :], 0), axis=1)
    perm = jnp.concatenate([slot_list, rest_list])

    b_slot, b_rest, d_slot, d_rest, hi_rest, lo_rest, rs, rr_local = local_part(
        perm, counts, diag_tiles, right_side, remote, maps
    )
    g, inverse = coarse_setup(operator, coarse_map.reshape(1, NC1))
    inverse_cols = lax.dynamic_slice_in_dim(coarsest_inverse, group * AGG, AGG, 1)

    def level_one(arrived):
        x, outgoing = lowest_part(arrived, g)
        lows = exchange(outgoing, "grp")
        return correct_part(lows, inverse_cols, g, x, inverse, operator)

    rr_local, g = lax.optimization_barrier((rr_local, g))
    gathered = exchange(first_restrict(side, rs, rr_local), GROUP_AXES)
    hi_pair, lo_pair, d_peer, m_peer, x_peer = pair_setup(perm, counts, diag_tiles, side, remote)
    gathered, hi_pair = lax.optimization_barrier((gathered, hi_pair))
    e, _ = level_one(gathered)
    z, w, w_peer, outgoing = forward_part(
        perm, member, e, b_slot, b_rest, d_slot, d_rest, x_peer, d_peer, m_peer, hi_pair, lo_pair, hi_rest, lo_rest, maps
    )
    e, dots = level_one(exchange(outgoing, GROUP_AXES))
    v, u, outgoing = second_part(
        perm, member, e, dots, b_slot, b_rest, d_slot, d_rest, d_peer, m_peer, hi_pair, lo_pair, hi_rest, lo_rest, maps, z, w, w_peer
    )
    sums = exchange(outgoing, ALL_AXES)
    return tuple(combine(perm, dots, sums, b_slot, b_rest, z, w, v, u))


def solution(mesh):
    placed = (
        P(None, ("grp", "sub", "chip")),
        P(("grp", "sub", "chip"), None, None),
        P(("grp", "sub", "chip"), None, None, None),
        P(("grp", "sub", "chip"), None),
        P(("grp", "sub", "chip"), None, None),
        P(("grp", "sub", "chip")),
        P("grp"),
        P("grp", None, None),
        P(),
    )
    return jax.shard_map(
        on_device,
        mesh=mesh,
        in_specs=placed,
        out_specs=(P(None, ("grp", "sub", "chip")), P(None, ("grp", "sub", "chip"))),
        check_vma=False,
    )
```

```python
import functools

import jax
import jax.numpy as jnp
from jax import lax
from jax.experimental import pallas as pl
from jax.experimental.pallas import tpu as pltpu
from jax.sharding import PartitionSpec as P

OMEGA = 0.6
F32 = jnp.float32
BF16 = jnp.bfloat16
COLS = 64
TILE = 128
BLK = 64
SLOTS = 32
PEERS = 16
GROUPS = 8
AGG = 64
NC1 = 1024
STEP = 8
NSTEP = SLOTS // STEP
SIDE = 136
ROWS = 40
VMEM_LIMIT = 24 * 1024 * 1024

GROUP_AXES = ("sub", "chip")
ALL_AXES = ("grp", "sub", "chip")


def params():
    return pltpu.CompilerParams(vmem_limit_bytes=VMEM_LIMIT)


def hbm(x):
    return pltpu.with_memory_space_constraint(x, pltpu.HBM)


def far(shape, dtype=F32):
    return pltpu.HBM(shape, dtype)


def cost(flops, moved):
    return pl.CostEstimate(flops=flops, bytes_accessed=moved, transcendentals=0)


def split2(x):
    hi = x.astype(BF16)
    lo = (x - hi.astype(F32)).astype(BF16)
    return hi, lo


def dot(a, b):
    return jnp.dot(a, b, preferred_element_type=F32)


def dot_nt(a, b):
    return lax.dot_general(a, b, (((1,), (1,)), ((), ())), preferred_element_type=F32)


def mm(x, whi, wlo, nt=False):
    op = dot_nt if nt else dot
    rows = x.shape[0]
    hi, lo = split2(x)
    both = op(jnp.concatenate([hi, lo], axis=0), whi)
    return both[:rows] + both[rows:] + op(hi, wlo)


def mm_exact(x, w, nt=False):
    op = dot_nt if nt else dot
    rows = x.shape[0]
    two = op(jnp.concatenate(split2(x), axis=0), w)
    return two[:rows] + two[rows:]


def beside(a, b):
    return jnp.concatenate([a, b], axis=1)


def eye_mask():
    r = lax.broadcasted_iota(jnp.int32, (TILE, TILE), 0)
    c = lax.broadcasted_iota(jnp.int32, (TILE, TILE), 1)
    return r, c


def tile_diag(tile):
    r, c = eye_mask()
    return jnp.sum(jnp.where(r == c, tile, 0.0), axis=0, keepdims=True)


def off_diag(tile):
    r, c = eye_mask()
    return jnp.where(r == c, 0.0, tile)


def one_hot(row):
    r = lax.broadcasted_iota(jnp.int32, (AGG, row.shape[1]), 0)
    return jnp.where(r == row, 1.0, 0.0).astype(BF16)


def pack_rows(x):
    wide = jnp.concatenate([x[:32], x[32:]], axis=1)
    return wide


def column(row):
    return jnp.broadcast_to(row, (TILE, TILE)).T


def boundary_kernel(slots, maps, tiles, cols, out, map_buf, tile_buf, col_buf, out_buf, map_sem, col_sem, tile_sem, out_sem):
    def tile_copy(j):
        return pltpu.make_async_copy(tiles.at[slots[0, j % 2, j // 2]], tile_buf.at[j], tile_sem.at[j])

    def col_copy(j):
        at = pl.ds(pl.multiple_of(slots[0, j % 2, j // 2] * TILE, TILE), TILE)
        return pltpu.make_async_copy(cols.at[:, at], col_buf.at[j], col_sem.at[j])

    def out_copy(j):
        at = pl.ds(j, STEP)
        return pltpu.make_async_copy(out_buf.at[at], out.at[at], out_sem.at[j // STEP])

    map_copy = pltpu.make_async_copy(maps, map_buf, map_sem)
    map_copy.start()
    for j in range(SLOTS):
        tile_copy(j).start()
        col_copy(j).start()
    r = lax.broadcasted_iota(jnp.int32, (64, TILE), 0)
    c = lax.broadcasted_iota(jnp.int32, (64, TILE), 1)
    r8 = lax.broadcasted_iota(jnp.int32, (8, TILE), 0)
    map_copy.wait()
    for j in range(0, SLOTS, STEP):
        for k in range(j, j + STEP):
            tile_copy(k).wait()
            col_copy(k).wait()
        tile = [tile_buf[k] for k in range(j, j + STEP)]
        diag = [tile_diag(t) for t in tile]
        for k in range(j, j + STEP):
            t, d = tile[k - j], diag[k - j]
            out_buf[k, 0:64] = col_buf[k] * (OMEGA / d)
            below = pltpu.roll(t[64:], 64, 1)
            out_buf[k, 64:128] = jnp.where((c < 64) & (r > c), below, t[:64])
            row = map_buf[pl.ds(slots[0, k % 2, k // 2], 1)].astype(F32)
            out_buf[k, 128:136] = jnp.where(r8 == 0, d, jnp.where(r8 == 1, row, 0.0))
        out_copy(j).start()
    for j in range(0, SLOTS, STEP):
        out_copy(j).wait()


def boundary_pack(slot_blocks, diag_tiles, right_side, maps):
    return pl.pallas_call(
        boundary_kernel,
        in_specs=[pl.BlockSpec(memory_space=pltpu.SMEM)] + [pl.BlockSpec(memory_space=pl.ANY)] * 3,
        out_specs=pl.BlockSpec(memory_space=pl.ANY),
        out_shape=far((SLOTS, SIDE, TILE)),
        scratch_shapes=[
            pltpu.VMEM((BLK, TILE), jnp.int32),
            pltpu.VMEM((SLOTS, TILE, TILE), F32),
            pltpu.VMEM((SLOTS, COLS, TILE), F32),
            pltpu.VMEM((SLOTS, SIDE, TILE), F32),
            pltpu.SemaphoreType.DMA,
            pltpu.SemaphoreType.DMA((SLOTS,)),
            pltpu.SemaphoreType.DMA((SLOTS,)),
            pltpu.SemaphoreType.DMA((NSTEP,)),
        ],
        compiler_params=params(),
        name="boundary_pack",
    )(slot_blocks.transpose(0, 2, 1), hbm(maps), hbm(diag_tiles), hbm(right_side))


def local_kernel(perm, counts, *refs):
    n = 2 * STEP
    tiles, cols = refs[:n], refs[n : 2 * n]
    remote, maps = refs[2 * n : 2 * n + 2]
    b_slot, b_rest, d_slot, d_rest, hi_rest, lo_rest, rs, rr = refs[2 * n + 2 :]
    step = pl.program_id(0)

    @pl.when(step == 0)
    def _():
        rr[...] = jnp.zeros_like(rr)

    index = [perm[(0 if i < STEP else SLOTS) + step * STEP + i % STEP] for i in range(n)]
    tile = [tiles[i][0] for i in range(n)]
    diag = [tile_diag(t) for t in tile]
    off = [split2(off_diag(t)) for t in tile]
    b = [cols[i][...] for i in range(n)]
    x = [OMEGA * bb / d for bb, d in zip(b, diag)]
    y = [bb - OMEGA * bb - mm(xx, *o) for bb, xx, o in zip(b, x, off)]
    spread = [one_hot(maps[pl.ds(i, 1)]) for i in index]
    total = rr[...]
    for i in range(0, n, 2):
        total = total + mm_exact(beside(y[i], y[i + 1]), beside(spread[i], spread[i + 1]), nt=True)
    for k in range(STEP):
        b_slot[k] = b[k]
        d_slot[k] = diag[k]
        b_rest[k] = b[STEP + k]
        d_rest[k] = diag[STEP + k]
        hi_rest[k], lo_rest[k] = off[STEP + k]
    scaled = []
    for k in range(STEP):
        j = step * STEP + k
        live = (j % 2) < counts[j // 2]
        scaled.append(split2(remote[k] * jnp.where(live, 1.0, 0.0)))
    for k in range(STEP):
        rs[k] = dot_nt(spread[k], scaled[k][0]) + dot_nt(spread[k], scaled[k][1])
    rr[...] = total


def local_part(perm, counts, diag_tiles, right_side, remote, maps):
    def where(i):
        return (0 if i < STEP else SLOTS) + i % STEP

    def tile_spec(i):
        return pl.BlockSpec((1, TILE, TILE), lambda s, p, c: (p[s * STEP + where(i)], 0, 0))

    def col_spec(i):
        return pl.BlockSpec((COLS, TILE), lambda s, p, c: (0, p[s * STEP + where(i)]))

    def out(*shape):
        return pl.BlockSpec((STEP,) + shape, lambda s, p, c: (s, 0, 0))

    n = 2 * STEP
    grid = pltpu.PrefetchScalarGridSpec(
        num_scalar_prefetch=2,
        grid=(NSTEP,),
        in_specs=[tile_spec(i) for i in range(n)]
        + [col_spec(i) for i in range(n)]
        + [
            pl.BlockSpec((STEP, TILE, TILE), lambda s, p, c: (s, 0, 0)),
            pl.BlockSpec((BLK, TILE), lambda s, p, c: (0, 0)),
        ],
        out_specs=[
            out(COLS, TILE),
            out(COLS, TILE),
            out(1, TILE),
            out(1, TILE),
            out(TILE, TILE),
            out(TILE, TILE),
            out(AGG, TILE),
            pl.BlockSpec((COLS, AGG), lambda s, p, c: (0, 0)),
        ],
    )

    def sds(shape, dtype=F32):
        return far((SLOTS,) + shape, dtype)

    return pl.pallas_call(
        local_kernel,
        grid_spec=grid,
        out_shape=[
            sds((COLS, TILE)),
            sds((COLS, TILE)),
            sds((1, TILE)),
            sds((1, TILE)),
            sds((TILE, TILE), BF16),
            sds((TILE, TILE), BF16),
            sds((AGG, TILE)),
            jax.ShapeDtypeStruct((COLS, AGG), F32),
        ],
        compiler_params=params(),
        cost_estimate=cost(2 * 64 * 3 * 64 * 128 * 128, 16 << 20),
        name="local_part",
    )(perm, counts, *([hbm(diag_tiles)] * n), *([hbm(right_side)] * n), hbm(remote), maps)


def coarse_kernel(op, cmap, g_out, d_out):
    spread = one_hot(cmap[...])
    product = exact_spread(spread, op)
    pieces = []
    for i in range(NC1 // TILE):
        pieces.append(tile_diag(op[i * TILE : (i + 1) * TILE, i * TILE : (i + 1) * TILE]))
    diag = jnp.concatenate(pieces, axis=1)
    inverse = 1.0 / diag
    d_out[...] = inverse
    g_out[...] = spread.astype(F32) - OMEGA * product * inverse


def exact_spread(spread, op):
    total = None
    for i in range(NC1 // 256):
        rows = slice(i * 256, (i + 1) * 256)
        hi, lo = split2(op[rows, :])
        part = dot(spread[:, rows], hi) + dot(spread[:, rows], lo)
        total = part if total is None else total + part
    return total


def coarse_setup(op, cmap):
    return pl.pallas_call(
        coarse_kernel,
        out_shape=[jax.ShapeDtypeStruct((AGG, NC1), F32), jax.ShapeDtypeStruct((1, NC1), F32)],
        compiler_params=params(),
        cost_estimate=cost(2 * 2 * 64 * 1024 * 1024, 5 << 20),
        name="coarse_setup",
    )(op, cmap)


def first_restrict_kernel(arrived, rs, rr, out, x_buf, rs_buf, x_sem, rs_sem):
    def copies(j):
        at = pl.ds(j * STEP, STEP)
        return (
            pltpu.make_async_copy(arrived.at[at, pl.ds(0, COLS)], x_buf.at[at], x_sem.at[j]),
            pltpu.make_async_copy(rs.at[at], rs_buf.at[at], rs_sem.at[j]),
        )

    for j in range(NSTEP):
        for copy in copies(j):
            copy.start()
    total = rr[...]
    for j in range(NSTEP):
        for copy in copies(j):
            copy.wait()
        for k in range(j * STEP, (j + 1) * STEP, 2):
            hi, lo = split2(beside(rs_buf[k], rs_buf[k + 1]))
            total = total + mm(beside(x_buf[k], x_buf[k + 1]), hi, lo, nt=True)
    packed = pack_rows(total)
    for q in range(PEERS):
        out[q, 0:32] = packed
        out[q, 32:40] = jnp.zeros((8, TILE), F32)


def first_restrict(arrived, rs, rr):
    return pl.pallas_call(
        first_restrict_kernel,
        in_specs=[pl.BlockSpec(memory_space=pl.ANY)] * 2 + [pl.BlockSpec(memory_space=pltpu.VMEM)],
        out_specs=pl.BlockSpec(memory_space=pltpu.VMEM),
        out_shape=jax.ShapeDtypeStruct((PEERS, ROWS, TILE), F32),
        scratch_shapes=[
            pltpu.VMEM((SLOTS, COLS, TILE), F32),
            pltpu.VMEM((SLOTS, AGG, TILE), F32),
            pltpu.SemaphoreType.DMA((NSTEP,)),
            pltpu.SemaphoreType.DMA((NSTEP,)),
        ],
        compiler_params=params(),
        name="first_restrict",
    )(hbm(arrived), hbm(rs), rr)


def pair_kernel(perm, counts, *refs):
    tiles, side, remote, hi_out, lo_out, diag_out, map_out, x_out = (refs[:STEP],) + tuple(refs[STEP:])
    step = pl.program_id(0)
    r = lax.broadcasted_iota(jnp.int32, (64, TILE), 0)
    c = lax.broadcasted_iota(jnp.int32, (64, TILE), 1)
    for k in range(STEP):
        own = off_diag(tiles[k][0])
        packed = side[k, 64:128]
        top = jnp.where((c >= 64) | (r < c), packed, 0.0)
        bottom = pltpu.roll(jnp.where((c < 64) & (r > c), packed, 0.0), 64, 1)
        half = jnp.concatenate([top, bottom], axis=0)
        other = half + half.T
        j = step * STEP + k
        live = (j % 2) < counts[j // 2]
        rem = remote[k] * jnp.where(live, -1.0, 0.0)
        block = jnp.concatenate(
            [jnp.concatenate([own, rem.T], axis=1), jnp.concatenate([rem, other], axis=1)], axis=0
        )
        hi, lo = split2(block)
        hi_out[k] = hi
        lo_out[k] = lo
        x_out[k] = side[k, 0:64]
        diag_out[k] = side[k, 128:129]
        map_out[k] = side[k, 129:130].astype(jnp.int32)


def pair_setup(perm, counts, diag_tiles, side, remote):
    def tile_spec(i):
        return pl.BlockSpec((1, TILE, TILE), lambda s, p, c: (p[s * STEP + i], 0, 0))

    def spec(*shape):
        return pl.BlockSpec((STEP,) + shape, lambda s, p, c: (s, 0, 0))

    grid = pltpu.PrefetchScalarGridSpec(
        num_scalar_prefetch=2,
        grid=(NSTEP,),
        in_specs=[tile_spec(i) for i in range(STEP)] + [spec(SIDE, TILE), spec(TILE, TILE)],
        out_specs=[spec(2 * TILE, 2 * TILE), spec(2 * TILE, 2 * TILE), spec(1, TILE), spec(1, TILE), spec(COLS, TILE)],
    )
    return pl.pallas_call(
        pair_kernel,
        grid_spec=grid,
        out_shape=[
            far((SLOTS, 2 * TILE, 2 * TILE), BF16),
            far((SLOTS, 2 * TILE, 2 * TILE), BF16),
            far((SLOTS, 1, TILE)),
            far((SLOTS, 1, TILE), jnp.int32),
            far((SLOTS, COLS, TILE)),
        ],
        compiler_params=params(),
        cost_estimate=cost(2 * 64 * 3 * 64 * 128 * 128, 16 << 20),
        name="pair_setup",
    )(perm, counts, *([hbm(diag_tiles)] * STEP), hbm(side), hbm(remote))


def gathered_rows(ref, count):
    lane = lax.broadcasted_iota(jnp.int32, (32, TILE), 1) < 64
    tops, bottoms = [], []
    for q in range(0, count, 2):
        a, b = ref[q, 0:32], ref[q + 1, 0:32]
        tops.append(jnp.where(lane, a, pltpu.roll(b, 64, 1)))
        bottoms.append(jnp.where(lane, pltpu.roll(a, 64, 1), b))
    return jnp.concatenate([jnp.concatenate(tops, axis=1), jnp.concatenate(bottoms, axis=1)], axis=0)


def lowest_kernel(arrived, g, x_out, out):
    x = gathered_rows(arrived, PEERS)
    x_out[...] = x
    hi, lo = split2(g[...])
    packed = pack_rows(mm(x, hi, lo, nt=True))
    extra = arrived[0, 32:40]
    for q in range(1, PEERS):
        extra = extra + arrived[q, 32:40]
    for q in range(GROUPS):
        out[q, 0:32] = packed
        out[q, 32:40] = extra


def lowest_part(arrived, g):
    return pl.pallas_call(
        lowest_kernel,
        out_shape=[
            jax.ShapeDtypeStruct((COLS, NC1), F32),
            jax.ShapeDtypeStruct((GROUPS, ROWS, TILE), F32),
        ],
        compiler_params=params(),
        name="lowest_part",
    )(arrived, g)


def correct_kernel(arrived, inverse_rows, g, x_ref, inverse_ref, op, e_out, dots):
    inverse = inverse_ref[...]
    scaled = x_ref[...] * inverse
    total = None
    for i in range(NC1 // 256):
        rows = slice(i * 256, (i + 1) * 256)
        hi, lo = split2(op[rows, :])
        term = mm(scaled[:, rows], hi, lo)
        total = term if total is None else total + term
    low = gathered_rows(arrived, GROUPS)
    hi, lo = split2(inverse_rows[...])
    corr = mm(low, hi, lo, nt=True)
    ghi, glo = split2(g[...])
    e = 2.0 * OMEGA * scaled - OMEGA * OMEGA * total * inverse + mm(corr, ghi, glo)
    for q in range(PEERS):
        e_out[q] = e[:, q * AGG : (q + 1) * AGG]
    extra = arrived[0, 32:40]
    for q in range(1, GROUPS):
        extra = extra + arrived[q, 32:40]
    dots[...] = extra


def correct_part(arrived, inverse_rows, g, x, inverse, op):
    return pl.pallas_call(
        correct_kernel,
        out_shape=[jax.ShapeDtypeStruct((PEERS, COLS, AGG), F32), jax.ShapeDtypeStruct((8, TILE), F32)],
        compiler_params=params(),
        name="correct_part",
    )(arrived, inverse_rows, g, x, inverse, op)


def apply_off(x, hi, lo):
    xh, xl = split2(x)
    rows = x.shape[0]
    both = dot(jnp.concatenate([xh, xl], axis=0), hi)
    return both[:rows] + both[rows:] + dot(xh, lo)


def apply_block(x, diag, hi, lo):
    xh, xl = split2(x)
    rows = x.shape[0]
    both = dot(jnp.concatenate([xh, xl], axis=0), hi)
    kept = xh.astype(F32) + xl.astype(F32)
    return both[:rows] + both[rows:] + dot(xh, lo) + kept[:, : diag.shape[1]] * diag


def lift(parts, spread):
    rows = parts.shape[0] // 2
    two = dot(parts, spread)
    return two[:rows] + two[rows:]


def two_parts(e):
    return jnp.concatenate(split2(e), axis=0)


def pair_spread(own, peer):
    none = jnp.zeros_like(own)
    return jnp.concatenate([beside(own, none), beside(none, peer)], axis=0)


def forward_kernel(
    perm, member, e, b_slot, b_rest, d_slot, d_rest, x_peer, d_peer, m_peer, hi_pair, lo_pair,
    hi_rest, lo_rest, maps, z_out, w_out, ws_out, out, acc_rr, acc_bz, acc_zw
):
    acc_rr[...] = jnp.zeros_like(acc_rr)
    acc_bz[...] = jnp.zeros_like(acc_bz)
    acc_zw[...] = jnp.zeros_like(acc_zw)
    e_own = e.at[pl.ds(member[0], 1)]
    views = (e, b_slot, b_rest, d_slot, d_rest, x_peer, d_peer, m_peer, hi_pair, lo_pair, hi_rest, lo_rest, ws_out)

    @pl.loop(0, NSTEP)
    def _(step):
        e_peer, *parts = [v.at[part(step, v.shape[0])] for v in views]
        both = [v.at[:, part(step, SLOTS)] for v in (z_out, w_out)]
        forward_step(step, perm, e_own, e_peer, *parts[:-1], maps, *both, parts[-1], acc_rr, acc_bz, acc_zw)

    packed = pack_rows(acc_rr[...])
    sums = jnp.sum(jnp.concatenate([acc_bz[...], acc_zw[...]], axis=0).T, axis=0, keepdims=True)
    r8 = lax.broadcasted_iota(jnp.int32, (8, TILE), 0)
    extra = jnp.where(r8 == 0, sums, 0.0)
    for q in range(PEERS):
        out[q, 0:32] = packed
        out[q, 32:40] = extra


def part(step, count):
    size = count // NSTEP
    return pl.ds(step * size, size)


def forward_step(
    step, perm, e_own, e_peer, b_slot, b_rest, d_slot, d_rest, x_peer, d_peer, m_peer, hi_pair, lo_pair,
    hi_rest, lo_rest, maps, z_out, w_out, ws_out, acc_rr, acc_bz, acc_zw
):
    e_mine = two_parts(e_own[0])
    e_both = [two_parts(beside(e_own[0], e_peer[q])) for q in range(STEP // 2)]
    rr, bz, zw = acc_rr[...], acc_bz[...], acc_zw[...]
    pairs, rest = range(STEP), range(STEP)
    rows = [maps[pl.ds(perm[at + step * STEP + k], 1)] for at in (0, SLOTS) for k in pairs]
    b_own = [b_slot[k] for k in pairs] + [b_rest[k] for k in rest]
    diag = [jnp.concatenate([d_slot[k], d_peer[k]], axis=1) for k in pairs] + [d_rest[k] for k in rest]
    rdiag = [OMEGA / d for d in diag]
    mats = [(hi_pair[k], lo_pair[k]) for k in pairs] + [(hi_rest[k], lo_rest[k]) for k in rest]
    x1 = [beside(b_own[k] * rdiag[k][:, :TILE], x_peer[k]) for k in pairs]
    x1 = x1 + [b * rd for b, rd in zip(b_own[STEP:], rdiag[STEP:])]
    spread = [one_hot(row) for row in rows]
    ups = [lift(e_both[k // 2], pair_spread(spread[k], one_hot(m_peer[k]))) for k in pairs]
    ups = ups + [lift(e_mine, sp) for sp in spread[STEP:]]
    x = [start + up for start, up in zip(x1, ups)]
    image = [apply_off(xx, *m) for xx, m in zip(x, mats)]
    z = [(1.0 - OMEGA) * xx + start - im * rd for xx, start, im, rd in zip(x, x1, image, rdiag)]
    w = [apply_block(zz, d, *m) for zz, d, m in zip(z, diag, mats)]
    x1 = [ww * rd for ww, rd in zip(w, rdiag)]
    left = [(m[0][:, :TILE], m[1][:, :TILE]) for m in mats]
    y = [(1.0 - OMEGA) * ww[:, :TILE] - apply_off(xx, *m) for ww, xx, m in zip(w, x1, left)]
    for i in range(0, 2 * STEP, 2):
        rr = rr + mm_exact(beside(y[i], y[i + 1]), beside(spread[i], spread[i + 1]), nt=True)
    for i in range(2 * STEP):
        zz, ww = z[i][:, :TILE], w[i][:, :TILE]
        bz = bz + b_own[i] * zz
        zw = zw + zz * ww
        z_out[i // STEP, i % STEP] = zz
        w_out[i // STEP, i % STEP] = ww
    for k in pairs:
        ws_out[k] = w[k][:, TILE:]
    acc_rr[...] = rr
    acc_bz[...] = bz
    acc_zw[...] = zw


def in_vmem(count):
    return [pl.BlockSpec(memory_space=pltpu.SMEM)] * 2 + [pl.BlockSpec(memory_space=pltpu.VMEM)] * count


def forward_part(perm, member, *arrays):
    return pl.pallas_call(
        forward_kernel,
        in_specs=in_vmem(len(arrays)),
        out_specs=[pl.BlockSpec(memory_space=pltpu.VMEM)] * 4,
        out_shape=[
            jax.ShapeDtypeStruct((2, SLOTS, COLS, TILE), F32),
            jax.ShapeDtypeStruct((2, SLOTS, COLS, TILE), F32),
            jax.ShapeDtypeStruct((SLOTS, COLS, TILE), F32),
            jax.ShapeDtypeStruct((PEERS, ROWS, TILE), F32),
        ],
        scratch_shapes=[pltpu.VMEM((COLS, AGG), F32), pltpu.VMEM((COLS, TILE), F32), pltpu.VMEM((COLS, TILE), F32)],
        compiler_params=params(),
        name="forward_part",
    )(perm, member, *arrays)


def second_kernel(
    perm, member, e, dots, b_slot, b_rest, d_slot, d_rest, d_peer, m_peer, hi_pair, lo_pair,
    hi_rest, lo_rest, maps, z_in, w_in, w_peer, v_out, u_out, out, acc_a, acc_b, acc_c, acc_alpha
):
    acc_a[...] = jnp.zeros_like(acc_a)
    acc_b[...] = jnp.zeros_like(acc_b)
    acc_c[...] = jnp.zeros_like(acc_c)
    col = column(dots[0:1])
    acc_alpha[...] = col[:COLS] / col[COLS:]
    e_own = e.at[pl.ds(member[0], 1)]
    views = (e, b_slot, b_rest, d_slot, d_rest, d_peer, m_peer, hi_pair, lo_pair, hi_rest, lo_rest, w_peer)

    @pl.loop(0, NSTEP)
    def _(step):
        e_peer, *parts = [v.at[part(step, v.shape[0])] for v in views]
        z_part, w_part, v_part, u_part = [v.at[:, part(step, SLOTS)] for v in (z_in, w_in, v_out, u_out)]
        second_step(
            step, perm, e_own, e_peer, *parts[:-1], maps, z_part, w_part, parts[-1], v_part, u_part,
            acc_a, acc_b, acc_c, acc_alpha
        )

    first = jnp.sum(jnp.concatenate([acc_a[...], acc_b[...]], axis=0).T, axis=0, keepdims=True)
    last = jnp.sum(jnp.concatenate([acc_c[...], acc_c[...]], axis=0).T, axis=0, keepdims=True)
    r8 = lax.broadcasted_iota(jnp.int32, (8, TILE), 0)
    extra = jnp.where(r8 == 0, first, jnp.where(r8 == 1, last, 0.0))
    for q in range(GROUPS * PEERS):
        out[q] = extra


def second_step(
    step, perm, e_own, e_peer, b_slot, b_rest, d_slot, d_rest, d_peer, m_peer, hi_pair, lo_pair,
    hi_rest, lo_rest, maps, z_in, w_in, w_peer, v_out, u_out, acc_a, acc_b, acc_c, acc_alpha
):
    alpha = acc_alpha[...]
    e_mine = two_parts(e_own[0])
    e_both = [two_parts(beside(e_own[0], e_peer[q])) for q in range(STEP // 2)]
    sums = [acc_a[...], acc_b[...], acc_c[...]]

    def gather(b, z, w, v, u):
        r1 = b - alpha * w
        z1 = z - alpha * v
        az1 = w - alpha * u
        sums[0] = sums[0] + r1 * z1
        sums[1] = sums[1] + z1 * az1
        sums[2] = sums[2] + (z1 * w + z * az1)

    pairs, rest = range(STEP), range(STEP)
    rows = [maps[pl.ds(perm[at + step * STEP + k], 1)] for at in (0, SLOTS) for k in pairs]
    diag = [jnp.concatenate([d_slot[k], d_peer[k]], axis=1) for k in pairs] + [d_rest[k] for k in rest]
    rdiag = [OMEGA / d for d in diag]
    mats = [(hi_pair[k], lo_pair[k]) for k in pairs] + [(hi_rest[k], lo_rest[k]) for k in rest]
    w = [jnp.concatenate([w_in[0, k], w_peer[k]], axis=1) for k in pairs] + [w_in[1, k] for k in rest]
    spread = [one_hot(row) for row in rows]
    ups = [lift(e_both[k // 2], pair_spread(spread[k], one_hot(m_peer[k]))) for k in pairs]
    ups = ups + [lift(e_mine, sp) for sp in spread[STEP:]]
    x1 = [ww * rd for ww, rd in zip(w, rdiag)]
    x = [start + up for start, up in zip(x1, ups)]
    image = [apply_off(xx, *m) for xx, m in zip(x, mats)]
    v = [(1.0 - OMEGA) * xx + start - im * rd for xx, start, im, rd in zip(x, x1, image, rdiag)]
    left = [(m[0][:, :TILE], m[1][:, :TILE]) for m in mats]
    u = [apply_block(vv, d[:, :TILE], *m) for vv, d, m in zip(v, diag, left)]
    for i in range(2 * STEP):
        vv, b_ref = v[i][:, :TILE], (b_slot if i < STEP else b_rest)
        v_out[i // STEP, i % STEP] = vv
        u_out[i // STEP, i % STEP] = u[i]
        gather(b_ref[i % STEP], z_in[i // STEP, i % STEP], w[i][:, :TILE], vv, u[i])
    acc_a[...] = sums[0]
    acc_b[...] = sums[1]
    acc_c[...] = sums[2]


def second_part(perm, member, *arrays):
    return pl.pallas_call(
        second_kernel,
        in_specs=in_vmem(len(arrays)),
        out_specs=[pl.BlockSpec(memory_space=pltpu.VMEM)] * 3,
        out_shape=[
            jax.ShapeDtypeStruct((2, SLOTS, COLS, TILE), F32),
            jax.ShapeDtypeStruct((2, SLOTS, COLS, TILE), F32),
            jax.ShapeDtypeStruct((GROUPS * PEERS, 8, TILE), F32),
        ],
        scratch_shapes=[pltpu.VMEM((COLS, TILE), F32)] * 4,
        compiler_params=params(),
        name="second_part",
    )(perm, member, *arrays)


def combine_kernel(perm, dots, arrived, b_slot, b_rest, z, w, v, u, solution, residual, coef):
    step = pl.program_id(0)

    @pl.when(step == 0)
    def _():
        total = arrived[0]
        for q in range(1, GROUPS * PEERS):
            total = total + arrived[q]
        old = column(dots[0:1])
        one = column(total[0:1])
        two = column(total[1:2])
        rho, zw = old[:COLS], old[COLS:]
        rho_next, zz = one[:COLS], one[COLS:]
        cross = two[:COLS]
        alpha = rho / zw
        beta = rho_next / rho
        alpha_next = rho_next / (zz + beta * cross + beta * beta * zw)
        coef[0] = alpha
        coef[1] = beta
        coef[2] = alpha_next

    alpha, beta, alpha_next = coef[0], coef[1], coef[2]
    for half, b_ref in ((0, b_slot), (1, b_rest)):
        for k in range(STEP):
            index = perm[half * SLOTS + step * STEP + k]
            at = pl.ds(pl.multiple_of(index * TILE, TILE), TILE)
            z0, w0 = z[half, k], w[half, k]
            z1 = z0 - alpha * v[half, k]
            az1 = w0 - alpha * u[half, k]
            solution[:, at] = alpha * z0 + alpha_next * (z1 + beta * z0)
            residual[:, at] = b_ref[k] - alpha * w0 - alpha_next * (az1 + beta * w0)


def combine(perm, dots, arrived, b_slot, b_rest, z, w, v, u):
    def pair():
        return pl.BlockSpec((2, STEP, COLS, TILE), lambda s, p: (0, s, 0, 0))

    def single():
        return pl.BlockSpec((STEP, COLS, TILE), lambda s, p: (s, 0, 0))

    def whole():
        return pl.BlockSpec((COLS, BLK * TILE), lambda s, p: (0, 0))

    grid = pltpu.PrefetchScalarGridSpec(
        num_scalar_prefetch=1,
        grid=(NSTEP,),
        in_specs=[
            pl.BlockSpec((8, TILE), lambda s, p: (0, 0)),
            pl.BlockSpec((GROUPS * PEERS, 8, TILE), lambda s, p: (0, 0, 0)),
            single(),
            single(),
            pair(),
            pair(),
            pair(),
            pair(),
        ],
        out_specs=[whole(), whole()],
        scratch_shapes=[pltpu.VMEM((3, COLS, TILE), F32)],
    )
    return pl.pallas_call(
        combine_kernel,
        grid_spec=grid,
        out_shape=[jax.ShapeDtypeStruct((COLS, BLK * TILE), F32)] * 2,
        compiler_params=params(),
        name="combine",
    )(perm, dots, arrived, b_slot, b_rest, z, w, v, u)


def exchange(x, axes):
    return lax.all_to_all(x, axes, 0, 0, tiled=True)


def on_device(
    right_side,
    diag_tiles,
    remote_tiles,
    slot_counts,
    slot_blocks,
    fine_map,
    coarse_map,
    level1_ops,
    coarsest_inverse,
):
    group = lax.axis_index("grp")
    member = lax.axis_index(GROUP_AXES).astype(jnp.int32).reshape(1)
    slot_list = slot_blocks.reshape(SLOTS)
    counts = slot_counts.reshape(PEERS)
    maps = fine_map.reshape(BLK, TILE)
    remote = remote_tiles.reshape(SLOTS, TILE, TILE)
    operator = level1_ops[0]

    outgoing = boundary_pack(slot_blocks, diag_tiles, right_side, maps)
    side = exchange(outgoing.reshape(PEERS, 2 * SIDE, TILE), GROUP_AXES).reshape(SLOTS, SIDE, TILE)

    tile_ids = jnp.arange(BLK, dtype=jnp.int32)
    free = jnp.logical_not(jnp.any(slot_list[:, None] == tile_ids[None, :], axis=0)).astype(jnp.int32)
    rank = jnp.sum(jnp.where(tile_ids[None, :] < tile_ids[:, None], free[None, :], 0), axis=1)
    chosen = (rank[None, :] == jnp.arange(SLOTS, dtype=jnp.int32)[:, None]) & (free[None, :] == 1)
    rest_list = jnp.sum(jnp.where(chosen, tile_ids[None, :], 0), axis=1)
    perm = jnp.concatenate([slot_list, rest_list])

    b_slot, b_rest, d_slot, d_rest, hi_rest, lo_rest, rs, rr_local = local_part(
        perm, counts, diag_tiles, right_side, remote, maps
    )
    g, inverse = coarse_setup(operator, coarse_map.reshape(1, NC1))
    inverse_rows = lax.dynamic_slice_in_dim(coarsest_inverse, group * AGG, AGG, 0)

    def level_one(arrived):
        x, outgoing = lowest_part(arrived, g)
        lows = exchange(outgoing, "grp")
        return correct_part(lows, inverse_rows, g, x, inverse, operator)

    rr_local, g, inverse_rows = lax.optimization_barrier((rr_local, g, inverse_rows))
    gathered = exchange(first_restrict(side, rs, rr_local), GROUP_AXES)
    hi_pair, lo_pair, d_peer, m_peer, x_peer = pair_setup(perm, counts, diag_tiles, side, remote)
    gathered, hi_pair = lax.optimization_barrier((gathered, hi_pair))
    e, _ = level_one(gathered)
    z, w, w_peer, outgoing = forward_part(
        perm, member, e, b_slot, b_rest, d_slot, d_rest, x_peer, d_peer, m_peer, hi_pair, lo_pair, hi_rest, lo_rest, maps
    )
    e, dots = level_one(exchange(outgoing, GROUP_AXES))
    v, u, outgoing = second_part(
        perm, member, e, dots, b_slot, b_rest, d_slot, d_rest, d_peer, m_peer, hi_pair, lo_pair, hi_rest, lo_rest, maps, z, w, w_peer
    )
    sums = exchange(outgoing, ALL_AXES)
    return tuple(combine(perm, dots, sums, b_slot, b_rest, z, w, v, u))


def solution(mesh):
    placed = (
        P(None, ("grp", "sub", "chip")),
        P(("grp", "sub", "chip"), None, None),
        P(("grp", "sub", "chip"), None, None, None),
        P(("grp", "sub", "chip"), None),
        P(("grp", "sub", "chip"), None, None),
        P(("grp", "sub", "chip")),
        P("grp"),
        P("grp", None, None),
        P(),
    )
    return jax.shard_map(
        on_device,
        mesh=mesh,
        in_specs=placed,
        out_specs=(P(None, ("grp", "sub", "chip")), P(None, ("grp", "sub", "chip"))),
        check_vma=False,
    )
```

```python
import functools

import jax
import jax.numpy as jnp
from jax import lax
from jax.experimental import pallas as pl
from jax.experimental.pallas import tpu as pltpu
from jax.sharding import PartitionSpec as P

OMEGA = 0.6
F32 = jnp.float32
BF16 = jnp.bfloat16
COLS = 64
TILE = 128
BLK = 64
SLOTS = 32
PEERS = 16
GROUPS = 8
AGG = 64
NC1 = 1024
STEP = 8
NSTEP = SLOTS // STEP
CHUNK = 16
CHUNKS = SLOTS // CHUNK
SIDE = 136
ROWS = 40
VMEM_LIMIT = 24 * 1024 * 1024

GROUP_AXES = ("sub", "chip")
ALL_AXES = ("grp", "sub", "chip")


def params():
    return pltpu.CompilerParams(vmem_limit_bytes=VMEM_LIMIT)


def hbm(x):
    return pltpu.with_memory_space_constraint(x, pltpu.HBM)


def far(shape, dtype=F32):
    return pltpu.HBM(shape, dtype)


def cost(flops, moved):
    return pl.CostEstimate(flops=flops, bytes_accessed=moved, transcendentals=0)


def split2(x):
    hi = x.astype(BF16)
    lo = (x - hi.astype(F32)).astype(BF16)
    return hi, lo


def dot(a, b):
    return jnp.dot(a, b, preferred_element_type=F32)


def dot_nt(a, b):
    return lax.dot_general(a, b, (((1,), (1,)), ((), ())), preferred_element_type=F32)


def mm(x, whi, wlo, nt=False):
    op = dot_nt if nt else dot
    rows = x.shape[0]
    hi, lo = split2(x)
    both = op(jnp.concatenate([hi, lo], axis=0), whi)
    return both[:rows] + both[rows:] + op(hi, wlo)


def mm_exact(x, w, nt=False):
    op = dot_nt if nt else dot
    rows = x.shape[0]
    two = op(jnp.concatenate(split2(x), axis=0), w)
    return two[:rows] + two[rows:]


def beside(a, b):
    return jnp.concatenate([a, b], axis=1)


def eye_mask():
    r = lax.broadcasted_iota(jnp.int32, (TILE, TILE), 0)
    c = lax.broadcasted_iota(jnp.int32, (TILE, TILE), 1)
    return r, c


def tile_diag(tile):
    r, c = eye_mask()
    return jnp.sum(jnp.where(r == c, tile, 0.0), axis=0, keepdims=True)


def off_diag(tile):
    r, c = eye_mask()
    return jnp.where(r == c, 0.0, tile)


def one_hot(row):
    r = lax.broadcasted_iota(jnp.int32, (AGG, row.shape[1]), 0)
    return jnp.where(r == row, 1.0, 0.0).astype(BF16)


def pack_rows(x):
    wide = jnp.concatenate([x[:32], x[32:]], axis=1)
    return wide


def column(row):
    return jnp.broadcast_to(row, (TILE, TILE)).T


def boundary_kernel(slots, maps, tiles, cols, out, map_buf, tile_buf, col_buf, out_buf, map_sem, col_sem, tile_sem, out_sem):
    def tile_copy(j):
        return pltpu.make_async_copy(tiles.at[slots[0, j % 2, j // 2]], tile_buf.at[j], tile_sem.at[j])

    def col_copy(j):
        at = pl.ds(pl.multiple_of(slots[0, j % 2, j // 2] * TILE, TILE), TILE)
        return pltpu.make_async_copy(cols.at[:, at], col_buf.at[j], col_sem.at[j])

    def out_copy(j):
        at = pl.ds(j, STEP)
        return pltpu.make_async_copy(out_buf.at[at], out.at[at], out_sem.at[j // STEP])

    map_copy = pltpu.make_async_copy(maps, map_buf, map_sem)
    map_copy.start()
    for j in range(SLOTS):
        tile_copy(j).start()
        col_copy(j).start()
    r = lax.broadcasted_iota(jnp.int32, (64, TILE), 0)
    c = lax.broadcasted_iota(jnp.int32, (64, TILE), 1)
    r8 = lax.broadcasted_iota(jnp.int32, (8, TILE), 0)
    map_copy.wait()
    for j in range(0, SLOTS, STEP):
        for k in range(j, j + STEP):
            tile_copy(k).wait()
            col_copy(k).wait()
        tile = [tile_buf[k] for k in range(j, j + STEP)]
        diag = [tile_diag(t) for t in tile]
        for k in range(j, j + STEP):
            t, d = tile[k - j], diag[k - j]
            out_buf[k, 0:64] = col_buf[k] * (OMEGA / d)
            below = pltpu.roll(t[64:], 64, 1)
            out_buf[k, 64:128] = jnp.where((c < 64) & (r > c), below, t[:64])
            row = map_buf[pl.ds(slots[0, k % 2, k // 2], 1)].astype(F32)
            out_buf[k, 128:136] = jnp.where(r8 == 0, d, jnp.where(r8 == 1, row, 0.0))
        out_copy(j).start()
    for j in range(0, SLOTS, STEP):
        out_copy(j).wait()


def boundary_pack(slot_blocks, diag_tiles, right_side, maps):
    return pl.pallas_call(
        boundary_kernel,
        in_specs=[pl.BlockSpec(memory_space=pltpu.SMEM)] + [pl.BlockSpec(memory_space=pl.ANY)] * 3,
        out_specs=pl.BlockSpec(memory_space=pl.ANY),
        out_shape=far((SLOTS, SIDE, TILE)),
        scratch_shapes=[
            pltpu.VMEM((BLK, TILE), jnp.int32),
            pltpu.VMEM((SLOTS, TILE, TILE), F32),
            pltpu.VMEM((SLOTS, COLS, TILE), F32),
            pltpu.VMEM((SLOTS, SIDE, TILE), F32),
            pltpu.SemaphoreType.DMA,
            pltpu.SemaphoreType.DMA((SLOTS,)),
            pltpu.SemaphoreType.DMA((SLOTS,)),
            pltpu.SemaphoreType.DMA((NSTEP,)),
        ],
        compiler_params=params(),
        name="boundary_pack",
    )(slot_blocks.transpose(0, 2, 1), hbm(maps), hbm(diag_tiles), hbm(right_side))


def local_kernel(perm, counts, *refs):
    n = 2 * STEP
    tiles, cols = refs[:n], refs[n : 2 * n]
    remote, maps = refs[2 * n : 2 * n + 2]
    b_slot, b_rest, d_slot, d_rest, hi_rest, lo_rest, rs, rr = refs[2 * n + 2 :]
    step = pl.program_id(0)

    @pl.when(step == 0)
    def _():
        rr[...] = jnp.zeros_like(rr)

    index = [perm[(0 if i < STEP else SLOTS) + step * STEP + i % STEP] for i in range(n)]
    tile = [tiles[i][0] for i in range(n)]
    diag = [tile_diag(t) for t in tile]
    off = [split2(off_diag(t)) for t in tile]
    b = [cols[i][...] for i in range(n)]
    x = [OMEGA * bb / d for bb, d in zip(b, diag)]
    y = [bb - OMEGA * bb - mm(xx, *o) for bb, xx, o in zip(b, x, off)]
    spread = [one_hot(maps[pl.ds(i, 1)]) for i in index]
    total = rr[...]
    for i in range(0, n, 2):
        total = total + mm_exact(beside(y[i], y[i + 1]), beside(spread[i], spread[i + 1]), nt=True)
    for k in range(STEP):
        b_slot[k] = b[k]
        d_slot[k] = diag[k]
        b_rest[k] = b[STEP + k]
        d_rest[k] = diag[STEP + k]
        hi_rest[k], lo_rest[k] = off[STEP + k]
    scaled = []
    for k in range(STEP):
        j = step * STEP + k
        live = (j % 2) < counts[j // 2]
        scaled.append(split2(remote[k] * jnp.where(live, 1.0, 0.0)))
    for k in range(STEP):
        rs[k] = dot_nt(spread[k], scaled[k][0]) + dot_nt(spread[k], scaled[k][1])
    rr[...] = total


def local_part(perm, counts, diag_tiles, right_side, remote, maps):
    def where(i):
        return (0 if i < STEP else SLOTS) + i % STEP

    def tile_spec(i):
        return pl.BlockSpec((1, TILE, TILE), lambda s, p, c: (p[s * STEP + where(i)], 0, 0))

    def col_spec(i):
        return pl.BlockSpec((COLS, TILE), lambda s, p, c: (0, p[s * STEP + where(i)]))

    def out(*shape):
        return pl.BlockSpec((STEP,) + shape, lambda s, p, c: (s, 0, 0))

    n = 2 * STEP
    grid = pltpu.PrefetchScalarGridSpec(
        num_scalar_prefetch=2,
        grid=(NSTEP,),
        in_specs=[tile_spec(i) for i in range(n)]
        + [col_spec(i) for i in range(n)]
        + [
            pl.BlockSpec((STEP, TILE, TILE), lambda s, p, c: (s, 0, 0)),
            pl.BlockSpec((BLK, TILE), lambda s, p, c: (0, 0)),
        ],
        out_specs=[
            out(COLS, TILE),
            out(COLS, TILE),
            out(1, TILE),
            out(1, TILE),
            out(TILE, TILE),
            out(TILE, TILE),
            out(AGG, TILE),
            pl.BlockSpec((COLS, AGG), lambda s, p, c: (0, 0)),
        ],
    )

    def sds(shape, dtype=F32):
        return far((SLOTS,) + shape, dtype)

    return pl.pallas_call(
        local_kernel,
        grid_spec=grid,
        out_shape=[
            sds((COLS, TILE)),
            sds((COLS, TILE)),
            sds((1, TILE)),
            sds((1, TILE)),
            sds((TILE, TILE), BF16),
            sds((TILE, TILE), BF16),
            sds((AGG, TILE)),
            jax.ShapeDtypeStruct((COLS, AGG), F32),
        ],
        compiler_params=params(),
        cost_estimate=cost(2 * 64 * 3 * 64 * 128 * 128, 16 << 20),
        name="local_part",
    )(perm, counts, *([hbm(diag_tiles)] * n), *([hbm(right_side)] * n), hbm(remote), maps)


def coarse_kernel(op, cmap, g_out, d_out):
    spread = one_hot(cmap[...])
    product = exact_spread(spread, op)
    pieces = []
    for i in range(NC1 // TILE):
        pieces.append(tile_diag(op[i * TILE : (i + 1) * TILE, i * TILE : (i + 1) * TILE]))
    diag = jnp.concatenate(pieces, axis=1)
    inverse = 1.0 / diag
    d_out[...] = inverse
    g_out[...] = spread.astype(F32) - OMEGA * product * inverse


def exact_spread(spread, op):
    total = None
    for i in range(NC1 // 256):
        rows = slice(i * 256, (i + 1) * 256)
        hi, lo = split2(op[rows, :])
        part = dot(spread[:, rows], hi) + dot(spread[:, rows], lo)
        total = part if total is None else total + part
    return total


def coarse_setup(op, cmap):
    return pl.pallas_call(
        coarse_kernel,
        out_shape=[jax.ShapeDtypeStruct((AGG, NC1), F32), jax.ShapeDtypeStruct((1, NC1), F32)],
        compiler_params=params(),
        cost_estimate=cost(2 * 2 * 64 * 1024 * 1024, 5 << 20),
        name="coarse_setup",
    )(op, cmap)


def first_restrict_kernel(arrived, rs, rr, out, x_buf, rs_buf, x_sem, rs_sem):
    def copies(j):
        at = pl.ds(j * STEP, STEP)
        return (
            pltpu.make_async_copy(arrived.at[at, pl.ds(0, COLS)], x_buf.at[at], x_sem.at[j]),
            pltpu.make_async_copy(rs.at[at], rs_buf.at[at], rs_sem.at[j]),
        )

    for j in range(NSTEP):
        for copy in copies(j):
            copy.start()
    total = rr[...]
    for j in range(NSTEP):
        for copy in copies(j):
            copy.wait()
        for k in range(j * STEP, (j + 1) * STEP, 2):
            hi, lo = split2(beside(rs_buf[k], rs_buf[k + 1]))
            total = total + mm(beside(x_buf[k], x_buf[k + 1]), hi, lo, nt=True)
    packed = pack_rows(total)
    for q in range(PEERS):
        out[q, 0:32] = packed
        out[q, 32:40] = jnp.zeros((8, TILE), F32)


def first_restrict(arrived, rs, rr):
    return pl.pallas_call(
        first_restrict_kernel,
        in_specs=[pl.BlockSpec(memory_space=pl.ANY)] * 2 + [pl.BlockSpec(memory_space=pltpu.VMEM)],
        out_specs=pl.BlockSpec(memory_space=pltpu.VMEM),
        out_shape=jax.ShapeDtypeStruct((PEERS, ROWS, TILE), F32),
        scratch_shapes=[
            pltpu.VMEM((SLOTS, COLS, TILE), F32),
            pltpu.VMEM((SLOTS, AGG, TILE), F32),
            pltpu.SemaphoreType.DMA((NSTEP,)),
            pltpu.SemaphoreType.DMA((NSTEP,)),
        ],
        compiler_params=params(),
        name="first_restrict",
    )(hbm(arrived), hbm(rs), rr)


def pair_kernel(perm, counts, *refs):
    tiles, side, remote, hi_out, lo_out, diag_out, map_out, x_out = (refs[:STEP],) + tuple(refs[STEP:])
    step = pl.program_id(0)
    r = lax.broadcasted_iota(jnp.int32, (64, TILE), 0)
    c = lax.broadcasted_iota(jnp.int32, (64, TILE), 1)
    for k in range(STEP):
        own = off_diag(tiles[k][0])
        packed = side[k, 64:128]
        top = jnp.where((c >= 64) | (r < c), packed, 0.0)
        bottom = pltpu.roll(jnp.where((c < 64) & (r > c), packed, 0.0), 64, 1)
        half = jnp.concatenate([top, bottom], axis=0)
        other = half + half.T
        j = step * STEP + k
        live = (j % 2) < counts[j // 2]
        rem = remote[k] * jnp.where(live, -1.0, 0.0)
        block = jnp.concatenate(
            [jnp.concatenate([own, rem.T], axis=1), jnp.concatenate([rem, other], axis=1)], axis=0
        )
        hi, lo = split2(block)
        hi_out[k] = hi
        lo_out[k] = lo
        x_out[k] = side[k, 0:64]
        diag_out[k] = side[k, 128:129]
        map_out[k] = side[k, 129:130].astype(jnp.int32)


def pair_setup(perm, counts, diag_tiles, side, remote):
    def tile_spec(i):
        return pl.BlockSpec((1, TILE, TILE), lambda s, p, c: (p[s * STEP + i], 0, 0))

    def spec(*shape):
        return pl.BlockSpec((STEP,) + shape, lambda s, p, c: (s, 0, 0))

    grid = pltpu.PrefetchScalarGridSpec(
        num_scalar_prefetch=2,
        grid=(NSTEP,),
        in_specs=[tile_spec(i) for i in range(STEP)] + [spec(SIDE, TILE), spec(TILE, TILE)],
        out_specs=[spec(2 * TILE, 2 * TILE), spec(2 * TILE, 2 * TILE), spec(1, TILE), spec(1, TILE), spec(COLS, TILE)],
    )
    return pl.pallas_call(
        pair_kernel,
        grid_spec=grid,
        out_shape=[
            far((SLOTS, 2 * TILE, 2 * TILE), BF16),
            far((SLOTS, 2 * TILE, 2 * TILE), BF16),
            far((SLOTS, 1, TILE)),
            far((SLOTS, 1, TILE), jnp.int32),
            far((SLOTS, COLS, TILE)),
        ],
        compiler_params=params(),
        cost_estimate=cost(2 * 64 * 3 * 64 * 128 * 128, 16 << 20),
        name="pair_setup",
    )(perm, counts, *([hbm(diag_tiles)] * STEP), hbm(side), hbm(remote))


def gathered_rows(ref, count):
    lane = lax.broadcasted_iota(jnp.int32, (32, TILE), 1) < 64
    tops, bottoms = [], []
    for q in range(0, count, 2):
        a, b = ref[q, 0:32], ref[q + 1, 0:32]
        tops.append(jnp.where(lane, a, pltpu.roll(b, 64, 1)))
        bottoms.append(jnp.where(lane, pltpu.roll(a, 64, 1), b))
    return jnp.concatenate([jnp.concatenate(tops, axis=1), jnp.concatenate(bottoms, axis=1)], axis=0)


def lowest_kernel(arrived, g, x_out, out):
    x = gathered_rows(arrived, PEERS)
    x_out[...] = x
    hi, lo = split2(g[...])
    packed = pack_rows(mm(x, hi, lo, nt=True))
    extra = arrived[0, 32:40]
    for q in range(1, PEERS):
        extra = extra + arrived[q, 32:40]
    for q in range(GROUPS):
        out[q, 0:32] = packed
        out[q, 32:40] = extra


def lowest_part(arrived, g):
    return pl.pallas_call(
        lowest_kernel,
        out_shape=[
            jax.ShapeDtypeStruct((COLS, NC1), F32),
            jax.ShapeDtypeStruct((GROUPS, ROWS, TILE), F32),
        ],
        compiler_params=params(),
        name="lowest_part",
    )(arrived, g)


def correct_kernel(arrived, inverse_rows, g, x_ref, inverse_ref, op, e_out, dots):
    inverse = inverse_ref[...]
    scaled = x_ref[...] * inverse
    total = None
    for i in range(NC1 // 256):
        rows = slice(i * 256, (i + 1) * 256)
        hi, lo = split2(op[rows, :])
        term = mm(scaled[:, rows], hi, lo)
        total = term if total is None else total + term
    low = gathered_rows(arrived, GROUPS)
    hi, lo = split2(inverse_rows[...])
    corr = mm(low, hi, lo, nt=True)
    ghi, glo = split2(g[...])
    e = 2.0 * OMEGA * scaled - OMEGA * OMEGA * total * inverse + mm(corr, ghi, glo)
    for q in range(PEERS):
        e_out[q] = e[:, q * AGG : (q + 1) * AGG]
    extra = arrived[0, 32:40]
    for q in range(1, GROUPS):
        extra = extra + arrived[q, 32:40]
    dots[...] = extra


def correct_part(arrived, inverse_rows, g, x, inverse, op):
    return pl.pallas_call(
        correct_kernel,
        out_shape=[jax.ShapeDtypeStruct((PEERS, COLS, AGG), F32), jax.ShapeDtypeStruct((8, TILE), F32)],
        compiler_params=params(),
        name="correct_part",
    )(arrived, inverse_rows, g, x, inverse, op)


def apply_off(x, hi, lo):
    xh, xl = split2(x)
    rows = x.shape[0]
    if x.shape[1] == TILE:
        return dot(beside(xh, xl), jnp.concatenate([hi, hi], axis=0)) + dot(xh, lo)
    both = dot(jnp.concatenate([xh, xl], axis=0), hi)
    return both[:rows] + both[rows:] + dot(xh, lo)


def apply_block(x, diag, hi, lo):
    xh, xl = split2(x)
    kept = xh.astype(F32) + xl.astype(F32)
    return apply_off(x, hi, lo) + kept[:, : diag.shape[1]] * diag


def lift(parts, spread):
    rows = parts.shape[0] // 2
    two = dot(parts, spread)
    return two[:rows] + two[rows:]


def two_parts(e):
    return jnp.concatenate(split2(e), axis=0)


def pair_spread(own, peer):
    none = jnp.zeros_like(own)
    return jnp.concatenate([beside(own, none), beside(none, peer)], axis=0)


def forward_kernel(
    perm, member, e, b_slot, b_rest, d_slot, d_rest, x_peer, d_peer, m_peer, hi_pair, lo_pair,
    hi_rest, lo_rest, maps, z_out, w_out, ws_out, out, acc_rr, acc_bz, acc_zw
):
    acc_rr[...] = jnp.zeros_like(acc_rr)
    acc_bz[...] = jnp.zeros_like(acc_bz)
    acc_zw[...] = jnp.zeros_like(acc_zw)
    e_own = e.at[pl.ds(member[0], 1)]
    views = (e, b_slot, b_rest, d_slot, d_rest, x_peer, d_peer, m_peer, hi_pair, lo_pair, hi_rest, lo_rest, ws_out)

    @pl.loop(0, CHUNKS)
    def _(step):
        e_peer, *parts = [v.at[part(step, v.shape[0])] for v in views]
        both = [v.at[:, part(step, SLOTS)] for v in (z_out, w_out)]
        forward_step(step, perm, e_own, e_peer, *parts[:-1], maps, *both, parts[-1], acc_rr, acc_bz, acc_zw)

    packed = pack_rows(acc_rr[...])
    sums = jnp.sum(jnp.concatenate([acc_bz[...], acc_zw[...]], axis=0).T, axis=0, keepdims=True)
    r8 = lax.broadcasted_iota(jnp.int32, (8, TILE), 0)
    extra = jnp.where(r8 == 0, sums, 0.0)
    for q in range(PEERS):
        out[q, 0:32] = packed
        out[q, 32:40] = extra


def part(step, count):
    size = count // CHUNKS
    return pl.ds(step * size, size)


def forward_step(
    step, perm, e_own, e_peer, b_slot, b_rest, d_slot, d_rest, x_peer, d_peer, m_peer, hi_pair, lo_pair,
    hi_rest, lo_rest, maps, z_out, w_out, ws_out, acc_rr, acc_bz, acc_zw
):
    e_mine = two_parts(e_own[0])
    e_both = [two_parts(beside(e_own[0], e_peer[q])) for q in range(CHUNK // 2)]
    rr, bz, zw = acc_rr[...], acc_bz[...], acc_zw[...]
    pairs, rest = range(CHUNK), range(CHUNK)
    rows = [maps[pl.ds(perm[at + step * CHUNK + k], 1)] for at in (0, SLOTS) for k in pairs]
    b_own = [b_slot[k] for k in pairs] + [b_rest[k] for k in rest]
    diag = [jnp.concatenate([d_slot[k], d_peer[k]], axis=1) for k in pairs] + [d_rest[k] for k in rest]
    rdiag = [OMEGA / d for d in diag]
    mats = [(hi_pair[k], lo_pair[k]) for k in pairs] + [(hi_rest[k], lo_rest[k]) for k in rest]
    x1 = [beside(b_own[k] * rdiag[k][:, :TILE], x_peer[k]) for k in pairs]
    x1 = x1 + [b * rd for b, rd in zip(b_own[CHUNK:], rdiag[CHUNK:])]
    spread = [one_hot(row) for row in rows]
    ups = [lift(e_both[k // 2], pair_spread(spread[k], one_hot(m_peer[k]))) for k in pairs]
    ups = ups + [lift(e_mine, sp) for sp in spread[CHUNK:]]
    x = [start + up for start, up in zip(x1, ups)]
    image = [apply_off(xx, *m) for xx, m in zip(x, mats)]
    z = [(1.0 - OMEGA) * xx + start - im * rd for xx, start, im, rd in zip(x, x1, image, rdiag)]
    w = [apply_block(zz, d, *m) for zz, d, m in zip(z, diag, mats)]
    x1 = [ww * rd for ww, rd in zip(w, rdiag)]
    left = [(m[0][:, :TILE], m[1][:, :TILE]) for m in mats]
    y = [(1.0 - OMEGA) * ww[:, :TILE] - apply_off(xx, *m) for ww, xx, m in zip(w, x1, left)]
    for i in range(0, 2 * CHUNK, 2):
        rr = rr + mm_exact(beside(y[i], y[i + 1]), beside(spread[i], spread[i + 1]), nt=True)
    for i in range(2 * CHUNK):
        zz, ww = z[i][:, :TILE], w[i][:, :TILE]
        bz = bz + b_own[i] * zz
        zw = zw + zz * ww
        z_out[i // CHUNK, i % CHUNK] = zz
        w_out[i // CHUNK, i % CHUNK] = ww
    for k in pairs:
        ws_out[k] = w[k][:, TILE:]
    acc_rr[...] = rr
    acc_bz[...] = bz
    acc_zw[...] = zw


def in_vmem(count):
    return [pl.BlockSpec(memory_space=pltpu.SMEM)] * 2 + [pl.BlockSpec(memory_space=pltpu.VMEM)] * count


def forward_part(perm, member, *arrays):
    return pl.pallas_call(
        forward_kernel,
        in_specs=in_vmem(len(arrays)),
        out_specs=[pl.BlockSpec(memory_space=pltpu.VMEM)] * 4,
        out_shape=[
            jax.ShapeDtypeStruct((2, SLOTS, COLS, TILE), F32),
            jax.ShapeDtypeStruct((2, SLOTS, COLS, TILE), F32),
            jax.ShapeDtypeStruct((SLOTS, COLS, TILE), F32),
            jax.ShapeDtypeStruct((PEERS, ROWS, TILE), F32),
        ],
        scratch_shapes=[pltpu.VMEM((COLS, AGG), F32), pltpu.VMEM((COLS, TILE), F32), pltpu.VMEM((COLS, TILE), F32)],
        compiler_params=params(),
        name="forward_part",
    )(perm, member, *arrays)


def second_kernel(
    perm, member, e, dots, b_slot, b_rest, d_slot, d_rest, d_peer, m_peer, hi_pair, lo_pair,
    hi_rest, lo_rest, maps, z_in, w_in, w_peer, v_out, u_out, out, acc_a, acc_b, acc_c, acc_alpha
):
    acc_a[...] = jnp.zeros_like(acc_a)
    acc_b[...] = jnp.zeros_like(acc_b)
    acc_c[...] = jnp.zeros_like(acc_c)
    col = column(dots[0:1])
    acc_alpha[...] = col[:COLS] / col[COLS:]
    e_own = e.at[pl.ds(member[0], 1)]
    views = (e, b_slot, b_rest, d_slot, d_rest, d_peer, m_peer, hi_pair, lo_pair, hi_rest, lo_rest, w_peer)

    @pl.loop(0, CHUNKS)
    def _(step):
        e_peer, *parts = [v.at[part(step, v.shape[0])] for v in views]
        z_part, w_part, v_part, u_part = [v.at[:, part(step, SLOTS)] for v in (z_in, w_in, v_out, u_out)]
        second_step(
            step, perm, e_own, e_peer, *parts[:-1], maps, z_part, w_part, parts[-1], v_part, u_part,
            acc_a, acc_b, acc_c, acc_alpha
        )

    first = jnp.sum(jnp.concatenate([acc_a[...], acc_b[...]], axis=0).T, axis=0, keepdims=True)
    last = jnp.sum(jnp.concatenate([acc_c[...], acc_c[...]], axis=0).T, axis=0, keepdims=True)
    out[...] = jnp.broadcast_to(jnp.concatenate([first, last], axis=0), out.shape)


def second_step(
    step, perm, e_own, e_peer, b_slot, b_rest, d_slot, d_rest, d_peer, m_peer, hi_pair, lo_pair,
    hi_rest, lo_rest, maps, z_in, w_in, w_peer, v_out, u_out, acc_a, acc_b, acc_c, acc_alpha
):
    alpha = acc_alpha[...]
    e_mine = two_parts(e_own[0])
    e_both = [two_parts(beside(e_own[0], e_peer[q])) for q in range(CHUNK // 2)]
    sums = [acc_a[...], acc_b[...], acc_c[...]]

    def gather(b, z, w, v, u):
        r1 = b - alpha * w
        z1 = z - alpha * v
        az1 = w - alpha * u
        sums[0] = sums[0] + r1 * z1
        sums[1] = sums[1] + z1 * az1
        sums[2] = sums[2] + (z1 * w + z * az1)

    pairs, rest = range(CHUNK), range(CHUNK)
    rows = [maps[pl.ds(perm[at + step * CHUNK + k], 1)] for at in (0, SLOTS) for k in pairs]
    diag = [jnp.concatenate([d_slot[k], d_peer[k]], axis=1) for k in pairs] + [d_rest[k] for k in rest]
    rdiag = [OMEGA / d for d in diag]
    mats = [(hi_pair[k], lo_pair[k]) for k in pairs] + [(hi_rest[k], lo_rest[k]) for k in rest]
    w = [jnp.concatenate([w_in[0, k], w_peer[k]], axis=1) for k in pairs] + [w_in[1, k] for k in rest]
    spread = [one_hot(row) for row in rows]
    ups = [lift(e_both[k // 2], pair_spread(spread[k], one_hot(m_peer[k]))) for k in pairs]
    ups = ups + [lift(e_mine, sp) for sp in spread[CHUNK:]]
    x1 = [ww * rd for ww, rd in zip(w, rdiag)]
    x = [start + up for start, up in zip(x1, ups)]
    image = [apply_off(xx, *m) for xx, m in zip(x, mats)]
    v = [(1.0 - OMEGA) * xx + start - im * rd for xx, start, im, rd in zip(x, x1, image, rdiag)]
    left = [(m[0][:, :TILE], m[1][:, :TILE]) for m in mats]
    u = [apply_block(vv, d[:, :TILE], *m) for vv, d, m in zip(v, diag, left)]
    for i in range(2 * CHUNK):
        vv, b_ref = v[i][:, :TILE], (b_slot if i < CHUNK else b_rest)
        v_out[i // CHUNK, i % CHUNK] = vv
        u_out[i // CHUNK, i % CHUNK] = u[i]
        gather(b_ref[i % CHUNK], z_in[i // CHUNK, i % CHUNK], w[i][:, :TILE], vv, u[i])
    acc_a[...] = sums[0]
    acc_b[...] = sums[1]
    acc_c[...] = sums[2]


def second_part(perm, member, *arrays):
    return pl.pallas_call(
        second_kernel,
        in_specs=in_vmem(len(arrays)),
        out_specs=[pl.BlockSpec(memory_space=pltpu.VMEM)] * 3,
        out_shape=[
            jax.ShapeDtypeStruct((2, SLOTS, COLS, TILE), F32),
            jax.ShapeDtypeStruct((2, SLOTS, COLS, TILE), F32),
            jax.ShapeDtypeStruct((GROUPS * PEERS, 2, TILE), F32),
        ],
        scratch_shapes=[pltpu.VMEM((COLS, TILE), F32)] * 4,
        compiler_params=params(),
        name="second_part",
    )(perm, member, *arrays)


def combine_kernel(perm, dots, arrived, b_slot, b_rest, z, w, v, u, solution, residual, coef):
    step = pl.program_id(0)

    @pl.when(step == 0)
    def _():
        total = jnp.sum(arrived[...], axis=0)
        old = column(dots[0:1])
        one = column(total[0:1])
        two = column(total[1:2])
        rho, zw = old[:COLS], old[COLS:]
        rho_next, zz = one[:COLS], one[COLS:]
        cross = two[:COLS]
        alpha = rho / zw
        beta = rho_next / rho
        alpha_next = rho_next / (zz + beta * cross + beta * beta * zw)
        coef[0] = alpha
        coef[1] = beta
        coef[2] = alpha_next

    alpha, beta, alpha_next = coef[0], coef[1], coef[2]
    for half, b_ref in ((0, b_slot), (1, b_rest)):
        for k in range(STEP):
            index = perm[half * SLOTS + step * STEP + k]
            at = pl.ds(pl.multiple_of(index * TILE, TILE), TILE)
            z0, w0 = z[half, k], w[half, k]
            z1 = z0 - alpha * v[half, k]
            az1 = w0 - alpha * u[half, k]
            solution[:, at] = alpha * z0 + alpha_next * (z1 + beta * z0)
            residual[:, at] = b_ref[k] - alpha * w0 - alpha_next * (az1 + beta * w0)


def combine(perm, dots, arrived, b_slot, b_rest, z, w, v, u):
    def pair():
        return pl.BlockSpec((2, STEP, COLS, TILE), lambda s, p: (0, s, 0, 0))

    def single():
        return pl.BlockSpec((STEP, COLS, TILE), lambda s, p: (s, 0, 0))

    def whole():
        return pl.BlockSpec((COLS, BLK * TILE), lambda s, p: (0, 0))

    grid = pltpu.PrefetchScalarGridSpec(
        num_scalar_prefetch=1,
        grid=(NSTEP,),
        in_specs=[
            pl.BlockSpec((8, TILE), lambda s, p: (0, 0)),
            pl.BlockSpec((GROUPS * PEERS, 2, TILE), lambda s, p: (0, 0, 0)),
            single(),
            single(),
            pair(),
            pair(),
            pair(),
            pair(),
        ],
        out_specs=[whole(), whole()],
        scratch_shapes=[pltpu.VMEM((3, COLS, TILE), F32)],
    )
    return pl.pallas_call(
        combine_kernel,
        grid_spec=grid,
        out_shape=[jax.ShapeDtypeStruct((COLS, BLK * TILE), F32)] * 2,
        compiler_params=params(),
        name="combine",
    )(perm, dots, arrived, b_slot, b_rest, z, w, v, u)


def exchange(x, axes):
    return lax.all_to_all(x, axes, 0, 0, tiled=True)


def on_device(
    right_side,
    diag_tiles,
    remote_tiles,
    slot_counts,
    slot_blocks,
    fine_map,
    coarse_map,
    level1_ops,
    coarsest_inverse,
):
    group = lax.axis_index("grp")
    member = lax.axis_index(GROUP_AXES).astype(jnp.int32).reshape(1)
    slot_list = slot_blocks.reshape(SLOTS)
    counts = slot_counts.reshape(PEERS)
    maps = fine_map.reshape(BLK, TILE)
    remote = remote_tiles.reshape(SLOTS, TILE, TILE)
    operator = level1_ops[0]

    outgoing = boundary_pack(slot_blocks, diag_tiles, right_side, maps)
    side = exchange(outgoing.reshape(PEERS, 2 * SIDE, TILE), GROUP_AXES).reshape(SLOTS, SIDE, TILE)

    tile_ids = jnp.arange(BLK, dtype=jnp.int32)
    free = jnp.logical_not(jnp.any(slot_list[:, None] == tile_ids[None, :], axis=0)).astype(jnp.int32)
    rank = jnp.sum(jnp.where(tile_ids[None, :] < tile_ids[:, None], free[None, :], 0), axis=1)
    chosen = (rank[None, :] == jnp.arange(SLOTS, dtype=jnp.int32)[:, None]) & (free[None, :] == 1)
    rest_list = jnp.sum(jnp.where(chosen, tile_ids[None, :], 0), axis=1)
    perm = jnp.concatenate([slot_list, rest_list])

    b_slot, b_rest, d_slot, d_rest, hi_rest, lo_rest, rs, rr_local = local_part(
        perm, counts, diag_tiles, right_side, remote, maps
    )
    g, inverse = coarse_setup(operator, coarse_map.reshape(1, NC1))
    inverse_rows = lax.dynamic_slice_in_dim(coarsest_inverse, group * AGG, AGG, 0)

    def level_one(arrived):
        x, outgoing = lowest_part(arrived, g)
        lows = exchange(outgoing, "grp")
        return correct_part(lows, inverse_rows, g, x, inverse, operator)

    rr_local, g, inverse_rows, member = lax.optimization_barrier((rr_local, g, inverse_rows, member))
    gathered = exchange(first_restrict(side, rs, rr_local), GROUP_AXES)
    hi_pair, lo_pair, d_peer, m_peer, x_peer = pair_setup(perm, counts, diag_tiles, side, remote)
    gathered, hi_pair = lax.optimization_barrier((gathered, hi_pair))
    e, _ = level_one(gathered)
    z, w, w_peer, outgoing = forward_part(
        perm, member, e, b_slot, b_rest, d_slot, d_rest, x_peer, d_peer, m_peer, hi_pair, lo_pair, hi_rest, lo_rest, maps
    )
    e, dots = level_one(exchange(outgoing, GROUP_AXES))
    v, u, outgoing = second_part(
        perm, member, e, dots, b_slot, b_rest, d_slot, d_rest, d_peer, m_peer, hi_pair, lo_pair, hi_rest, lo_rest, maps, z, w, w_peer
    )
    sums = exchange(outgoing, ALL_AXES)
    return tuple(combine(perm, dots, sums, b_slot, b_rest, z, w, v, u))


def solution(mesh):
    placed = (
        P(None, ("grp", "sub", "chip")),
        P(("grp", "sub", "chip"), None, None),
        P(("grp", "sub", "chip"), None, None, None),
        P(("grp", "sub", "chip"), None),
        P(("grp", "sub", "chip"), None, None),
        P(("grp", "sub", "chip")),
        P("grp"),
        P("grp", None, None),
        P(),
    )
    return jax.shard_map(
        on_device,
        mesh=mesh,
        in_specs=placed,
        out_specs=(P(None, ("grp", "sub", "chip")), P(None, ("grp", "sub", "chip"))),
        check_vma=False,
    )
```

```python
import functools

import jax
import jax.numpy as jnp
from jax import lax
from jax.experimental import pallas as pl
from jax.experimental.pallas import tpu as pltpu
from jax.sharding import PartitionSpec as P

OMEGA = 0.6
F32 = jnp.float32
BF16 = jnp.bfloat16
COLS = 64
TILE = 128
BLK = 64
SLOTS = 32
PEERS = 16
GROUPS = 8
AGG = 64
NC1 = 1024
STEP = 8
NSTEP = SLOTS // STEP
CHUNK = 16
CHUNKS = SLOTS // CHUNK
SIDE = 136
ROWS = 40
VMEM_LIMIT = 24 * 1024 * 1024

GROUP_AXES = ("sub", "chip")
ALL_AXES = ("grp", "sub", "chip")


def params():
    return pltpu.CompilerParams(vmem_limit_bytes=VMEM_LIMIT)


def hbm(x):
    return pltpu.with_memory_space_constraint(x, pltpu.HBM)


def near(shape, dtype=F32):
    return pltpu.VMEM(shape, dtype)


def far(shape, dtype=F32):
    return pltpu.HBM(shape, dtype)


def cost(flops, moved):
    return pl.CostEstimate(flops=flops, bytes_accessed=moved, transcendentals=0)


def split2(x):
    hi = x.astype(BF16)
    lo = (x - hi.astype(F32)).astype(BF16)
    return hi, lo


def dot(a, b):
    return jnp.dot(a, b, preferred_element_type=F32)


def dot_nt(a, b):
    return lax.dot_general(a, b, (((1,), (1,)), ((), ())), preferred_element_type=F32)


def mm(x, whi, wlo, nt=False):
    op = dot_nt if nt else dot
    rows = x.shape[0]
    hi, lo = split2(x)
    both = op(jnp.concatenate([hi, lo], axis=0), whi)
    return both[:rows] + both[rows:] + op(hi, wlo)


def mm_exact(x, w, nt=False):
    op = dot_nt if nt else dot
    rows = x.shape[0]
    two = op(jnp.concatenate(split2(x), axis=0), w)
    return two[:rows] + two[rows:]


def beside(a, b):
    return jnp.concatenate([a, b], axis=1)


def eye_mask():
    r = lax.broadcasted_iota(jnp.int32, (TILE, TILE), 0)
    c = lax.broadcasted_iota(jnp.int32, (TILE, TILE), 1)
    return r, c


def tile_diag(tile):
    r, c = eye_mask()
    return jnp.sum(jnp.where(r == c, tile, 0.0), axis=0, keepdims=True)


def off_diag(tile):
    r, c = eye_mask()
    return jnp.where(r == c, 0.0, tile)


def one_hot(row):
    r = lax.broadcasted_iota(jnp.int32, (AGG, row.shape[1]), 0)
    return jnp.where(r == row, 1.0, 0.0).astype(BF16)


def pack_rows(x):
    wide = jnp.concatenate([x[:32], x[32:]], axis=1)
    return wide


def column(row):
    return jnp.broadcast_to(row, (TILE, TILE)).T


def boundary_kernel(slots, maps, tiles, cols, out, map_buf, tile_buf, col_buf, out_buf, map_sem, col_sem, tile_sem, out_sem):
    def tile_copy(j):
        return pltpu.make_async_copy(tiles.at[slots[0, j % 2, j // 2]], tile_buf.at[j], tile_sem.at[j])

    def col_copy(j):
        at = pl.ds(pl.multiple_of(slots[0, j % 2, j // 2] * TILE, TILE), TILE)
        return pltpu.make_async_copy(cols.at[:, at], col_buf.at[j], col_sem.at[j])

    def out_copy(j):
        at = pl.ds(j, STEP)
        return pltpu.make_async_copy(out_buf.at[at], out.at[at], out_sem.at[j // STEP])

    map_copy = pltpu.make_async_copy(maps, map_buf, map_sem)
    map_copy.start()
    for j in range(SLOTS):
        tile_copy(j).start()
        col_copy(j).start()
    r = lax.broadcasted_iota(jnp.int32, (64, TILE), 0)
    c = lax.broadcasted_iota(jnp.int32, (64, TILE), 1)
    r8 = lax.broadcasted_iota(jnp.int32, (8, TILE), 0)
    map_copy.wait()
    for j in range(0, SLOTS, STEP):
        for k in range(j, j + STEP):
            tile_copy(k).wait()
            col_copy(k).wait()
        tile = [tile_buf[k] for k in range(j, j + STEP)]
        diag = [tile_diag(t) for t in tile]
        for k in range(j, j + STEP):
            t, d = tile[k - j], diag[k - j]
            out_buf[k, 0:64] = col_buf[k] * (OMEGA / d)
            below = pltpu.roll(t[64:], 64, 1)
            out_buf[k, 64:128] = jnp.where((c < 64) & (r > c), below, t[:64])
            row = map_buf[pl.ds(slots[0, k % 2, k // 2], 1)].astype(F32)
            out_buf[k, 128:136] = jnp.where(r8 == 0, d, jnp.where(r8 == 1, row, 0.0))
        out_copy(j).start()
    for j in range(0, SLOTS, STEP):
        out_copy(j).wait()


def boundary_pack(slot_blocks, diag_tiles, right_side, maps):
    return pl.pallas_call(
        boundary_kernel,
        in_specs=[pl.BlockSpec(memory_space=pltpu.SMEM)] + [pl.BlockSpec(memory_space=pl.ANY)] * 3,
        out_specs=pl.BlockSpec(memory_space=pl.ANY),
        out_shape=far((SLOTS, SIDE, TILE)),
        scratch_shapes=[
            pltpu.VMEM((BLK, TILE), jnp.int32),
            pltpu.VMEM((SLOTS, TILE, TILE), F32),
            pltpu.VMEM((SLOTS, COLS, TILE), F32),
            pltpu.VMEM((SLOTS, SIDE, TILE), F32),
            pltpu.SemaphoreType.DMA,
            pltpu.SemaphoreType.DMA((SLOTS,)),
            pltpu.SemaphoreType.DMA((SLOTS,)),
            pltpu.SemaphoreType.DMA((NSTEP,)),
        ],
        compiler_params=params(),
        name="boundary_pack",
    )(slot_blocks.transpose(0, 2, 1), hbm(maps), hbm(diag_tiles), hbm(right_side))


def local_kernel(perm, counts, *refs):
    n = 2 * STEP
    tiles, cols = refs[:n], refs[n : 2 * n]
    remote, maps = refs[2 * n : 2 * n + 2]
    b_slot, b_rest, d_slot, d_rest, hi_rest, lo_rest, rs, rr = refs[2 * n + 2 :]
    step = pl.program_id(0)

    @pl.when(step == 0)
    def _():
        rr[...] = jnp.zeros_like(rr)

    index = [perm[(0 if i < STEP else SLOTS) + step * STEP + i % STEP] for i in range(n)]
    tile = [tiles[i][0] for i in range(n)]
    diag = [tile_diag(t) for t in tile]
    off = [split2(off_diag(t)) for t in tile]
    b = [cols[i][...] for i in range(n)]
    x = [OMEGA * bb / d for bb, d in zip(b, diag)]
    y = [bb - OMEGA * bb - mm(xx, *o) for bb, xx, o in zip(b, x, off)]
    spread = [one_hot(maps[pl.ds(i, 1)]) for i in index]
    total = rr[...]
    for i in range(0, n, 2):
        total = total + mm_exact(beside(y[i], y[i + 1]), beside(spread[i], spread[i + 1]), nt=True)
    for k in range(STEP):
        b_slot[k] = b[k]
        d_slot[k] = diag[k]
        b_rest[k] = b[STEP + k]
        d_rest[k] = diag[STEP + k]
        hi_rest[k], lo_rest[k] = off[STEP + k]
    scaled = []
    for k in range(STEP):
        j = step * STEP + k
        live = (j % 2) < counts[j // 2]
        scaled.append(split2(remote[k] * jnp.where(live, 1.0, 0.0)))
    for k in range(STEP):
        rs[k] = dot_nt(spread[k], scaled[k][0]) + dot_nt(spread[k], scaled[k][1])
    rr[...] = total


def local_part(perm, counts, diag_tiles, right_side, remote, maps):
    def where(i):
        return (0 if i < STEP else SLOTS) + i % STEP

    def tile_spec(i):
        return pl.BlockSpec((1, TILE, TILE), lambda s, p, c: (p[s * STEP + where(i)], 0, 0))

    def col_spec(i):
        return pl.BlockSpec((COLS, TILE), lambda s, p, c: (0, p[s * STEP + where(i)]))

    def out(*shape):
        return pl.BlockSpec((STEP,) + shape, lambda s, p, c: (s, 0, 0))

    n = 2 * STEP
    grid = pltpu.PrefetchScalarGridSpec(
        num_scalar_prefetch=2,
        grid=(NSTEP,),
        in_specs=[tile_spec(i) for i in range(n)]
        + [col_spec(i) for i in range(n)]
        + [
            pl.BlockSpec((STEP, TILE, TILE), lambda s, p, c: (s, 0, 0)),
            pl.BlockSpec((BLK, TILE), lambda s, p, c: (0, 0)),
        ],
        out_specs=[
            out(COLS, TILE),
            out(COLS, TILE),
            out(1, TILE),
            out(1, TILE),
            out(TILE, TILE),
            out(TILE, TILE),
            out(AGG, TILE),
            pl.BlockSpec((COLS, AGG), lambda s, p, c: (0, 0)),
        ],
    )

    def sds(shape, dtype=F32):
        return far((SLOTS,) + shape, dtype)

    return pl.pallas_call(
        local_kernel,
        grid_spec=grid,
        out_shape=[
            sds((COLS, TILE)),
            sds((COLS, TILE)),
            sds((1, TILE)),
            sds((1, TILE)),
            sds((TILE, TILE), BF16),
            sds((TILE, TILE), BF16),
            sds((AGG, TILE)),
            jax.ShapeDtypeStruct((COLS, AGG), F32),
        ],
        compiler_params=params(),
        cost_estimate=cost(2 * 64 * 3 * 64 * 128 * 128, 16 << 20),
        name="local_part",
    )(perm, counts, *([hbm(diag_tiles)] * n), *([hbm(right_side)] * n), hbm(remote), maps)


def coarse_kernel(op, cmap, g_out, d_out):
    spread = one_hot(cmap[...])
    product = exact_spread(spread, op)
    pieces = []
    for i in range(NC1 // TILE):
        pieces.append(tile_diag(op[i * TILE : (i + 1) * TILE, i * TILE : (i + 1) * TILE]))
    diag = jnp.concatenate(pieces, axis=1)
    inverse = 1.0 / diag
    d_out[...] = inverse
    g_out[...] = spread.astype(F32) - OMEGA * product * inverse


def exact_spread(spread, op):
    total = None
    for i in range(NC1 // 256):
        rows = slice(i * 256, (i + 1) * 256)
        hi, lo = split2(op[rows, :])
        part = dot(spread[:, rows], hi) + dot(spread[:, rows], lo)
        total = part if total is None else total + part
    return total


def coarse_setup(op, cmap):
    return pl.pallas_call(
        coarse_kernel,
        out_shape=[jax.ShapeDtypeStruct((AGG, NC1), F32), jax.ShapeDtypeStruct((1, NC1), F32)],
        compiler_params=params(),
        cost_estimate=cost(2 * 2 * 64 * 1024 * 1024, 5 << 20),
        name="coarse_setup",
    )(op, cmap)


def first_restrict_kernel(arrived, rs, rr, out, x_buf, rs_buf, x_sem, rs_sem):
    def copies(j):
        at = pl.ds(j * STEP, STEP)
        return (
            pltpu.make_async_copy(arrived.at[at, pl.ds(0, COLS)], x_buf.at[at], x_sem.at[j]),
            pltpu.make_async_copy(rs.at[at], rs_buf.at[at], rs_sem.at[j]),
        )

    for j in range(NSTEP):
        for copy in copies(j):
            copy.start()
    total = rr[...]
    for j in range(NSTEP):
        for copy in copies(j):
            copy.wait()
        for k in range(j * STEP, (j + 1) * STEP, 2):
            hi, lo = split2(beside(rs_buf[k], rs_buf[k + 1]))
            total = total + mm(beside(x_buf[k], x_buf[k + 1]), hi, lo, nt=True)
    packed = pack_rows(total)
    for q in range(PEERS):
        out[q, 0:32] = packed
        out[q, 32:40] = jnp.zeros((8, TILE), F32)


def first_restrict(arrived, rs, rr):
    return pl.pallas_call(
        first_restrict_kernel,
        in_specs=[pl.BlockSpec(memory_space=pl.ANY)] * 2 + [pl.BlockSpec(memory_space=pltpu.VMEM)],
        out_specs=pl.BlockSpec(memory_space=pltpu.VMEM),
        out_shape=jax.ShapeDtypeStruct((PEERS, ROWS, TILE), F32),
        scratch_shapes=[
            pltpu.VMEM((SLOTS, COLS, TILE), F32),
            pltpu.VMEM((SLOTS, AGG, TILE), F32),
            pltpu.SemaphoreType.DMA((NSTEP,)),
            pltpu.SemaphoreType.DMA((NSTEP,)),
        ],
        compiler_params=params(),
        name="first_restrict",
    )(hbm(arrived), hbm(rs), rr)


def pair_kernel(perm, counts, *refs):
    tiles, side, remote, hi_out, lo_out, diag_out, map_out, x_out = (refs[:STEP],) + tuple(refs[STEP:])
    step = pl.program_id(0)
    r = lax.broadcasted_iota(jnp.int32, (64, TILE), 0)
    c = lax.broadcasted_iota(jnp.int32, (64, TILE), 1)
    for k in range(STEP):
        own = off_diag(tiles[k][0])
        packed = side[k, 64:128]
        top = jnp.where((c >= 64) | (r < c), packed, 0.0)
        bottom = pltpu.roll(jnp.where((c < 64) & (r > c), packed, 0.0), 64, 1)
        half = jnp.concatenate([top, bottom], axis=0)
        other = half + half.T
        j = step * STEP + k
        live = (j % 2) < counts[j // 2]
        rem = remote[k] * jnp.where(live, -1.0, 0.0)
        block = jnp.concatenate(
            [jnp.concatenate([own, rem.T], axis=1), jnp.concatenate([rem, other], axis=1)], axis=0
        )
        hi, lo = split2(block)
        hi_out[k] = hi
        lo_out[k] = lo
        x_out[k] = side[k, 0:64]
        diag_out[k] = side[k, 128:129]
        map_out[k] = side[k, 129:130].astype(jnp.int32)


def pair_setup(perm, counts, diag_tiles, side, remote):
    def tile_spec(i):
        return pl.BlockSpec((1, TILE, TILE), lambda s, p, c: (p[s * STEP + i], 0, 0))

    def spec(*shape):
        return pl.BlockSpec((STEP,) + shape, lambda s, p, c: (s, 0, 0))

    grid = pltpu.PrefetchScalarGridSpec(
        num_scalar_prefetch=2,
        grid=(NSTEP,),
        in_specs=[tile_spec(i) for i in range(STEP)] + [spec(SIDE, TILE), spec(TILE, TILE)],
        out_specs=[spec(2 * TILE, 2 * TILE), spec(2 * TILE, 2 * TILE), spec(1, TILE), spec(1, TILE), spec(COLS, TILE)],
    )
    return pl.pallas_call(
        pair_kernel,
        grid_spec=grid,
        out_shape=[
            far((SLOTS, 2 * TILE, 2 * TILE), BF16),
            far((SLOTS, 2 * TILE, 2 * TILE), BF16),
            far((SLOTS, 1, TILE)),
            far((SLOTS, 1, TILE), jnp.int32),
            far((SLOTS, COLS, TILE)),
        ],
        compiler_params=params(),
        cost_estimate=cost(2 * 64 * 3 * 64 * 128 * 128, 16 << 20),
        name="pair_setup",
    )(perm, counts, *([hbm(diag_tiles)] * STEP), hbm(side), hbm(remote))


def gathered_rows(ref, count):
    lane = lax.broadcasted_iota(jnp.int32, (32, TILE), 1) < 64
    tops, bottoms = [], []
    for q in range(0, count, 2):
        a, b = ref[q, 0:32], ref[q + 1, 0:32]
        tops.append(jnp.where(lane, a, pltpu.roll(b, 64, 1)))
        bottoms.append(jnp.where(lane, pltpu.roll(a, 64, 1), b))
    return jnp.concatenate([jnp.concatenate(tops, axis=1), jnp.concatenate(bottoms, axis=1)], axis=0)


def lowest_kernel(arrived, g, x_out, out):
    x = gathered_rows(arrived, PEERS)
    x_out[...] = x
    hi, lo = split2(g[...])
    packed = pack_rows(mm(x, hi, lo, nt=True))
    extra = arrived[0, 32:40]
    for q in range(1, PEERS):
        extra = extra + arrived[q, 32:40]
    for q in range(GROUPS):
        out[q, 0:32] = packed
        out[q, 32:40] = extra


def lowest_part(arrived, g):
    return pl.pallas_call(
        lowest_kernel,
        out_shape=[
            jax.ShapeDtypeStruct((COLS, NC1), F32),
            jax.ShapeDtypeStruct((GROUPS, ROWS, TILE), F32),
        ],
        compiler_params=params(),
        cost_estimate=cost(20_000_000_000, 32 << 20),
        name="lowest_part",
    )(arrived, g)


def level_one(arrived, inverse_rows, g, x_ref, inverse_ref, op, e_out):
    low = gathered_rows(arrived, GROUPS)
    hi, lo = split2(inverse_rows[...])
    corr = mm(low, hi, lo, nt=True)
    ghi, glo = split2(g[...])
    lifted = mm(corr, ghi, glo)
    inverse = inverse_ref[...]
    scaled = x_ref[...] * inverse
    total = None
    for i in range(NC1 // 256):
        rows = slice(i * 256, (i + 1) * 256)
        hi, lo = split2(op[rows, :])
        term = mm(scaled[:, rows], hi, lo)
        total = term if total is None else total + term
    e = 2.0 * OMEGA * scaled - OMEGA * OMEGA * total * inverse + lifted
    for q in range(PEERS):
        e_out[q] = e[:, q * AGG : (q + 1) * AGG]


def apply_off(x, hi, lo):
    xh, xl = split2(x)
    rows = x.shape[0]
    if x.shape[1] == TILE:
        return dot(beside(xh, xl), jnp.concatenate([hi, hi], axis=0)) + dot(xh, lo)
    both = dot(jnp.concatenate([xh, xl], axis=0), hi)
    return both[:rows] + both[rows:] + dot(xh, lo)


def apply_block(x, diag, hi, lo):
    xh, xl = split2(x)
    kept = xh.astype(F32) + xl.astype(F32)
    return apply_off(x, hi, lo) + kept[:, : diag.shape[1]] * diag


def lift(parts, spread):
    rows = parts.shape[0] // 2
    two = dot(parts, spread)
    return two[:rows] + two[rows:]


def two_parts(e):
    return jnp.concatenate(split2(e), axis=0)


def pair_spread(own, peer):
    none = jnp.zeros_like(own)
    return jnp.concatenate([beside(own, none), beside(none, peer)], axis=0)


def forward_kernel(
    perm, member, arrived, inverse_rows, g, x, inverse, op, b_slot, b_rest, d_slot, d_rest, x_peer, d_peer, m_peer,
    hi_pair, lo_pair, hi_rest, lo_rest, maps, z_out, w_out, ws_out, out, e, acc_rr, acc_bz, acc_zw
):
    level_one(arrived, inverse_rows, g, x, inverse, op, e)
    acc_rr[...] = jnp.zeros_like(acc_rr)
    acc_bz[...] = jnp.zeros_like(acc_bz)
    acc_zw[...] = jnp.zeros_like(acc_zw)
    e_own = e.at[pl.ds(member[0], 1)]
    views = (e, b_slot, b_rest, d_slot, d_rest, x_peer, d_peer, m_peer, hi_pair, lo_pair, hi_rest, lo_rest, ws_out)

    @pl.loop(0, CHUNKS)
    def _(step):
        e_peer, *parts = [v.at[part(step, v.shape[0])] for v in views]
        both = [v.at[:, part(step, SLOTS)] for v in (z_out, w_out)]
        forward_step(step, perm, e_own, e_peer, *parts[:-1], maps, *both, parts[-1], acc_rr, acc_bz, acc_zw)

    packed = pack_rows(acc_rr[...])
    sums = jnp.sum(jnp.concatenate([acc_bz[...], acc_zw[...]], axis=0).T, axis=0, keepdims=True)
    r8 = lax.broadcasted_iota(jnp.int32, (8, TILE), 0)
    extra = jnp.where(r8 == 0, sums, 0.0)
    for q in range(PEERS):
        out[q, 0:32] = packed
        out[q, 32:40] = extra


def part(step, count):
    size = count // CHUNKS
    return pl.ds(step * size, size)


def forward_step(
    step, perm, e_own, e_peer, b_slot, b_rest, d_slot, d_rest, x_peer, d_peer, m_peer, hi_pair, lo_pair,
    hi_rest, lo_rest, maps, z_out, w_out, ws_out, acc_rr, acc_bz, acc_zw
):
    e_mine = two_parts(e_own[0])
    e_both = [two_parts(beside(e_own[0], e_peer[q])) for q in range(CHUNK // 2)]
    rr, bz, zw = acc_rr[...], acc_bz[...], acc_zw[...]
    pairs, rest = range(CHUNK), range(CHUNK)
    rows = [maps[pl.ds(perm[at + step * CHUNK + k], 1)] for at in (0, SLOTS) for k in pairs]
    b_own = [b_slot[k] for k in pairs] + [b_rest[k] for k in rest]
    diag = [jnp.concatenate([d_slot[k], d_peer[k]], axis=1) for k in pairs] + [d_rest[k] for k in rest]
    rdiag = [OMEGA / d for d in diag]
    mats = [(hi_pair[k], lo_pair[k]) for k in pairs] + [(hi_rest[k], lo_rest[k]) for k in rest]
    x1 = [beside(b_own[k] * rdiag[k][:, :TILE], x_peer[k]) for k in pairs]
    x1 = x1 + [b * rd for b, rd in zip(b_own[CHUNK:], rdiag[CHUNK:])]
    spread = [one_hot(row) for row in rows]
    ups = [lift(e_both[k // 2], pair_spread(spread[k], one_hot(m_peer[k]))) for k in pairs]
    ups = ups + [lift(e_mine, sp) for sp in spread[CHUNK:]]
    x = [start + up for start, up in zip(x1, ups)]
    image = [apply_off(xx, *m) for xx, m in zip(x, mats)]
    z = [(1.0 - OMEGA) * xx + start - im * rd for xx, start, im, rd in zip(x, x1, image, rdiag)]
    w = [apply_block(zz, d, *m) for zz, d, m in zip(z, diag, mats)]
    x1 = [ww * rd for ww, rd in zip(w, rdiag)]
    left = [(m[0][:, :TILE], m[1][:, :TILE]) for m in mats]
    y = [(1.0 - OMEGA) * ww[:, :TILE] - apply_off(xx, *m) for ww, xx, m in zip(w, x1, left)]
    for i in range(0, 2 * CHUNK, 2):
        rr = rr + mm_exact(beside(y[i], y[i + 1]), beside(spread[i], spread[i + 1]), nt=True)
    for i in range(2 * CHUNK):
        zz, ww = z[i][:, :TILE], w[i][:, :TILE]
        bz = bz + b_own[i] * zz
        zw = zw + zz * ww
        z_out[i // CHUNK, i % CHUNK] = zz
        w_out[i // CHUNK, i % CHUNK] = ww
    for k in pairs:
        ws_out[k] = w[k][:, TILE:]
    acc_rr[...] = rr
    acc_bz[...] = bz
    acc_zw[...] = zw


def specs(smem, vmem):
    return [pl.BlockSpec(memory_space=pltpu.SMEM)] * smem + [pl.BlockSpec(memory_space=pltpu.VMEM)] * vmem


def forward_part(scalars, arrays):
    return pl.pallas_call(
        forward_kernel,
        in_specs=specs(len(scalars), len(arrays)),
        out_specs=specs(0, 4),
        out_shape=[
            near((2, SLOTS, COLS, TILE)),
            near((2, SLOTS, COLS, TILE)),
            near((SLOTS, COLS, TILE)),
            jax.ShapeDtypeStruct((PEERS, ROWS, TILE), F32),
        ],
        scratch_shapes=[
            pltpu.VMEM((PEERS, COLS, AGG), F32),
            pltpu.VMEM((COLS, AGG), F32),
            pltpu.VMEM((COLS, TILE), F32),
            pltpu.VMEM((COLS, TILE), F32),
        ],
        compiler_params=params(),
        name="forward_part",
    )(*scalars, *arrays)


def second_kernel(
    perm, member, arrived, inverse_rows, g, x, inverse, op, b_slot, b_rest, d_slot, d_rest, d_peer, m_peer, hi_pair, lo_pair,
    hi_rest, lo_rest, maps, z_in, w_in, w_peer, v_out, u_out, out, dots, e, acc_a, acc_b, acc_c, acc_alpha
):
    extra = arrived[0, 32:40]
    for q in range(1, GROUPS):
        extra = extra + arrived[q, 32:40]
    dots[...] = extra
    level_one(arrived, inverse_rows, g, x, inverse, op, e)
    acc_a[...] = jnp.zeros_like(acc_a)
    acc_b[...] = jnp.zeros_like(acc_b)
    acc_c[...] = jnp.zeros_like(acc_c)
    col = column(dots[0:1])
    acc_alpha[...] = col[:COLS] / col[COLS:]
    e_own = e.at[pl.ds(member[0], 1)]
    views = (e, b_slot, b_rest, d_slot, d_rest, d_peer, m_peer, hi_pair, lo_pair, hi_rest, lo_rest, w_peer)

    @pl.loop(0, CHUNKS)
    def _(step):
        e_peer, *parts = [v.at[part(step, v.shape[0])] for v in views]
        z_part, w_part, v_part, u_part = [v.at[:, part(step, SLOTS)] for v in (z_in, w_in, v_out, u_out)]
        second_step(
            step, perm, e_own, e_peer, *parts[:-1], maps, z_part, w_part, parts[-1], v_part, u_part,
            acc_a, acc_b, acc_c, acc_alpha
        )

    first = jnp.sum(jnp.concatenate([acc_a[...], acc_b[...]], axis=0).T, axis=0, keepdims=True)
    last = jnp.sum(jnp.concatenate([acc_c[...], acc_c[...]], axis=0).T, axis=0, keepdims=True)
    out[...] = jnp.broadcast_to(jnp.concatenate([first, last], axis=0), out.shape)


def second_step(
    step, perm, e_own, e_peer, b_slot, b_rest, d_slot, d_rest, d_peer, m_peer, hi_pair, lo_pair,
    hi_rest, lo_rest, maps, z_in, w_in, w_peer, v_out, u_out, acc_a, acc_b, acc_c, acc_alpha
):
    alpha = acc_alpha[...]
    e_mine = two_parts(e_own[0])
    e_both = [two_parts(beside(e_own[0], e_peer[q])) for q in range(CHUNK // 2)]
    sums = [acc_a[...], acc_b[...], acc_c[...]]

    def gather(b, z, w, v, u):
        r1 = b - alpha * w
        z1 = z - alpha * v
        az1 = w - alpha * u
        sums[0] = sums[0] + r1 * z1
        sums[1] = sums[1] + z1 * az1
        sums[2] = sums[2] + (z1 * w + z * az1)

    pairs, rest = range(CHUNK), range(CHUNK)
    rows = [maps[pl.ds(perm[at + step * CHUNK + k], 1)] for at in (0, SLOTS) for k in pairs]
    diag = [jnp.concatenate([d_slot[k], d_peer[k]], axis=1) for k in pairs] + [d_rest[k] for k in rest]
    rdiag = [OMEGA / d for d in diag]
    mats = [(hi_pair[k], lo_pair[k]) for k in pairs] + [(hi_rest[k], lo_rest[k]) for k in rest]
    w = [jnp.concatenate([w_in[0, k], w_peer[k]], axis=1) for k in pairs] + [w_in[1, k] for k in rest]
    spread = [one_hot(row) for row in rows]
    ups = [lift(e_both[k // 2], pair_spread(spread[k], one_hot(m_peer[k]))) for k in pairs]
    ups = ups + [lift(e_mine, sp) for sp in spread[CHUNK:]]
    x1 = [ww * rd for ww, rd in zip(w, rdiag)]
    x = [start + up for start, up in zip(x1, ups)]
    image = [apply_off(xx, *m) for xx, m in zip(x, mats)]
    v = [(1.0 - OMEGA) * xx + start - im * rd for xx, start, im, rd in zip(x, x1, image, rdiag)]
    left = [(m[0][:, :TILE], m[1][:, :TILE]) for m in mats]
    u = [apply_block(vv, d[:, :TILE], *m) for vv, d, m in zip(v, diag, left)]
    for i in range(2 * CHUNK):
        vv, b_ref = v[i][:, :TILE], (b_slot if i < CHUNK else b_rest)
        v_out[i // CHUNK, i % CHUNK] = vv
        u_out[i // CHUNK, i % CHUNK] = u[i]
        gather(b_ref[i % CHUNK], z_in[i // CHUNK, i % CHUNK], w[i][:, :TILE], vv, u[i])
    acc_a[...] = sums[0]
    acc_b[...] = sums[1]
    acc_c[...] = sums[2]


def second_part(scalars, arrays):
    return pl.pallas_call(
        second_kernel,
        in_specs=specs(len(scalars), len(arrays)),
        out_specs=specs(0, 4),
        out_shape=[
            near((2, SLOTS, COLS, TILE)),
            near((2, SLOTS, COLS, TILE)),
            jax.ShapeDtypeStruct((GROUPS * PEERS, 2, TILE), F32),
            jax.ShapeDtypeStruct((8, TILE), F32),
        ],
        scratch_shapes=[pltpu.VMEM((PEERS, COLS, AGG), F32)] + [pltpu.VMEM((COLS, TILE), F32)] * 4,
        compiler_params=params(),
        name="second_part",
    )(*scalars, *arrays)


def combine_kernel(perm, dots, arrived, b_slot, b_rest, z, w, v, u, solution, residual, coef):
    step = pl.program_id(0)

    @pl.when(step == 0)
    def _():
        total = jnp.sum(arrived[...], axis=0)
        old = column(dots[0:1])
        one = column(total[0:1])
        two = column(total[1:2])
        rho, zw = old[:COLS], old[COLS:]
        rho_next, zz = one[:COLS], one[COLS:]
        cross = two[:COLS]
        alpha = rho / zw
        beta = rho_next / rho
        alpha_next = rho_next / (zz + beta * cross + beta * beta * zw)
        coef[0] = alpha
        coef[1] = beta
        coef[2] = alpha_next

    alpha, beta, alpha_next = coef[0], coef[1], coef[2]
    for half, b_ref in ((0, b_slot), (1, b_rest)):
        for k in range(STEP):
            index = perm[half * SLOTS + step * STEP + k]
            at = pl.ds(pl.multiple_of(index * TILE, TILE), TILE)
            z0, w0 = z[half, k], w[half, k]
            z1 = z0 - alpha * v[half, k]
            az1 = w0 - alpha * u[half, k]
            solution[:, at] = alpha * z0 + alpha_next * (z1 + beta * z0)
            residual[:, at] = b_ref[k] - alpha * w0 - alpha_next * (az1 + beta * w0)


def combine(perm, dots, arrived, b_slot, b_rest, z, w, v, u):
    def pair():
        return pl.BlockSpec((2, STEP, COLS, TILE), lambda s, p: (0, s, 0, 0))

    def single():
        return pl.BlockSpec((STEP, COLS, TILE), lambda s, p: (s, 0, 0))

    def whole():
        return pl.BlockSpec((COLS, BLK * TILE), lambda s, p: (0, 0))

    grid = pltpu.PrefetchScalarGridSpec(
        num_scalar_prefetch=1,
        grid=(NSTEP,),
        in_specs=[
            pl.BlockSpec((8, TILE), lambda s, p: (0, 0)),
            pl.BlockSpec((GROUPS * PEERS, 2, TILE), lambda s, p: (0, 0, 0)),
            single(),
            single(),
            pair(),
            pair(),
            pair(),
            pair(),
        ],
        out_specs=[whole(), whole()],
        scratch_shapes=[pltpu.VMEM((3, COLS, TILE), F32)],
    )
    return pl.pallas_call(
        combine_kernel,
        grid_spec=grid,
        out_shape=[jax.ShapeDtypeStruct((COLS, BLK * TILE), F32)] * 2,
        compiler_params=params(),
        name="combine",
    )(perm, dots, arrived, b_slot, b_rest, z, w, v, u)


def exchange(x, axes):
    return lax.all_to_all(x, axes, 0, 0, tiled=True)


def on_device(
    right_side,
    diag_tiles,
    remote_tiles,
    slot_counts,
    slot_blocks,
    fine_map,
    coarse_map,
    level1_ops,
    coarsest_inverse,
):
    group = lax.axis_index("grp")
    member = lax.axis_index(GROUP_AXES).astype(jnp.int32).reshape(1)
    slot_list = slot_blocks.reshape(SLOTS)
    counts = slot_counts.reshape(PEERS)
    maps = fine_map.reshape(BLK, TILE)
    remote = remote_tiles.reshape(SLOTS, TILE, TILE)
    operator = level1_ops[0]

    outgoing = boundary_pack(slot_blocks, diag_tiles, right_side, maps)
    side = exchange(outgoing.reshape(PEERS, 2 * SIDE, TILE), GROUP_AXES).reshape(SLOTS, SIDE, TILE)

    tile_ids = jnp.arange(BLK, dtype=jnp.int32)
    free = jnp.logical_not(jnp.any(slot_list[:, None] == tile_ids[None, :], axis=0)).astype(jnp.int32)
    rank = jnp.sum(jnp.where(tile_ids[None, :] < tile_ids[:, None], free[None, :], 0), axis=1)
    chosen = (rank[None, :] == jnp.arange(SLOTS, dtype=jnp.int32)[:, None]) & (free[None, :] == 1)
    rest_list = jnp.sum(jnp.where(chosen, tile_ids[None, :], 0), axis=1)
    perm = jnp.concatenate([slot_list, rest_list])

    b_slot, b_rest, d_slot, d_rest, hi_rest, lo_rest, rs, rr_local = local_part(
        perm, counts, diag_tiles, right_side, remote, maps
    )
    g, inverse = coarse_setup(operator, coarse_map.reshape(1, NC1))
    inverse_rows = lax.dynamic_slice_in_dim(coarsest_inverse, group * AGG, AGG, 0)

    rr_local, g, inverse_rows, member = lax.optimization_barrier((rr_local, g, inverse_rows, member))
    gathered = exchange(first_restrict(side, rs, rr_local), GROUP_AXES)
    hi_pair, lo_pair, d_peer, m_peer, x_peer = pair_setup(perm, counts, diag_tiles, side, remote)
    gathered, hi_pair = lax.optimization_barrier((gathered, hi_pair))

    scalars = (perm, member)
    x, outgoing = lowest_part(gathered, g)
    coarse = (exchange(outgoing, "grp"), inverse_rows, g, x, inverse)
    fixed = (d_slot, d_rest, d_peer, m_peer, hi_pair, lo_pair, hi_rest, lo_rest, maps)
    z, w, w_peer, outgoing = forward_part(
        scalars, coarse + (operator, b_slot, b_rest, d_slot, d_rest, x_peer) + fixed[2:]
    )
    x, outgoing = lowest_part(exchange(outgoing, GROUP_AXES), g)
    coarse = (exchange(outgoing, "grp"), inverse_rows, g, x, inverse)
    v, u, outgoing, dots = second_part(scalars, coarse + (operator, b_slot, b_rest) + fixed + (z, w, w_peer))
    sums = exchange(outgoing, ALL_AXES)
    return tuple(combine(perm, dots, sums, b_slot, b_rest, z, w, v, u))


def solution(mesh):
    placed = (
        P(None, ("grp", "sub", "chip")),
        P(("grp", "sub", "chip"), None, None),
        P(("grp", "sub", "chip"), None, None, None),
        P(("grp", "sub", "chip"), None),
        P(("grp", "sub", "chip"), None, None),
        P(("grp", "sub", "chip")),
        P("grp"),
        P("grp", None, None),
        P(),
    )
    return jax.shard_map(
        on_device,
        mesh=mesh,
        in_specs=placed,
        out_specs=(P(None, ("grp", "sub", "chip")), P(None, ("grp", "sub", "chip"))),
        check_vma=False,
    )
```

```python
import functools

import jax
import jax.numpy as jnp
from jax import lax
from jax.experimental import pallas as pl
from jax.experimental.pallas import tpu as pltpu
from jax.sharding import PartitionSpec as P

OMEGA = 0.6
F32 = jnp.float32
BF16 = jnp.bfloat16
COLS = 64
TILE = 128
BLK = 64
SLOTS = 32
PEERS = 16
GROUPS = 8
AGG = 64
NC1 = 1024
STEP = 8
NSTEP = SLOTS // STEP
CHUNK = 16
CHUNKS = SLOTS // CHUNK
SIDE = 264
PEER_STEP = 4
ROWS = 40

GROUP_AXES = ("sub", "chip")
ALL_AXES = ("grp", "sub", "chip")


def params(mib=20):
    return pltpu.CompilerParams(vmem_limit_bytes=mib * 1024 * 1024)


def hbm(x):
    return pltpu.with_memory_space_constraint(x, pltpu.HBM)


def near(shape, dtype=F32):
    return pltpu.VMEM(shape, dtype)


def far(shape, dtype=F32):
    return pltpu.HBM(shape, dtype)


def cost(flops, moved):
    return pl.CostEstimate(flops=flops, bytes_accessed=moved, transcendentals=0)


def split2(x):
    hi = x.astype(BF16)
    lo = (x - hi.astype(F32)).astype(BF16)
    return hi, lo


def dot(a, b):
    return jnp.dot(a, b, preferred_element_type=F32)


def dot_nt(a, b):
    return lax.dot_general(a, b, (((1,), (1,)), ((), ())), preferred_element_type=F32)


def mm(x, whi, wlo, nt=False):
    op = dot_nt if nt else dot
    rows = x.shape[0]
    hi, lo = split2(x)
    both = op(jnp.concatenate([hi, lo], axis=0), whi)
    return both[:rows] + both[rows:] + op(hi, wlo)


def mm_exact(x, w, nt=False):
    op = dot_nt if nt else dot
    rows = x.shape[0]
    two = op(jnp.concatenate(split2(x), axis=0), w)
    return two[:rows] + two[rows:]


def beside(a, b):
    return jnp.concatenate([a, b], axis=1)


def eye_mask():
    r = lax.broadcasted_iota(jnp.int32, (TILE, TILE), 0)
    c = lax.broadcasted_iota(jnp.int32, (TILE, TILE), 1)
    return r, c


def tile_diag(tile):
    r, c = eye_mask()
    return jnp.sum(jnp.where(r == c, tile, 0.0), axis=0, keepdims=True)


def off_diag(tile):
    r, c = eye_mask()
    return jnp.where(r == c, 0.0, tile)


def one_hot(row):
    r = lax.broadcasted_iota(jnp.int32, (AGG, row.shape[1]), 0)
    return jnp.where(r == row, 1.0, 0.0).astype(BF16)


def pack_rows(x):
    wide = jnp.concatenate([x[:32], x[32:]], axis=1)
    return wide


def column(row):
    return jnp.broadcast_to(row, (TILE, TILE)).T


def boundary_kernel(slots, maps, tiles, cols, out, map_buf, tile_buf, col_buf, out_buf, map_sem, col_sem, tile_sem, out_sem):
    def tile_copy(j):
        return pltpu.make_async_copy(tiles.at[slots[0, j % 2, j // 2]], tile_buf.at[j], tile_sem.at[j])

    def col_copy(j):
        at = pl.ds(pl.multiple_of(slots[0, j % 2, j // 2] * TILE, TILE), TILE)
        return pltpu.make_async_copy(cols.at[:, at], col_buf.at[j], col_sem.at[j])

    def out_copy(j):
        at = pl.ds(j // 2, PEER_STEP)
        return pltpu.make_async_copy(out_buf.at[at], out.at[at], out_sem.at[j // STEP])

    map_copy = pltpu.make_async_copy(maps, map_buf, map_sem)
    map_copy.start()
    for j in range(SLOTS):
        tile_copy(j).start()
        col_copy(j).start()
    r = lax.broadcasted_iota(jnp.int32, (64, TILE), 0)
    c = lax.broadcasted_iota(jnp.int32, (64, TILE), 1)
    r8 = lax.broadcasted_iota(jnp.int32, (8, TILE), 0)
    map_copy.wait()
    for j in range(0, SLOTS, STEP):
        for k in range(j, j + STEP):
            tile_copy(k).wait()
            col_copy(k).wait()
        tile = [tile_buf[k] for k in range(j, j + STEP)]
        diag = [tile_diag(t) for t in tile]
        for k in range(j, j + STEP):
            t, d = tile[k - j], diag[k - j]
            q, base = k // 2, (k % 2) * 128
            out_buf[q, base : base + 64] = col_buf[k] * (OMEGA / d)
            below = pltpu.roll(t[64:], 64, 1)
            out_buf[q, base + 64 : base + 128] = jnp.where((c < 64) & (r > c), below, t[:64])
        for k in range(j, j + STEP, 2):
            own = [map_buf[pl.ds(slots[0, i, k // 2], 1)].astype(F32) for i in range(2)]
            d0, d1 = diag[k - j], diag[k - j + 1]
            out_buf[k // 2, 256:264] = jnp.where(
                r8 == 0, d0, jnp.where(r8 == 1, own[0], jnp.where(r8 == 2, d1, jnp.where(r8 == 3, own[1], 0.0)))
            )
        out_copy(j).start()
    for j in range(0, SLOTS, STEP):
        out_copy(j).wait()


def boundary_pack(slot_blocks, diag_tiles, right_side, maps):
    return pl.pallas_call(
        boundary_kernel,
        in_specs=[pl.BlockSpec(memory_space=pltpu.SMEM)] + [pl.BlockSpec(memory_space=pl.ANY)] * 3,
        out_specs=pl.BlockSpec(memory_space=pl.ANY),
        out_shape=far((PEERS, SIDE, TILE)),
        scratch_shapes=[
            pltpu.VMEM((BLK, TILE), jnp.int32),
            pltpu.VMEM((SLOTS, TILE, TILE), F32),
            pltpu.VMEM((SLOTS, COLS, TILE), F32),
            pltpu.VMEM((PEERS, SIDE, TILE), F32),
            pltpu.SemaphoreType.DMA,
            pltpu.SemaphoreType.DMA((SLOTS,)),
            pltpu.SemaphoreType.DMA((SLOTS,)),
            pltpu.SemaphoreType.DMA((NSTEP,)),
        ],
        compiler_params=params(),
        name="boundary_pack",
    )(slot_blocks.transpose(0, 2, 1), hbm(maps), hbm(diag_tiles), hbm(right_side))


def local_kernel(perm, counts, *refs):
    n = 2 * STEP
    tiles, cols = refs[:n], refs[n : 2 * n]
    remote, maps = refs[2 * n : 2 * n + 2]
    b_slot, b_rest, d_slot, d_rest, hi_rest, lo_rest, hi_top, lo_top, hi_side, lo_side, rs, rr = refs[2 * n + 2 :]
    step = pl.program_id(0)

    @pl.when(step == 0)
    def _():
        rr[...] = jnp.zeros_like(rr)

    index = [perm[(0 if i < STEP else SLOTS) + step * STEP + i % STEP] for i in range(n)]
    tile = [tiles[i][0] for i in range(n)]
    diag = [tile_diag(t) for t in tile]
    off = [split2(off_diag(t)) for t in tile]
    b = [cols[i][...] for i in range(n)]
    x = [OMEGA * bb / d for bb, d in zip(b, diag)]
    y = [bb - OMEGA * bb - mm(xx, *o) for bb, xx, o in zip(b, x, off)]
    spread = [one_hot(maps[pl.ds(i, 1)]) for i in index]
    total = rr[...]
    for i in range(0, n, 2):
        total = total + mm_exact(beside(y[i], y[i + 1]), beside(spread[i], spread[i + 1]), nt=True)
    for k in range(STEP):
        b_slot[k] = b[k]
        d_slot[k] = diag[k]
        b_rest[k] = b[STEP + k]
        d_rest[k] = diag[STEP + k]
        hi_rest[k], lo_rest[k] = off[STEP + k]
    coupling, turned = [], []
    for k in range(STEP):
        j = step * STEP + k
        live = (j % 2) < counts[j // 2]
        scaled = remote[k] * jnp.where(live, -1.0, 0.0)
        coupling.append(split2(scaled))
        turned.append(split2(scaled.T))
    for k in range(STEP):
        rs[k] = -(dot_nt(spread[k], coupling[k][0]) + dot_nt(spread[k], coupling[k][1]))
        hi_top[k] = beside(off[k][0], turned[k][0])
        lo_top[k] = beside(off[k][1], turned[k][1])
        hi_side[k], lo_side[k] = coupling[k]
    rr[...] = total


def local_part(perm, counts, diag_tiles, right_side, remote, maps):
    def where(i):
        return (0 if i < STEP else SLOTS) + i % STEP

    def tile_spec(i):
        return pl.BlockSpec((1, TILE, TILE), lambda s, p, c: (p[s * STEP + where(i)], 0, 0))

    def col_spec(i):
        return pl.BlockSpec((COLS, TILE), lambda s, p, c: (0, p[s * STEP + where(i)]))

    def out(*shape):
        return pl.BlockSpec((STEP,) + shape, lambda s, p, c: (s, 0, 0))

    n = 2 * STEP
    grid = pltpu.PrefetchScalarGridSpec(
        num_scalar_prefetch=2,
        grid=(NSTEP,),
        in_specs=[tile_spec(i) for i in range(n)]
        + [col_spec(i) for i in range(n)]
        + [
            pl.BlockSpec((STEP, TILE, TILE), lambda s, p, c: (s, 0, 0)),
            pl.BlockSpec((BLK, TILE), lambda s, p, c: (0, 0)),
        ],
        out_specs=[
            out(COLS, TILE),
            out(COLS, TILE),
            out(1, TILE),
            out(1, TILE),
            out(TILE, TILE),
            out(TILE, TILE),
            out(TILE, 2 * TILE),
            out(TILE, 2 * TILE),
            out(TILE, TILE),
            out(TILE, TILE),
            out(AGG, TILE),
            pl.BlockSpec((COLS, AGG), lambda s, p, c: (0, 0)),
        ],
    )

    def sds(shape, dtype=F32):
        return far((SLOTS,) + shape, dtype)

    return pl.pallas_call(
        local_kernel,
        grid_spec=grid,
        out_shape=[
            sds((COLS, TILE)),
            sds((COLS, TILE)),
            sds((1, TILE)),
            sds((1, TILE)),
            sds((TILE, TILE), BF16),
            sds((TILE, TILE), BF16),
            sds((TILE, 2 * TILE), BF16),
            sds((TILE, 2 * TILE), BF16),
            sds((TILE, TILE), BF16),
            sds((TILE, TILE), BF16),
            sds((AGG, TILE)),
            jax.ShapeDtypeStruct((COLS, AGG), F32),
        ],
        compiler_params=params(),
        cost_estimate=cost(2 * 64 * 3 * 64 * 128 * 128, 16 << 20),
        name="local_part",
    )(perm, counts, *([hbm(diag_tiles)] * n), *([hbm(right_side)] * n), hbm(remote), maps)


def coarse_kernel(op, cmap, g_out, d_out, hi_out, lo_out):
    spread = one_hot(cmap[...])
    product = None
    for i in range(NC1 // 256):
        rows = slice(i * 256, (i + 1) * 256)
        hi, lo = split2(op[rows, :])
        hi_out[rows, :] = hi
        lo_out[rows, :] = lo
        term = dot(spread[:, rows], hi) + dot(spread[:, rows], lo)
        product = term if product is None else product + term
    pieces = []
    for i in range(NC1 // TILE):
        pieces.append(tile_diag(op[i * TILE : (i + 1) * TILE, i * TILE : (i + 1) * TILE]))
    diag = jnp.concatenate(pieces, axis=1)
    inverse = 1.0 / diag
    d_out[...] = inverse
    g_out[...] = spread.astype(F32) - OMEGA * product * inverse


def coarse_setup(op, cmap):
    return pl.pallas_call(
        coarse_kernel,
        out_shape=[
            jax.ShapeDtypeStruct((AGG, NC1), F32),
            jax.ShapeDtypeStruct((1, NC1), F32),
            far((NC1, NC1), BF16),
            far((NC1, NC1), BF16),
        ],
        compiler_params=params(),
        cost_estimate=cost(2 * 2 * 64 * 1024 * 1024, 5 << 20),
        name="coarse_setup",
    )(op, cmap)


def first_restrict_kernel(arrived, rs, rr, out, x_buf, rs_buf, x_sem, rs_sem):
    def copies(j):
        peers, slots = pl.ds(j * PEER_STEP, PEER_STEP), pl.ds(j * STEP, STEP)
        return [
            pltpu.make_async_copy(arrived.at[peers, pl.ds(c * 128, COLS)], x_buf.at[c, peers], x_sem.at[c, j])
            for c in range(2)
        ] + [pltpu.make_async_copy(rs.at[slots], rs_buf.at[slots], rs_sem.at[j])]

    for j in range(NSTEP):
        for copy in copies(j):
            copy.start()
    total = rr[...]
    for j in range(NSTEP):
        for copy in copies(j):
            copy.wait()
        for q in range(j * PEER_STEP, (j + 1) * PEER_STEP):
            hi, lo = split2(beside(rs_buf[2 * q], rs_buf[2 * q + 1]))
            total = total + mm(beside(x_buf[0, q], x_buf[1, q]), hi, lo, nt=True)
    out[...] = jnp.broadcast_to(pack_rows(total), out.shape)


def first_restrict(arrived, rs, rr):
    return pl.pallas_call(
        first_restrict_kernel,
        in_specs=[pl.BlockSpec(memory_space=pl.ANY)] * 2 + [pl.BlockSpec(memory_space=pltpu.VMEM)],
        out_specs=pl.BlockSpec(memory_space=pltpu.VMEM),
        out_shape=jax.ShapeDtypeStruct((PEERS, 32, TILE), F32),
        scratch_shapes=[
            pltpu.VMEM((2, PEERS, COLS, TILE), F32),
            pltpu.VMEM((SLOTS, AGG, TILE), F32),
            pltpu.SemaphoreType.DMA((2, NSTEP)),
            pltpu.SemaphoreType.DMA((NSTEP,)),
        ],
        compiler_params=params(8),
        name="first_restrict",
    )(hbm(arrived), hbm(rs), rr)


def pair_kernel(side0, side1, extra, hi_out, lo_out, diag_out, map_out):
    r = lax.broadcasted_iota(jnp.int32, (64, TILE), 0)
    c = lax.broadcasted_iota(jnp.int32, (64, TILE), 1)
    for k in range(STEP):
        packed = (side0, side1)[k % 2][k // 2]
        top = jnp.where((c >= 64) | (r < c), packed, 0.0)
        bottom = pltpu.roll(jnp.where((c < 64) & (r > c), packed, 0.0), 64, 1)
        half = jnp.concatenate([top, bottom], axis=0)
        hi_out[k], lo_out[k] = split2(half + half.T)
        at = 2 * (k % 2)
        diag_out[k] = extra[k // 2, at : at + 1]
        map_out[k] = extra[k // 2, at + 1 : at + 2].astype(jnp.int32)


def pair_setup(side):
    def spec(*shape):
        return pl.BlockSpec((STEP,) + shape, lambda s: (s, 0, 0))

    return pl.pallas_call(
        pair_kernel,
        grid=(NSTEP,),
        in_specs=[
            pl.BlockSpec((PEER_STEP, 64, TILE), lambda s: (s, 1, 0)),
            pl.BlockSpec((PEER_STEP, 64, TILE), lambda s: (s, 3, 0)),
            pl.BlockSpec((PEER_STEP, 8, TILE), lambda s: (s, 32, 0)),
        ],
        out_specs=[spec(TILE, TILE), spec(TILE, TILE), spec(1, TILE), spec(1, TILE)],
        out_shape=[
            far((SLOTS, TILE, TILE), BF16),
            far((SLOTS, TILE, TILE), BF16),
            far((SLOTS, 1, TILE)),
            far((SLOTS, 1, TILE), jnp.int32),
        ],
        compiler_params=params(),
        cost_estimate=cost(2 * 64 * 3 * 64 * 128 * 128, 16 << 20),
        name="pair_setup",
    )(*([hbm(side)] * 3))


def gathered_rows(ref, count):
    lane = lax.broadcasted_iota(jnp.int32, (32, TILE), 1) < 64
    tops, bottoms = [], []
    for q in range(0, count, 2):
        a, b = ref[q, 0:32], ref[q + 1, 0:32]
        tops.append(jnp.where(lane, a, pltpu.roll(b, 64, 1)))
        bottoms.append(jnp.where(lane, pltpu.roll(a, 64, 1), b))
    return jnp.concatenate([jnp.concatenate(tops, axis=1), jnp.concatenate(bottoms, axis=1)], axis=0)


def lowest_kernel(arrived, g, x_out, out):
    x = gathered_rows(arrived, PEERS)
    x_out[...] = x
    hi, lo = split2(g[...])
    packed = pack_rows(mm(x, hi, lo, nt=True))
    if arrived.shape[1] == ROWS:
        extra = arrived[0, 32:40]
        for q in range(1, PEERS):
            extra = extra + arrived[q, 32:40]
        packed = jnp.concatenate([packed, extra], axis=0)
    out[...] = jnp.broadcast_to(packed, out.shape)


def lowest_part(arrived, g):
    return pl.pallas_call(
        lowest_kernel,
        out_shape=[
            jax.ShapeDtypeStruct((COLS, NC1), F32),
            jax.ShapeDtypeStruct((GROUPS, arrived.shape[1], TILE), F32),
        ],
        compiler_params=params(6),
        cost_estimate=cost(20_000_000_000, 32 << 20),
        name="lowest_part",
    )(arrived, g)


def level_one(arrived, inverse_rows, g, x_ref, inverse_ref, op_hi, op_lo, e_out):
    low = gathered_rows(arrived, GROUPS)
    hi, lo = split2(inverse_rows[...])
    corr = mm(low, hi, lo, nt=True)
    ghi, glo = split2(g[...])
    lifted = mm(corr, ghi, glo)
    inverse = inverse_ref[...]
    scaled = x_ref[...] * inverse
    total = None
    for i in range(NC1 // 256):
        rows = slice(i * 256, (i + 1) * 256)
        term = mm(scaled[:, rows], op_hi[rows, :], op_lo[rows, :])
        total = term if total is None else total + term
    e = 2.0 * OMEGA * scaled - OMEGA * OMEGA * total * inverse + lifted
    for q in range(PEERS):
        e_out[q] = e[:, q * AGG : (q + 1) * AGG]


def apply_off(x, hi, lo):
    xh, xl = split2(x)
    rows = x.shape[0]
    if x.shape[1] == TILE:
        return dot(beside(xh, xl), jnp.concatenate([hi, hi], axis=0)) + dot(xh, lo)
    both = dot(jnp.concatenate([xh, xl], axis=0), hi)
    return both[:rows] + both[rows:] + dot(xh, lo)


def apply_block(x, diag, hi, lo):
    xh, xl = split2(x)
    kept = xh.astype(F32) + xl.astype(F32)
    return apply_off(x, hi, lo) + kept[:, : diag.shape[1]] * diag


def lift(parts, spread):
    rows = parts.shape[0] // 2
    two = dot(parts, spread)
    return two[:rows] + two[rows:]


def two_parts(e):
    return jnp.concatenate(split2(e), axis=0)


def block(top, side, peer, k):
    return jnp.concatenate([top[k], beside(side[k], peer[k])], axis=0)


def pair_spread(own, peer):
    none = jnp.zeros_like(own)
    return jnp.concatenate([beside(own, none), beside(none, peer)], axis=0)


def forward_kernel(
    perm, member, arrived, inverse_rows, g, x, inverse, op_hi, op_lo, b_slot, b_rest, d_slot, d_rest, x_peer, d_peer, m_peer,
    hi_top, lo_top, hi_side, lo_side, hi_peer, lo_peer, hi_rest, lo_rest, maps, z_out, w_out, ws_out, out, e, acc_rr, acc_bz, acc_zw
):
    level_one(arrived, inverse_rows, g, x, inverse, op_hi, op_lo, e)
    acc_rr[...] = jnp.zeros_like(acc_rr)
    acc_bz[...] = jnp.zeros_like(acc_bz)
    acc_zw[...] = jnp.zeros_like(acc_zw)
    e_own = e.at[pl.ds(member[0], 1)]
    views = (e, b_slot, b_rest, d_slot, d_rest, x_peer, d_peer, m_peer, hi_top, lo_top, hi_side, lo_side, hi_peer, lo_peer, hi_rest, lo_rest, ws_out)

    @pl.loop(0, CHUNKS)
    def _(step):
        e_peer, *parts = [v.at[part(step, v.shape[0])] for v in views]
        both = [v.at[:, part(step, SLOTS)] for v in (z_out, w_out)]
        forward_step(step, perm, e_own, e_peer, *parts[:-1], maps, *both, parts[-1], acc_rr, acc_bz, acc_zw)

    packed = pack_rows(acc_rr[...])
    sums = jnp.sum(jnp.concatenate([acc_bz[...], acc_zw[...]], axis=0).T, axis=0, keepdims=True)
    r8 = lax.broadcasted_iota(jnp.int32, (8, TILE), 0)
    extra = jnp.where(r8 == 0, sums, 0.0)
    for q in range(PEERS):
        out[q, 0:32] = packed
        out[q, 32:40] = extra


def part(step, count):
    size = count // CHUNKS
    return pl.ds(step * size, size)


def forward_step(
    step, perm, e_own, e_peer, b_slot, b_rest, d_slot, d_rest, x_peer, d_peer, m_peer,
    hi_top, lo_top, hi_side, lo_side, hi_peer, lo_peer, hi_rest, lo_rest, maps, z_out, w_out, ws_out, acc_rr, acc_bz, acc_zw
):
    e_mine = two_parts(e_own[0])
    e_both = [two_parts(beside(e_own[0], e_peer[q])) for q in range(CHUNK // 2)]
    rr, bz, zw = acc_rr[...], acc_bz[...], acc_zw[...]
    pairs, rest = range(CHUNK), range(CHUNK)
    rows = [maps[pl.ds(perm[at + step * CHUNK + k], 1)] for at in (0, SLOTS) for k in pairs]
    b_own = [b_slot[k] for k in pairs] + [b_rest[k] for k in rest]
    diag = [jnp.concatenate([d_slot[k], d_peer[k]], axis=1) for k in pairs] + [d_rest[k] for k in rest]
    rdiag = [OMEGA / d for d in diag]
    mats = [(block(hi_top, hi_side, hi_peer, k), block(lo_top, lo_side, lo_peer, k)) for k in pairs]
    mats = mats + [(hi_rest[k], lo_rest[k]) for k in rest]
    peers = [x_peer[k // 2, (k % 2) * 128 : (k % 2) * 128 + COLS] for k in pairs]
    x1 = [beside(b_own[k] * rdiag[k][:, :TILE], peers[k]) for k in pairs]
    x1 = x1 + [b * rd for b, rd in zip(b_own[CHUNK:], rdiag[CHUNK:])]
    spread = [one_hot(row) for row in rows]
    ups = [lift(e_both[k // 2], pair_spread(spread[k], one_hot(m_peer[k]))) for k in pairs]
    ups = ups + [lift(e_mine, sp) for sp in spread[CHUNK:]]
    x = [start + up for start, up in zip(x1, ups)]
    image = [apply_off(xx, *m) for xx, m in zip(x, mats)]
    z = [(1.0 - OMEGA) * xx + start - im * rd for xx, start, im, rd in zip(x, x1, image, rdiag)]
    w = [apply_block(zz, d, *m) for zz, d, m in zip(z, diag, mats)]
    x1 = [ww * rd for ww, rd in zip(w, rdiag)]
    left = [(m[0][:, :TILE], m[1][:, :TILE]) for m in mats]
    y = [(1.0 - OMEGA) * ww[:, :TILE] - apply_off(xx, *m) for ww, xx, m in zip(w, x1, left)]
    for i in range(0, 2 * CHUNK, 2):
        rr = rr + mm_exact(beside(y[i], y[i + 1]), beside(spread[i], spread[i + 1]), nt=True)
    for i in range(2 * CHUNK):
        zz, ww = z[i][:, :TILE], w[i][:, :TILE]
        bz = bz + b_own[i] * zz
        zw = zw + zz * ww
        z_out[i // CHUNK, i % CHUNK] = zz
        w_out[i // CHUNK, i % CHUNK] = ww
    for k in pairs:
        ws_out[k] = w[k][:, TILE:]
    acc_rr[...] = rr
    acc_bz[...] = bz
    acc_zw[...] = zw


def specs(smem, vmem):
    return [pl.BlockSpec(memory_space=pltpu.SMEM)] * smem + [pl.BlockSpec(memory_space=pltpu.VMEM)] * vmem


def forward_part(scalars, arrays):
    return pl.pallas_call(
        forward_kernel,
        in_specs=specs(len(scalars), len(arrays)),
        out_specs=specs(0, 4),
        out_shape=[
            near((2, SLOTS, COLS, TILE)),
            near((2, SLOTS, COLS, TILE)),
            near((SLOTS, COLS, TILE)),
            jax.ShapeDtypeStruct((PEERS, ROWS, TILE), F32),
        ],
        scratch_shapes=[
            pltpu.VMEM((PEERS, COLS, AGG), F32),
            pltpu.VMEM((COLS, AGG), F32),
            pltpu.VMEM((COLS, TILE), F32),
            pltpu.VMEM((COLS, TILE), F32),
        ],
        compiler_params=params(10),
        name="forward_part",
    )(*scalars, *arrays)


def second_kernel(
    perm, member, arrived, inverse_rows, g, x, inverse, op_hi, op_lo, b_slot, b_rest, d_slot, d_rest, d_peer, m_peer,
    hi_top, lo_top, hi_side, lo_side, hi_peer, lo_peer, hi_rest, lo_rest, maps, z_in, w_in, w_peer, v_out, u_out, out, dots, e, acc_a, acc_b, acc_c, acc_alpha
):
    extra = arrived[0, 32:40]
    for q in range(1, GROUPS):
        extra = extra + arrived[q, 32:40]
    dots[...] = extra
    level_one(arrived, inverse_rows, g, x, inverse, op_hi, op_lo, e)
    acc_a[...] = jnp.zeros_like(acc_a)
    acc_b[...] = jnp.zeros_like(acc_b)
    acc_c[...] = jnp.zeros_like(acc_c)
    col = column(dots[0:1])
    acc_alpha[...] = col[:COLS] / col[COLS:]
    e_own = e.at[pl.ds(member[0], 1)]
    views = (e, b_slot, b_rest, d_slot, d_rest, d_peer, m_peer, hi_top, lo_top, hi_side, lo_side, hi_peer, lo_peer, hi_rest, lo_rest, w_peer)

    @pl.loop(0, CHUNKS)
    def _(step):
        e_peer, *parts = [v.at[part(step, v.shape[0])] for v in views]
        z_part, w_part, v_part, u_part = [v.at[:, part(step, SLOTS)] for v in (z_in, w_in, v_out, u_out)]
        second_step(
            step, perm, e_own, e_peer, *parts[:-1], maps, z_part, w_part, parts[-1], v_part, u_part,
            acc_a, acc_b, acc_c, acc_alpha
        )

    first = jnp.sum(jnp.concatenate([acc_a[...], acc_b[...]], axis=0).T, axis=0, keepdims=True)
    last = jnp.sum(jnp.concatenate([acc_c[...], acc_c[...]], axis=0).T, axis=0, keepdims=True)
    out[...] = jnp.broadcast_to(jnp.concatenate([first, last], axis=0), out.shape)


def second_step(
    step, perm, e_own, e_peer, b_slot, b_rest, d_slot, d_rest, d_peer, m_peer,
    hi_top, lo_top, hi_side, lo_side, hi_peer, lo_peer, hi_rest, lo_rest, maps, z_in, w_in, w_peer, v_out, u_out, acc_a, acc_b, acc_c, acc_alpha
):
    alpha = acc_alpha[...]
    e_mine = two_parts(e_own[0])
    e_both = [two_parts(beside(e_own[0], e_peer[q])) for q in range(CHUNK // 2)]
    sums = [acc_a[...], acc_b[...], acc_c[...]]

    def gather(b, z, w, v, u):
        r1 = b - alpha * w
        z1 = z - alpha * v
        az1 = w - alpha * u
        sums[0] = sums[0] + r1 * z1
        sums[1] = sums[1] + z1 * az1
        sums[2] = sums[2] + (z1 * w + z * az1)

    pairs, rest = range(CHUNK), range(CHUNK)
    rows = [maps[pl.ds(perm[at + step * CHUNK + k], 1)] for at in (0, SLOTS) for k in pairs]
    diag = [jnp.concatenate([d_slot[k], d_peer[k]], axis=1) for k in pairs] + [d_rest[k] for k in rest]
    rdiag = [OMEGA / d for d in diag]
    mats = [(block(hi_top, hi_side, hi_peer, k), block(lo_top, lo_side, lo_peer, k)) for k in pairs]
    mats = mats + [(hi_rest[k], lo_rest[k]) for k in rest]
    w = [jnp.concatenate([w_in[0, k], w_peer[k]], axis=1) for k in pairs] + [w_in[1, k] for k in rest]
    spread = [one_hot(row) for row in rows]
    ups = [lift(e_both[k // 2], pair_spread(spread[k], one_hot(m_peer[k]))) for k in pairs]
    ups = ups + [lift(e_mine, sp) for sp in spread[CHUNK:]]
    x1 = [ww * rd for ww, rd in zip(w, rdiag)]
    x = [start + up for start, up in zip(x1, ups)]
    image = [apply_off(xx, *m) for xx, m in zip(x, mats)]
    v = [(1.0 - OMEGA) * xx + start - im * rd for xx, start, im, rd in zip(x, x1, image, rdiag)]
    left = [(m[0][:, :TILE], m[1][:, :TILE]) for m in mats]
    u = [apply_block(vv, d[:, :TILE], *m) for vv, d, m in zip(v, diag, left)]
    for i in range(2 * CHUNK):
        vv, b_ref = v[i][:, :TILE], (b_slot if i < CHUNK else b_rest)
        v_out[i // CHUNK, i % CHUNK] = vv
        u_out[i // CHUNK, i % CHUNK] = u[i]
        gather(b_ref[i % CHUNK], z_in[i // CHUNK, i % CHUNK], w[i][:, :TILE], vv, u[i])
    acc_a[...] = sums[0]
    acc_b[...] = sums[1]
    acc_c[...] = sums[2]


def second_part(scalars, arrays):
    return pl.pallas_call(
        second_kernel,
        in_specs=specs(len(scalars), len(arrays)),
        out_specs=specs(0, 4),
        out_shape=[
            near((2, SLOTS, COLS, TILE)),
            near((2, SLOTS, COLS, TILE)),
            jax.ShapeDtypeStruct((GROUPS * PEERS, 2, TILE), F32),
            jax.ShapeDtypeStruct((8, TILE), F32),
        ],
        scratch_shapes=[pltpu.VMEM((PEERS, COLS, AGG), F32)] + [pltpu.VMEM((COLS, TILE), F32)] * 4,
        compiler_params=params(10),
        name="second_part",
    )(*scalars, *arrays)


def combine_kernel(where, dots, arrived, b, z, w, v, u, solution, residual, sol_buf, res_buf, sem):
    total = jnp.sum(arrived[...], axis=0)
    old = column(dots[0:1])
    one = column(total[0:1])
    two = column(total[1:2])
    rho, zw = old[:COLS], old[COLS:]
    rho_next, zz = one[:COLS], one[COLS:]
    alpha = rho / zw
    beta = rho_next / rho
    alpha_next = rho_next / (zz + beta * two[:COLS] + beta * beta * zw)
    first = alpha + alpha_next * (1.0 + beta)
    second = alpha_next * alpha

    def copies(i):
        at = pl.ds(i * (STEP * TILE), STEP * TILE)
        return (
            pltpu.make_async_copy(sol_buf.at[:, at], solution.at[:, at], sem.at[0, i]),
            pltpu.make_async_copy(res_buf.at[:, at], residual.at[:, at], sem.at[1, i]),
        )

    for i in range(BLK // STEP):
        for t in range(i * STEP, (i + 1) * STEP):
            half, k = where[t] // SLOTS, lax.rem(where[t], SLOTS)
            at = slice(t * TILE, (t + 1) * TILE)
            sol_buf[:, at] = first * z[half, k] - second * v[half, k]
            res_buf[:, at] = b[:, at] - first * w[half, k] + second * u[half, k]
        for copy in copies(i):
            copy.start()
    for i in range(BLK // STEP):
        for copy in copies(i):
            copy.wait()


def combine(where, dots, arrived, b, z, w, v, u):
    return pl.pallas_call(
        combine_kernel,
        in_specs=specs(1, 7),
        out_specs=[pl.BlockSpec(memory_space=pl.ANY)] * 2,
        out_shape=[far((COLS, BLK * TILE))] * 2,
        scratch_shapes=[
            pltpu.VMEM((COLS, BLK * TILE), F32),
            pltpu.VMEM((COLS, BLK * TILE), F32),
            pltpu.SemaphoreType.DMA((2, BLK // STEP)),
        ],
        compiler_params=params(8),
        name="combine",
    )(where, dots, arrived, b, z, w, v, u)


def exchange(x, axes):
    return lax.all_to_all(x, axes, 0, 0, tiled=True)


def on_device(
    right_side,
    diag_tiles,
    remote_tiles,
    slot_counts,
    slot_blocks,
    fine_map,
    coarse_map,
    level1_ops,
    coarsest_inverse,
):
    group = lax.axis_index("grp")
    member = lax.axis_index(GROUP_AXES).astype(jnp.int32).reshape(1)
    slot_list = slot_blocks.reshape(SLOTS)
    counts = slot_counts.reshape(PEERS)
    maps = fine_map.reshape(BLK, TILE)
    remote = remote_tiles.reshape(SLOTS, TILE, TILE)
    operator = level1_ops[0]

    outgoing = boundary_pack(slot_blocks, diag_tiles, right_side, maps)
    side = exchange(outgoing, GROUP_AXES)

    tile_ids = jnp.arange(BLK, dtype=jnp.int32)
    free = jnp.logical_not(jnp.any(slot_list[:, None] == tile_ids[None, :], axis=0)).astype(jnp.int32)
    rank = jnp.sum(jnp.where(tile_ids[None, :] < tile_ids[:, None], free[None, :], 0), axis=1)
    chosen = (rank[None, :] == jnp.arange(SLOTS, dtype=jnp.int32)[:, None]) & (free[None, :] == 1)
    rest_list = jnp.sum(jnp.where(chosen, tile_ids[None, :], 0), axis=1)
    perm = jnp.concatenate([slot_list, rest_list])
    where = jnp.sum(jnp.where(perm[None, :] == tile_ids[:, None], tile_ids[None, :], 0), axis=1)

    b_slot, b_rest, d_slot, d_rest, hi_rest, lo_rest, hi_top, lo_top, hi_side, lo_side, rs, rr_local = local_part(
        perm, counts, diag_tiles, right_side, remote, maps
    )
    g, inverse, op_hi, op_lo = coarse_setup(operator, coarse_map.reshape(1, NC1))
    inverse_rows = lax.dynamic_slice_in_dim(coarsest_inverse, group * AGG, AGG, 0)

    rr_local, g, inverse_rows, member, where = lax.optimization_barrier(
        (rr_local, g, inverse_rows, member, where)
    )
    gathered = exchange(first_restrict(side, rs, rr_local), GROUP_AXES)
    hi_peer, lo_peer, d_peer, m_peer = pair_setup(side)
    gathered, hi_peer = lax.optimization_barrier((gathered, hi_peer))

    scalars = (perm, member)
    x, outgoing = lowest_part(gathered, g)
    coarse = (exchange(outgoing, "grp"), inverse_rows, g, x, inverse)
    fixed = (d_slot, d_rest, d_peer, m_peer, hi_top, lo_top, hi_side, lo_side, hi_peer, lo_peer, hi_rest, lo_rest, maps)
    z, w, w_peer, outgoing = forward_part(
        scalars, coarse + (op_hi, op_lo, b_slot, b_rest, d_slot, d_rest, side) + fixed[2:]
    )
    x, outgoing = lowest_part(exchange(outgoing, GROUP_AXES), g)
    coarse = (exchange(outgoing, "grp"), inverse_rows, g, x, inverse)
    v, u, outgoing, dots = second_part(scalars, coarse + (op_hi, op_lo, b_slot, b_rest) + fixed + (z, w, w_peer))
    sums = exchange(outgoing, ALL_AXES)
    return tuple(combine(where, dots, sums, right_side, z, w, v, u))


def solution(mesh):
    placed = (
        P(None, ("grp", "sub", "chip")),
        P(("grp", "sub", "chip"), None, None),
        P(("grp", "sub", "chip"), None, None, None),
        P(("grp", "sub", "chip"), None),
        P(("grp", "sub", "chip"), None, None),
        P(("grp", "sub", "chip")),
        P("grp"),
        P("grp", None, None),
        P(),
    )
    return jax.shard_map(
        on_device,
        mesh=mesh,
        in_specs=placed,
        out_specs=(P(None, ("grp", "sub", "chip")), P(None, ("grp", "sub", "chip"))),
        check_vma=False,
    )
```

```python
import functools

import jax
import jax.numpy as jnp
from jax import lax
from jax.experimental import pallas as pl
from jax.experimental.pallas import tpu as pltpu
from jax.sharding import PartitionSpec as P

OMEGA = 0.6
F32 = jnp.float32
BF16 = jnp.bfloat16
COLS = 64
TILE = 128
BLK = 64
SLOTS = 32
PEERS = 16
GROUPS = 8
AGG = 64
NC1 = 1024
STEP = 8
NSTEP = SLOTS // STEP
CHUNK = 16
CHUNKS = SLOTS // CHUNK
SIDE = 264
PEER_STEP = 4
ROWS = 40

GROUP_AXES = ("sub", "chip")
ALL_AXES = ("grp", "sub", "chip")


def params(mib=20):
    return pltpu.CompilerParams(vmem_limit_bytes=mib * 1024 * 1024)


def hbm(x):
    return pltpu.with_memory_space_constraint(x, pltpu.HBM)


def near(shape, dtype=F32):
    return pltpu.VMEM(shape, dtype)


def far(shape, dtype=F32):
    return pltpu.HBM(shape, dtype)


def cost(flops, moved):
    return pl.CostEstimate(flops=flops, bytes_accessed=moved, transcendentals=0)


def split2(x):
    hi = x.astype(BF16)
    lo = (x - hi.astype(F32)).astype(BF16)
    return hi, lo


def dot(a, b):
    return jnp.dot(a, b, preferred_element_type=F32)


def dot_nt(a, b):
    return lax.dot_general(a, b, (((1,), (1,)), ((), ())), preferred_element_type=F32)


def mm(x, whi, wlo, nt=False):
    op = dot_nt if nt else dot
    rows = x.shape[0]
    hi, lo = split2(x)
    both = op(jnp.concatenate([hi, lo], axis=0), whi)
    return both[:rows] + both[rows:] + op(hi, wlo)


def mm_exact(x, w, nt=False):
    op = dot_nt if nt else dot
    rows = x.shape[0]
    two = op(jnp.concatenate(split2(x), axis=0), w)
    return two[:rows] + two[rows:]


def beside(a, b):
    return jnp.concatenate([a, b], axis=1)


def eye_mask():
    r = lax.broadcasted_iota(jnp.int32, (TILE, TILE), 0)
    c = lax.broadcasted_iota(jnp.int32, (TILE, TILE), 1)
    return r, c


def tile_diag(tile):
    r, c = eye_mask()
    return jnp.sum(jnp.where(r == c, tile, 0.0), axis=0, keepdims=True)


def off_diag(tile):
    r, c = eye_mask()
    return jnp.where(r == c, 0.0, tile)


def one_hot(row):
    r = lax.broadcasted_iota(jnp.int32, (AGG, row.shape[1]), 0)
    return jnp.where(r == row, 1.0, 0.0).astype(BF16)


def pack_rows(x):
    wide = jnp.concatenate([x[:32], x[32:]], axis=1)
    return wide


def column(row):
    return jnp.broadcast_to(row, (TILE, TILE)).T


def boundary_kernel(slots, maps, tiles, cols, out, map_buf, tile_buf, col_buf, out_buf, map_sem, col_sem, tile_sem, out_sem):
    def tile_copy(j):
        return pltpu.make_async_copy(tiles.at[slots[0, j % 2, j // 2]], tile_buf.at[j], tile_sem.at[j])

    def col_copy(j):
        at = pl.ds(pl.multiple_of(slots[0, j % 2, j // 2] * TILE, TILE), TILE)
        return pltpu.make_async_copy(cols.at[:, at], col_buf.at[j], col_sem.at[j])

    def out_copy(j):
        at = pl.ds(j // 2, PEER_STEP)
        return pltpu.make_async_copy(out_buf.at[at], out.at[at], out_sem.at[j // STEP])

    map_copy = pltpu.make_async_copy(maps, map_buf, map_sem)
    map_copy.start()
    for j in range(SLOTS):
        tile_copy(j).start()
        col_copy(j).start()
    r = lax.broadcasted_iota(jnp.int32, (64, TILE), 0)
    c = lax.broadcasted_iota(jnp.int32, (64, TILE), 1)
    r8 = lax.broadcasted_iota(jnp.int32, (8, TILE), 0)
    map_copy.wait()
    for j in range(0, SLOTS, STEP):
        for k in range(j, j + STEP):
            tile_copy(k).wait()
            col_copy(k).wait()
        tile = [tile_buf[k] for k in range(j, j + STEP)]
        diag = [tile_diag(t) for t in tile]
        for k in range(j, j + STEP):
            t, d = tile[k - j], diag[k - j]
            q, base = k // 2, (k % 2) * 128
            out_buf[q, base : base + 64] = col_buf[k] * (OMEGA / d)
            below = pltpu.roll(t[64:], 64, 1)
            out_buf[q, base + 64 : base + 128] = jnp.where((c < 64) & (r > c), below, t[:64])
        for k in range(j, j + STEP, 2):
            own = [map_buf[pl.ds(slots[0, i, k // 2], 1)].astype(F32) for i in range(2)]
            d0, d1 = diag[k - j], diag[k - j + 1]
            out_buf[k // 2, 256:264] = jnp.where(
                r8 == 0, d0, jnp.where(r8 == 1, own[0], jnp.where(r8 == 2, d1, jnp.where(r8 == 3, own[1], 0.0)))
            )
        out_copy(j).start()
    for j in range(0, SLOTS, STEP):
        out_copy(j).wait()


def boundary_pack(slot_blocks, diag_tiles, right_side, maps):
    return pl.pallas_call(
        boundary_kernel,
        in_specs=[pl.BlockSpec(memory_space=pltpu.SMEM)] + [pl.BlockSpec(memory_space=pl.ANY)] * 3,
        out_specs=pl.BlockSpec(memory_space=pl.ANY),
        out_shape=far((PEERS, SIDE, TILE)),
        scratch_shapes=[
            pltpu.VMEM((BLK, TILE), jnp.int32),
            pltpu.VMEM((SLOTS, TILE, TILE), F32),
            pltpu.VMEM((SLOTS, COLS, TILE), F32),
            pltpu.VMEM((PEERS, SIDE, TILE), F32),
            pltpu.SemaphoreType.DMA,
            pltpu.SemaphoreType.DMA((SLOTS,)),
            pltpu.SemaphoreType.DMA((SLOTS,)),
            pltpu.SemaphoreType.DMA((NSTEP,)),
        ],
        compiler_params=params(),
        name="boundary_pack",
    )(slot_blocks.transpose(0, 2, 1), hbm(maps), hbm(diag_tiles), hbm(right_side))


def local_kernel(perm, counts, *refs):
    n = 2 * STEP
    tiles, cols = refs[:n], refs[n : 2 * n]
    remote, maps = refs[2 * n : 2 * n + 2]
    b_slot, b_rest, d_slot, d_rest, hi_rest, lo_rest, hi_top, lo_top, hi_side, lo_side, rs, rr = refs[2 * n + 2 :]
    step = pl.program_id(0)

    @pl.when(step == 0)
    def _():
        rr[...] = jnp.zeros_like(rr)

    index = [perm[(0 if i < STEP else SLOTS) + step * STEP + i % STEP] for i in range(n)]
    tile = [tiles[i][0] for i in range(n)]
    diag = [tile_diag(t) for t in tile]
    off = [split2(off_diag(t)) for t in tile]
    b = [cols[i][...] for i in range(n)]
    x = [OMEGA * bb / d for bb, d in zip(b, diag)]
    y = [bb - OMEGA * bb - mm(xx, *o) for bb, xx, o in zip(b, x, off)]
    spread = [one_hot(maps[pl.ds(i, 1)]) for i in index]
    total = rr[...]
    for i in range(0, n, 2):
        total = total + mm_exact(beside(y[i], y[i + 1]), beside(spread[i], spread[i + 1]), nt=True)
    for k in range(STEP):
        b_slot[k] = b[k]
        d_slot[k] = diag[k]
        b_rest[k] = b[STEP + k]
        d_rest[k] = diag[STEP + k]
        hi_rest[k], lo_rest[k] = off[STEP + k]
    coupling, turned, restricted = [], [], []
    for k in range(STEP):
        j = step * STEP + k
        live = (j % 2) < counts[j // 2]
        scaled = remote[k] * jnp.where(live, -1.0, 0.0)
        coupling.append(split2(scaled))
        turned.append(split2(scaled.T))
    for k in range(STEP):
        restricted.append(-(dot_nt(coupling[k][0], spread[k]) + dot_nt(coupling[k][1], spread[k])))
        hi_top[k] = beside(off[k][0], turned[k][0])
        lo_top[k] = beside(off[k][1], turned[k][1])
        hi_side[k], lo_side[k] = coupling[k]
    for q in range(PEER_STEP):
        rs[q, 0], rs[q, 1] = split2(beside(restricted[2 * q], restricted[2 * q + 1]))
    rr[...] = total


def local_part(perm, counts, diag_tiles, right_side, remote, maps):
    def where(i):
        return (0 if i < STEP else SLOTS) + i % STEP

    def tile_spec(i):
        return pl.BlockSpec((1, TILE, TILE), lambda s, p, c: (p[s * STEP + where(i)], 0, 0))

    def col_spec(i):
        return pl.BlockSpec((COLS, TILE), lambda s, p, c: (0, p[s * STEP + where(i)]))

    def out(*shape):
        return pl.BlockSpec((STEP,) + shape, lambda s, p, c: (s, 0, 0))

    n = 2 * STEP
    grid = pltpu.PrefetchScalarGridSpec(
        num_scalar_prefetch=2,
        grid=(NSTEP,),
        in_specs=[tile_spec(i) for i in range(n)]
        + [col_spec(i) for i in range(n)]
        + [
            pl.BlockSpec((STEP, TILE, TILE), lambda s, p, c: (s, 0, 0)),
            pl.BlockSpec((BLK, TILE), lambda s, p, c: (0, 0)),
        ],
        out_specs=[
            out(COLS, TILE),
            out(COLS, TILE),
            out(1, TILE),
            out(1, TILE),
            out(TILE, TILE),
            out(TILE, TILE),
            out(TILE, 2 * TILE),
            out(TILE, 2 * TILE),
            out(TILE, TILE),
            out(TILE, TILE),
            pl.BlockSpec((PEER_STEP, 2, TILE, TILE), lambda s, p, c: (s, 0, 0, 0)),
            pl.BlockSpec((COLS, AGG), lambda s, p, c: (0, 0)),
        ],
    )

    def sds(shape, dtype=F32):
        return far((SLOTS,) + shape, dtype)

    return pl.pallas_call(
        local_kernel,
        grid_spec=grid,
        out_shape=[
            sds((COLS, TILE)),
            sds((COLS, TILE)),
            sds((1, TILE)),
            sds((1, TILE)),
            sds((TILE, TILE), BF16),
            sds((TILE, TILE), BF16),
            sds((TILE, 2 * TILE), BF16),
            sds((TILE, 2 * TILE), BF16),
            sds((TILE, TILE), BF16),
            sds((TILE, TILE), BF16),
            far((PEERS, 2, TILE, TILE), BF16),
            jax.ShapeDtypeStruct((COLS, AGG), F32),
        ],
        compiler_params=params(),
        cost_estimate=cost(2 * 64 * 3 * 64 * 128 * 128, 16 << 20),
        name="local_part",
    )(perm, counts, *([hbm(diag_tiles)] * n), *([hbm(right_side)] * n), hbm(remote), maps)


def coarse_kernel(op, cmap, g_out, d_out, hi_out, lo_out):
    spread = one_hot(cmap[...])
    product = None
    for i in range(NC1 // 256):
        rows = slice(i * 256, (i + 1) * 256)
        hi, lo = split2(op[rows, :])
        hi_out[rows, :] = hi
        lo_out[rows, :] = lo
        term = dot(spread[:, rows], hi) + dot(spread[:, rows], lo)
        product = term if product is None else product + term
    pieces = []
    for i in range(NC1 // TILE):
        pieces.append(tile_diag(op[i * TILE : (i + 1) * TILE, i * TILE : (i + 1) * TILE]))
    diag = jnp.concatenate(pieces, axis=1)
    inverse = 1.0 / diag
    d_out[...] = inverse
    g_out[...] = spread.astype(F32) - OMEGA * product * inverse


def coarse_setup(op, cmap):
    return pl.pallas_call(
        coarse_kernel,
        out_shape=[
            jax.ShapeDtypeStruct((AGG, NC1), F32),
            jax.ShapeDtypeStruct((1, NC1), F32),
            far((NC1, NC1), BF16),
            far((NC1, NC1), BF16),
        ],
        compiler_params=params(),
        cost_estimate=cost(2 * 2 * 64 * 1024 * 1024, 5 << 20),
        name="coarse_setup",
    )(op, cmap)


def first_restrict_kernel(arrived, rs, rr, out, hi_out, lo_out, diag_out, map_out, rs_buf, rs_sem):
    def copy(j):
        at = pl.ds(j * PEER_STEP, PEER_STEP)
        return pltpu.make_async_copy(rs.at[at], rs_buf.at[at], rs_sem.at[j])

    for j in range(NSTEP):
        copy(j).start()
    r = lax.broadcasted_iota(jnp.int32, (64, TILE), 0)
    c = lax.broadcasted_iota(jnp.int32, (64, TILE), 1)
    for k in range(SLOTS):
        q, base, at = k // 2, 128 * (k % 2) + 64, 256 + 2 * (k % 2)
        packed = arrived[q, base : base + 64]
        top = jnp.where((c >= 64) | (r < c), packed, 0.0)
        bottom = pltpu.roll(jnp.where((c < 64) & (r > c), packed, 0.0), 64, 1)
        half = jnp.concatenate([top, bottom], axis=0)
        hi_out[k], lo_out[k] = split2(half + half.T)
        diag_out[k] = arrived[q, at : at + 1]
        map_out[k] = arrived[q, at + 1 : at + 2].astype(jnp.int32)
    main, rest = [], []
    for j in range(NSTEP):
        copy(j).wait()
        for q in range(j * PEER_STEP, (j + 1) * PEER_STEP):
            hi0, lo0 = split2(arrived[q, 0:COLS])
            hi1, lo1 = split2(arrived[q, 128 : 128 + COLS])
            main.append(dot(jnp.concatenate([hi0, lo0, hi1, lo1], axis=0), rs_buf[q, 0]))
            rest.append(dot(jnp.concatenate([hi0, hi1], axis=0), rs_buf[q, 1]))
    main, rest = sum(main), sum(rest)
    first = main[:COLS] + main[COLS : 2 * COLS] + rest[:COLS]
    second = main[2 * COLS : 3 * COLS] + main[3 * COLS :] + rest[COLS:]
    total = rr[...] + first[:, :AGG] + second[:, AGG:]
    out[...] = jnp.broadcast_to(pack_rows(total), out.shape)


def first_restrict(arrived, rs, rr):
    return pl.pallas_call(
        first_restrict_kernel,
        in_specs=[
            pl.BlockSpec(memory_space=pltpu.VMEM),
            pl.BlockSpec(memory_space=pl.ANY),
            pl.BlockSpec(memory_space=pltpu.VMEM),
        ],
        out_specs=[pl.BlockSpec(memory_space=pltpu.VMEM)] * 5,
        out_shape=[
            jax.ShapeDtypeStruct((PEERS, 32, TILE), F32),
            near((SLOTS, TILE, TILE), BF16),
            near((SLOTS, TILE, TILE), BF16),
            near((SLOTS, 1, TILE)),
            near((SLOTS, 1, TILE), jnp.int32),
        ],
        scratch_shapes=[
            pltpu.VMEM((PEERS, 2, TILE, TILE), BF16),
            pltpu.SemaphoreType.DMA((NSTEP,)),
        ],
        compiler_params=params(8),
        name="first_restrict",
    )(pltpu.with_memory_space_constraint(arrived, pltpu.VMEM), hbm(rs), rr)


def gathered_rows(ref, count):
    lane = lax.broadcasted_iota(jnp.int32, (32, TILE), 1) < 64
    tops, bottoms = [], []
    for q in range(0, count, 2):
        a, b = ref[q, 0:32], ref[q + 1, 0:32]
        tops.append(jnp.where(lane, a, pltpu.roll(b, 64, 1)))
        bottoms.append(jnp.where(lane, pltpu.roll(a, 64, 1), b))
    return jnp.concatenate([jnp.concatenate(tops, axis=1), jnp.concatenate(bottoms, axis=1)], axis=0)


def lowest_kernel(arrived, g, x_out, out):
    x = gathered_rows(arrived, PEERS)
    x_out[...] = x
    hi, lo = split2(g[...])
    packed = pack_rows(mm(x, hi, lo, nt=True))
    if arrived.shape[1] == ROWS:
        extra = arrived[0, 32:40]
        for q in range(1, PEERS):
            extra = extra + arrived[q, 32:40]
        packed = jnp.concatenate([packed, extra], axis=0)
    out[...] = jnp.broadcast_to(packed, out.shape)


def lowest_part(arrived, g):
    return pl.pallas_call(
        lowest_kernel,
        out_shape=[
            jax.ShapeDtypeStruct((COLS, NC1), F32),
            jax.ShapeDtypeStruct((GROUPS, arrived.shape[1], TILE), F32),
        ],
        compiler_params=params(6),
        cost_estimate=cost(20_000_000_000, 32 << 20),
        name="lowest_part",
    )(arrived, g)


def level_one(arrived, inverse_rows, g, x_ref, inverse_ref, op_hi, op_lo, e_out):
    low = gathered_rows(arrived, GROUPS)
    hi, lo = split2(inverse_rows[...])
    corr = mm(low, hi, lo, nt=True)
    ghi, glo = split2(g[...])
    lifted = mm(corr, ghi, glo)
    inverse = inverse_ref[...]
    scaled = x_ref[...] * inverse
    total = None
    for i in range(NC1 // 256):
        rows = slice(i * 256, (i + 1) * 256)
        term = mm(scaled[:, rows], op_hi[rows, :], op_lo[rows, :])
        total = term if total is None else total + term
    e = 2.0 * OMEGA * scaled - OMEGA * OMEGA * total * inverse + lifted
    for q in range(PEERS):
        e_out[q] = e[:, q * AGG : (q + 1) * AGG]


def apply_off(x, hi, lo):
    xh, xl = split2(x)
    rows = x.shape[0]
    if x.shape[1] == TILE:
        return dot(beside(xh, xl), jnp.concatenate([hi, hi], axis=0)) + dot(xh, lo)
    both = dot(jnp.concatenate([xh, xl], axis=0), hi)
    return both[:rows] + both[rows:] + dot(xh, lo)


def apply_block(x, diag, hi, lo):
    xh, xl = split2(x)
    kept = xh.astype(F32) + xl.astype(F32)
    return apply_off(x, hi, lo) + kept[:, : diag.shape[1]] * diag


def lift(parts, spread):
    rows = parts.shape[0] // 2
    two = dot(parts, spread)
    return two[:rows] + two[rows:]


def two_parts(e):
    return jnp.concatenate(split2(e), axis=0)


def block(top, side, peer, k):
    return jnp.concatenate([top[k], beside(side[k], peer[k])], axis=0)


def pair_spread(own, peer):
    none = jnp.zeros_like(own)
    return jnp.concatenate([beside(own, none), beside(none, peer)], axis=0)


def forward_kernel(
    perm, member, arrived, inverse_rows, g, x, inverse, op_hi, op_lo, b_slot, b_rest, d_slot, d_rest, x_peer, d_peer, m_peer,
    hi_top, lo_top, hi_side, lo_side, hi_peer, lo_peer, hi_rest, lo_rest, maps, z_out, w_out, ws_out, out, e, acc_rr, acc_bz, acc_zw
):
    level_one(arrived, inverse_rows, g, x, inverse, op_hi, op_lo, e)
    acc_rr[...] = jnp.zeros_like(acc_rr)
    acc_bz[...] = jnp.zeros_like(acc_bz)
    acc_zw[...] = jnp.zeros_like(acc_zw)
    e_own = e.at[pl.ds(member[0], 1)]
    views = (e, b_slot, b_rest, d_slot, d_rest, x_peer, d_peer, m_peer, hi_top, lo_top, hi_side, lo_side, hi_peer, lo_peer, hi_rest, lo_rest, ws_out)

    @pl.loop(0, CHUNKS)
    def _(step):
        e_peer, *parts = [v.at[part(step, v.shape[0])] for v in views]
        both = [v.at[:, part(step, SLOTS)] for v in (z_out, w_out)]
        forward_step(step, perm, e_own, e_peer, *parts[:-1], maps, *both, parts[-1], acc_rr, acc_bz, acc_zw)

    packed = pack_rows(acc_rr[...])
    sums = jnp.sum(jnp.concatenate([acc_bz[...], acc_zw[...]], axis=0).T, axis=0, keepdims=True)
    r8 = lax.broadcasted_iota(jnp.int32, (8, TILE), 0)
    extra = jnp.where(r8 == 0, sums, 0.0)
    for q in range(PEERS):
        out[q, 0:32] = packed
        out[q, 32:40] = extra


def part(step, count):
    size = count // CHUNKS
    return pl.ds(step * size, size)


def forward_step(
    step, perm, e_own, e_peer, b_slot, b_rest, d_slot, d_rest, x_peer, d_peer, m_peer,
    hi_top, lo_top, hi_side, lo_side, hi_peer, lo_peer, hi_rest, lo_rest, maps, z_out, w_out, ws_out, acc_rr, acc_bz, acc_zw
):
    e_mine = two_parts(e_own[0])
    e_both = [two_parts(beside(e_own[0], e_peer[q])) for q in range(CHUNK // 2)]
    rr, bz, zw = acc_rr[...], acc_bz[...], acc_zw[...]
    pairs, rest = range(CHUNK), range(CHUNK)
    rows = [maps[pl.ds(perm[at + step * CHUNK + k], 1)] for at in (0, SLOTS) for k in pairs]
    b_own = [b_slot[k] for k in pairs] + [b_rest[k] for k in rest]
    diag = [jnp.concatenate([d_slot[k], d_peer[k]], axis=1) for k in pairs] + [d_rest[k] for k in rest]
    rdiag = [OMEGA / d for d in diag]
    mats = [(block(hi_top, hi_side, hi_peer, k), block(lo_top, lo_side, lo_peer, k)) for k in pairs]
    mats = mats + [(hi_rest[k], lo_rest[k]) for k in rest]
    peers = [x_peer[k // 2, (k % 2) * 128 : (k % 2) * 128 + COLS] for k in pairs]
    x1 = [beside(b_own[k] * rdiag[k][:, :TILE], peers[k]) for k in pairs]
    x1 = x1 + [b * rd for b, rd in zip(b_own[CHUNK:], rdiag[CHUNK:])]
    spread = [one_hot(row) for row in rows]
    ups = [lift(e_both[k // 2], pair_spread(spread[k], one_hot(m_peer[k]))) for k in pairs]
    ups = ups + [lift(e_mine, sp) for sp in spread[CHUNK:]]
    x = [start + up for start, up in zip(x1, ups)]
    image = [apply_off(xx, *m) for xx, m in zip(x, mats)]
    z = [(1.0 - OMEGA) * xx + start - im * rd for xx, start, im, rd in zip(x, x1, image, rdiag)]
    w = [apply_block(zz, d, *m) for zz, d, m in zip(z, diag, mats)]
    x1 = [ww * rd for ww, rd in zip(w, rdiag)]
    left = [(m[0][:, :TILE], m[1][:, :TILE]) for m in mats]
    y = [(1.0 - OMEGA) * ww[:, :TILE] - apply_off(xx, *m) for ww, xx, m in zip(w, x1, left)]
    for i in range(0, 2 * CHUNK, 2):
        rr = rr + mm_exact(beside(y[i], y[i + 1]), beside(spread[i], spread[i + 1]), nt=True)
    for i in range(2 * CHUNK):
        zz, ww = z[i][:, :TILE], w[i][:, :TILE]
        bz = bz + b_own[i] * zz
        zw = zw + zz * ww
        z_out[i // CHUNK, i % CHUNK] = zz
        w_out[i // CHUNK, i % CHUNK] = ww
    for k in pairs:
        ws_out[k] = w[k][:, TILE:]
    acc_rr[...] = rr
    acc_bz[...] = bz
    acc_zw[...] = zw


def specs(smem, vmem):
    return [pl.BlockSpec(memory_space=pltpu.SMEM)] * smem + [pl.BlockSpec(memory_space=pltpu.VMEM)] * vmem


def forward_part(scalars, arrays):
    return pl.pallas_call(
        forward_kernel,
        in_specs=specs(len(scalars), len(arrays)),
        out_specs=specs(0, 4),
        out_shape=[
            near((2, SLOTS, COLS, TILE)),
            near((2, SLOTS, COLS, TILE)),
            near((SLOTS, COLS, TILE)),
            jax.ShapeDtypeStruct((PEERS, ROWS, TILE), F32),
        ],
        scratch_shapes=[
            pltpu.VMEM((PEERS, COLS, AGG), F32),
            pltpu.VMEM((COLS, AGG), F32),
            pltpu.VMEM((COLS, TILE), F32),
            pltpu.VMEM((COLS, TILE), F32),
        ],
        compiler_params=params(10),
        name="forward_part",
    )(*scalars, *arrays)


def second_kernel(
    perm, member, arrived, inverse_rows, g, x, inverse, op_hi, op_lo, b_slot, b_rest, d_slot, d_rest, d_peer, m_peer,
    hi_top, lo_top, hi_side, lo_side, hi_peer, lo_peer, hi_rest, lo_rest, maps, z_in, w_in, w_peer, v_out, u_out, out, dots, e, acc_a, acc_b, acc_c, acc_alpha
):
    extra = arrived[0, 32:40]
    for q in range(1, GROUPS):
        extra = extra + arrived[q, 32:40]
    dots[...] = extra
    level_one(arrived, inverse_rows, g, x, inverse, op_hi, op_lo, e)
    acc_a[...] = jnp.zeros_like(acc_a)
    acc_b[...] = jnp.zeros_like(acc_b)
    acc_c[...] = jnp.zeros_like(acc_c)
    col = column(dots[0:1])
    acc_alpha[...] = col[:COLS] / col[COLS:]
    e_own = e.at[pl.ds(member[0], 1)]
    views = (e, b_slot, b_rest, d_slot, d_rest, d_peer, m_peer, hi_top, lo_top, hi_side, lo_side, hi_peer, lo_peer, hi_rest, lo_rest, w_peer)

    @pl.loop(0, CHUNKS)
    def _(step):
        e_peer, *parts = [v.at[part(step, v.shape[0])] for v in views]
        z_part, w_part, v_part, u_part = [v.at[:, part(step, SLOTS)] for v in (z_in, w_in, v_out, u_out)]
        second_step(
            step, perm, e_own, e_peer, *parts[:-1], maps, z_part, w_part, parts[-1], v_part, u_part,
            acc_a, acc_b, acc_c, acc_alpha
        )

    first = jnp.sum(jnp.concatenate([acc_a[...], acc_b[...]], axis=0).T, axis=0, keepdims=True)
    last = jnp.sum(jnp.concatenate([acc_c[...], acc_c[...]], axis=0).T, axis=0, keepdims=True)
    out[...] = jnp.broadcast_to(jnp.concatenate([first, last], axis=0), out.shape)


def second_step(
    step, perm, e_own, e_peer, b_slot, b_rest, d_slot, d_rest, d_peer, m_peer,
    hi_top, lo_top, hi_side, lo_side, hi_peer, lo_peer, hi_rest, lo_rest, maps, z_in, w_in, w_peer, v_out, u_out, acc_a, acc_b, acc_c, acc_alpha
):
    alpha = acc_alpha[...]
    e_mine = two_parts(e_own[0])
    e_both = [two_parts(beside(e_own[0], e_peer[q])) for q in range(CHUNK // 2)]
    sums = [acc_a[...], acc_b[...], acc_c[...]]

    def gather(b, z, w, v, u):
        r1 = b - alpha * w
        z1 = z - alpha * v
        az1 = w - alpha * u
        sums[0] = sums[0] + r1 * z1
        sums[1] = sums[1] + z1 * az1
        sums[2] = sums[2] + (z1 * w + z * az1)

    pairs, rest = range(CHUNK), range(CHUNK)
    rows = [maps[pl.ds(perm[at + step * CHUNK + k], 1)] for at in (0, SLOTS) for k in pairs]
    diag = [jnp.concatenate([d_slot[k], d_peer[k]], axis=1) for k in pairs] + [d_rest[k] for k in rest]
    rdiag = [OMEGA / d for d in diag]
    mats = [(block(hi_top, hi_side, hi_peer, k), block(lo_top, lo_side, lo_peer, k)) for k in pairs]
    mats = mats + [(hi_rest[k], lo_rest[k]) for k in rest]
    w = [jnp.concatenate([w_in[0, k], w_peer[k]], axis=1) for k in pairs] + [w_in[1, k] for k in rest]
    spread = [one_hot(row) for row in rows]
    ups = [lift(e_both[k // 2], pair_spread(spread[k], one_hot(m_peer[k]))) for k in pairs]
    ups = ups + [lift(e_mine, sp) for sp in spread[CHUNK:]]
    x1 = [ww * rd for ww, rd in zip(w, rdiag)]
    x = [start + up for start, up in zip(x1, ups)]
    image = [apply_off(xx, *m) for xx, m in zip(x, mats)]
    v = [(1.0 - OMEGA) * xx + start - im * rd for xx, start, im, rd in zip(x, x1, image, rdiag)]
    left = [(m[0][:, :TILE], m[1][:, :TILE]) for m in mats]
    u = [apply_block(vv, d[:, :TILE], *m) for vv, d, m in zip(v, diag, left)]
    for i in range(2 * CHUNK):
        vv, b_ref = v[i][:, :TILE], (b_slot if i < CHUNK else b_rest)
        v_out[i // CHUNK, i % CHUNK] = vv
        u_out[i // CHUNK, i % CHUNK] = u[i]
        gather(b_ref[i % CHUNK], z_in[i // CHUNK, i % CHUNK], w[i][:, :TILE], vv, u[i])
    acc_a[...] = sums[0]
    acc_b[...] = sums[1]
    acc_c[...] = sums[2]


def second_part(scalars, arrays):
    return pl.pallas_call(
        second_kernel,
        in_specs=specs(len(scalars), len(arrays)),
        out_specs=specs(0, 4),
        out_shape=[
            near((2, SLOTS, COLS, TILE)),
            near((2, SLOTS, COLS, TILE)),
            jax.ShapeDtypeStruct((GROUPS * PEERS, 2, TILE), F32),
            jax.ShapeDtypeStruct((8, TILE), F32),
        ],
        scratch_shapes=[pltpu.VMEM((PEERS, COLS, AGG), F32)] + [pltpu.VMEM((COLS, TILE), F32)] * 4,
        compiler_params=params(10),
        name="second_part",
    )(*scalars, *arrays)


def combine_kernel(where, dots, arrived, b, z, w, v, u, solution, residual, sol_buf, res_buf, sem):
    total = jnp.sum(arrived[...], axis=0)
    old = column(dots[0:1])
    one = column(total[0:1])
    two = column(total[1:2])
    rho, zw = old[:COLS], old[COLS:]
    rho_next, zz = one[:COLS], one[COLS:]
    alpha = rho / zw
    beta = rho_next / rho
    alpha_next = rho_next / (zz + beta * two[:COLS] + beta * beta * zw)
    first = alpha + alpha_next * (1.0 + beta)
    second = alpha_next * alpha

    def copies(i):
        at = pl.ds(i * (STEP * TILE), STEP * TILE)
        return (
            pltpu.make_async_copy(sol_buf.at[:, at], solution.at[:, at], sem.at[0, i]),
            pltpu.make_async_copy(res_buf.at[:, at], residual.at[:, at], sem.at[1, i]),
        )

    for i in range(BLK // STEP):
        for t in range(i * STEP, (i + 1) * STEP):
            half, k = where[t] // SLOTS, lax.rem(where[t], SLOTS)
            at = slice(t * TILE, (t + 1) * TILE)
            sol_buf[:, at] = first * z[half, k] - second * v[half, k]
            res_buf[:, at] = b[:, at] - first * w[half, k] + second * u[half, k]
        for copy in copies(i):
            copy.start()
    for i in range(BLK // STEP):
        for copy in copies(i):
            copy.wait()


def combine(where, dots, arrived, b, z, w, v, u):
    return pl.pallas_call(
        combine_kernel,
        in_specs=specs(1, 7),
        out_specs=[pl.BlockSpec(memory_space=pl.ANY)] * 2,
        out_shape=[far((COLS, BLK * TILE))] * 2,
        scratch_shapes=[
            pltpu.VMEM((COLS, BLK * TILE), F32),
            pltpu.VMEM((COLS, BLK * TILE), F32),
            pltpu.SemaphoreType.DMA((2, BLK // STEP)),
        ],
        compiler_params=params(8),
        name="combine",
    )(where, dots, arrived, b, z, w, v, u)


def exchange(x, axes):
    return lax.all_to_all(x, axes, 0, 0, tiled=True)


def on_device(
    right_side,
    diag_tiles,
    remote_tiles,
    slot_counts,
    slot_blocks,
    fine_map,
    coarse_map,
    level1_ops,
    coarsest_inverse,
):
    group = lax.axis_index("grp")
    member = lax.axis_index(GROUP_AXES).astype(jnp.int32).reshape(1)
    slot_list = slot_blocks.reshape(SLOTS)
    counts = slot_counts.reshape(PEERS)
    maps = fine_map.reshape(BLK, TILE)
    remote = remote_tiles.reshape(SLOTS, TILE, TILE)
    operator = level1_ops[0]

    outgoing = boundary_pack(slot_blocks, diag_tiles, right_side, maps)
    side = exchange(outgoing, GROUP_AXES)

    tile_ids = jnp.arange(BLK, dtype=jnp.int32)
    free = jnp.logical_not(jnp.any(slot_list[:, None] == tile_ids[None, :], axis=0)).astype(jnp.int32)
    rank = jnp.sum(jnp.where(tile_ids[None, :] < tile_ids[:, None], free[None, :], 0), axis=1)
    chosen = (rank[None, :] == jnp.arange(SLOTS, dtype=jnp.int32)[:, None]) & (free[None, :] == 1)
    rest_list = jnp.sum(jnp.where(chosen, tile_ids[None, :], 0), axis=1)
    perm = jnp.concatenate([slot_list, rest_list])
    where = jnp.sum(jnp.where(perm[None, :] == tile_ids[:, None], tile_ids[None, :], 0), axis=1)

    b_slot, b_rest, d_slot, d_rest, hi_rest, lo_rest, hi_top, lo_top, hi_side, lo_side, rs, rr_local = local_part(
        perm, counts, diag_tiles, right_side, remote, maps
    )
    g, inverse, op_hi, op_lo = coarse_setup(operator, coarse_map.reshape(1, NC1))
    inverse_rows = lax.dynamic_slice_in_dim(coarsest_inverse, group * AGG, AGG, 0)

    rr_local, g, inverse_rows, member, where = lax.optimization_barrier(
        (rr_local, g, inverse_rows, member, where)
    )
    outgoing, hi_peer, lo_peer, d_peer, m_peer = first_restrict(side, rs, rr_local)
    gathered = exchange(outgoing, GROUP_AXES)

    scalars = (perm, member)
    x, outgoing = lowest_part(gathered, g)
    coarse = (exchange(outgoing, "grp"), inverse_rows, g, x, inverse)
    fixed = (d_slot, d_rest, d_peer, m_peer, hi_top, lo_top, hi_side, lo_side, hi_peer, lo_peer, hi_rest, lo_rest, maps)
    z, w, w_peer, outgoing = forward_part(
        scalars, coarse + (op_hi, op_lo, b_slot, b_rest, d_slot, d_rest, side) + fixed[2:]
    )
    x, outgoing = lowest_part(exchange(outgoing, GROUP_AXES), g)
    coarse = (exchange(outgoing, "grp"), inverse_rows, g, x, inverse)
    v, u, outgoing, dots = second_part(scalars, coarse + (op_hi, op_lo, b_slot, b_rest) + fixed + (z, w, w_peer))
    sums = exchange(outgoing, ALL_AXES)
    return tuple(combine(where, dots, sums, right_side, z, w, v, u))


def solution(mesh):
    placed = (
        P(None, ("grp", "sub", "chip")),
        P(("grp", "sub", "chip"), None, None),
        P(("grp", "sub", "chip"), None, None, None),
        P(("grp", "sub", "chip"), None),
        P(("grp", "sub", "chip"), None, None),
        P(("grp", "sub", "chip")),
        P("grp"),
        P("grp", None, None),
        P(),
    )
    return jax.shard_map(
        on_device,
        mesh=mesh,
        in_specs=placed,
        out_specs=(P(None, ("grp", "sub", "chip")), P(None, ("grp", "sub", "chip"))),
        check_vma=False,
    )
```

```python
import functools

import jax
import jax.numpy as jnp
from jax import lax
from jax.experimental import pallas as pl
from jax.experimental.pallas import tpu as pltpu
from jax.sharding import PartitionSpec as P

OMEGA = 0.6
F32 = jnp.float32
BF16 = jnp.bfloat16
COLS = 64
TILE = 128
BLK = 64
SLOTS = 32
PEERS = 16
GROUPS = 8
AGG = 64
NC1 = 1024
STEP = 8
NSTEP = SLOTS // STEP
CHUNK = 16
CHUNKS = SLOTS // CHUNK
SIDE = 264
PEER_STEP = 4
ROWS = 40

GROUP_AXES = ("sub", "chip")
ALL_AXES = ("grp", "sub", "chip")


def params(mib=20):
    return pltpu.CompilerParams(vmem_limit_bytes=mib * 1024 * 1024)


def hbm(x):
    return pltpu.with_memory_space_constraint(x, pltpu.HBM)


def near(shape, dtype=F32):
    return pltpu.VMEM(shape, dtype)


def far(shape, dtype=F32):
    return pltpu.HBM(shape, dtype)


def cost(flops, moved):
    return pl.CostEstimate(flops=flops, bytes_accessed=moved, transcendentals=0)


def split2(x):
    hi = x.astype(BF16)
    lo = (x - hi.astype(F32)).astype(BF16)
    return hi, lo


def dot(a, b):
    return jnp.dot(a, b, preferred_element_type=F32)


def dot_nt(a, b):
    return lax.dot_general(a, b, (((1,), (1,)), ((), ())), preferred_element_type=F32)


def mm(x, whi, wlo, nt=False):
    op = dot_nt if nt else dot
    rows = x.shape[0]
    hi, lo = split2(x)
    both = op(jnp.concatenate([hi, lo], axis=0), whi)
    return both[:rows] + both[rows:] + op(hi, wlo)


def mm_exact(x, w, nt=False):
    op = dot_nt if nt else dot
    rows = x.shape[0]
    two = op(jnp.concatenate(split2(x), axis=0), w)
    return two[:rows] + two[rows:]


def beside(a, b):
    return jnp.concatenate([a, b], axis=1)


def eye_mask():
    r = lax.broadcasted_iota(jnp.int32, (TILE, TILE), 0)
    c = lax.broadcasted_iota(jnp.int32, (TILE, TILE), 1)
    return r, c


def tile_diag(tile):
    r, c = eye_mask()
    return jnp.sum(jnp.where(r == c, tile, 0.0), axis=0, keepdims=True)


def off_diag(tile):
    r, c = eye_mask()
    return jnp.where(r == c, 0.0, tile)


def one_hot(row):
    r = lax.broadcasted_iota(jnp.int32, (AGG, row.shape[1]), 0)
    return jnp.where(r == row, 1.0, 0.0).astype(BF16)


def pack_rows(x):
    wide = jnp.concatenate([x[:32], x[32:]], axis=1)
    return wide


def column(row):
    return jnp.broadcast_to(row, (TILE, TILE)).T


def boundary_kernel(slots_in, maps, tiles, cols, out, slots, slot_sem, map_buf, tile_buf, col_buf, out_buf, map_sem, col_sem, tile_sem, out_sem):
    def tile_copy(j):
        return pltpu.make_async_copy(tiles.at[slots[0, j % 2, j // 2]], tile_buf.at[j], tile_sem.at[j])

    def col_copy(j):
        at = pl.ds(pl.multiple_of(slots[0, j % 2, j // 2] * TILE, TILE), TILE)
        return pltpu.make_async_copy(cols.at[:, at], col_buf.at[j], col_sem.at[j])

    def out_copy(j):
        at = pl.ds(j // 2, PEER_STEP)
        return pltpu.make_async_copy(out_buf.at[at], out.at[at], out_sem.at[j // STEP])

    slot_copy = pltpu.make_async_copy(slots_in, slots, slot_sem)
    slot_copy.start()
    map_copy = pltpu.make_async_copy(maps, map_buf, map_sem)
    map_copy.start()
    slot_copy.wait()
    for j in range(SLOTS):
        tile_copy(j).start()
        col_copy(j).start()
    r = lax.broadcasted_iota(jnp.int32, (64, TILE), 0)
    c = lax.broadcasted_iota(jnp.int32, (64, TILE), 1)
    r8 = lax.broadcasted_iota(jnp.int32, (8, TILE), 0)
    map_copy.wait()
    for j in range(0, SLOTS, STEP):
        for k in range(j, j + STEP):
            tile_copy(k).wait()
            col_copy(k).wait()
        tile = [tile_buf[k] for k in range(j, j + STEP)]
        diag = [tile_diag(t) for t in tile]
        for k in range(j, j + STEP):
            t, d = tile[k - j], diag[k - j]
            q, base = k // 2, (k % 2) * 128
            out_buf[q, base : base + 64] = col_buf[k] * (OMEGA / d)
            below = pltpu.roll(t[64:], 64, 1)
            out_buf[q, base + 64 : base + 128] = jnp.where((c < 64) & (r > c), below, t[:64])
        for k in range(j, j + STEP, 2):
            own = [map_buf[pl.ds(slots[0, i, k // 2], 1)].astype(F32) for i in range(2)]
            d0, d1 = diag[k - j], diag[k - j + 1]
            out_buf[k // 2, 256:264] = jnp.where(
                r8 == 0, d0, jnp.where(r8 == 1, own[0], jnp.where(r8 == 2, d1, jnp.where(r8 == 3, own[1], 0.0)))
            )
        out_copy(j).start()
    for j in range(0, SLOTS, STEP):
        out_copy(j).wait()


def boundary_pack(slot_blocks, diag_tiles, right_side, maps):
    return pl.pallas_call(
        boundary_kernel,
        in_specs=[pl.BlockSpec(memory_space=pl.ANY)] * 4,
        out_specs=pl.BlockSpec(memory_space=pl.ANY),
        out_shape=far((PEERS, SIDE, TILE)),
        scratch_shapes=[
            pltpu.SMEM((1, 2, PEERS), jnp.int32),
            pltpu.SemaphoreType.DMA,
            pltpu.VMEM((BLK, TILE), jnp.int32),
            pltpu.VMEM((SLOTS, TILE, TILE), F32),
            pltpu.VMEM((SLOTS, COLS, TILE), F32),
            pltpu.VMEM((PEERS, SIDE, TILE), F32),
            pltpu.SemaphoreType.DMA,
            pltpu.SemaphoreType.DMA((SLOTS,)),
            pltpu.SemaphoreType.DMA((SLOTS,)),
            pltpu.SemaphoreType.DMA((NSTEP,)),
        ],
        compiler_params=params(),
        name="boundary_pack",
    )(hbm(slot_blocks.transpose(0, 2, 1)), hbm(maps), hbm(diag_tiles), hbm(right_side))


def local_kernel(perm, counts, *refs):
    n = 2 * STEP
    tiles, cols = refs[:n], refs[n : 2 * n]
    remote, maps = refs[2 * n : 2 * n + 2]
    b_slot, b_rest, d_slot, d_rest, hi_rest, lo_rest, hi_top, lo_top, hi_side, lo_side, s_slot, s_rest, rs, rr = (
        refs[2 * n + 2 :]
    )
    step = pl.program_id(0)

    @pl.when(step == 0)
    def _():
        rr[...] = jnp.zeros_like(rr)

    index = [perm[(0 if i < STEP else SLOTS) + step * STEP + i % STEP] for i in range(n)]
    tile = [tiles[i][0] for i in range(n)]
    diag = [tile_diag(t) for t in tile]
    off = [split2(off_diag(t)) for t in tile]
    b = [cols[i][...] for i in range(n)]
    x = [OMEGA * bb / d for bb, d in zip(b, diag)]
    y = [bb - OMEGA * bb - mm(xx, *o) for bb, xx, o in zip(b, x, off)]
    spread = [one_hot(maps[pl.ds(i, 1)]) for i in index]
    total = rr[...]
    for i in range(0, n, 2):
        total = total + mm_exact(beside(y[i], y[i + 1]), beside(spread[i], spread[i + 1]), nt=True)
    for k in range(STEP):
        b_slot[k] = b[k]
        d_slot[k] = diag[k]
        b_rest[k] = b[STEP + k]
        d_rest[k] = diag[STEP + k]
        hi_rest[k], lo_rest[k] = off[STEP + k]
        s_slot[k] = spread[k]
        s_rest[k] = spread[STEP + k]
    coupling, turned, restricted = [], [], []
    for k in range(STEP):
        j = step * STEP + k
        live = (j % 2) < counts[j // 2]
        scaled = remote[k] * jnp.where(live, -1.0, 0.0)
        coupling.append(split2(scaled))
        turned.append(split2(scaled.T))
    for k in range(STEP):
        restricted.append(-(dot_nt(coupling[k][0], spread[k]) + dot_nt(coupling[k][1], spread[k])))
        hi_top[k] = beside(off[k][0], turned[k][0])
        lo_top[k] = beside(off[k][1], turned[k][1])
        hi_side[k], lo_side[k] = coupling[k]
    for q in range(PEER_STEP):
        rs[q, 0], rs[q, 1] = split2(beside(restricted[2 * q], restricted[2 * q + 1]))
    rr[...] = total


def local_part(perm, counts, diag_tiles, right_side, remote, maps):
    def where(i):
        return (0 if i < STEP else SLOTS) + i % STEP

    def tile_spec(i):
        return pl.BlockSpec((1, TILE, TILE), lambda s, p, c: (p[s * STEP + where(i)], 0, 0))

    def col_spec(i):
        return pl.BlockSpec((COLS, TILE), lambda s, p, c: (0, p[s * STEP + where(i)]))

    def out(*shape):
        return pl.BlockSpec((STEP,) + shape, lambda s, p, c: (s, 0, 0))

    n = 2 * STEP
    grid = pltpu.PrefetchScalarGridSpec(
        num_scalar_prefetch=2,
        grid=(NSTEP,),
        in_specs=[tile_spec(i) for i in range(n)]
        + [col_spec(i) for i in range(n)]
        + [
            pl.BlockSpec((STEP, TILE, TILE), lambda s, p, c: (s, 0, 0)),
            pl.BlockSpec((BLK, TILE), lambda s, p, c: (0, 0)),
        ],
        out_specs=[
            out(COLS, TILE),
            out(COLS, TILE),
            out(1, TILE),
            out(1, TILE),
            out(TILE, TILE),
            out(TILE, TILE),
            out(TILE, 2 * TILE),
            out(TILE, 2 * TILE),
            out(TILE, TILE),
            out(TILE, TILE),
            out(AGG, TILE),
            out(AGG, TILE),
            pl.BlockSpec((PEER_STEP, 2, TILE, TILE), lambda s, p, c: (s, 0, 0, 0)),
            pl.BlockSpec((COLS, AGG), lambda s, p, c: (0, 0)),
        ],
    )

    def sds(shape, dtype=F32):
        return far((SLOTS,) + shape, dtype)

    return pl.pallas_call(
        local_kernel,
        grid_spec=grid,
        out_shape=[
            sds((COLS, TILE)),
            sds((COLS, TILE)),
            sds((1, TILE)),
            sds((1, TILE)),
            sds((TILE, TILE), BF16),
            sds((TILE, TILE), BF16),
            sds((TILE, 2 * TILE), BF16),
            sds((TILE, 2 * TILE), BF16),
            sds((TILE, TILE), BF16),
            sds((TILE, TILE), BF16),
            sds((AGG, TILE), BF16),
            sds((AGG, TILE), BF16),
            far((PEERS, 2, TILE, TILE), BF16),
            jax.ShapeDtypeStruct((COLS, AGG), F32),
        ],
        compiler_params=params(),
        cost_estimate=cost(2 * 64 * 3 * 64 * 128 * 128, 16 << 20),
        name="local_part",
    )(perm, counts, *([hbm(diag_tiles)] * n), *([hbm(right_side)] * n), hbm(remote), maps)


def coarse_kernel(op, cmap, g_out, d_out, hi_out, lo_out):
    spread = one_hot(cmap[...])
    product = None
    for i in range(NC1 // 256):
        rows = slice(i * 256, (i + 1) * 256)
        hi, lo = split2(op[rows, :])
        hi_out[rows, :] = hi
        lo_out[rows, :] = lo
        term = dot(spread[:, rows], hi) + dot(spread[:, rows], lo)
        product = term if product is None else product + term
    pieces = []
    for i in range(NC1 // TILE):
        pieces.append(tile_diag(op[i * TILE : (i + 1) * TILE, i * TILE : (i + 1) * TILE]))
    diag = jnp.concatenate(pieces, axis=1)
    inverse = 1.0 / diag
    d_out[...] = inverse
    g_out[...] = spread.astype(F32) - OMEGA * product * inverse


def coarse_setup(op, cmap):
    return pl.pallas_call(
        coarse_kernel,
        out_shape=[
            jax.ShapeDtypeStruct((AGG, NC1), F32),
            jax.ShapeDtypeStruct((1, NC1), F32),
            far((NC1, NC1), BF16),
            far((NC1, NC1), BF16),
        ],
        compiler_params=params(),
        cost_estimate=cost(2 * 2 * 64 * 1024 * 1024, 5 << 20),
        name="coarse_setup",
    )(op, cmap)


def first_restrict_kernel(arrived, rs, rr, out, hi_out, lo_out, diag_out, spread_out, rs_buf, rs_sem):
    def copy(j):
        at = pl.ds(j * PEER_STEP, PEER_STEP)
        return pltpu.make_async_copy(rs.at[at], rs_buf.at[at], rs_sem.at[j])

    for j in range(NSTEP):
        copy(j).start()
    r = lax.broadcasted_iota(jnp.int32, (64, TILE), 0)
    c = lax.broadcasted_iota(jnp.int32, (64, TILE), 1)
    for k in range(SLOTS):
        q, base, at = k // 2, 128 * (k % 2) + 64, 256 + 2 * (k % 2)
        packed = arrived[q, base : base + 64]
        top = jnp.where((c >= 64) | (r < c), packed, 0.0)
        bottom = pltpu.roll(jnp.where((c < 64) & (r > c), packed, 0.0), 64, 1)
        half = jnp.concatenate([top, bottom], axis=0)
        hi_out[k], lo_out[k] = split2(half + half.T)
        diag_out[k] = arrived[q, at : at + 1]
        spread_out[k] = one_hot(arrived[q, at + 1 : at + 2].astype(jnp.int32))
    main, rest = [], []
    for j in range(NSTEP):
        copy(j).wait()
        for q in range(j * PEER_STEP, (j + 1) * PEER_STEP):
            hi0, lo0 = split2(arrived[q, 0:COLS])
            hi1, lo1 = split2(arrived[q, 128 : 128 + COLS])
            main.append(dot(jnp.concatenate([hi0, lo0, hi1, lo1], axis=0), rs_buf[q, 0]))
            rest.append(dot(jnp.concatenate([hi0, hi1], axis=0), rs_buf[q, 1]))
    main, rest = sum(main), sum(rest)
    first = main[:COLS] + main[COLS : 2 * COLS] + rest[:COLS]
    second = main[2 * COLS : 3 * COLS] + main[3 * COLS :] + rest[COLS:]
    total = rr[...] + first[:, :AGG] + second[:, AGG:]
    out[...] = jnp.broadcast_to(pack_rows(total), out.shape)


def first_restrict(arrived, rs, rr):
    return pl.pallas_call(
        first_restrict_kernel,
        in_specs=[
            pl.BlockSpec(memory_space=pltpu.VMEM),
            pl.BlockSpec(memory_space=pl.ANY),
            pl.BlockSpec(memory_space=pltpu.VMEM),
        ],
        out_specs=[pl.BlockSpec(memory_space=pltpu.VMEM)] * 5,
        out_shape=[
            jax.ShapeDtypeStruct((PEERS, 32, TILE), F32),
            near((SLOTS, TILE, TILE), BF16),
            near((SLOTS, TILE, TILE), BF16),
            near((SLOTS, 1, TILE)),
            near((SLOTS, AGG, TILE), BF16),
        ],
        scratch_shapes=[
            pltpu.VMEM((PEERS, 2, TILE, TILE), BF16),
            pltpu.SemaphoreType.DMA((NSTEP,)),
        ],
        compiler_params=params(8),
        name="first_restrict",
    )(pltpu.with_memory_space_constraint(arrived, pltpu.VMEM), hbm(rs), rr)


def gathered_rows(ref, count):
    lane = lax.broadcasted_iota(jnp.int32, (32, TILE), 1) < 64
    tops, bottoms = [], []
    for q in range(0, count, 2):
        a, b = ref[q, 0:32], ref[q + 1, 0:32]
        tops.append(jnp.where(lane, a, pltpu.roll(b, 64, 1)))
        bottoms.append(jnp.where(lane, pltpu.roll(a, 64, 1), b))
    return jnp.concatenate([jnp.concatenate(tops, axis=1), jnp.concatenate(bottoms, axis=1)], axis=0)


def lowest_kernel(arrived, g, x_out, out):
    x = gathered_rows(arrived, PEERS)
    x_out[...] = x
    hi, lo = split2(g[...])
    packed = pack_rows(mm(x, hi, lo, nt=True))
    if arrived.shape[1] == ROWS:
        extra = arrived[0, 32:40]
        for q in range(1, PEERS):
            extra = extra + arrived[q, 32:40]
        packed = jnp.concatenate([packed, extra], axis=0)
    out[...] = jnp.broadcast_to(packed, out.shape)


def lowest_part(arrived, g):
    return pl.pallas_call(
        lowest_kernel,
        out_shape=[
            jax.ShapeDtypeStruct((COLS, NC1), F32),
            jax.ShapeDtypeStruct((GROUPS, arrived.shape[1], TILE), F32),
        ],
        compiler_params=params(6),
        cost_estimate=cost(20_000_000_000, 32 << 20),
        name="lowest_part",
    )(arrived, g)


def level_one(arrived, inverse_rows, g, x_ref, inverse_ref, op_hi, op_lo, e_out):
    low = gathered_rows(arrived, GROUPS)
    hi, lo = split2(inverse_rows[...])
    corr = mm(low, hi, lo, nt=True)
    ghi, glo = split2(g[...])
    lifted = mm(corr, ghi, glo)
    inverse = inverse_ref[...]
    scaled = x_ref[...] * inverse
    total = None
    for i in range(NC1 // 256):
        rows = slice(i * 256, (i + 1) * 256)
        term = mm(scaled[:, rows], op_hi[rows, :], op_lo[rows, :])
        total = term if total is None else total + term
    e = 2.0 * OMEGA * scaled - OMEGA * OMEGA * total * inverse + lifted
    for q in range(PEERS):
        e_out[q] = e[:, q * AGG : (q + 1) * AGG]


def apply_off(x, hi, lo):
    xh, xl = split2(x)
    rows = x.shape[0]
    if x.shape[1] == TILE:
        return dot(beside(xh, xl), jnp.concatenate([hi, hi], axis=0)) + dot(xh, lo)
    both = dot(jnp.concatenate([xh, xl], axis=0), hi)
    return both[:rows] + both[rows:] + dot(xh, lo)


def apply_block(x, diag, hi, lo):
    xh, xl = split2(x)
    kept = xh.astype(F32) + xl.astype(F32)
    return apply_off(x, hi, lo) + kept[:, : diag.shape[1]] * diag


def lift(parts, spread):
    rows = parts.shape[0] // 2
    two = dot(parts, spread)
    return two[:rows] + two[rows:]


def two_parts(e):
    return jnp.concatenate(split2(e), axis=0)


def block(top, side, peer, k):
    return jnp.concatenate([top[k], beside(side[k], peer[k])], axis=0)


def pair_spread(own, peer):
    none = jnp.zeros_like(own)
    return jnp.concatenate([beside(own, none), beside(none, peer)], axis=0)


def forward_kernel(
    member, arrived, inverse_rows, g, x, inverse, op_hi, op_lo, b_slot, b_rest, d_slot, d_rest, x_peer, d_peer, s_slot, s_rest, s_peer,
    hi_top, lo_top, hi_side, lo_side, hi_peer, lo_peer, hi_rest, lo_rest, z_out, w_out, ws_out, out, e, acc_rr, acc_bz, acc_zw
):
    level_one(arrived, inverse_rows, g, x, inverse, op_hi, op_lo, e)
    acc_rr[...] = jnp.zeros_like(acc_rr)
    acc_bz[...] = jnp.zeros_like(acc_bz)
    acc_zw[...] = jnp.zeros_like(acc_zw)
    e_own = e.at[pl.ds(member[0], 1)]
    views = (e, b_slot, b_rest, d_slot, d_rest, x_peer, d_peer, s_slot, s_rest, s_peer, hi_top, lo_top, hi_side, lo_side, hi_peer, lo_peer, hi_rest, lo_rest, ws_out)

    @pl.loop(0, CHUNKS)
    def _(step):
        e_peer, *parts = [v.at[part(step, v.shape[0])] for v in views]
        both = [v.at[:, part(step, SLOTS)] for v in (z_out, w_out)]
        forward_step(e_own, e_peer, *parts[:-1], *both, parts[-1], acc_rr, acc_bz, acc_zw)

    packed = pack_rows(acc_rr[...])
    sums = jnp.sum(jnp.concatenate([acc_bz[...], acc_zw[...]], axis=0).T, axis=0, keepdims=True)
    r8 = lax.broadcasted_iota(jnp.int32, (8, TILE), 0)
    extra = jnp.where(r8 == 0, sums, 0.0)
    for q in range(PEERS):
        out[q, 0:32] = packed
        out[q, 32:40] = extra


def part(step, count):
    size = count // CHUNKS
    return pl.ds(step * size, size)


def forward_step(
    e_own, e_peer, b_slot, b_rest, d_slot, d_rest, x_peer, d_peer, s_slot, s_rest, s_peer,
    hi_top, lo_top, hi_side, lo_side, hi_peer, lo_peer, hi_rest, lo_rest, z_out, w_out, ws_out, acc_rr, acc_bz, acc_zw
):
    e_mine = two_parts(e_own[0])
    e_both = [two_parts(beside(e_own[0], e_peer[q])) for q in range(CHUNK // 2)]
    rr, bz, zw = acc_rr[...], acc_bz[...], acc_zw[...]
    pairs, rest = range(CHUNK), range(CHUNK)
    b_own = [b_slot[k] for k in pairs] + [b_rest[k] for k in rest]
    diag = [jnp.concatenate([d_slot[k], d_peer[k]], axis=1) for k in pairs] + [d_rest[k] for k in rest]
    rdiag = [OMEGA / d for d in diag]
    mats = [(block(hi_top, hi_side, hi_peer, k), block(lo_top, lo_side, lo_peer, k)) for k in pairs]
    mats = mats + [(hi_rest[k], lo_rest[k]) for k in rest]
    peers = [x_peer[k // 2, (k % 2) * 128 : (k % 2) * 128 + COLS] for k in pairs]
    x1 = [beside(b_own[k] * rdiag[k][:, :TILE], peers[k]) for k in pairs]
    x1 = x1 + [b * rd for b, rd in zip(b_own[CHUNK:], rdiag[CHUNK:])]
    spread = [s_slot[k] for k in pairs] + [s_rest[k] for k in rest]
    ups = [lift(e_both[k // 2], pair_spread(spread[k], s_peer[k])) for k in pairs]
    ups = ups + [lift(e_mine, sp) for sp in spread[CHUNK:]]
    x = [start + up for start, up in zip(x1, ups)]
    image = [apply_off(xx, *m) for xx, m in zip(x, mats)]
    z = [(1.0 - OMEGA) * xx + start - im * rd for xx, start, im, rd in zip(x, x1, image, rdiag)]
    w = [apply_block(zz, d, *m) for zz, d, m in zip(z, diag, mats)]
    x1 = [ww * rd for ww, rd in zip(w, rdiag)]
    left = [(m[0][:, :TILE], m[1][:, :TILE]) for m in mats]
    y = [(1.0 - OMEGA) * ww[:, :TILE] - apply_off(xx, *m) for ww, xx, m in zip(w, x1, left)]
    for i in range(0, 2 * CHUNK, 2):
        rr = rr + mm_exact(beside(y[i], y[i + 1]), beside(spread[i], spread[i + 1]), nt=True)
    for i in range(2 * CHUNK):
        zz, ww = z[i][:, :TILE], w[i][:, :TILE]
        bz = bz + b_own[i] * zz
        zw = zw + zz * ww
        z_out[i // CHUNK, i % CHUNK] = zz
        w_out[i // CHUNK, i % CHUNK] = ww
    for k in pairs:
        ws_out[k] = w[k][:, TILE:]
    acc_rr[...] = rr
    acc_bz[...] = bz
    acc_zw[...] = zw


def specs(smem, vmem):
    return [pl.BlockSpec(memory_space=pltpu.SMEM)] * smem + [pl.BlockSpec(memory_space=pltpu.VMEM)] * vmem


def forward_part(scalars, arrays):
    return pl.pallas_call(
        forward_kernel,
        in_specs=specs(len(scalars), len(arrays)),
        out_specs=specs(0, 4),
        out_shape=[
            near((2, SLOTS, COLS, TILE)),
            near((2, SLOTS, COLS, TILE)),
            near((SLOTS, COLS, TILE)),
            jax.ShapeDtypeStruct((PEERS, ROWS, TILE), F32),
        ],
        scratch_shapes=[
            pltpu.VMEM((PEERS, COLS, AGG), F32),
            pltpu.VMEM((COLS, AGG), F32),
            pltpu.VMEM((COLS, TILE), F32),
            pltpu.VMEM((COLS, TILE), F32),
        ],
        compiler_params=params(10),
        name="forward_part",
    )(*scalars, *arrays)


def second_kernel(
    member, arrived, inverse_rows, g, x, inverse, op_hi, op_lo, b_slot, b_rest, d_slot, d_rest, d_peer, s_slot, s_rest, s_peer,
    hi_top, lo_top, hi_side, lo_side, hi_peer, lo_peer, hi_rest, lo_rest, z_in, w_in, w_peer, v_out, u_out, out, dots, e, acc_a, acc_b, acc_c, acc_alpha
):
    extra = arrived[0, 32:40]
    for q in range(1, GROUPS):
        extra = extra + arrived[q, 32:40]
    dots[...] = extra
    level_one(arrived, inverse_rows, g, x, inverse, op_hi, op_lo, e)
    acc_a[...] = jnp.zeros_like(acc_a)
    acc_b[...] = jnp.zeros_like(acc_b)
    acc_c[...] = jnp.zeros_like(acc_c)
    col = column(dots[0:1])
    acc_alpha[...] = col[:COLS] / col[COLS:]
    e_own = e.at[pl.ds(member[0], 1)]
    views = (e, b_slot, b_rest, d_slot, d_rest, d_peer, s_slot, s_rest, s_peer, hi_top, lo_top, hi_side, lo_side, hi_peer, lo_peer, hi_rest, lo_rest, w_peer)

    @pl.loop(0, CHUNKS)
    def _(step):
        e_peer, *parts = [v.at[part(step, v.shape[0])] for v in views]
        z_part, w_part, v_part, u_part = [v.at[:, part(step, SLOTS)] for v in (z_in, w_in, v_out, u_out)]
        second_step(
            e_own, e_peer, *parts[:-1], z_part, w_part, parts[-1], v_part, u_part,
            acc_a, acc_b, acc_c, acc_alpha
        )

    first = jnp.sum(jnp.concatenate([acc_a[...], acc_b[...]], axis=0).T, axis=0, keepdims=True)
    last = jnp.sum(jnp.concatenate([acc_c[...], acc_c[...]], axis=0).T, axis=0, keepdims=True)
    out[...] = jnp.broadcast_to(jnp.concatenate([first, last], axis=0), out.shape)


def second_step(
    e_own, e_peer, b_slot, b_rest, d_slot, d_rest, d_peer, s_slot, s_rest, s_peer,
    hi_top, lo_top, hi_side, lo_side, hi_peer, lo_peer, hi_rest, lo_rest, z_in, w_in, w_peer, v_out, u_out, acc_a, acc_b, acc_c, acc_alpha
):
    alpha = acc_alpha[...]
    e_mine = two_parts(e_own[0])
    e_both = [two_parts(beside(e_own[0], e_peer[q])) for q in range(CHUNK // 2)]
    sums = [acc_a[...], acc_b[...], acc_c[...]]

    def gather(b, z, w, v, u):
        r1 = b - alpha * w
        z1 = z - alpha * v
        az1 = w - alpha * u
        sums[0] = sums[0] + r1 * z1
        sums[1] = sums[1] + z1 * az1
        sums[2] = sums[2] + (z1 * w + z * az1)

    pairs, rest = range(CHUNK), range(CHUNK)
    diag = [jnp.concatenate([d_slot[k], d_peer[k]], axis=1) for k in pairs] + [d_rest[k] for k in rest]
    rdiag = [OMEGA / d for d in diag]
    mats = [(block(hi_top, hi_side, hi_peer, k), block(lo_top, lo_side, lo_peer, k)) for k in pairs]
    mats = mats + [(hi_rest[k], lo_rest[k]) for k in rest]
    w = [jnp.concatenate([w_in[0, k], w_peer[k]], axis=1) for k in pairs] + [w_in[1, k] for k in rest]
    spread = [s_slot[k] for k in pairs] + [s_rest[k] for k in rest]
    ups = [lift(e_both[k // 2], pair_spread(spread[k], s_peer[k])) for k in pairs]
    ups = ups + [lift(e_mine, sp) for sp in spread[CHUNK:]]
    x1 = [ww * rd for ww, rd in zip(w, rdiag)]
    x = [start + up for start, up in zip(x1, ups)]
    image = [apply_off(xx, *m) for xx, m in zip(x, mats)]
    v = [(1.0 - OMEGA) * xx + start - im * rd for xx, start, im, rd in zip(x, x1, image, rdiag)]
    left = [(m[0][:, :TILE], m[1][:, :TILE]) for m in mats]
    u = [apply_block(vv, d[:, :TILE], *m) for vv, d, m in zip(v, diag, left)]
    for i in range(2 * CHUNK):
        vv, b_ref = v[i][:, :TILE], (b_slot if i < CHUNK else b_rest)
        v_out[i // CHUNK, i % CHUNK] = vv
        u_out[i // CHUNK, i % CHUNK] = u[i]
        gather(b_ref[i % CHUNK], z_in[i // CHUNK, i % CHUNK], w[i][:, :TILE], vv, u[i])
    acc_a[...] = sums[0]
    acc_b[...] = sums[1]
    acc_c[...] = sums[2]


def second_part(scalars, arrays):
    return pl.pallas_call(
        second_kernel,
        in_specs=specs(len(scalars), len(arrays)),
        out_specs=specs(0, 4),
        out_shape=[
            near((2, SLOTS, COLS, TILE)),
            near((2, SLOTS, COLS, TILE)),
            jax.ShapeDtypeStruct((GROUPS * PEERS, 2, TILE), F32),
            jax.ShapeDtypeStruct((8, TILE), F32),
        ],
        scratch_shapes=[pltpu.VMEM((PEERS, COLS, AGG), F32)] + [pltpu.VMEM((COLS, TILE), F32)] * 4,
        compiler_params=params(10),
        name="second_part",
    )(*scalars, *arrays)


def combine_kernel(where, dots, arrived, b, z, w, v, u, solution, residual, sol_buf, res_buf, sem):
    total = jnp.sum(arrived[...], axis=0)
    old = column(dots[0:1])
    one = column(total[0:1])
    two = column(total[1:2])
    rho, zw = old[:COLS], old[COLS:]
    rho_next, zz = one[:COLS], one[COLS:]
    alpha = rho / zw
    beta = rho_next / rho
    alpha_next = rho_next / (zz + beta * two[:COLS] + beta * beta * zw)
    first = alpha + alpha_next * (1.0 + beta)
    second = alpha_next * alpha

    def copies(i):
        at = pl.ds(i * (STEP * TILE), STEP * TILE)
        return (
            pltpu.make_async_copy(sol_buf.at[:, at], solution.at[:, at], sem.at[0, i]),
            pltpu.make_async_copy(res_buf.at[:, at], residual.at[:, at], sem.at[1, i]),
        )

    for i in range(BLK // STEP):
        for t in range(i * STEP, (i + 1) * STEP):
            half, k = where[t] // SLOTS, lax.rem(where[t], SLOTS)
            at = slice(t * TILE, (t + 1) * TILE)
            sol_buf[:, at] = first * z[half, k] - second * v[half, k]
            res_buf[:, at] = b[:, at] - first * w[half, k] + second * u[half, k]
        for copy in copies(i):
            copy.start()
    for i in range(BLK // STEP):
        for copy in copies(i):
            copy.wait()


def combine(where, dots, arrived, b, z, w, v, u):
    return pl.pallas_call(
        combine_kernel,
        in_specs=specs(1, 7),
        out_specs=[pl.BlockSpec(memory_space=pl.ANY)] * 2,
        out_shape=[far((COLS, BLK * TILE))] * 2,
        scratch_shapes=[
            pltpu.VMEM((COLS, BLK * TILE), F32),
            pltpu.VMEM((COLS, BLK * TILE), F32),
            pltpu.SemaphoreType.DMA((2, BLK // STEP)),
        ],
        compiler_params=params(8),
        name="combine",
    )(where, dots, arrived, b, z, w, v, u)


def exchange(x, axes):
    return lax.all_to_all(x, axes, 0, 0, tiled=True)


def on_device(
    right_side,
    diag_tiles,
    remote_tiles,
    slot_counts,
    slot_blocks,
    fine_map,
    coarse_map,
    level1_ops,
    coarsest_inverse,
):
    group = lax.axis_index("grp")
    member = lax.axis_index(GROUP_AXES).astype(jnp.int32).reshape(1)
    slot_list = slot_blocks.reshape(SLOTS)
    counts = slot_counts.reshape(PEERS)
    maps = fine_map.reshape(BLK, TILE)
    remote = remote_tiles.reshape(SLOTS, TILE, TILE)
    operator = level1_ops[0]

    outgoing = boundary_pack(slot_blocks, diag_tiles, right_side, maps)
    side = exchange(outgoing, GROUP_AXES)

    tile_ids = jnp.arange(BLK, dtype=jnp.int32)
    free = jnp.logical_not(jnp.any(slot_list[:, None] == tile_ids[None, :], axis=0)).astype(jnp.int32)
    rank = jnp.sum(jnp.where(tile_ids[None, :] < tile_ids[:, None], free[None, :], 0), axis=1)
    chosen = (rank[None, :] == jnp.arange(SLOTS, dtype=jnp.int32)[:, None]) & (free[None, :] == 1)
    rest_list = jnp.sum(jnp.where(chosen, tile_ids[None, :], 0), axis=1)
    perm = jnp.concatenate([slot_list, rest_list])
    where = jnp.sum(jnp.where(perm[None, :] == tile_ids[:, None], tile_ids[None, :], 0), axis=1)

    b_slot, b_rest, d_slot, d_rest, hi_rest, lo_rest, hi_top, lo_top, hi_side, lo_side, s_slot, s_rest, rs, rr_local = (
        local_part(
        perm, counts, diag_tiles, right_side, remote, maps)
    )
    g, inverse, op_hi, op_lo = coarse_setup(operator, coarse_map.reshape(1, NC1))
    inverse_rows = lax.dynamic_slice_in_dim(coarsest_inverse, group * AGG, AGG, 0)

    rr_local, g, inverse_rows, member, where = lax.optimization_barrier(
        (rr_local, g, inverse_rows, member, where)
    )
    outgoing, hi_peer, lo_peer, d_peer, s_peer = first_restrict(side, rs, rr_local)
    gathered = exchange(outgoing, GROUP_AXES)

    scalars = (member,)
    x, outgoing = lowest_part(gathered, g)
    coarse = (exchange(outgoing, "grp"), inverse_rows, g, x, inverse)
    fixed = (d_slot, d_rest, d_peer, s_slot, s_rest, s_peer, hi_top, lo_top, hi_side, lo_side, hi_peer, lo_peer, hi_rest, lo_rest)
    z, w, w_peer, outgoing = forward_part(
        scalars, coarse + (op_hi, op_lo, b_slot, b_rest, d_slot, d_rest, side) + fixed[2:]
    )
    x, outgoing = lowest_part(exchange(outgoing, GROUP_AXES), g)
    coarse = (exchange(outgoing, "grp"), inverse_rows, g, x, inverse)
    v, u, outgoing, dots = second_part(scalars, coarse + (op_hi, op_lo, b_slot, b_rest) + fixed + (z, w, w_peer))
    sums = exchange(outgoing, ALL_AXES)
    return tuple(combine(where, dots, sums, right_side, z, w, v, u))


def solution(mesh):
    placed = (
        P(None, ("grp", "sub", "chip")),
        P(("grp", "sub", "chip"), None, None),
        P(("grp", "sub", "chip"), None, None, None),
        P(("grp", "sub", "chip"), None),
        P(("grp", "sub", "chip"), None, None),
        P(("grp", "sub", "chip")),
        P("grp"),
        P("grp", None, None),
        P(),
    )
    return jax.shard_map(
        on_device,
        mesh=mesh,
        in_specs=placed,
        out_specs=(P(None, ("grp", "sub", "chip")), P(None, ("grp", "sub", "chip"))),
        check_vma=False,
    )
```

```python
import functools

import jax
import jax.numpy as jnp
from jax import lax
from jax.experimental import pallas as pl
from jax.experimental.pallas import tpu as pltpu
from jax.sharding import PartitionSpec as P

OMEGA = 0.6
F32 = jnp.float32
BF16 = jnp.bfloat16
COLS = 64
TILE = 128
BLK = 64
SLOTS = 32
PEERS = 16
GROUPS = 8
AGG = 64
NC1 = 1024
STEP = 8
NSTEP = SLOTS // STEP
CHUNK = 16
CHUNKS = SLOTS // CHUNK
SIDE = 264
PEER_STEP = 4
ROWS = 40

GROUP_AXES = ("sub", "chip")
ALL_AXES = ("grp", "sub", "chip")


def params(mib=20):
    return pltpu.CompilerParams(vmem_limit_bytes=mib * 1024 * 1024)


def hbm(x):
    return pltpu.with_memory_space_constraint(x, pltpu.HBM)


def near(shape, dtype=F32):
    return pltpu.VMEM(shape, dtype)


def far(shape, dtype=F32):
    return pltpu.HBM(shape, dtype)


def cost(flops, moved):
    return pl.CostEstimate(flops=flops, bytes_accessed=moved, transcendentals=0)


def split2(x):
    hi = x.astype(BF16)
    lo = (x - hi.astype(F32)).astype(BF16)
    return hi, lo


def dot(a, b):
    return jnp.dot(a, b, preferred_element_type=F32)


def dot_nt(a, b):
    return lax.dot_general(a, b, (((1,), (1,)), ((), ())), preferred_element_type=F32)


def mm(x, whi, wlo, nt=False):
    op = dot_nt if nt else dot
    rows = x.shape[0]
    hi, lo = split2(x)
    both = op(jnp.concatenate([hi, lo], axis=0), whi)
    return both[:rows] + both[rows:] + op(hi, wlo)


def mm_exact(x, w, nt=False):
    op = dot_nt if nt else dot
    rows = x.shape[0]
    two = op(jnp.concatenate(split2(x), axis=0), w)
    return two[:rows] + two[rows:]


def beside(a, b):
    return jnp.concatenate([a, b], axis=1)


def eye_mask():
    r = lax.broadcasted_iota(jnp.int32, (TILE, TILE), 0)
    c = lax.broadcasted_iota(jnp.int32, (TILE, TILE), 1)
    return r, c


def tile_diag(tile):
    r, c = eye_mask()
    return jnp.sum(jnp.where(r == c, tile, 0.0), axis=0, keepdims=True)


def off_diag(tile):
    r, c = eye_mask()
    return jnp.where(r == c, 0.0, tile)


def one_hot(row):
    r = lax.broadcasted_iota(jnp.int32, (AGG, row.shape[1]), 0)
    return jnp.where(r == row, 1.0, 0.0).astype(BF16)


def pack_rows(x):
    wide = jnp.concatenate([x[:32], x[32:]], axis=1)
    return wide


def column(row):
    return jnp.broadcast_to(row, (TILE, TILE)).T


def boundary_kernel(slots_in, maps, tiles, cols, out, slots, slot_sem, map_buf, tile_buf, col_buf, out_buf, map_sem, col_sem, tile_sem, out_sem):
    def tile_copy(j):
        return pltpu.make_async_copy(tiles.at[slots[0, j % 2, j // 2]], tile_buf.at[j], tile_sem.at[j])

    def col_copy(j):
        at = pl.ds(pl.multiple_of(slots[0, j % 2, j // 2] * TILE, TILE), TILE)
        return pltpu.make_async_copy(cols.at[:, at], col_buf.at[j], col_sem.at[j])

    def out_copy(j):
        at = pl.ds(j // 2, PEER_STEP)
        return pltpu.make_async_copy(out_buf.at[at], out.at[at], out_sem.at[j // STEP])

    slot_copy = pltpu.make_async_copy(slots_in, slots, slot_sem)
    slot_copy.start()
    map_copy = pltpu.make_async_copy(maps, map_buf, map_sem)
    map_copy.start()
    slot_copy.wait()
    for j in range(SLOTS):
        tile_copy(j).start()
        col_copy(j).start()
    r = lax.broadcasted_iota(jnp.int32, (64, TILE), 0)
    c = lax.broadcasted_iota(jnp.int32, (64, TILE), 1)
    r8 = lax.broadcasted_iota(jnp.int32, (8, TILE), 0)
    map_copy.wait()
    for j in range(0, SLOTS, STEP):
        for k in range(j, j + STEP):
            tile_copy(k).wait()
            col_copy(k).wait()
        tile = [tile_buf[k] for k in range(j, j + STEP)]
        diag = [tile_diag(t) for t in tile]
        for k in range(j, j + STEP):
            t, d = tile[k - j], diag[k - j]
            q, base = k // 2, (k % 2) * 128
            out_buf[q, base : base + 64] = col_buf[k] * (OMEGA / d)
            below = pltpu.roll(t[64:], 64, 1)
            out_buf[q, base + 64 : base + 128] = jnp.where((c < 64) & (r > c), below, t[:64])
        for k in range(j, j + STEP, 2):
            own = [map_buf[pl.ds(slots[0, i, k // 2], 1)].astype(F32) for i in range(2)]
            d0, d1 = diag[k - j], diag[k - j + 1]
            out_buf[k // 2, 256:264] = jnp.where(
                r8 == 0, d0, jnp.where(r8 == 1, own[0], jnp.where(r8 == 2, d1, jnp.where(r8 == 3, own[1], 0.0)))
            )
        out_copy(j).start()
    for j in range(0, SLOTS, STEP):
        out_copy(j).wait()


def boundary_pack(slot_blocks, diag_tiles, right_side, maps):
    return pl.pallas_call(
        boundary_kernel,
        in_specs=[pl.BlockSpec(memory_space=pl.ANY)] * 4,
        out_specs=pl.BlockSpec(memory_space=pl.ANY),
        out_shape=far((PEERS, SIDE, TILE)),
        scratch_shapes=[
            pltpu.SMEM((1, 2, PEERS), jnp.int32),
            pltpu.SemaphoreType.DMA,
            pltpu.VMEM((BLK, TILE), jnp.int32),
            pltpu.VMEM((SLOTS, TILE, TILE), F32),
            pltpu.VMEM((SLOTS, COLS, TILE), F32),
            pltpu.VMEM((PEERS, SIDE, TILE), F32),
            pltpu.SemaphoreType.DMA,
            pltpu.SemaphoreType.DMA((SLOTS,)),
            pltpu.SemaphoreType.DMA((SLOTS,)),
            pltpu.SemaphoreType.DMA((NSTEP,)),
        ],
        compiler_params=params(),
        name="boundary_pack",
    )(hbm(slot_blocks.transpose(0, 2, 1)), hbm(maps), hbm(diag_tiles), hbm(right_side))


def local_kernel(perm, counts, *refs):
    n = 2 * STEP
    tiles, cols = refs[:n], refs[n : 2 * n]
    remote, maps = refs[2 * n : 2 * n + 2]
    b_slot, b_rest, d_slot, d_rest, hi_rest, lo_rest, hi_top, lo_top, hi_side, lo_side, s_slot, s_rest = refs[
        2 * n + 2 : 2 * n + 14
    ]
    z_rest, w_rest, hi_unit, lo_unit, rr_unit, rs, rr = refs[2 * n + 14 :]
    step = pl.program_id(0)

    @pl.when(step == 0)
    def _():
        rr[...] = jnp.zeros_like(rr)
        rr_unit[...] = jnp.zeros_like(rr_unit)

    index = [perm[(0 if i < STEP else SLOTS) + step * STEP + i % STEP] for i in range(n)]
    tile = [tiles[i][0] for i in range(n)]
    diag = [tile_diag(t) for t in tile]
    off = [split2(off_diag(t)) for t in tile]
    b = [cols[i][...] for i in range(n)]
    x = [OMEGA * bb / d for bb, d in zip(b, diag)]
    spread = [one_hot(maps[pl.ds(i, 1)]) for i in index]
    rest = range(STEP, n)
    rdiag = [OMEGA / diag[i] for i in rest]
    start = [jnp.concatenate([x[i], jnp.zeros_like(x[i])], axis=0) for i in rest]
    both = [jnp.concatenate([x[i], spread[i].astype(F32)], axis=0) for i in rest]
    image = [apply_off(xx, *off[i]) for xx, i in zip(both, rest)]
    z = [(1.0 - OMEGA) * xx + st - im * rd for xx, st, im, rd in zip(both, start, image, rdiag)]
    w = [apply_block(zz, diag[i], *off[i]) for zz, i in zip(z, rest)]
    left = [(1.0 - OMEGA) * ww - apply_off(ww * rd, *off[i]) for ww, rd, i in zip(w, rdiag, rest)]
    unit_total = rr_unit[...]
    for k in range(0, STEP, 2):
        pair = beside(spread[STEP + k], spread[STEP + k + 1])
        unit_total = unit_total + mm_exact(beside(left[k], left[k + 1]), pair, nt=True)
    rr_unit[...] = unit_total
    for k in range(STEP):
        z_rest[k] = z[k][:COLS]
        w_rest[k] = w[k][:COLS]
        hi_unit[k], lo_unit[k] = split2(beside(z[k][COLS:], w[k][COLS:]))
    y = [b[i] - OMEGA * b[i] - mm(x[i], *off[i]) for i in range(STEP)]
    y = y + [b[i] - OMEGA * b[i] - im[:COLS] for i, im in zip(rest, image)]
    total = rr[...]
    for i in range(0, n, 2):
        total = total + mm_exact(beside(y[i], y[i + 1]), beside(spread[i], spread[i + 1]), nt=True)
    for k in range(STEP):
        b_slot[k] = b[k]
        d_slot[k] = diag[k]
        b_rest[k] = b[STEP + k]
        d_rest[k] = diag[STEP + k]
        hi_rest[k], lo_rest[k] = off[STEP + k]
        s_slot[k] = spread[k]
        s_rest[k] = spread[STEP + k]
    coupling, turned, restricted = [], [], []
    for k in range(STEP):
        j = step * STEP + k
        live = (j % 2) < counts[j // 2]
        scaled = remote[k] * jnp.where(live, -1.0, 0.0)
        coupling.append(split2(scaled))
        turned.append(split2(scaled.T))
    for k in range(STEP):
        restricted.append(-(dot_nt(coupling[k][0], spread[k]) + dot_nt(coupling[k][1], spread[k])))
        hi_top[k] = beside(off[k][0], turned[k][0])
        lo_top[k] = beside(off[k][1], turned[k][1])
        hi_side[k], lo_side[k] = coupling[k]
    for q in range(PEER_STEP):
        rs[q, 0], rs[q, 1] = split2(beside(restricted[2 * q], restricted[2 * q + 1]))
    rr[...] = total


def local_part(perm, counts, diag_tiles, right_side, remote, maps):
    def where(i):
        return (0 if i < STEP else SLOTS) + i % STEP

    def tile_spec(i):
        return pl.BlockSpec((1, TILE, TILE), lambda s, p, c: (p[s * STEP + where(i)], 0, 0))

    def col_spec(i):
        return pl.BlockSpec((COLS, TILE), lambda s, p, c: (0, p[s * STEP + where(i)]))

    def out(*shape):
        return pl.BlockSpec((STEP,) + shape, lambda s, p, c: (s, 0, 0))

    n = 2 * STEP
    grid = pltpu.PrefetchScalarGridSpec(
        num_scalar_prefetch=2,
        grid=(NSTEP,),
        in_specs=[tile_spec(i) for i in range(n)]
        + [col_spec(i) for i in range(n)]
        + [
            pl.BlockSpec((STEP, TILE, TILE), lambda s, p, c: (s, 0, 0)),
            pl.BlockSpec((BLK, TILE), lambda s, p, c: (0, 0)),
        ],
        out_specs=[
            out(COLS, TILE),
            out(COLS, TILE),
            out(1, TILE),
            out(1, TILE),
            out(TILE, TILE),
            out(TILE, TILE),
            out(TILE, 2 * TILE),
            out(TILE, 2 * TILE),
            out(TILE, TILE),
            out(TILE, TILE),
            out(AGG, TILE),
            out(AGG, TILE),
            out(COLS, TILE),
            out(COLS, TILE),
            out(AGG, 2 * TILE),
            out(AGG, 2 * TILE),
            pl.BlockSpec((COLS + AGG, AGG), lambda s, p, c: (0, 0)),
            pl.BlockSpec((PEER_STEP, 2, TILE, TILE), lambda s, p, c: (s, 0, 0, 0)),
            pl.BlockSpec((COLS, AGG), lambda s, p, c: (0, 0)),
        ],
    )

    def sds(shape, dtype=F32):
        return far((SLOTS,) + shape, dtype)

    return pl.pallas_call(
        local_kernel,
        grid_spec=grid,
        out_shape=[
            sds((COLS, TILE)),
            sds((COLS, TILE)),
            sds((1, TILE)),
            sds((1, TILE)),
            sds((TILE, TILE), BF16),
            sds((TILE, TILE), BF16),
            sds((TILE, 2 * TILE), BF16),
            sds((TILE, 2 * TILE), BF16),
            sds((TILE, TILE), BF16),
            sds((TILE, TILE), BF16),
            sds((AGG, TILE), BF16),
            sds((AGG, TILE), BF16),
            sds((COLS, TILE)),
            sds((COLS, TILE)),
            sds((AGG, 2 * TILE), BF16),
            sds((AGG, 2 * TILE), BF16),
            jax.ShapeDtypeStruct((COLS + AGG, AGG), F32),
            far((PEERS, 2, TILE, TILE), BF16),
            jax.ShapeDtypeStruct((COLS, AGG), F32),
        ],
        compiler_params=params(),
        cost_estimate=cost(2 * 64 * 3 * 64 * 128 * 128, 16 << 20),
        name="local_part",
    )(perm, counts, *([hbm(diag_tiles)] * n), *([hbm(right_side)] * n), hbm(remote), maps)


def coarse_kernel(op, cmap, g_out, d_out, hi_out, lo_out):
    spread = one_hot(cmap[...])
    product = None
    for i in range(NC1 // 256):
        rows = slice(i * 256, (i + 1) * 256)
        hi, lo = split2(op[rows, :])
        hi_out[rows, :] = hi
        lo_out[rows, :] = lo
        term = dot(spread[:, rows], hi) + dot(spread[:, rows], lo)
        product = term if product is None else product + term
    pieces = []
    for i in range(NC1 // TILE):
        pieces.append(tile_diag(op[i * TILE : (i + 1) * TILE, i * TILE : (i + 1) * TILE]))
    diag = jnp.concatenate(pieces, axis=1)
    inverse = 1.0 / diag
    d_out[...] = inverse
    g_out[...] = spread.astype(F32) - OMEGA * product * inverse


def coarse_setup(op, cmap):
    return pl.pallas_call(
        coarse_kernel,
        out_shape=[
            jax.ShapeDtypeStruct((AGG, NC1), F32),
            jax.ShapeDtypeStruct((1, NC1), F32),
            far((NC1, NC1), BF16),
            far((NC1, NC1), BF16),
        ],
        compiler_params=params(),
        cost_estimate=cost(2 * 2 * 64 * 1024 * 1024, 5 << 20),
        name="coarse_setup",
    )(op, cmap)


def first_restrict_kernel(arrived, rs, rr, out, hi_out, lo_out, diag_out, spread_out, rs_buf, rs_sem):
    def copy(j):
        at = pl.ds(j * PEER_STEP, PEER_STEP)
        return pltpu.make_async_copy(rs.at[at], rs_buf.at[at], rs_sem.at[j])

    for j in range(NSTEP):
        copy(j).start()
    r = lax.broadcasted_iota(jnp.int32, (64, TILE), 0)
    c = lax.broadcasted_iota(jnp.int32, (64, TILE), 1)
    for k in range(SLOTS):
        q, base, at = k // 2, 128 * (k % 2) + 64, 256 + 2 * (k % 2)
        packed = arrived[q, base : base + 64]
        top = jnp.where((c >= 64) | (r < c), packed, 0.0)
        bottom = pltpu.roll(jnp.where((c < 64) & (r > c), packed, 0.0), 64, 1)
        half = jnp.concatenate([top, bottom], axis=0)
        hi_out[k], lo_out[k] = split2(half + half.T)
        diag_out[k] = arrived[q, at : at + 1]
        spread_out[k] = one_hot(arrived[q, at + 1 : at + 2].astype(jnp.int32))
    main, rest = [], []
    for j in range(NSTEP):
        copy(j).wait()
        for q in range(j * PEER_STEP, (j + 1) * PEER_STEP):
            hi0, lo0 = split2(arrived[q, 0:COLS])
            hi1, lo1 = split2(arrived[q, 128 : 128 + COLS])
            main.append(dot(jnp.concatenate([hi0, lo0, hi1, lo1], axis=0), rs_buf[q, 0]))
            rest.append(dot(jnp.concatenate([hi0, hi1], axis=0), rs_buf[q, 1]))
    main, rest = sum(main), sum(rest)
    first = main[:COLS] + main[COLS : 2 * COLS] + rest[:COLS]
    second = main[2 * COLS : 3 * COLS] + main[3 * COLS :] + rest[COLS:]
    total = rr[...] + first[:, :AGG] + second[:, AGG:]
    out[...] = jnp.broadcast_to(pack_rows(total), out.shape)


def first_restrict(arrived, rs, rr):
    return pl.pallas_call(
        first_restrict_kernel,
        in_specs=[
            pl.BlockSpec(memory_space=pltpu.VMEM),
            pl.BlockSpec(memory_space=pl.ANY),
            pl.BlockSpec(memory_space=pltpu.VMEM),
        ],
        out_specs=[pl.BlockSpec(memory_space=pltpu.VMEM)] * 5,
        out_shape=[
            jax.ShapeDtypeStruct((PEERS, 32, TILE), F32),
            near((SLOTS, TILE, TILE), BF16),
            near((SLOTS, TILE, TILE), BF16),
            near((SLOTS, 1, TILE)),
            near((SLOTS, AGG, TILE), BF16),
        ],
        scratch_shapes=[
            pltpu.VMEM((PEERS, 2, TILE, TILE), BF16),
            pltpu.SemaphoreType.DMA((NSTEP,)),
        ],
        compiler_params=params(8),
        name="first_restrict",
    )(pltpu.with_memory_space_constraint(arrived, pltpu.VMEM), hbm(rs), rr)


def gathered_rows(ref, count):
    lane = lax.broadcasted_iota(jnp.int32, (32, TILE), 1) < 64
    tops, bottoms = [], []
    for q in range(0, count, 2):
        a, b = ref[q, 0:32], ref[q + 1, 0:32]
        tops.append(jnp.where(lane, a, pltpu.roll(b, 64, 1)))
        bottoms.append(jnp.where(lane, pltpu.roll(a, 64, 1), b))
    return jnp.concatenate([jnp.concatenate(tops, axis=1), jnp.concatenate(bottoms, axis=1)], axis=0)


def lowest_kernel(arrived, g, x_out, out):
    x = gathered_rows(arrived, PEERS)
    x_out[...] = x
    hi, lo = split2(g[...])
    packed = pack_rows(mm(x, hi, lo, nt=True))
    if arrived.shape[1] == ROWS:
        extra = arrived[0, 32:40]
        for q in range(1, PEERS):
            extra = extra + arrived[q, 32:40]
        packed = jnp.concatenate([packed, extra], axis=0)
    out[...] = jnp.broadcast_to(packed, out.shape)


def lowest_part(arrived, g):
    return pl.pallas_call(
        lowest_kernel,
        out_shape=[
            jax.ShapeDtypeStruct((COLS, NC1), F32),
            jax.ShapeDtypeStruct((GROUPS, arrived.shape[1], TILE), F32),
        ],
        compiler_params=params(6),
        cost_estimate=cost(20_000_000_000, 32 << 20),
        name="lowest_part",
    )(arrived, g)


def level_one(arrived, inverse_rows, g, x_ref, inverse_ref, op_hi, op_lo, e_out):
    low = gathered_rows(arrived, GROUPS)
    hi, lo = split2(inverse_rows[...])
    corr = mm(low, hi, lo, nt=True)
    ghi, glo = split2(g[...])
    lifted = mm(corr, ghi, glo)
    inverse = inverse_ref[...]
    scaled = x_ref[...] * inverse
    total = None
    for i in range(NC1 // 256):
        rows = slice(i * 256, (i + 1) * 256)
        term = mm(scaled[:, rows], op_hi[rows, :], op_lo[rows, :])
        total = term if total is None else total + term
    e = 2.0 * OMEGA * scaled - OMEGA * OMEGA * total * inverse + lifted
    for q in range(PEERS):
        e_out[q] = e[:, q * AGG : (q + 1) * AGG]


def apply_off(x, hi, lo):
    xh, xl = split2(x)
    rows = x.shape[0]
    if x.shape[1] == TILE:
        return dot(beside(xh, xl), jnp.concatenate([hi, hi], axis=0)) + dot(xh, lo)
    both = dot(jnp.concatenate([xh, xl], axis=0), hi)
    return both[:rows] + both[rows:] + dot(xh, lo)


def apply_block(x, diag, hi, lo):
    xh, xl = split2(x)
    kept = xh.astype(F32) + xl.astype(F32)
    return apply_off(x, hi, lo) + kept[:, : diag.shape[1]] * diag


def lift(parts, spread):
    rows = parts.shape[0] // 2
    two = dot(parts, spread)
    return two[:rows] + two[rows:]


def two_parts(e):
    return jnp.concatenate(split2(e), axis=0)


def block(top, side, peer, k):
    return jnp.concatenate([top[k], beside(side[k], peer[k])], axis=0)


def pair_spread(own, peer):
    none = jnp.zeros_like(own)
    return jnp.concatenate([beside(own, none), beside(none, peer)], axis=0)


def forward_kernel(
    member, arrived, inverse_rows, g, x, inverse, op_hi, op_lo, b_slot, b_rest, d_slot, x_peer, d_peer, s_slot, s_peer,
    hi_top, lo_top, hi_side, lo_side, hi_peer, lo_peer, z_rest, w_rest, hi_unit, lo_unit, rr_unit,
    z_out, w_out, ws_out, out, e, acc_rr, acc_bz, acc_zw
):
    level_one(arrived, inverse_rows, g, x, inverse, op_hi, op_lo, e)
    e_own = e.at[pl.ds(member[0], 1)]
    unit_hi, unit_lo = split2(rr_unit[COLS:])
    acc_rr[...] = rr_unit[:COLS] + mm(e_own[0], unit_hi, unit_lo)
    acc_bz[...] = jnp.zeros_like(acc_bz)
    acc_zw[...] = jnp.zeros_like(acc_zw)
    views = (
        e, b_slot, b_rest, d_slot, x_peer, d_peer, s_slot, s_peer, hi_top, lo_top, hi_side, lo_side, hi_peer, lo_peer,
        z_rest, w_rest, hi_unit, lo_unit, ws_out
    )

    @pl.loop(0, CHUNKS)
    def _(step):
        e_peer, *parts = [v.at[part(step, v.shape[0])] for v in views]
        both = [v.at[:, part(step, SLOTS)] for v in (z_out, w_out)]
        forward_step(e_own, e_peer, *parts[:-1], *both, parts[-1], acc_rr, acc_bz, acc_zw)

    packed = pack_rows(acc_rr[...])
    sums = jnp.sum(jnp.concatenate([acc_bz[...], acc_zw[...]], axis=0).T, axis=0, keepdims=True)
    r8 = lax.broadcasted_iota(jnp.int32, (8, TILE), 0)
    extra = jnp.where(r8 == 0, sums, 0.0)
    for q in range(PEERS):
        out[q, 0:32] = packed
        out[q, 32:40] = extra


def part(step, count):
    size = count // CHUNKS
    return pl.ds(step * size, size)


def forward_step(
    e_own, e_peer, b_slot, b_rest, d_slot, x_peer, d_peer, s_slot, s_peer, hi_top, lo_top, hi_side, lo_side,
    hi_peer, lo_peer, z_rest, w_rest, hi_unit, lo_unit, z_out, w_out, ws_out, acc_rr, acc_bz, acc_zw
):
    e_mine = two_parts(e_own[0])
    e_both = [two_parts(beside(e_own[0], e_peer[q])) for q in range(CHUNK // 2)]
    rr, bz, zw = acc_rr[...], acc_bz[...], acc_zw[...]
    pairs = range(CHUNK)
    diag = [beside(d_slot[k], d_peer[k]) for k in pairs]
    rdiag = [OMEGA / d for d in diag]
    mats = [(block(hi_top, hi_side, hi_peer, k), block(lo_top, lo_side, lo_peer, k)) for k in pairs]
    peers = [x_peer[k // 2, (k % 2) * 128 : (k % 2) * 128 + COLS] for k in pairs]
    x1 = [beside(b_slot[k] * rdiag[k][:, :TILE], peers[k]) for k in pairs]
    spread = [s_slot[k] for k in pairs]
    ups = [lift(e_both[k // 2], pair_spread(spread[k], s_peer[k])) for k in pairs]
    x = [start + up for start, up in zip(x1, ups)]
    image = [apply_off(xx, *m) for xx, m in zip(x, mats)]
    z = [(1.0 - OMEGA) * xx + start - im * rd for xx, start, im, rd in zip(x, x1, image, rdiag)]
    w = [apply_block(zz, d, *m) for zz, d, m in zip(z, diag, mats)]
    x1 = [ww * rd for ww, rd in zip(w, rdiag)]
    left = [(m[0][:, :TILE], m[1][:, :TILE]) for m in mats]
    y = [(1.0 - OMEGA) * ww[:, :TILE] - apply_off(xx, *m) for ww, xx, m in zip(w, x1, left)]
    for i in range(0, CHUNK, 2):
        rr = rr + mm_exact(beside(y[i], y[i + 1]), beside(spread[i], spread[i + 1]), nt=True)
    for k in pairs:
        ws_out[k] = w[k][:, TILE:]
    z = [zz[:, :TILE] for zz in z]
    w = [ww[:, :TILE] for ww in w]
    for k in range(CHUNK):
        two = dot(e_mine, hi_unit[k])
        found = two[:COLS] + two[COLS:] + dot(e_mine[:COLS], lo_unit[k])
        z.append(z_rest[k] + found[:, :TILE])
        w.append(w_rest[k] + found[:, TILE:])
    for i in range(2 * CHUNK):
        bz = bz + (b_slot if i < CHUNK else b_rest)[i % CHUNK] * z[i]
        zw = zw + z[i] * w[i]
        z_out[i // CHUNK, i % CHUNK] = z[i]
        w_out[i // CHUNK, i % CHUNK] = w[i]
    acc_rr[...] = rr
    acc_bz[...] = bz
    acc_zw[...] = zw


def specs(smem, vmem):
    return [pl.BlockSpec(memory_space=pltpu.SMEM)] * smem + [pl.BlockSpec(memory_space=pltpu.VMEM)] * vmem


def forward_part(scalars, arrays):
    return pl.pallas_call(
        forward_kernel,
        in_specs=specs(len(scalars), len(arrays)),
        out_specs=specs(0, 4),
        out_shape=[
            near((2, SLOTS, COLS, TILE)),
            near((2, SLOTS, COLS, TILE)),
            near((SLOTS, COLS, TILE)),
            jax.ShapeDtypeStruct((PEERS, ROWS, TILE), F32),
        ],
        scratch_shapes=[
            pltpu.VMEM((PEERS, COLS, AGG), F32),
            pltpu.VMEM((COLS, AGG), F32),
            pltpu.VMEM((COLS, TILE), F32),
            pltpu.VMEM((COLS, TILE), F32),
        ],
        compiler_params=params(10),
        name="forward_part",
    )(*scalars, *arrays)


def second_kernel(
    member, arrived, inverse_rows, g, x, inverse, op_hi, op_lo, b_slot, b_rest, d_slot, d_rest, d_peer, s_slot, s_rest, s_peer,
    hi_top, lo_top, hi_side, lo_side, hi_peer, lo_peer, hi_rest, lo_rest, z_in, w_in, w_peer, v_out, u_out, out, dots, e, acc_a, acc_b, acc_c, acc_alpha
):
    extra = arrived[0, 32:40]
    for q in range(1, GROUPS):
        extra = extra + arrived[q, 32:40]
    dots[...] = extra
    level_one(arrived, inverse_rows, g, x, inverse, op_hi, op_lo, e)
    acc_a[...] = jnp.zeros_like(acc_a)
    acc_b[...] = jnp.zeros_like(acc_b)
    acc_c[...] = jnp.zeros_like(acc_c)
    col = column(dots[0:1])
    acc_alpha[...] = col[:COLS] / col[COLS:]
    e_own = e.at[pl.ds(member[0], 1)]
    views = (e, b_slot, b_rest, d_slot, d_rest, d_peer, s_slot, s_rest, s_peer, hi_top, lo_top, hi_side, lo_side, hi_peer, lo_peer, hi_rest, lo_rest, w_peer)

    @pl.loop(0, CHUNKS)
    def _(step):
        e_peer, *parts = [v.at[part(step, v.shape[0])] for v in views]
        z_part, w_part, v_part, u_part = [v.at[:, part(step, SLOTS)] for v in (z_in, w_in, v_out, u_out)]
        second_step(
            e_own, e_peer, *parts[:-1], z_part, w_part, parts[-1], v_part, u_part,
            acc_a, acc_b, acc_c, acc_alpha
        )

    first = jnp.sum(jnp.concatenate([acc_a[...], acc_b[...]], axis=0).T, axis=0, keepdims=True)
    last = jnp.sum(jnp.concatenate([acc_c[...], acc_c[...]], axis=0).T, axis=0, keepdims=True)
    out[...] = jnp.broadcast_to(jnp.concatenate([first, last], axis=0), out.shape)


def second_step(
    e_own, e_peer, b_slot, b_rest, d_slot, d_rest, d_peer, s_slot, s_rest, s_peer,
    hi_top, lo_top, hi_side, lo_side, hi_peer, lo_peer, hi_rest, lo_rest, z_in, w_in, w_peer, v_out, u_out, acc_a, acc_b, acc_c, acc_alpha
):
    alpha = acc_alpha[...]
    e_mine = two_parts(e_own[0])
    e_both = [two_parts(beside(e_own[0], e_peer[q])) for q in range(CHUNK // 2)]
    sums = [acc_a[...], acc_b[...], acc_c[...]]

    def gather(b, z, w, v, u):
        r1 = b - alpha * w
        z1 = z - alpha * v
        az1 = w - alpha * u
        sums[0] = sums[0] + r1 * z1
        sums[1] = sums[1] + z1 * az1
        sums[2] = sums[2] + (z1 * w + z * az1)

    pairs, rest = range(CHUNK), range(CHUNK)
    diag = [jnp.concatenate([d_slot[k], d_peer[k]], axis=1) for k in pairs] + [d_rest[k] for k in rest]
    rdiag = [OMEGA / d for d in diag]
    mats = [(block(hi_top, hi_side, hi_peer, k), block(lo_top, lo_side, lo_peer, k)) for k in pairs]
    mats = mats + [(hi_rest[k], lo_rest[k]) for k in rest]
    w = [jnp.concatenate([w_in[0, k], w_peer[k]], axis=1) for k in pairs] + [w_in[1, k] for k in rest]
    spread = [s_slot[k] for k in pairs] + [s_rest[k] for k in rest]
    ups = [lift(e_both[k // 2], pair_spread(spread[k], s_peer[k])) for k in pairs]
    ups = ups + [lift(e_mine, sp) for sp in spread[CHUNK:]]
    x1 = [ww * rd for ww, rd in zip(w, rdiag)]
    x = [start + up for start, up in zip(x1, ups)]
    image = [apply_off(xx, *m) for xx, m in zip(x, mats)]
    v = [(1.0 - OMEGA) * xx + start - im * rd for xx, start, im, rd in zip(x, x1, image, rdiag)]
    left = [(m[0][:, :TILE], m[1][:, :TILE]) for m in mats]
    u = [apply_block(vv, d[:, :TILE], *m) for vv, d, m in zip(v, diag, left)]
    for i in range(2 * CHUNK):
        vv, b_ref = v[i][:, :TILE], (b_slot if i < CHUNK else b_rest)
        v_out[i // CHUNK, i % CHUNK] = vv
        u_out[i // CHUNK, i % CHUNK] = u[i]
        gather(b_ref[i % CHUNK], z_in[i // CHUNK, i % CHUNK], w[i][:, :TILE], vv, u[i])
    acc_a[...] = sums[0]
    acc_b[...] = sums[1]
    acc_c[...] = sums[2]


def second_part(scalars, arrays):
    return pl.pallas_call(
        second_kernel,
        in_specs=specs(len(scalars), len(arrays)),
        out_specs=specs(0, 4),
        out_shape=[
            near((2, SLOTS, COLS, TILE)),
            near((2, SLOTS, COLS, TILE)),
            jax.ShapeDtypeStruct((GROUPS * PEERS, 2, TILE), F32),
            jax.ShapeDtypeStruct((8, TILE), F32),
        ],
        scratch_shapes=[pltpu.VMEM((PEERS, COLS, AGG), F32)] + [pltpu.VMEM((COLS, TILE), F32)] * 4,
        compiler_params=params(10),
        name="second_part",
    )(*scalars, *arrays)


def combine_kernel(where, dots, arrived, b, z, w, v, u, solution, residual, sol_buf, res_buf, sem):
    total = jnp.sum(arrived[...], axis=0)
    old = column(dots[0:1])
    one = column(total[0:1])
    two = column(total[1:2])
    rho, zw = old[:COLS], old[COLS:]
    rho_next, zz = one[:COLS], one[COLS:]
    alpha = rho / zw
    beta = rho_next / rho
    alpha_next = rho_next / (zz + beta * two[:COLS] + beta * beta * zw)
    first = alpha + alpha_next * (1.0 + beta)
    second = alpha_next * alpha

    def copies(i):
        at = pl.ds(i * (STEP * TILE), STEP * TILE)
        return (
            pltpu.make_async_copy(sol_buf.at[:, at], solution.at[:, at], sem.at[0, i]),
            pltpu.make_async_copy(res_buf.at[:, at], residual.at[:, at], sem.at[1, i]),
        )

    for i in range(BLK // STEP):
        for t in range(i * STEP, (i + 1) * STEP):
            half, k = where[t] // SLOTS, lax.rem(where[t], SLOTS)
            at = slice(t * TILE, (t + 1) * TILE)
            sol_buf[:, at] = first * z[half, k] - second * v[half, k]
            res_buf[:, at] = b[:, at] - first * w[half, k] + second * u[half, k]
        for copy in copies(i):
            copy.start()
    for i in range(BLK // STEP):
        for copy in copies(i):
            copy.wait()


def combine(where, dots, arrived, b, z, w, v, u):
    return pl.pallas_call(
        combine_kernel,
        in_specs=specs(1, 7),
        out_specs=[pl.BlockSpec(memory_space=pl.ANY)] * 2,
        out_shape=[far((COLS, BLK * TILE))] * 2,
        scratch_shapes=[
            pltpu.VMEM((COLS, BLK * TILE), F32),
            pltpu.VMEM((COLS, BLK * TILE), F32),
            pltpu.SemaphoreType.DMA((2, BLK // STEP)),
        ],
        compiler_params=params(8),
        name="combine",
    )(where, dots, arrived, b, z, w, v, u)


def exchange(x, axes):
    return lax.all_to_all(x, axes, 0, 0, tiled=True)


def on_device(
    right_side,
    diag_tiles,
    remote_tiles,
    slot_counts,
    slot_blocks,
    fine_map,
    coarse_map,
    level1_ops,
    coarsest_inverse,
):
    group = lax.axis_index("grp")
    member = lax.axis_index(GROUP_AXES).astype(jnp.int32).reshape(1)
    slot_list = slot_blocks.reshape(SLOTS)
    counts = slot_counts.reshape(PEERS)
    maps = fine_map.reshape(BLK, TILE)
    remote = remote_tiles.reshape(SLOTS, TILE, TILE)
    operator = level1_ops[0]

    outgoing = boundary_pack(slot_blocks, diag_tiles, right_side, maps)
    side = exchange(outgoing, GROUP_AXES)

    tile_ids = jnp.arange(BLK, dtype=jnp.int32)
    free = jnp.logical_not(jnp.any(slot_list[:, None] == tile_ids[None, :], axis=0)).astype(jnp.int32)
    rank = jnp.sum(jnp.where(tile_ids[None, :] < tile_ids[:, None], free[None, :], 0), axis=1)
    chosen = (rank[None, :] == jnp.arange(SLOTS, dtype=jnp.int32)[:, None]) & (free[None, :] == 1)
    rest_list = jnp.sum(jnp.where(chosen, tile_ids[None, :], 0), axis=1)
    perm = jnp.concatenate([slot_list, rest_list])
    where = jnp.sum(jnp.where(perm[None, :] == tile_ids[:, None], tile_ids[None, :], 0), axis=1)

    *local, rs, rr_local = local_part(
        perm, counts, diag_tiles, right_side, remote, maps
    )
    b_slot, b_rest, d_slot, d_rest, hi_rest, lo_rest, hi_top, lo_top, hi_side, lo_side, s_slot, s_rest = local[:12]
    affine = tuple(local[12:])
    g, inverse, op_hi, op_lo = coarse_setup(operator, coarse_map.reshape(1, NC1))
    inverse_rows = lax.dynamic_slice_in_dim(coarsest_inverse, group * AGG, AGG, 0)

    rr_local, g, inverse_rows, member, where = lax.optimization_barrier(
        (rr_local, g, inverse_rows, member, where)
    )
    outgoing, hi_peer, lo_peer, d_peer, s_peer = first_restrict(side, rs, rr_local)
    gathered = exchange(outgoing, GROUP_AXES)

    scalars = (member,)
    x, outgoing = lowest_part(gathered, g)
    coarse = (exchange(outgoing, "grp"), inverse_rows, g, x, inverse)
    pairs = (hi_top, lo_top, hi_side, lo_side, hi_peer, lo_peer)
    z, w, w_peer, outgoing = forward_part(
        scalars, coarse + (op_hi, op_lo, b_slot, b_rest, d_slot, side, d_peer, s_slot, s_peer) + pairs + affine
    )
    x, outgoing = lowest_part(exchange(outgoing, GROUP_AXES), g)
    coarse = (exchange(outgoing, "grp"), inverse_rows, g, x, inverse)
    v, u, outgoing, dots = second_part(
        scalars,
        coarse
        + (op_hi, op_lo, b_slot, b_rest, d_slot, d_rest, d_peer, s_slot, s_rest, s_peer)
        + pairs
        + (hi_rest, lo_rest, z, w, w_peer),
    )
    sums = exchange(outgoing, ALL_AXES)
    return tuple(combine(where, dots, sums, right_side, z, w, v, u))


def solution(mesh):
    placed = (
        P(None, ("grp", "sub", "chip")),
        P(("grp", "sub", "chip"), None, None),
        P(("grp", "sub", "chip"), None, None, None),
        P(("grp", "sub", "chip"), None),
        P(("grp", "sub", "chip"), None, None),
        P(("grp", "sub", "chip")),
        P("grp"),
        P("grp", None, None),
        P(),
    )
    return jax.shard_map(
        on_device,
        mesh=mesh,
        in_specs=placed,
        out_specs=(P(None, ("grp", "sub", "chip")), P(None, ("grp", "sub", "chip"))),
        check_vma=False,
    )
```

```python
import functools

import jax
import jax.numpy as jnp
from jax import lax
from jax.experimental import pallas as pl
from jax.experimental.pallas import tpu as pltpu
from jax.sharding import PartitionSpec as P

OMEGA = 0.6
F32 = jnp.float32
BF16 = jnp.bfloat16
COLS = 64
TILE = 128
BLK = 64
SLOTS = 32
PEERS = 16
GROUPS = 8
AGG = 64
NC1 = 1024
STEP = 8
NSTEP = SLOTS // STEP
CHUNK = 16
CHUNKS = SLOTS // CHUNK
SIDE = 264
PEER_STEP = 4
ROWS = 40

GROUP_AXES = ("sub", "chip")
ALL_AXES = ("grp", "sub", "chip")


def params(mib=20):
    return pltpu.CompilerParams(vmem_limit_bytes=mib * 1024 * 1024)


def hbm(x):
    return pltpu.with_memory_space_constraint(x, pltpu.HBM)


def near(shape, dtype=F32):
    return pltpu.VMEM(shape, dtype)


def far(shape, dtype=F32):
    return pltpu.HBM(shape, dtype)


def cost(flops, moved):
    return pl.CostEstimate(flops=flops, bytes_accessed=moved, transcendentals=0)


def split2(x):
    hi = x.astype(BF16)
    lo = (x - hi.astype(F32)).astype(BF16)
    return hi, lo


def dot(a, b):
    return jnp.dot(a, b, preferred_element_type=F32)


def dot_nt(a, b):
    return lax.dot_general(a, b, (((1,), (1,)), ((), ())), preferred_element_type=F32)


def mm(x, whi, wlo, nt=False):
    op = dot_nt if nt else dot
    rows = x.shape[0]
    hi, lo = split2(x)
    both = op(jnp.concatenate([hi, lo], axis=0), whi)
    return both[:rows] + both[rows:] + op(hi, wlo)


def mm_exact(x, w, nt=False):
    op = dot_nt if nt else dot
    rows = x.shape[0]
    two = op(jnp.concatenate(split2(x), axis=0), w)
    return two[:rows] + two[rows:]


def beside(a, b):
    return jnp.concatenate([a, b], axis=1)


def eye_mask():
    r = lax.broadcasted_iota(jnp.int32, (TILE, TILE), 0)
    c = lax.broadcasted_iota(jnp.int32, (TILE, TILE), 1)
    return r, c


def tile_diag(tile):
    r, c = eye_mask()
    return jnp.sum(jnp.where(r == c, tile, 0.0), axis=0, keepdims=True)


def off_diag(tile):
    r, c = eye_mask()
    return jnp.where(r == c, 0.0, tile)


def one_hot(row):
    r = lax.broadcasted_iota(jnp.int32, (AGG, row.shape[1]), 0)
    return jnp.where(r == row, 1.0, 0.0).astype(BF16)


def pack_rows(x):
    wide = jnp.concatenate([x[:32], x[32:]], axis=1)
    return wide


def column(row):
    return jnp.broadcast_to(row, (TILE, TILE)).T


def boundary_kernel(slots_in, maps, tiles, cols, out, slots, slot_sem, map_buf, tile_buf, col_buf, out_buf, map_sem, col_sem, tile_sem, out_sem):
    def tile_copy(j):
        return pltpu.make_async_copy(tiles.at[slots[0, j % 2, j // 2]], tile_buf.at[j], tile_sem.at[j])

    def col_copy(j):
        at = pl.ds(pl.multiple_of(slots[0, j % 2, j // 2] * TILE, TILE), TILE)
        return pltpu.make_async_copy(cols.at[:, at], col_buf.at[j], col_sem.at[j])

    def out_copy(j):
        at = pl.ds(j // 2, PEER_STEP)
        return pltpu.make_async_copy(out_buf.at[at], out.at[at], out_sem.at[j // STEP])

    slot_copy = pltpu.make_async_copy(slots_in, slots, slot_sem)
    slot_copy.start()
    map_copy = pltpu.make_async_copy(maps, map_buf, map_sem)
    map_copy.start()
    slot_copy.wait()
    for j in range(SLOTS):
        tile_copy(j).start()
        col_copy(j).start()
    r = lax.broadcasted_iota(jnp.int32, (64, TILE), 0)
    c = lax.broadcasted_iota(jnp.int32, (64, TILE), 1)
    r8 = lax.broadcasted_iota(jnp.int32, (8, TILE), 0)
    map_copy.wait()
    for j in range(0, SLOTS, STEP):
        for k in range(j, j + STEP):
            tile_copy(k).wait()
            col_copy(k).wait()
        tile = [tile_buf[k] for k in range(j, j + STEP)]
        diag = [tile_diag(t) for t in tile]
        for k in range(j, j + STEP):
            t, d = tile[k - j], diag[k - j]
            q, base = k // 2, (k % 2) * 128
            out_buf[q, base : base + 64] = col_buf[k] * (OMEGA / d)
            below = pltpu.roll(t[64:], 64, 1)
            out_buf[q, base + 64 : base + 128] = jnp.where((c < 64) & (r > c), below, t[:64])
        for k in range(j, j + STEP, 2):
            own = [map_buf[pl.ds(slots[0, i, k // 2], 1)].astype(F32) for i in range(2)]
            d0, d1 = diag[k - j], diag[k - j + 1]
            out_buf[k // 2, 256:264] = jnp.where(
                r8 == 0, d0, jnp.where(r8 == 1, own[0], jnp.where(r8 == 2, d1, jnp.where(r8 == 3, own[1], 0.0)))
            )
        out_copy(j).start()
    for j in range(0, SLOTS, STEP):
        out_copy(j).wait()


def boundary_pack(slot_blocks, diag_tiles, right_side, maps):
    return pl.pallas_call(
        boundary_kernel,
        in_specs=[pl.BlockSpec(memory_space=pl.ANY)] * 4,
        out_specs=pl.BlockSpec(memory_space=pl.ANY),
        out_shape=far((PEERS, SIDE, TILE)),
        scratch_shapes=[
            pltpu.SMEM((1, 2, PEERS), jnp.int32),
            pltpu.SemaphoreType.DMA,
            pltpu.VMEM((BLK, TILE), jnp.int32),
            pltpu.VMEM((SLOTS, TILE, TILE), F32),
            pltpu.VMEM((SLOTS, COLS, TILE), F32),
            pltpu.VMEM((PEERS, SIDE, TILE), F32),
            pltpu.SemaphoreType.DMA,
            pltpu.SemaphoreType.DMA((SLOTS,)),
            pltpu.SemaphoreType.DMA((SLOTS,)),
            pltpu.SemaphoreType.DMA((NSTEP,)),
        ],
        compiler_params=params(),
        name="boundary_pack",
    )(hbm(slot_blocks.transpose(0, 2, 1)), hbm(maps), hbm(diag_tiles), hbm(right_side))


def local_kernel(perm, counts, *refs):
    n = 2 * STEP
    tiles, cols = refs[:n], refs[n : 2 * n]
    remote, maps = refs[2 * n : 2 * n + 2]
    b_slot, b_rest, d_slot, hi_top, lo_top, hi_side, lo_side, s_slot = refs[2 * n + 2 : 2 * n + 10]
    z_rest, w_rest, v_rest, u_rest, hi_unit, lo_unit, rr_unit, rs, rr = refs[2 * n + 10 :]
    step = pl.program_id(0)

    @pl.when(step == 0)
    def _():
        rr[...] = jnp.zeros_like(rr)
        rr_unit[...] = jnp.zeros_like(rr_unit)

    index = [perm[(0 if i < STEP else SLOTS) + step * STEP + i % STEP] for i in range(n)]
    tile = [tiles[i][0] for i in range(n)]
    diag = [tile_diag(t) for t in tile]
    off = [split2(off_diag(t)) for t in tile]
    b = [cols[i][...] for i in range(n)]
    x = [OMEGA * bb / d for bb, d in zip(b, diag)]
    spread = [one_hot(maps[pl.ds(i, 1)]) for i in index]
    rest = range(STEP, n)
    rdiag = [OMEGA / diag[i] for i in rest]
    start = [jnp.concatenate([x[i], jnp.zeros_like(x[i])], axis=0) for i in rest]
    both = [jnp.concatenate([x[i], spread[i].astype(F32)], axis=0) for i in rest]
    image = [apply_off(xx, *off[i]) for xx, i in zip(both, rest)]
    z = [(1.0 - OMEGA) * xx + st - im * rd for xx, st, im, rd in zip(both, start, image, rdiag)]
    w = [apply_block(zz, diag[i], *off[i]) for zz, i in zip(z, rest)]
    start = [ww * rd for ww, rd in zip(w, rdiag)]
    again = [apply_off(xx, *off[i]) for xx, i in zip(start, rest)]
    left = [(1.0 - OMEGA) * ww - im for ww, im in zip(w, again)]
    v = [(2.0 - OMEGA) * xx - im * rd for xx, im, rd in zip(start, again, rdiag)]
    u = [apply_block(vv, diag[i], *off[i]) for vv, i in zip(v, rest)]
    unit_total = rr_unit[...]
    for k in range(0, STEP, 2):
        pair = beside(spread[STEP + k], spread[STEP + k + 1])
        unit_total = unit_total + mm_exact(beside(left[k], left[k + 1]), pair, nt=True)
    rr_unit[...] = unit_total
    for k in range(STEP):
        z_rest[k] = z[k][:COLS]
        w_rest[k] = w[k][:COLS]
        v_rest[k] = v[k][:COLS]
        u_rest[k] = u[k][:COLS]
        units = [beside(v[k][COLS:], u[k][COLS:]), beside(z[k][COLS:], w[k][COLS:])]
        hi_unit[k], lo_unit[k] = split2(jnp.concatenate(units, axis=0))
    y = [b[i] - OMEGA * b[i] - mm(x[i], *off[i]) for i in range(STEP)]
    y = y + [b[i] - OMEGA * b[i] - im[:COLS] for i, im in zip(rest, image)]
    total = rr[...]
    for i in range(0, n, 2):
        total = total + mm_exact(beside(y[i], y[i + 1]), beside(spread[i], spread[i + 1]), nt=True)
    for k in range(STEP):
        b_slot[k] = b[k]
        d_slot[k] = diag[k]
        b_rest[k] = b[STEP + k]
        s_slot[k] = spread[k]
    coupling, turned, restricted = [], [], []
    for k in range(STEP):
        j = step * STEP + k
        live = (j % 2) < counts[j // 2]
        scaled = remote[k] * jnp.where(live, -1.0, 0.0)
        coupling.append(split2(scaled))
        turned.append(split2(scaled.T))
    for k in range(STEP):
        restricted.append(-(dot_nt(coupling[k][0], spread[k]) + dot_nt(coupling[k][1], spread[k])))
        hi_top[k] = beside(off[k][0], turned[k][0])
        lo_top[k] = beside(off[k][1], turned[k][1])
        hi_side[k], lo_side[k] = coupling[k]
    for q in range(PEER_STEP):
        rs[q, 0], rs[q, 1] = split2(beside(restricted[2 * q], restricted[2 * q + 1]))
    rr[...] = total


def local_part(perm, counts, diag_tiles, right_side, remote, maps):
    def where(i):
        return (0 if i < STEP else SLOTS) + i % STEP

    def tile_spec(i):
        return pl.BlockSpec((1, TILE, TILE), lambda s, p, c: (p[s * STEP + where(i)], 0, 0))

    def col_spec(i):
        return pl.BlockSpec((COLS, TILE), lambda s, p, c: (0, p[s * STEP + where(i)]))

    def out(*shape):
        return pl.BlockSpec((STEP,) + shape, lambda s, p, c: (s, 0, 0))

    n = 2 * STEP
    grid = pltpu.PrefetchScalarGridSpec(
        num_scalar_prefetch=2,
        grid=(NSTEP,),
        in_specs=[tile_spec(i) for i in range(n)]
        + [col_spec(i) for i in range(n)]
        + [
            pl.BlockSpec((STEP, TILE, TILE), lambda s, p, c: (s, 0, 0)),
            pl.BlockSpec((BLK, TILE), lambda s, p, c: (0, 0)),
        ],
        out_specs=[
            out(COLS, TILE),
            out(COLS, TILE),
            out(1, TILE),
            out(TILE, 2 * TILE),
            out(TILE, 2 * TILE),
            out(TILE, TILE),
            out(TILE, TILE),
            out(AGG, TILE),
            out(COLS, TILE),
            out(COLS, TILE),
            out(COLS, TILE),
            out(COLS, TILE),
            out(2 * AGG, 2 * TILE),
            out(2 * AGG, 2 * TILE),
            pl.BlockSpec((COLS + AGG, AGG), lambda s, p, c: (0, 0)),
            pl.BlockSpec((PEER_STEP, 2, TILE, TILE), lambda s, p, c: (s, 0, 0, 0)),
            pl.BlockSpec((COLS, AGG), lambda s, p, c: (0, 0)),
        ],
    )

    def sds(shape, dtype=F32):
        return far((SLOTS,) + shape, dtype)

    return pl.pallas_call(
        local_kernel,
        grid_spec=grid,
        out_shape=[
            sds((COLS, TILE)),
            sds((COLS, TILE)),
            sds((1, TILE)),
            sds((TILE, 2 * TILE), BF16),
            sds((TILE, 2 * TILE), BF16),
            sds((TILE, TILE), BF16),
            sds((TILE, TILE), BF16),
            sds((AGG, TILE), BF16),
            sds((COLS, TILE)),
            sds((COLS, TILE)),
            sds((COLS, TILE)),
            sds((COLS, TILE)),
            sds((2 * AGG, 2 * TILE), BF16),
            sds((2 * AGG, 2 * TILE), BF16),
            jax.ShapeDtypeStruct((COLS + AGG, AGG), F32),
            far((PEERS, 2, TILE, TILE), BF16),
            jax.ShapeDtypeStruct((COLS, AGG), F32),
        ],
        compiler_params=params(),
        cost_estimate=cost(2 * 64 * 3 * 64 * 128 * 128, 16 << 20),
        name="local_part",
    )(perm, counts, *([hbm(diag_tiles)] * n), *([hbm(right_side)] * n), hbm(remote), maps)


def coarse_kernel(op, cmap, g_out, d_out, hi_out, lo_out):
    spread = one_hot(cmap[...])
    product = None
    for i in range(NC1 // 256):
        rows = slice(i * 256, (i + 1) * 256)
        hi, lo = split2(op[rows, :])
        hi_out[rows, :] = hi
        lo_out[rows, :] = lo
        term = dot(spread[:, rows], hi) + dot(spread[:, rows], lo)
        product = term if product is None else product + term
    pieces = []
    for i in range(NC1 // TILE):
        pieces.append(tile_diag(op[i * TILE : (i + 1) * TILE, i * TILE : (i + 1) * TILE]))
    diag = jnp.concatenate(pieces, axis=1)
    inverse = 1.0 / diag
    d_out[...] = inverse
    g_out[...] = spread.astype(F32) - OMEGA * product * inverse


def coarse_setup(op, cmap):
    return pl.pallas_call(
        coarse_kernel,
        out_shape=[
            jax.ShapeDtypeStruct((AGG, NC1), F32),
            jax.ShapeDtypeStruct((1, NC1), F32),
            far((NC1, NC1), BF16),
            far((NC1, NC1), BF16),
        ],
        compiler_params=params(),
        cost_estimate=cost(2 * 2 * 64 * 1024 * 1024, 5 << 20),
        name="coarse_setup",
    )(op, cmap)


def first_restrict_kernel(arrived, rs, rr, out, hi_out, lo_out, diag_out, spread_out, rs_buf, rs_sem):
    def copy(j):
        at = pl.ds(j * PEER_STEP, PEER_STEP)
        return pltpu.make_async_copy(rs.at[at], rs_buf.at[at], rs_sem.at[j])

    for j in range(NSTEP):
        copy(j).start()
    r = lax.broadcasted_iota(jnp.int32, (64, TILE), 0)
    c = lax.broadcasted_iota(jnp.int32, (64, TILE), 1)
    for k in range(SLOTS):
        q, base, at = k // 2, 128 * (k % 2) + 64, 256 + 2 * (k % 2)
        packed = arrived[q, base : base + 64]
        top = jnp.where((c >= 64) | (r < c), packed, 0.0)
        bottom = pltpu.roll(jnp.where((c < 64) & (r > c), packed, 0.0), 64, 1)
        half = jnp.concatenate([top, bottom], axis=0)
        hi_out[k], lo_out[k] = split2(half + half.T)
        diag_out[k] = arrived[q, at : at + 1]
        spread_out[k] = one_hot(arrived[q, at + 1 : at + 2].astype(jnp.int32))
    main, rest = [], []
    for j in range(NSTEP):
        copy(j).wait()
        for q in range(j * PEER_STEP, (j + 1) * PEER_STEP):
            hi0, lo0 = split2(arrived[q, 0:COLS])
            hi1, lo1 = split2(arrived[q, 128 : 128 + COLS])
            main.append(dot(jnp.concatenate([hi0, lo0, hi1, lo1], axis=0), rs_buf[q, 0]))
            rest.append(dot(jnp.concatenate([hi0, hi1], axis=0), rs_buf[q, 1]))
    main, rest = sum(main), sum(rest)
    first = main[:COLS] + main[COLS : 2 * COLS] + rest[:COLS]
    second = main[2 * COLS : 3 * COLS] + main[3 * COLS :] + rest[COLS:]
    total = rr[...] + first[:, :AGG] + second[:, AGG:]
    out[...] = jnp.broadcast_to(pack_rows(total), out.shape)


def first_restrict(arrived, rs, rr):
    return pl.pallas_call(
        first_restrict_kernel,
        in_specs=[
            pl.BlockSpec(memory_space=pltpu.VMEM),
            pl.BlockSpec(memory_space=pl.ANY),
            pl.BlockSpec(memory_space=pltpu.VMEM),
        ],
        out_specs=[pl.BlockSpec(memory_space=pltpu.VMEM)] * 5,
        out_shape=[
            jax.ShapeDtypeStruct((PEERS, 32, TILE), F32),
            near((SLOTS, TILE, TILE), BF16),
            near((SLOTS, TILE, TILE), BF16),
            near((SLOTS, 1, TILE)),
            near((SLOTS, AGG, TILE), BF16),
        ],
        scratch_shapes=[
            pltpu.VMEM((PEERS, 2, TILE, TILE), BF16),
            pltpu.SemaphoreType.DMA((NSTEP,)),
        ],
        compiler_params=params(8),
        name="first_restrict",
    )(pltpu.with_memory_space_constraint(arrived, pltpu.VMEM), hbm(rs), rr)


def gathered_rows(ref, count):
    lane = lax.broadcasted_iota(jnp.int32, (32, TILE), 1) < 64
    tops, bottoms = [], []
    for q in range(0, count, 2):
        a, b = ref[q, 0:32], ref[q + 1, 0:32]
        tops.append(jnp.where(lane, a, pltpu.roll(b, 64, 1)))
        bottoms.append(jnp.where(lane, pltpu.roll(a, 64, 1), b))
    return jnp.concatenate([jnp.concatenate(tops, axis=1), jnp.concatenate(bottoms, axis=1)], axis=0)


def lowest_kernel(arrived, g, x_out, out):
    x = gathered_rows(arrived, PEERS)
    x_out[...] = x
    hi, lo = split2(g[...])
    packed = pack_rows(mm(x, hi, lo, nt=True))
    if arrived.shape[1] == ROWS:
        extra = arrived[0, 32:40]
        for q in range(1, PEERS):
            extra = extra + arrived[q, 32:40]
        packed = jnp.concatenate([packed, extra], axis=0)
    out[...] = jnp.broadcast_to(packed, out.shape)


def lowest_part(arrived, g):
    return pl.pallas_call(
        lowest_kernel,
        out_shape=[
            jax.ShapeDtypeStruct((COLS, NC1), F32),
            jax.ShapeDtypeStruct((GROUPS, arrived.shape[1], TILE), F32),
        ],
        compiler_params=params(6),
        cost_estimate=cost(20_000_000_000, 32 << 20),
        name="lowest_part",
    )(arrived, g)


def level_one(arrived, inverse_rows, g, x_ref, inverse_ref, op_hi, op_lo, e_out):
    low = gathered_rows(arrived, GROUPS)
    hi, lo = split2(inverse_rows[...])
    corr = mm(low, hi, lo, nt=True)
    ghi, glo = split2(g[...])
    lifted = mm(corr, ghi, glo)
    inverse = inverse_ref[...]
    scaled = x_ref[...] * inverse
    total = None
    for i in range(NC1 // 256):
        rows = slice(i * 256, (i + 1) * 256)
        term = mm(scaled[:, rows], op_hi[rows, :], op_lo[rows, :])
        total = term if total is None else total + term
    e = 2.0 * OMEGA * scaled - OMEGA * OMEGA * total * inverse + lifted
    for q in range(PEERS):
        e_out[q] = e[:, q * AGG : (q + 1) * AGG]


def apply_off(x, hi, lo):
    xh, xl = split2(x)
    rows = x.shape[0]
    if x.shape[1] == TILE:
        return dot(beside(xh, xl), jnp.concatenate([hi, hi], axis=0)) + dot(xh, lo)
    both = dot(jnp.concatenate([xh, xl], axis=0), hi)
    return both[:rows] + both[rows:] + dot(xh, lo)


def apply_block(x, diag, hi, lo):
    xh, xl = split2(x)
    kept = xh.astype(F32) + xl.astype(F32)
    return apply_off(x, hi, lo) + kept[:, : diag.shape[1]] * diag


def lift(parts, spread):
    rows = parts.shape[0] // 2
    two = dot(parts, spread)
    return two[:rows] + two[rows:]


def two_parts(e):
    return jnp.concatenate(split2(e), axis=0)


def block(top, side, peer, k):
    return jnp.concatenate([top[k], beside(side[k], peer[k])], axis=0)


def pair_spread(own, peer):
    none = jnp.zeros_like(own)
    return jnp.concatenate([beside(own, none), beside(none, peer)], axis=0)


def forward_kernel(
    member, arrived, inverse_rows, g, x, inverse, op_hi, op_lo, b_slot, b_rest, d_slot, x_peer, d_peer, s_slot, s_peer,
    hi_top, lo_top, hi_side, lo_side, hi_peer, lo_peer, z_rest, w_rest, hi_unit, lo_unit, rr_unit,
    z_out, w_out, ws_out, out, e_keep, e, acc_rr, acc_bz, acc_zw
):
    level_one(arrived, inverse_rows, g, x, inverse, op_hi, op_lo, e)
    e_own = e.at[pl.ds(member[0], 1)]
    e_keep[...] = e_own[0]
    unit_hi, unit_lo = split2(rr_unit[COLS:])
    acc_rr[...] = rr_unit[:COLS] + mm(e_own[0], unit_hi, unit_lo)
    acc_bz[...] = jnp.zeros_like(acc_bz)
    acc_zw[...] = jnp.zeros_like(acc_zw)
    views = (
        e, b_slot, b_rest, d_slot, x_peer, d_peer, s_slot, s_peer, hi_top, lo_top, hi_side, lo_side, hi_peer, lo_peer,
        z_rest, w_rest, hi_unit, lo_unit, ws_out
    )

    @pl.loop(0, CHUNKS)
    def _(step):
        e_peer, *parts = [v.at[part(step, v.shape[0])] for v in views]
        both = [v.at[:, part(step, SLOTS)] for v in (z_out, w_out)]
        forward_step(e_own, e_peer, *parts[:-1], *both, parts[-1], acc_rr, acc_bz, acc_zw)

    packed = pack_rows(acc_rr[...])
    sums = jnp.sum(jnp.concatenate([acc_bz[...], acc_zw[...]], axis=0).T, axis=0, keepdims=True)
    r8 = lax.broadcasted_iota(jnp.int32, (8, TILE), 0)
    extra = jnp.where(r8 == 0, sums, 0.0)
    for q in range(PEERS):
        out[q, 0:32] = packed
        out[q, 32:40] = extra


def part(step, count):
    size = count // CHUNKS
    return pl.ds(step * size, size)


def forward_step(
    e_own, e_peer, b_slot, b_rest, d_slot, x_peer, d_peer, s_slot, s_peer, hi_top, lo_top, hi_side, lo_side,
    hi_peer, lo_peer, z_rest, w_rest, hi_unit, lo_unit, z_out, w_out, ws_out, acc_rr, acc_bz, acc_zw
):
    e_mine = two_parts(e_own[0])
    e_both = [two_parts(beside(e_own[0], e_peer[q])) for q in range(CHUNK // 2)]
    rr, bz, zw = acc_rr[...], acc_bz[...], acc_zw[...]
    pairs = range(CHUNK)
    diag = [beside(d_slot[k], d_peer[k]) for k in pairs]
    rdiag = [OMEGA / d for d in diag]
    mats = [(block(hi_top, hi_side, hi_peer, k), block(lo_top, lo_side, lo_peer, k)) for k in pairs]
    peers = [x_peer[k // 2, (k % 2) * 128 : (k % 2) * 128 + COLS] for k in pairs]
    x1 = [beside(b_slot[k] * rdiag[k][:, :TILE], peers[k]) for k in pairs]
    spread = [s_slot[k] for k in pairs]
    ups = [lift(e_both[k // 2], pair_spread(spread[k], s_peer[k])) for k in pairs]
    x = [start + up for start, up in zip(x1, ups)]
    image = [apply_off(xx, *m) for xx, m in zip(x, mats)]
    z = [(1.0 - OMEGA) * xx + start - im * rd for xx, start, im, rd in zip(x, x1, image, rdiag)]
    w = [apply_block(zz, d, *m) for zz, d, m in zip(z, diag, mats)]
    x1 = [ww * rd for ww, rd in zip(w, rdiag)]
    left = [(m[0][:, :TILE], m[1][:, :TILE]) for m in mats]
    y = [(1.0 - OMEGA) * ww[:, :TILE] - apply_off(xx, *m) for ww, xx, m in zip(w, x1, left)]
    for i in range(0, CHUNK, 2):
        rr = rr + mm_exact(beside(y[i], y[i + 1]), beside(spread[i], spread[i + 1]), nt=True)
    for k in pairs:
        ws_out[k] = w[k][:, TILE:]
    z = [zz[:, :TILE] for zz in z]
    w = [ww[:, :TILE] for ww in w]
    for k in range(CHUNK):
        two = dot(e_mine, hi_unit[k, AGG:])
        found = two[:COLS] + two[COLS:] + dot(e_mine[:COLS], lo_unit[k, AGG:])
        z.append(z_rest[k] + found[:, :TILE])
        w.append(w_rest[k] + found[:, TILE:])
    for i in range(2 * CHUNK):
        bz = bz + (b_slot if i < CHUNK else b_rest)[i % CHUNK] * z[i]
        zw = zw + z[i] * w[i]
        z_out[i // CHUNK, i % CHUNK] = z[i]
        w_out[i // CHUNK, i % CHUNK] = w[i]
    acc_rr[...] = rr
    acc_bz[...] = bz
    acc_zw[...] = zw


def specs(smem, vmem):
    return [pl.BlockSpec(memory_space=pltpu.SMEM)] * smem + [pl.BlockSpec(memory_space=pltpu.VMEM)] * vmem


def forward_part(scalars, arrays):
    return pl.pallas_call(
        forward_kernel,
        in_specs=specs(len(scalars), len(arrays)),
        out_specs=specs(0, 5),
        out_shape=[
            near((2, SLOTS, COLS, TILE)),
            near((2, SLOTS, COLS, TILE)),
            near((SLOTS, COLS, TILE)),
            jax.ShapeDtypeStruct((PEERS, ROWS, TILE), F32),
            jax.ShapeDtypeStruct((COLS, AGG), F32),
        ],
        scratch_shapes=[
            pltpu.VMEM((PEERS, COLS, AGG), F32),
            pltpu.VMEM((COLS, AGG), F32),
            pltpu.VMEM((COLS, TILE), F32),
            pltpu.VMEM((COLS, TILE), F32),
        ],
        compiler_params=params(10),
        name="forward_part",
    )(*scalars, *arrays)


def second_kernel(
    member, arrived, inverse_rows, g, x, inverse, op_hi, op_lo, e_first, b_slot, b_rest, d_slot, d_peer, s_slot, s_peer,
    hi_top, lo_top, hi_side, lo_side, hi_peer, lo_peer, z_in, w_in, w_peer, v_rest, u_rest, hi_unit, lo_unit,
    v_out, u_out, out, dots, e, acc_a, acc_b, acc_c, acc_alpha
):
    extra = arrived[0, 32:40]
    for q in range(1, GROUPS):
        extra = extra + arrived[q, 32:40]
    dots[...] = extra
    level_one(arrived, inverse_rows, g, x, inverse, op_hi, op_lo, e)
    acc_a[...] = jnp.zeros_like(acc_a)
    acc_b[...] = jnp.zeros_like(acc_b)
    acc_c[...] = jnp.zeros_like(acc_c)
    col = column(dots[0:1])
    acc_alpha[...] = col[:COLS] / col[COLS:]
    e_own = e.at[pl.ds(member[0], 1)]
    views = (
        e, b_slot, b_rest, d_slot, d_peer, s_slot, s_peer, hi_top, lo_top, hi_side, lo_side, hi_peer, lo_peer,
        v_rest, u_rest, hi_unit, lo_unit, w_peer
    )

    @pl.loop(0, CHUNKS)
    def _(step):
        e_peer, *parts = [v.at[part(step, v.shape[0])] for v in views]
        both = [v.at[:, part(step, SLOTS)] for v in (z_in, w_in, v_out, u_out)]
        second_step(e_first, e_own, e_peer, *parts, *both, acc_a, acc_b, acc_c, acc_alpha)

    first = jnp.sum(jnp.concatenate([acc_a[...], acc_b[...]], axis=0).T, axis=0, keepdims=True)
    last = jnp.sum(jnp.concatenate([acc_c[...], acc_c[...]], axis=0).T, axis=0, keepdims=True)
    out[...] = jnp.broadcast_to(jnp.concatenate([first, last], axis=0), out.shape)


def second_step(
    e_first, e_own, e_peer, b_slot, b_rest, d_slot, d_peer, s_slot, s_peer, hi_top, lo_top, hi_side, lo_side,
    hi_peer, lo_peer, v_rest, u_rest, hi_unit, lo_unit, w_peer, z_in, w_in, v_out, u_out, acc_a, acc_b, acc_c, acc_alpha
):
    alpha = acc_alpha[...]
    e_twice = two_parts(beside(e_first[...], e_own[0]))
    e_both = [two_parts(beside(e_own[0], e_peer[q])) for q in range(CHUNK // 2)]
    sums = [acc_a[...], acc_b[...], acc_c[...]]

    def gather(b, z, w, v, u):
        r1 = b - alpha * w
        z1 = z - alpha * v
        az1 = w - alpha * u
        sums[0] = sums[0] + r1 * z1
        sums[1] = sums[1] + z1 * az1
        sums[2] = sums[2] + (z1 * w + z * az1)

    pairs = range(CHUNK)
    diag = [beside(d_slot[k], d_peer[k]) for k in pairs]
    rdiag = [OMEGA / d for d in diag]
    mats = [(block(hi_top, hi_side, hi_peer, k), block(lo_top, lo_side, lo_peer, k)) for k in pairs]
    w = [beside(w_in[0, k], w_peer[k]) for k in pairs]
    ups = [lift(e_both[k // 2], pair_spread(s_slot[k], s_peer[k])) for k in pairs]
    x1 = [ww * rd for ww, rd in zip(w, rdiag)]
    x = [start + up for start, up in zip(x1, ups)]
    image = [apply_off(xx, *m) for xx, m in zip(x, mats)]
    v = [(1.0 - OMEGA) * xx + start - im * rd for xx, start, im, rd in zip(x, x1, image, rdiag)]
    left = [(m[0][:, :TILE], m[1][:, :TILE]) for m in mats]
    u = [apply_block(vv, d[:, :TILE], *m) for vv, d, m in zip(v, diag, left)]
    v = [vv[:, :TILE] for vv in v]
    for k in range(CHUNK):
        two = dot(e_twice, hi_unit[k])
        found = two[:COLS] + two[COLS:] + dot(e_twice[:COLS], lo_unit[k])
        v.append(v_rest[k] + found[:, :TILE])
        u.append(u_rest[k] + found[:, TILE:])
    for i in range(2 * CHUNK):
        half, k = i // CHUNK, i % CHUNK
        v_out[half, k] = v[i]
        u_out[half, k] = u[i]
        gather((b_slot, b_rest)[half][k], z_in[half, k], w_in[half, k], v[i], u[i])
    acc_a[...] = sums[0]
    acc_b[...] = sums[1]
    acc_c[...] = sums[2]


def second_part(scalars, arrays):
    return pl.pallas_call(
        second_kernel,
        in_specs=specs(len(scalars), len(arrays)),
        out_specs=specs(0, 4),
        out_shape=[
            near((2, SLOTS, COLS, TILE)),
            near((2, SLOTS, COLS, TILE)),
            jax.ShapeDtypeStruct((GROUPS * PEERS, 2, TILE), F32),
            jax.ShapeDtypeStruct((8, TILE), F32),
        ],
        scratch_shapes=[pltpu.VMEM((PEERS, COLS, AGG), F32)] + [pltpu.VMEM((COLS, TILE), F32)] * 4,
        compiler_params=params(10),
        name="second_part",
    )(*scalars, *arrays)


def combine_kernel(where, dots, arrived, b, z, w, v, u, solution, residual, sol_buf, res_buf, sem):
    total = jnp.sum(arrived[...], axis=0)
    old = column(dots[0:1])
    one = column(total[0:1])
    two = column(total[1:2])
    rho, zw = old[:COLS], old[COLS:]
    rho_next, zz = one[:COLS], one[COLS:]
    alpha = rho / zw
    beta = rho_next / rho
    alpha_next = rho_next / (zz + beta * two[:COLS] + beta * beta * zw)
    first = alpha + alpha_next * (1.0 + beta)
    second = alpha_next * alpha

    def copies(i):
        at = pl.ds(i * (STEP * TILE), STEP * TILE)
        return (
            pltpu.make_async_copy(sol_buf.at[:, at], solution.at[:, at], sem.at[0, i]),
            pltpu.make_async_copy(res_buf.at[:, at], residual.at[:, at], sem.at[1, i]),
        )

    for i in range(BLK // STEP):
        for t in range(i * STEP, (i + 1) * STEP):
            half, k = where[t] // SLOTS, lax.rem(where[t], SLOTS)
            at = slice(t * TILE, (t + 1) * TILE)
            sol_buf[:, at] = first * z[half, k] - second * v[half, k]
            res_buf[:, at] = b[:, at] - first * w[half, k] + second * u[half, k]
        for copy in copies(i):
            copy.start()
    for i in range(BLK // STEP):
        for copy in copies(i):
            copy.wait()


def combine(where, dots, arrived, b, z, w, v, u):
    return pl.pallas_call(
        combine_kernel,
        in_specs=specs(1, 7),
        out_specs=[pl.BlockSpec(memory_space=pl.ANY)] * 2,
        out_shape=[far((COLS, BLK * TILE))] * 2,
        scratch_shapes=[
            pltpu.VMEM((COLS, BLK * TILE), F32),
            pltpu.VMEM((COLS, BLK * TILE), F32),
            pltpu.SemaphoreType.DMA((2, BLK // STEP)),
        ],
        compiler_params=params(8),
        name="combine",
    )(where, dots, arrived, b, z, w, v, u)


def exchange(x, axes):
    return lax.all_to_all(x, axes, 0, 0, tiled=True)


def on_device(
    right_side,
    diag_tiles,
    remote_tiles,
    slot_counts,
    slot_blocks,
    fine_map,
    coarse_map,
    level1_ops,
    coarsest_inverse,
):
    group = lax.axis_index("grp")
    member = lax.axis_index(GROUP_AXES).astype(jnp.int32).reshape(1)
    slot_list = slot_blocks.reshape(SLOTS)
    counts = slot_counts.reshape(PEERS)
    maps = fine_map.reshape(BLK, TILE)
    remote = remote_tiles.reshape(SLOTS, TILE, TILE)
    operator = level1_ops[0]

    outgoing = boundary_pack(slot_blocks, diag_tiles, right_side, maps)
    side = exchange(outgoing, GROUP_AXES)

    tile_ids = jnp.arange(BLK, dtype=jnp.int32)
    free = jnp.logical_not(jnp.any(slot_list[:, None] == tile_ids[None, :], axis=0)).astype(jnp.int32)
    rank = jnp.sum(jnp.where(tile_ids[None, :] < tile_ids[:, None], free[None, :], 0), axis=1)
    chosen = (rank[None, :] == jnp.arange(SLOTS, dtype=jnp.int32)[:, None]) & (free[None, :] == 1)
    rest_list = jnp.sum(jnp.where(chosen, tile_ids[None, :], 0), axis=1)
    perm = jnp.concatenate([slot_list, rest_list])
    where = jnp.sum(jnp.where(perm[None, :] == tile_ids[:, None], tile_ids[None, :], 0), axis=1)

    *local, rs, rr_local = local_part(
        perm, counts, diag_tiles, right_side, remote, maps
    )
    b_slot, b_rest, d_slot, hi_top, lo_top, hi_side, lo_side, s_slot = local[:8]
    z_rest, w_rest, v_rest, u_rest, hi_unit, lo_unit, rr_unit = local[8:]
    g, inverse, op_hi, op_lo = coarse_setup(operator, coarse_map.reshape(1, NC1))
    inverse_rows = lax.dynamic_slice_in_dim(coarsest_inverse, group * AGG, AGG, 0)

    rr_local, g, inverse_rows, member, where = lax.optimization_barrier(
        (rr_local, g, inverse_rows, member, where)
    )
    outgoing, hi_peer, lo_peer, d_peer, s_peer = first_restrict(side, rs, rr_local)
    gathered = exchange(outgoing, GROUP_AXES)

    scalars = (member,)
    x, outgoing = lowest_part(gathered, g)
    coarse = (exchange(outgoing, "grp"), inverse_rows, g, x, inverse)
    pairs = (hi_top, lo_top, hi_side, lo_side, hi_peer, lo_peer)
    z, w, w_peer, outgoing, e_first = forward_part(
        scalars,
        coarse
        + (op_hi, op_lo, b_slot, b_rest, d_slot, side, d_peer, s_slot, s_peer)
        + pairs
        + (z_rest, w_rest, hi_unit, lo_unit, rr_unit),
    )
    x, outgoing = lowest_part(exchange(outgoing, GROUP_AXES), g)
    coarse = (exchange(outgoing, "grp"), inverse_rows, g, x, inverse)
    v, u, outgoing, dots = second_part(
        scalars,
        coarse
        + (op_hi, op_lo, e_first, b_slot, b_rest, d_slot, d_peer, s_slot, s_peer)
        + pairs
        + (z, w, w_peer, v_rest, u_rest, hi_unit, lo_unit),
    )
    sums = exchange(outgoing, ALL_AXES)
    return tuple(combine(where, dots, sums, right_side, z, w, v, u))


def solution(mesh):
    placed = (
        P(None, ("grp", "sub", "chip")),
        P(("grp", "sub", "chip"), None, None),
        P(("grp", "sub", "chip"), None, None, None),
        P(("grp", "sub", "chip"), None),
        P(("grp", "sub", "chip"), None, None),
        P(("grp", "sub", "chip")),
        P("grp"),
        P("grp", None, None),
        P(),
    )
    return jax.shard_map(
        on_device,
        mesh=mesh,
        in_specs=placed,
        out_specs=(P(None, ("grp", "sub", "chip")), P(None, ("grp", "sub", "chip"))),
        check_vma=False,
    )
```

```python
import functools

import jax
import jax.numpy as jnp
from jax import lax
from jax.experimental import pallas as pl
from jax.experimental.pallas import tpu as pltpu
from jax.sharding import PartitionSpec as P

OMEGA = 0.6
F32 = jnp.float32
BF16 = jnp.bfloat16
COLS = 64
TILE = 128
BLK = 64
SLOTS = 32
PEERS = 16
GROUPS = 8
AGG = 64
NC1 = 1024
STEP = 8
NSTEP = SLOTS // STEP
CHUNK = 32
CHUNKS = SLOTS // CHUNK
SIDE = 264
PEER_STEP = 4
ROWS = 40

GROUP_AXES = ("sub", "chip")
ALL_AXES = ("grp", "sub", "chip")


def params(mib=20):
    return pltpu.CompilerParams(vmem_limit_bytes=mib * 1024 * 1024)


def hbm(x):
    return pltpu.with_memory_space_constraint(x, pltpu.HBM)


def near(shape, dtype=F32):
    return pltpu.VMEM(shape, dtype)


def far(shape, dtype=F32):
    return pltpu.HBM(shape, dtype)


def cost(flops, moved):
    return pl.CostEstimate(flops=flops, bytes_accessed=moved, transcendentals=0)


def split2(x):
    hi = x.astype(BF16)
    lo = (x - hi.astype(F32)).astype(BF16)
    return hi, lo


def dot(a, b):
    return jnp.dot(a, b, preferred_element_type=F32)


def dot_nt(a, b):
    return lax.dot_general(a, b, (((1,), (1,)), ((), ())), preferred_element_type=F32)


def mm(x, whi, wlo, nt=False):
    op = dot_nt if nt else dot
    rows = x.shape[0]
    hi, lo = split2(x)
    both = op(jnp.concatenate([hi, lo], axis=0), whi)
    return both[:rows] + both[rows:] + op(hi, wlo)


def mm_exact(x, w, nt=False):
    op = dot_nt if nt else dot
    rows = x.shape[0]
    two = op(jnp.concatenate(split2(x), axis=0), w)
    return two[:rows] + two[rows:]


def beside(a, b):
    return jnp.concatenate([a, b], axis=1)


def eye_mask():
    r = lax.broadcasted_iota(jnp.int32, (TILE, TILE), 0)
    c = lax.broadcasted_iota(jnp.int32, (TILE, TILE), 1)
    return r, c


def tile_diag(tile):
    r, c = eye_mask()
    return jnp.sum(jnp.where(r == c, tile, 0.0), axis=0, keepdims=True)


def off_diag(tile):
    r, c = eye_mask()
    return jnp.where(r == c, 0.0, tile)


def one_hot(row):
    r = lax.broadcasted_iota(jnp.int32, (AGG, row.shape[1]), 0)
    return jnp.where(r == row, 1.0, 0.0).astype(BF16)


def pack_rows(x):
    wide = jnp.concatenate([x[:32], x[32:]], axis=1)
    return wide


def column(row):
    return jnp.broadcast_to(row, (TILE, TILE)).T


def boundary_kernel(slots_in, maps, tiles, cols, out, slots, slot_sem, map_buf, tile_buf, col_buf, out_buf, map_sem, col_sem, tile_sem, out_sem):
    def tile_copy(j):
        return pltpu.make_async_copy(tiles.at[slots[0, j % 2, j // 2]], tile_buf.at[j], tile_sem.at[j])

    def col_copy(j):
        at = pl.ds(pl.multiple_of(slots[0, j % 2, j // 2] * TILE, TILE), TILE)
        return pltpu.make_async_copy(cols.at[:, at], col_buf.at[j], col_sem.at[j])

    def out_copy(j):
        at = pl.ds(j // 2, PEER_STEP)
        return pltpu.make_async_copy(out_buf.at[at], out.at[at], out_sem.at[j // STEP])

    slot_copy = pltpu.make_async_copy(slots_in, slots, slot_sem)
    slot_copy.start()
    map_copy = pltpu.make_async_copy(maps, map_buf, map_sem)
    map_copy.start()
    slot_copy.wait()
    for j in range(SLOTS):
        tile_copy(j).start()
        col_copy(j).start()
    r = lax.broadcasted_iota(jnp.int32, (64, TILE), 0)
    c = lax.broadcasted_iota(jnp.int32, (64, TILE), 1)
    r8 = lax.broadcasted_iota(jnp.int32, (8, TILE), 0)
    map_copy.wait()
    for j in range(0, SLOTS, STEP):
        for k in range(j, j + STEP):
            tile_copy(k).wait()
            col_copy(k).wait()
        tile = [tile_buf[k] for k in range(j, j + STEP)]
        diag = [tile_diag(t) for t in tile]
        for k in range(j, j + STEP):
            t, d = tile[k - j], diag[k - j]
            q, base = k // 2, (k % 2) * 128
            out_buf[q, base : base + 64] = col_buf[k] * (OMEGA / d)
            below = pltpu.roll(t[64:], 64, 1)
            out_buf[q, base + 64 : base + 128] = jnp.where((c < 64) & (r > c), below, t[:64])
        for k in range(j, j + STEP, 2):
            own = [map_buf[pl.ds(slots[0, i, k // 2], 1)].astype(F32) for i in range(2)]
            d0, d1 = diag[k - j], diag[k - j + 1]
            out_buf[k // 2, 256:264] = jnp.where(
                r8 == 0, d0, jnp.where(r8 == 1, own[0], jnp.where(r8 == 2, d1, jnp.where(r8 == 3, own[1], 0.0)))
            )
        out_copy(j).start()
    for j in range(0, SLOTS, STEP):
        out_copy(j).wait()


def boundary_pack(slot_blocks, diag_tiles, right_side, maps):
    return pl.pallas_call(
        boundary_kernel,
        in_specs=[pl.BlockSpec(memory_space=pl.ANY)] * 4,
        out_specs=pl.BlockSpec(memory_space=pl.ANY),
        out_shape=far((PEERS, SIDE, TILE)),
        scratch_shapes=[
            pltpu.SMEM((1, 2, PEERS), jnp.int32),
            pltpu.SemaphoreType.DMA,
            pltpu.VMEM((BLK, TILE), jnp.int32),
            pltpu.VMEM((SLOTS, TILE, TILE), F32),
            pltpu.VMEM((SLOTS, COLS, TILE), F32),
            pltpu.VMEM((PEERS, SIDE, TILE), F32),
            pltpu.SemaphoreType.DMA,
            pltpu.SemaphoreType.DMA((SLOTS,)),
            pltpu.SemaphoreType.DMA((SLOTS,)),
            pltpu.SemaphoreType.DMA((NSTEP,)),
        ],
        compiler_params=params(),
        name="boundary_pack",
    )(hbm(slot_blocks.transpose(0, 2, 1)), hbm(maps), hbm(diag_tiles), hbm(right_side))


def local_kernel(perm, counts, *refs):
    n = 2 * STEP
    tiles, cols = refs[:n], refs[n : 2 * n]
    remote, maps = refs[2 * n : 2 * n + 2]
    b_slot, b_rest, d_slot, hi_top, lo_top, hi_side, lo_side, s_slot = refs[2 * n + 2 : 2 * n + 10]
    z_rest, w_rest, v_rest, u_rest, hi_unit, lo_unit, rr_unit, rs, rr = refs[2 * n + 10 :]
    step = pl.program_id(0)

    @pl.when(step == 0)
    def _():
        rr[...] = jnp.zeros_like(rr)
        rr_unit[...] = jnp.zeros_like(rr_unit)

    index = [perm[(0 if i < STEP else SLOTS) + step * STEP + i % STEP] for i in range(n)]
    tile = [tiles[i][0] for i in range(n)]
    diag = [tile_diag(t) for t in tile]
    off = [split2(off_diag(t)) for t in tile]
    b = [cols[i][...] for i in range(n)]
    x = [OMEGA * bb / d for bb, d in zip(b, diag)]
    spread = [one_hot(maps[pl.ds(i, 1)]) for i in index]
    rest = range(STEP, n)
    rdiag = [OMEGA / diag[i] for i in rest]
    start = [jnp.concatenate([x[i], jnp.zeros_like(x[i])], axis=0) for i in rest]
    both = [jnp.concatenate([x[i], spread[i].astype(F32)], axis=0) for i in rest]
    image = [apply_off(xx, *off[i]) for xx, i in zip(both, rest)]
    z = [(1.0 - OMEGA) * xx + st - im * rd for xx, st, im, rd in zip(both, start, image, rdiag)]
    w = [apply_block(zz, diag[i], *off[i]) for zz, i in zip(z, rest)]
    start = [ww * rd for ww, rd in zip(w, rdiag)]
    again = [apply_off(xx, *off[i]) for xx, i in zip(start, rest)]
    left = [(1.0 - OMEGA) * ww - im for ww, im in zip(w, again)]
    v = [(2.0 - OMEGA) * xx - im * rd for xx, im, rd in zip(start, again, rdiag)]
    u = [apply_block(vv, diag[i], *off[i]) for vv, i in zip(v, rest)]
    unit_total = rr_unit[...]
    for k in range(0, STEP, 2):
        pair = beside(spread[STEP + k], spread[STEP + k + 1])
        unit_total = unit_total + mm_exact(beside(left[k], left[k + 1]), pair, nt=True)
    rr_unit[...] = unit_total
    for k in range(STEP):
        z_rest[k] = z[k][:COLS]
        w_rest[k] = w[k][:COLS]
        v_rest[k] = v[k][:COLS]
        u_rest[k] = u[k][:COLS]
        units = [beside(v[k][COLS:], u[k][COLS:]), beside(z[k][COLS:], w[k][COLS:])]
        hi_unit[k], lo_unit[k] = split2(jnp.concatenate(units, axis=0))
    y = [b[i] - OMEGA * b[i] - mm(x[i], *off[i]) for i in range(STEP)]
    y = y + [b[i] - OMEGA * b[i] - im[:COLS] for i, im in zip(rest, image)]
    total = rr[...]
    for i in range(0, n, 2):
        total = total + mm_exact(beside(y[i], y[i + 1]), beside(spread[i], spread[i + 1]), nt=True)
    for k in range(STEP):
        b_slot[k] = b[k]
        d_slot[k] = diag[k]
        b_rest[k] = b[STEP + k]
        s_slot[k] = spread[k]
    coupling, turned, restricted = [], [], []
    for k in range(STEP):
        j = step * STEP + k
        live = (j % 2) < counts[j // 2]
        scaled = remote[k] * jnp.where(live, -1.0, 0.0)
        coupling.append(split2(scaled))
        turned.append(split2(scaled.T))
    for k in range(STEP):
        restricted.append(-(dot_nt(coupling[k][0], spread[k]) + dot_nt(coupling[k][1], spread[k])))
        hi_top[k] = beside(off[k][0], turned[k][0])
        lo_top[k] = beside(off[k][1], turned[k][1])
        hi_side[k], lo_side[k] = coupling[k]
    for q in range(PEER_STEP):
        rs[q, 0], rs[q, 1] = split2(beside(restricted[2 * q], restricted[2 * q + 1]))
    rr[...] = total


def local_part(perm, counts, diag_tiles, right_side, remote, maps):
    def where(i):
        return (0 if i < STEP else SLOTS) + i % STEP

    def tile_spec(i):
        return pl.BlockSpec((1, TILE, TILE), lambda s, p, c: (p[s * STEP + where(i)], 0, 0))

    def col_spec(i):
        return pl.BlockSpec((COLS, TILE), lambda s, p, c: (0, p[s * STEP + where(i)]))

    def out(*shape):
        return pl.BlockSpec((STEP,) + shape, lambda s, p, c: (s, 0, 0))

    n = 2 * STEP
    grid = pltpu.PrefetchScalarGridSpec(
        num_scalar_prefetch=2,
        grid=(NSTEP,),
        in_specs=[tile_spec(i) for i in range(n)]
        + [col_spec(i) for i in range(n)]
        + [
            pl.BlockSpec((STEP, TILE, TILE), lambda s, p, c: (s, 0, 0)),
            pl.BlockSpec((BLK, TILE), lambda s, p, c: (0, 0)),
        ],
        out_specs=[
            out(COLS, TILE),
            out(COLS, TILE),
            out(1, TILE),
            out(TILE, 2 * TILE),
            out(TILE, 2 * TILE),
            out(TILE, TILE),
            out(TILE, TILE),
            out(AGG, TILE),
            out(COLS, TILE),
            out(COLS, TILE),
            out(COLS, TILE),
            out(COLS, TILE),
            out(2 * AGG, 2 * TILE),
            out(2 * AGG, 2 * TILE),
            pl.BlockSpec((COLS + AGG, AGG), lambda s, p, c: (0, 0)),
            pl.BlockSpec((PEER_STEP, 2, TILE, TILE), lambda s, p, c: (s, 0, 0, 0)),
            pl.BlockSpec((COLS, AGG), lambda s, p, c: (0, 0)),
        ],
    )

    def sds(shape, dtype=F32):
        return far((SLOTS,) + shape, dtype)

    return pl.pallas_call(
        local_kernel,
        grid_spec=grid,
        out_shape=[
            sds((COLS, TILE)),
            sds((COLS, TILE)),
            sds((1, TILE)),
            sds((TILE, 2 * TILE), BF16),
            sds((TILE, 2 * TILE), BF16),
            sds((TILE, TILE), BF16),
            sds((TILE, TILE), BF16),
            sds((AGG, TILE), BF16),
            sds((COLS, TILE)),
            sds((COLS, TILE)),
            sds((COLS, TILE)),
            sds((COLS, TILE)),
            sds((2 * AGG, 2 * TILE), BF16),
            sds((2 * AGG, 2 * TILE), BF16),
            jax.ShapeDtypeStruct((COLS + AGG, AGG), F32),
            far((PEERS, 2, TILE, TILE), BF16),
            jax.ShapeDtypeStruct((COLS, AGG), F32),
        ],
        compiler_params=params(),
        cost_estimate=cost(2 * 64 * 3 * 64 * 128 * 128, 16 << 20),
        name="local_part",
    )(perm, counts, *([hbm(diag_tiles)] * n), *([hbm(right_side)] * n), hbm(remote), maps)


def coarse_kernel(op, cmap, g_out, d_out, hi_out, lo_out):
    spread = one_hot(cmap[...])
    product = None
    for i in range(NC1 // 256):
        rows = slice(i * 256, (i + 1) * 256)
        hi, lo = split2(op[rows, :])
        hi_out[rows, :] = hi
        lo_out[rows, :] = lo
        term = dot(spread[:, rows], hi) + dot(spread[:, rows], lo)
        product = term if product is None else product + term
    pieces = []
    for i in range(NC1 // TILE):
        pieces.append(tile_diag(op[i * TILE : (i + 1) * TILE, i * TILE : (i + 1) * TILE]))
    diag = jnp.concatenate(pieces, axis=1)
    inverse = 1.0 / diag
    d_out[...] = inverse
    g_out[...] = spread.astype(F32) - OMEGA * product * inverse


def coarse_setup(op, cmap):
    return pl.pallas_call(
        coarse_kernel,
        out_shape=[
            jax.ShapeDtypeStruct((AGG, NC1), F32),
            jax.ShapeDtypeStruct((1, NC1), F32),
            far((NC1, NC1), BF16),
            far((NC1, NC1), BF16),
        ],
        compiler_params=params(),
        cost_estimate=cost(2 * 2 * 64 * 1024 * 1024, 5 << 20),
        name="coarse_setup",
    )(op, cmap)


def first_restrict_kernel(arrived, rs, rr, out, hi_out, lo_out, diag_out, spread_out, rs_buf, rs_sem):
    def copy(j):
        at = pl.ds(j * PEER_STEP, PEER_STEP)
        return pltpu.make_async_copy(rs.at[at], rs_buf.at[at], rs_sem.at[j])

    for j in range(NSTEP):
        copy(j).start()
    r = lax.broadcasted_iota(jnp.int32, (64, TILE), 0)
    c = lax.broadcasted_iota(jnp.int32, (64, TILE), 1)
    for k in range(SLOTS):
        q, base, at = k // 2, 128 * (k % 2) + 64, 256 + 2 * (k % 2)
        packed = arrived[q, base : base + 64]
        top = jnp.where((c >= 64) | (r < c), packed, 0.0)
        bottom = pltpu.roll(jnp.where((c < 64) & (r > c), packed, 0.0), 64, 1)
        half = jnp.concatenate([top, bottom], axis=0)
        hi_out[k], lo_out[k] = split2(half + half.T)
        diag_out[k] = arrived[q, at : at + 1]
        spread_out[k] = one_hot(arrived[q, at + 1 : at + 2].astype(jnp.int32))
    main, rest = [], []
    for j in range(NSTEP):
        copy(j).wait()
        for q in range(j * PEER_STEP, (j + 1) * PEER_STEP):
            hi0, lo0 = split2(arrived[q, 0:COLS])
            hi1, lo1 = split2(arrived[q, 128 : 128 + COLS])
            main.append(dot(jnp.concatenate([hi0, lo0, hi1, lo1], axis=0), rs_buf[q, 0]))
            rest.append(dot(jnp.concatenate([hi0, hi1], axis=0), rs_buf[q, 1]))
    main, rest = sum(main), sum(rest)
    first = main[:COLS] + main[COLS : 2 * COLS] + rest[:COLS]
    second = main[2 * COLS : 3 * COLS] + main[3 * COLS :] + rest[COLS:]
    total = rr[...] + first[:, :AGG] + second[:, AGG:]
    out[...] = jnp.broadcast_to(pack_rows(total), out.shape)


def first_restrict(arrived, rs, rr):
    return pl.pallas_call(
        first_restrict_kernel,
        in_specs=[
            pl.BlockSpec(memory_space=pltpu.VMEM),
            pl.BlockSpec(memory_space=pl.ANY),
            pl.BlockSpec(memory_space=pltpu.VMEM),
        ],
        out_specs=[pl.BlockSpec(memory_space=pltpu.VMEM)] * 5,
        out_shape=[
            jax.ShapeDtypeStruct((PEERS, 32, TILE), F32),
            near((SLOTS, TILE, TILE), BF16),
            near((SLOTS, TILE, TILE), BF16),
            near((SLOTS, 1, TILE)),
            near((SLOTS, AGG, TILE), BF16),
        ],
        scratch_shapes=[
            pltpu.VMEM((PEERS, 2, TILE, TILE), BF16),
            pltpu.SemaphoreType.DMA((NSTEP,)),
        ],
        compiler_params=params(8),
        name="first_restrict",
    )(pltpu.with_memory_space_constraint(arrived, pltpu.VMEM), hbm(rs), rr)


def gathered_rows(ref, count):
    lane = lax.broadcasted_iota(jnp.int32, (32, TILE), 1) < 64
    tops, bottoms = [], []
    for q in range(0, count, 2):
        a, b = ref[q, 0:32], ref[q + 1, 0:32]
        tops.append(jnp.where(lane, a, pltpu.roll(b, 64, 1)))
        bottoms.append(jnp.where(lane, pltpu.roll(a, 64, 1), b))
    return jnp.concatenate([jnp.concatenate(tops, axis=1), jnp.concatenate(bottoms, axis=1)], axis=0)


def lowest_kernel(arrived, g, x_out, out):
    x = gathered_rows(arrived, PEERS)
    x_out[...] = x
    hi, lo = split2(g[...])
    packed = pack_rows(mm(x, hi, lo, nt=True))
    if arrived.shape[1] == ROWS:
        extra = arrived[0, 32:40]
        for q in range(1, PEERS):
            extra = extra + arrived[q, 32:40]
        packed = jnp.concatenate([packed, extra], axis=0)
    out[...] = jnp.broadcast_to(packed, out.shape)


def lowest_part(arrived, g):
    return pl.pallas_call(
        lowest_kernel,
        out_shape=[
            jax.ShapeDtypeStruct((COLS, NC1), F32),
            jax.ShapeDtypeStruct((GROUPS, arrived.shape[1], TILE), F32),
        ],
        compiler_params=params(6),
        cost_estimate=cost(20_000_000_000, 32 << 20),
        name="lowest_part",
    )(arrived, g)


def level_one(arrived, inverse_rows, g, x_ref, inverse_ref, op_hi, op_lo, e_out):
    low = gathered_rows(arrived, GROUPS)
    hi, lo = split2(inverse_rows[...])
    corr = mm(low, hi, lo, nt=True)
    ghi, glo = split2(g[...])
    lifted = mm(corr, ghi, glo)
    inverse = inverse_ref[...]
    scaled = x_ref[...] * inverse
    total = None
    for i in range(NC1 // 256):
        rows = slice(i * 256, (i + 1) * 256)
        term = mm(scaled[:, rows], op_hi[rows, :], op_lo[rows, :])
        total = term if total is None else total + term
    e = 2.0 * OMEGA * scaled - OMEGA * OMEGA * total * inverse + lifted
    for q in range(PEERS):
        e_out[q] = e[:, q * AGG : (q + 1) * AGG]


def apply_off(x, hi, lo):
    xh, xl = split2(x)
    rows = x.shape[0]
    if x.shape[1] == TILE:
        return dot(beside(xh, xl), jnp.concatenate([hi, hi], axis=0)) + dot(xh, lo)
    both = dot(jnp.concatenate([xh, xl], axis=0), hi)
    return both[:rows] + both[rows:] + dot(xh, lo)


def apply_block(x, diag, hi, lo):
    xh, xl = split2(x)
    kept = xh.astype(F32) + xl.astype(F32)
    return apply_off(x, hi, lo) + kept[:, : diag.shape[1]] * diag


def lift(parts, spread):
    rows = parts.shape[0] // 2
    two = dot(parts, spread)
    return two[:rows] + two[rows:]


def two_parts(e):
    return jnp.concatenate(split2(e), axis=0)


def block(top, side, peer, k):
    return jnp.concatenate([top[k], beside(side[k], peer[k])], axis=0)


def pair_spread(own, peer):
    none = jnp.zeros_like(own)
    return jnp.concatenate([beside(own, none), beside(none, peer)], axis=0)


def forward_kernel(
    member, arrived, inverse_rows, g, x, inverse, op_hi, op_lo, b_slot, b_rest, d_slot, x_peer, d_peer, s_slot, s_peer,
    hi_top, lo_top, hi_side, lo_side, hi_peer, lo_peer, z_rest, w_rest, hi_unit, lo_unit, rr_unit,
    z_out, w_out, ws_out, out, e_keep, e, acc_rr, acc_bz, acc_zw
):
    level_one(arrived, inverse_rows, g, x, inverse, op_hi, op_lo, e)
    e_own = e.at[pl.ds(member[0], 1)]
    e_keep[...] = e_own[0]
    unit_hi, unit_lo = split2(rr_unit[COLS:])
    acc_rr[...] = rr_unit[:COLS] + mm(e_own[0], unit_hi, unit_lo)
    acc_bz[...] = jnp.zeros_like(acc_bz)
    acc_zw[...] = jnp.zeros_like(acc_zw)
    views = (
        e, b_slot, b_rest, d_slot, x_peer, d_peer, s_slot, s_peer, hi_top, lo_top, hi_side, lo_side, hi_peer, lo_peer,
        z_rest, w_rest, hi_unit, lo_unit, ws_out
    )

    @pl.loop(0, CHUNKS)
    def _(step):
        e_peer, *parts = [v.at[part(step, v.shape[0])] for v in views]
        both = [v.at[:, part(step, SLOTS)] for v in (z_out, w_out)]
        forward_step(e_own, e_peer, *parts[:-1], *both, parts[-1], acc_rr, acc_bz, acc_zw)

    packed = pack_rows(acc_rr[...])
    sums = jnp.sum(jnp.concatenate([acc_bz[...], acc_zw[...]], axis=0).T, axis=0, keepdims=True)
    r8 = lax.broadcasted_iota(jnp.int32, (8, TILE), 0)
    extra = jnp.where(r8 == 0, sums, 0.0)
    for q in range(PEERS):
        out[q, 0:32] = packed
        out[q, 32:40] = extra


def part(step, count):
    size = count // CHUNKS
    return pl.ds(step * size, size)


def forward_step(
    e_own, e_peer, b_slot, b_rest, d_slot, x_peer, d_peer, s_slot, s_peer, hi_top, lo_top, hi_side, lo_side,
    hi_peer, lo_peer, z_rest, w_rest, hi_unit, lo_unit, z_out, w_out, ws_out, acc_rr, acc_bz, acc_zw
):
    e_mine = two_parts(e_own[0])
    e_both = [two_parts(beside(e_own[0], e_peer[q])) for q in range(CHUNK // 2)]
    rr, bz, zw = acc_rr[...], acc_bz[...], acc_zw[...]
    pairs = range(CHUNK)
    diag = [beside(d_slot[k], d_peer[k]) for k in pairs]
    rdiag = [OMEGA / d for d in diag]
    mats = [(block(hi_top, hi_side, hi_peer, k), block(lo_top, lo_side, lo_peer, k)) for k in pairs]
    peers = [x_peer[k // 2, (k % 2) * 128 : (k % 2) * 128 + COLS] for k in pairs]
    x1 = [beside(b_slot[k] * rdiag[k][:, :TILE], peers[k]) for k in pairs]
    spread = [s_slot[k] for k in pairs]
    ups = [lift(e_both[k // 2], pair_spread(spread[k], s_peer[k])) for k in pairs]
    x = [start + up for start, up in zip(x1, ups)]
    image = [apply_off(xx, *m) for xx, m in zip(x, mats)]
    z = [(1.0 - OMEGA) * xx + start - im * rd for xx, start, im, rd in zip(x, x1, image, rdiag)]
    w = [apply_block(zz, d, *m) for zz, d, m in zip(z, diag, mats)]
    x1 = [ww * rd for ww, rd in zip(w, rdiag)]
    left = [(m[0][:, :TILE], m[1][:, :TILE]) for m in mats]
    y = [(1.0 - OMEGA) * ww[:, :TILE] - apply_off(xx, *m) for ww, xx, m in zip(w, x1, left)]
    for i in range(0, CHUNK, 2):
        rr = rr + mm_exact(beside(y[i], y[i + 1]), beside(spread[i], spread[i + 1]), nt=True)
    for k in pairs:
        ws_out[k] = w[k][:, TILE:]
    z = [zz[:, :TILE] for zz in z]
    w = [ww[:, :TILE] for ww in w]
    for k in range(CHUNK):
        two = dot(e_mine, hi_unit[k, AGG:])
        found = two[:COLS] + two[COLS:] + dot(e_mine[:COLS], lo_unit[k, AGG:])
        z.append(z_rest[k] + found[:, :TILE])
        w.append(w_rest[k] + found[:, TILE:])
    for i in range(2 * CHUNK):
        bz = bz + (b_slot if i < CHUNK else b_rest)[i % CHUNK] * z[i]
        zw = zw + z[i] * w[i]
        z_out[i // CHUNK, i % CHUNK] = z[i]
        w_out[i // CHUNK, i % CHUNK] = w[i]
    acc_rr[...] = rr
    acc_bz[...] = bz
    acc_zw[...] = zw


def specs(smem, vmem):
    return [pl.BlockSpec(memory_space=pltpu.SMEM)] * smem + [pl.BlockSpec(memory_space=pltpu.VMEM)] * vmem


def forward_part(scalars, arrays):
    return pl.pallas_call(
        forward_kernel,
        in_specs=specs(len(scalars), len(arrays)),
        out_specs=specs(0, 5),
        out_shape=[
            near((2, SLOTS, COLS, TILE)),
            near((2, SLOTS, COLS, TILE)),
            near((SLOTS, COLS, TILE)),
            jax.ShapeDtypeStruct((PEERS, ROWS, TILE), F32),
            jax.ShapeDtypeStruct((COLS, AGG), F32),
        ],
        scratch_shapes=[
            pltpu.VMEM((PEERS, COLS, AGG), F32),
            pltpu.VMEM((COLS, AGG), F32),
            pltpu.VMEM((COLS, TILE), F32),
            pltpu.VMEM((COLS, TILE), F32),
        ],
        compiler_params=params(10),
        name="forward_part",
    )(*scalars, *arrays)


def second_kernel(
    member, arrived, inverse_rows, g, x, inverse, op_hi, op_lo, e_first, b_slot, b_rest, d_slot, d_peer, s_slot, s_peer,
    hi_top, lo_top, hi_side, lo_side, hi_peer, lo_peer, z_in, w_in, w_peer, v_rest, u_rest, hi_unit, lo_unit,
    v_out, u_out, out, dots, e, acc_a, acc_b, acc_c, acc_alpha
):
    extra = arrived[0, 32:40]
    for q in range(1, GROUPS):
        extra = extra + arrived[q, 32:40]
    dots[...] = extra
    level_one(arrived, inverse_rows, g, x, inverse, op_hi, op_lo, e)
    acc_a[...] = jnp.zeros_like(acc_a)
    acc_b[...] = jnp.zeros_like(acc_b)
    acc_c[...] = jnp.zeros_like(acc_c)
    col = column(dots[0:1])
    acc_alpha[...] = col[:COLS] / col[COLS:]
    e_own = e.at[pl.ds(member[0], 1)]
    views = (
        e, b_slot, b_rest, d_slot, d_peer, s_slot, s_peer, hi_top, lo_top, hi_side, lo_side, hi_peer, lo_peer,
        v_rest, u_rest, hi_unit, lo_unit, w_peer
    )

    @pl.loop(0, CHUNKS)
    def _(step):
        e_peer, *parts = [v.at[part(step, v.shape[0])] for v in views]
        both = [v.at[:, part(step, SLOTS)] for v in (z_in, w_in, v_out, u_out)]
        second_step(e_first, e_own, e_peer, *parts, *both, acc_a, acc_b, acc_c, acc_alpha)

    first = jnp.sum(jnp.concatenate([acc_a[...], acc_b[...]], axis=0).T, axis=0, keepdims=True)
    last = jnp.sum(jnp.concatenate([acc_c[...], acc_c[...]], axis=0).T, axis=0, keepdims=True)
    out[...] = jnp.broadcast_to(jnp.concatenate([first, last], axis=0), out.shape)


def second_step(
    e_first, e_own, e_peer, b_slot, b_rest, d_slot, d_peer, s_slot, s_peer, hi_top, lo_top, hi_side, lo_side,
    hi_peer, lo_peer, v_rest, u_rest, hi_unit, lo_unit, w_peer, z_in, w_in, v_out, u_out, acc_a, acc_b, acc_c, acc_alpha
):
    alpha = acc_alpha[...]
    e_twice = two_parts(beside(e_first[...], e_own[0]))
    e_both = [two_parts(beside(e_own[0], e_peer[q])) for q in range(CHUNK // 2)]
    sums = [acc_a[...], acc_b[...], acc_c[...]]

    def gather(b, z, w, v, u):
        r1 = b - alpha * w
        z1 = z - alpha * v
        az1 = w - alpha * u
        sums[0] = sums[0] + r1 * z1
        sums[1] = sums[1] + z1 * az1
        sums[2] = sums[2] + (z1 * w + z * az1)

    pairs = range(CHUNK)
    diag = [beside(d_slot[k], d_peer[k]) for k in pairs]
    rdiag = [OMEGA / d for d in diag]
    mats = [(block(hi_top, hi_side, hi_peer, k), block(lo_top, lo_side, lo_peer, k)) for k in pairs]
    w = [beside(w_in[0, k], w_peer[k]) for k in pairs]
    ups = [lift(e_both[k // 2], pair_spread(s_slot[k], s_peer[k])) for k in pairs]
    x1 = [ww * rd for ww, rd in zip(w, rdiag)]
    x = [start + up for start, up in zip(x1, ups)]
    image = [apply_off(xx, *m) for xx, m in zip(x, mats)]
    v = [(1.0 - OMEGA) * xx + start - im * rd for xx, start, im, rd in zip(x, x1, image, rdiag)]
    left = [(m[0][:, :TILE], m[1][:, :TILE]) for m in mats]
    u = [apply_block(vv, d[:, :TILE], *m) for vv, d, m in zip(v, diag, left)]
    v = [vv[:, :TILE] for vv in v]
    for k in range(CHUNK):
        two = dot(e_twice, hi_unit[k])
        found = two[:COLS] + two[COLS:] + dot(e_twice[:COLS], lo_unit[k])
        v.append(v_rest[k] + found[:, :TILE])
        u.append(u_rest[k] + found[:, TILE:])
    for i in range(2 * CHUNK):
        half, k = i // CHUNK, i % CHUNK
        v_out[half, k] = v[i]
        u_out[half, k] = u[i]
        gather((b_slot, b_rest)[half][k], z_in[half, k], w_in[half, k], v[i], u[i])
    acc_a[...] = sums[0]
    acc_b[...] = sums[1]
    acc_c[...] = sums[2]


def second_part(scalars, arrays):
    return pl.pallas_call(
        second_kernel,
        in_specs=specs(len(scalars), len(arrays)),
        out_specs=specs(0, 4),
        out_shape=[
            near((2, SLOTS, COLS, TILE)),
            near((2, SLOTS, COLS, TILE)),
            jax.ShapeDtypeStruct((GROUPS * PEERS, 2, TILE), F32),
            jax.ShapeDtypeStruct((8, TILE), F32),
        ],
        scratch_shapes=[pltpu.VMEM((PEERS, COLS, AGG), F32)] + [pltpu.VMEM((COLS, TILE), F32)] * 4,
        compiler_params=params(10),
        name="second_part",
    )(*scalars, *arrays)


def combine_kernel(where, dots, arrived, b, z, w, v, u, solution, residual, sol_buf, res_buf, sem):
    total = jnp.sum(arrived[...], axis=0)
    old = column(dots[0:1])
    one = column(total[0:1])
    two = column(total[1:2])
    rho, zw = old[:COLS], old[COLS:]
    rho_next, zz = one[:COLS], one[COLS:]
    alpha = rho / zw
    beta = rho_next / rho
    alpha_next = rho_next / (zz + beta * two[:COLS] + beta * beta * zw)
    first = alpha + alpha_next * (1.0 + beta)
    second = alpha_next * alpha

    def copies(i):
        at = pl.ds(i * (STEP * TILE), STEP * TILE)
        return (
            pltpu.make_async_copy(sol_buf.at[:, at], solution.at[:, at], sem.at[0, i]),
            pltpu.make_async_copy(res_buf.at[:, at], residual.at[:, at], sem.at[1, i]),
        )

    for i in range(BLK // STEP):
        for t in range(i * STEP, (i + 1) * STEP):
            half, k = where[t] // SLOTS, lax.rem(where[t], SLOTS)
            at = slice(t * TILE, (t + 1) * TILE)
            sol_buf[:, at] = first * z[half, k] - second * v[half, k]
            res_buf[:, at] = b[:, at] - first * w[half, k] + second * u[half, k]
        for copy in copies(i):
            copy.start()
    for i in range(BLK // STEP):
        for copy in copies(i):
            copy.wait()


def combine(where, dots, arrived, b, z, w, v, u):
    return pl.pallas_call(
        combine_kernel,
        in_specs=specs(1, 7),
        out_specs=[pl.BlockSpec(memory_space=pl.ANY)] * 2,
        out_shape=[far((COLS, BLK * TILE))] * 2,
        scratch_shapes=[
            pltpu.VMEM((COLS, BLK * TILE), F32),
            pltpu.VMEM((COLS, BLK * TILE), F32),
            pltpu.SemaphoreType.DMA((2, BLK // STEP)),
        ],
        compiler_params=params(8),
        name="combine",
    )(where, dots, arrived, b, z, w, v, u)


def exchange(x, axes):
    return lax.all_to_all(x, axes, 0, 0, tiled=True)


def on_device(
    right_side,
    diag_tiles,
    remote_tiles,
    slot_counts,
    slot_blocks,
    fine_map,
    coarse_map,
    level1_ops,
    coarsest_inverse,
):
    group = lax.axis_index("grp")
    member = lax.axis_index(GROUP_AXES).astype(jnp.int32).reshape(1)
    slot_list = slot_blocks.reshape(SLOTS)
    counts = slot_counts.reshape(PEERS)
    maps = fine_map.reshape(BLK, TILE)
    remote = remote_tiles.reshape(SLOTS, TILE, TILE)
    operator = level1_ops[0]

    outgoing = boundary_pack(slot_blocks, diag_tiles, right_side, maps)
    side = exchange(outgoing, GROUP_AXES)

    tile_ids = jnp.arange(BLK, dtype=jnp.int32)
    free = jnp.logical_not(jnp.any(slot_list[:, None] == tile_ids[None, :], axis=0)).astype(jnp.int32)
    rank = jnp.sum(jnp.where(tile_ids[None, :] < tile_ids[:, None], free[None, :], 0), axis=1)
    chosen = (rank[None, :] == jnp.arange(SLOTS, dtype=jnp.int32)[:, None]) & (free[None, :] == 1)
    rest_list = jnp.sum(jnp.where(chosen, tile_ids[None, :], 0), axis=1)
    perm = jnp.concatenate([slot_list, rest_list])
    where = jnp.sum(jnp.where(perm[None, :] == tile_ids[:, None], tile_ids[None, :], 0), axis=1)

    *local, rs, rr_local = local_part(
        perm, counts, diag_tiles, right_side, remote, maps
    )
    b_slot, b_rest, d_slot, hi_top, lo_top, hi_side, lo_side, s_slot = local[:8]
    z_rest, w_rest, v_rest, u_rest, hi_unit, lo_unit, rr_unit = local[8:]
    g, inverse, op_hi, op_lo = coarse_setup(operator, coarse_map.reshape(1, NC1))
    inverse_rows = lax.dynamic_slice_in_dim(coarsest_inverse, group * AGG, AGG, 0)

    rr_local, g, inverse_rows, member, where = lax.optimization_barrier(
        (rr_local, g, inverse_rows, member, where)
    )
    outgoing, hi_peer, lo_peer, d_peer, s_peer = first_restrict(side, rs, rr_local)
    gathered = exchange(outgoing, GROUP_AXES)

    scalars = (member,)
    x, outgoing = lowest_part(gathered, g)
    coarse = (exchange(outgoing, "grp"), inverse_rows, g, x, inverse)
    pairs = (hi_top, lo_top, hi_side, lo_side, hi_peer, lo_peer)
    z, w, w_peer, outgoing, e_first = forward_part(
        scalars,
        coarse
        + (op_hi, op_lo, b_slot, b_rest, d_slot, side, d_peer, s_slot, s_peer)
        + pairs
        + (z_rest, w_rest, hi_unit, lo_unit, rr_unit),
    )
    x, outgoing = lowest_part(exchange(outgoing, GROUP_AXES), g)
    coarse = (exchange(outgoing, "grp"), inverse_rows, g, x, inverse)
    v, u, outgoing, dots = second_part(
        scalars,
        coarse
        + (op_hi, op_lo, e_first, b_slot, b_rest, d_slot, d_peer, s_slot, s_peer)
        + pairs
        + (z, w, w_peer, v_rest, u_rest, hi_unit, lo_unit),
    )
    sums = exchange(outgoing, ALL_AXES)
    return tuple(combine(where, dots, sums, right_side, z, w, v, u))


def solution(mesh):
    placed = (
        P(None, ("grp", "sub", "chip")),
        P(("grp", "sub", "chip"), None, None),
        P(("grp", "sub", "chip"), None, None, None),
        P(("grp", "sub", "chip"), None),
        P(("grp", "sub", "chip"), None, None),
        P(("grp", "sub", "chip")),
        P("grp"),
        P("grp", None, None),
        P(),
    )
    return jax.shard_map(
        on_device,
        mesh=mesh,
        in_specs=placed,
        out_specs=(P(None, ("grp", "sub", "chip")), P(None, ("grp", "sub", "chip"))),
        check_vma=False,
    )
```
